32 devices in a mesh: groups: 2 (over y), dp: 8 (over z, x), tensor: 2 (over core).
Axes of the slice: x: 2, y: 2, z: 4, core: 2. Of those that a mesh axis runs over, the one named last changes fastest.
Arguments:
- saved_input: bfloat16 [2048, 5120], P(('groups', 'dp'), 'tensor'), parts along dimension 0, may hold values from -6 to 6
- saved_pre: bfloat16 [2048, 10240], P(('groups', 'dp'), 'tensor'), parts along dimension 0, may hold values from -8 to 8
- grad_act: bfloat16 [2048, 10240], P(('groups', 'dp'), 'tensor'), parts along dimension 0, may hold values from -6 to 6
Outputs:
- a_factor: float32 [2, 5120, 128], P('tensor', ('groups', 'dp')), parts along dimension 1
- g_factor: float32 [2, 10240, 128], P('tensor', ('groups', 'dp')), parts along dimension 1
The draws below stay inside these ranges and needn't reach their ends.
There are 2 independent parts, one for each index of `groups`. The reference program is written for one: setup_inputs(seed, part) draws one part's arguments, and reference() takes and returns one part's arrays. A program takes and returns all parts, laid end to end along the dimension named above; each array names one. Nothing has to cross between parts.
All inputs are finite; a program needn't handle non-finite values.
Results may differ from the reference program's by a relative error of at most 0.001.
The reference program's roundings to bfloat16 on the way (of `grad_pre`) count: a program that leaves them out, or rounds other values in their place, can miss the bound.
Values sent between devices are 32-bit elements; how exact they have to be, the bound alone decides.
No kernel may reach another device: no remote copies, remote signals or barrier semaphores. Data moves between devices by JAX's collectives and lax.ppermute only.
A program may use at most 64 MiB of HBM per device.

```python
import jax
import jax.numpy as jnp
from jax import lax

D = 5120
FFW = 10240
B = 128
TOKENS = 1024
N_TENSOR = 2


def level_of(own_key, extent, shards, least, largest):
    loudness, own = 1.0, jax.random.fold_in(own_key, 6)
    for dim, parts in shards:
        heights = jnp.exp(jax.random.uniform(jax.random.fold_in(own, dim), (parts,), jnp.float32, least / len(shards), largest / len(shards)))
        loudness = loudness * jnp.repeat(heights, extent[dim] // parts).reshape([-1 if axis == dim else 1 for axis in range(len(extent))])
    return loudness


def normal_values(own_key, dims, scale, bound, split=(), held_as=jnp.bfloat16):
    values = scale * jax.random.normal(own_key, dims, jnp.float32)
    if split:
        values = values * level_of(own_key, dims, split, -0.22, 0.18)
    return jnp.clip(values, -bound, bound).astype(held_as)


def setup_inputs(seed: int = 0, part: int = 0) -> dict:
    key_list = jax.random.split(jax.random.key(seed), 4)
    part_splits = jax.random.split(jax.random.fold_in(key_list[3], part), 4)
    saved_input = normal_values(part_splits[0], (TOKENS, D), 1.0, 6.0, ((0, 8), (1, 2)))
    saved_pre = normal_values(part_splits[1], (TOKENS, FFW), 1.5, 8.0, ((0, 8), (1, 2)))
    grad_act = normal_values(part_splits[2], (TOKENS, FFW), 1.0, 6.0, ((0, 8), (1, 2)))
    return dict(saved_input=saved_input, saved_pre=saved_pre, grad_act=grad_act)


def gelu_slope(value):
    return 0.5 * (1.0 + lax.erf(value * 0.7071067811865476)) + value * jnp.exp(-0.5 * value * value) * 0.3989422804014327

def block_cov(matrix):
    tokens, width = matrix.shape
    blocks = matrix.astype(jnp.float32).reshape(tokens, width // B, B)
    cov = jnp.einsum('tkb,tkc->kbc', blocks, blocks) / TOKENS
    return cov

def reference(saved_input, saved_pre, grad_act):
    slope = gelu_slope(saved_pre.astype(jnp.float32))
    grad_pre = (grad_act.astype(jnp.float32) * slope).astype(jnp.bfloat16)
    cov_a = block_cov(saved_input)
    cov_g = block_cov(grad_pre)
    trace_a = jnp.sum(jnp.diagonal(cov_a, axis1=1, axis2=2))
    trace_g = jnp.sum(jnp.diagonal(cov_g, axis1=1, axis2=2))
    ratio = jnp.sqrt(trace_a / D / (trace_g / FFW))
    unit = jnp.eye(B, dtype=jnp.float32)
    damp = jnp.sqrt(jnp.float32(0.1))
    a_factor = (cov_a + ratio * damp * unit).reshape(N_TENSOR, D // N_TENSOR, B)
    g_factor = (cov_g + damp / ratio * unit).reshape(N_TENSOR, FFW // N_TENSOR, B)
    return (a_factor, g_factor)
```

```python
import functools

import jax
import jax.numpy as jnp
from jax import lax
from jax.experimental import pallas as pl
from jax.experimental.pallas import tpu as pltpu
from jax.sharding import PartitionSpec as P

D = 5120
FFW = 10240
B = 128
H = B // 2
EDGE = 8


def gelu_slope(value):
    return (
        0.5 * (1.0 + lax.erf(value * 0.7071067811865476))
        + value * jnp.exp(-0.5 * value * value) * 0.3989422804014327
    )


def local_blocks(matrix, block, total):
    tokens, width = matrix.shape
    pieces = matrix.reshape(tokens, width // block, block)
    cov = jnp.einsum("tkb,tkc->kbc", pieces, pieces, preferred_element_type=jnp.float32)
    return cov.reshape(width, block) / total


def owned_unit(owned, block):
    count = owned.shape[0]
    rows = lax.axis_index("dp") * count + jnp.arange(count, dtype=jnp.int32)
    cols = jnp.arange(block, dtype=jnp.int32)
    return (cols[None, :] == (rows % block)[:, None]).astype(jnp.float32)


def plain(saved_input, saved_pre, grad_act):
    total = jnp.float32(saved_input.shape[0] * lax.axis_size("dp"))
    slope = gelu_slope(saved_pre.astype(jnp.float32))
    grad_pre = (grad_act.astype(jnp.float32) * slope).astype(jnp.bfloat16)
    terms_a = local_blocks(saved_input, B, total)
    terms_g = local_blocks(grad_pre, B, total)
    owned_a = lax.psum_scatter(terms_a, "dp", scatter_dimension=0, tiled=True)
    owned_g = lax.psum_scatter(terms_g, "dp", scatter_dimension=0, tiled=True)
    unit_a = owned_unit(owned_a, B)
    unit_g = owned_unit(owned_g, B)
    trace_a, trace_g = lax.psum(
        (jnp.sum(owned_a * unit_a), jnp.sum(owned_g * unit_g)), ("dp", "tensor")
    )
    ratio = jnp.sqrt(trace_a / D / (trace_g / FFW))
    damp = jnp.sqrt(jnp.float32(0.1))
    return (
        (owned_a + ratio * damp * unit_a)[None],
        (owned_g + damp / ratio * unit_g)[None],
    )


def split_rows(count):
    return count // B, (count % B) // H


def chunk_rows(count):
    full, half = split_rows(count)
    return (full + half) * H + EDGE


def iotas():
    shape = (H, B)
    return lax.broadcasted_iota(jnp.int32, shape, 0), lax.broadcasted_iota(jnp.int32, shape, 1)


def slot_mask(slot, order):
    bits = len(order)
    mask = 0
    for place, bit in enumerate(order):
        mask = mask + (((slot >> (bits - 1 - place)) & 1) << bit)
    return mask


def pack_chunk(read_block, odd, full, half, out_ref):
    row, col = iotas()
    low = col < row
    diag_low = col == row
    diag_high = col == row + H
    zero = jnp.zeros((H, B), jnp.float32)
    trace = zero

    def cov(block):
        piece = read_block(block)
        return lax.dot_general(
            piece, piece, (((0,), (0,)), ((), ())), preferred_element_type=jnp.float32
        )

    for i in range(full):
        block = cov((half * odd) * ((full + half)) + i if half else i)
        top, bottom = block[:H], block[H:]
        out_ref[0, i * H : (i + 1) * H, :] = jnp.where(low, pltpu.roll(bottom, H, 1), top)
        corner = jnp.where(diag_high, bottom, zero)
        out_ref[0, (full + half) * H + i : (full + half) * H + i + 1, :] = jnp.sum(
            corner, axis=0, keepdims=True
        )
        trace = trace + corner + jnp.where(diag_low, top, zero)
    if half:
        block = cov(full)
        piece = jnp.where(odd == 1, block[H:], block[:H])
        out_ref[0, full * H : (full + 1) * H, :] = piece
        trace = trace + jnp.where(col == row + odd * H, piece, zero)
    out_ref[0, (full + half) * H + full :, :] = jnp.zeros((EDGE - full, B), jnp.float32)
    return jnp.sum(trace, axis=0, keepdims=True)


def pack_body(order, first, full, half, slope, row_out, n_in, *refs):
    ins, (trace_in, out_ref, trace_ref) = refs[:n_in], refs[n_in:]
    step = pl.program_id(0)
    owner = lax.axis_index("dp") ^ slot_mask(first + step, order)
    odd = owner & 1

    def read_block(block):
        start = block * B
        if not isinstance(start, int):
            start = pl.multiple_of(start, B)
        part = pl.ds(start, B)
        if slope:
            value = ins[0][:, part].astype(jnp.float32)
            grad = ins[1][:, part].astype(jnp.float32)
            return (grad * gelu_slope(value)).astype(jnp.bfloat16)
        return ins[0][:, part]

    line = pack_chunk(read_block, odd, full, half, out_ref)

    @pl.when(step == 0)
    def _():
        trace_ref[...] = trace_in[...]

    trace_ref[row_out : row_out + 1, :] += line


def pack(arrays, order, first, slots, count, trace, row_out):
    full, half = split_rows(count)
    tokens = arrays[0].shape[0]
    span = (2 * full + 1) * B if half else full * B

    def in_map(step):
        owner = lax.axis_index("dp") ^ slot_mask(first + step, order)
        return 0, owner >> half

    rows = chunk_rows(count)
    n = len(arrays)
    return pl.pallas_call(
        functools.partial(pack_body, order, first, full, half, n == 2, row_out, n),
        grid=(slots,),
        in_specs=[pl.BlockSpec((tokens, span), in_map) for _ in arrays]
        + [pl.BlockSpec((EDGE, B), lambda step: (0, 0))],
        out_specs=[
            pl.BlockSpec((1, rows, B), lambda step: (step, 0, 0)),
            pl.BlockSpec((EDGE, B), lambda step: (0, 0)),
        ],
        out_shape=[
            jax.ShapeDtypeStruct((slots, rows, B), jnp.float32),
            jax.ShapeDtypeStruct((EDGE, B), jnp.float32),
        ],
        compiler_params=pltpu.CompilerParams(vmem_limit_bytes=32 * 2**20),
        cost_estimate=pl.CostEstimate(
            flops=slots * count * B * tokens * 2,
            bytes_accessed=slots * rows * B * 4 + n * slots * count * tokens * 2,
            transcendentals=0,
        ),
    )(*arrays, trace)


def unfold(own, recv, count, odd, shift, total, out_ref):
    full, half = split_rows(count)
    row, col = iotas()
    edge = (full + half) * H
    unit_low = jnp.where(col == row, shift, 0.0)
    unit_high = jnp.where(col == row + H, shift, 0.0)
    for i in range(full):
        part = slice(i * H, (i + 1) * H)
        folded = (own[0, part, :] + recv[0, part, :]) / total
        corner = (own[0, edge + i : edge + i + 1, :] + recv[0, edge + i : edge + i + 1, :]) / total
        turned = jnp.concatenate([folded, folded], axis=0).T
        top = jnp.where(col < row, turned[:H], folded) + unit_low
        last = pltpu.roll(jnp.where(col < row, folded, turned[:H]), H, 1)
        bottom = jnp.where(col < H, turned[H:], jnp.where(col == row + H, corner, last)) + unit_high
        start = i * B + odd * H if half else i * B
        if half:
            start = pl.multiple_of(start, H)
        out_ref[pl.ds(start, H), :] = top
        out_ref[pl.ds(start + H, H), :] = bottom
    if half:
        part = slice(full * H, (full + 1) * H)
        piece = (own[0, part, :] + recv[0, part, :]) / total
        start = pl.multiple_of((1 - odd) * full * B, H)
        out_ref[pl.ds(start, H), :] = piece + jnp.where(col == row + odd * H, shift, 0.0)


def finish_body(count_a, count_g, total, n_traces, *refs):
    traces, (own_a, recv_a, own_g, recv_g, a_ref, g_ref) = refs[:n_traces], refs[n_traces:]
    odd = lax.axis_index("dp") & 1
    tile = traces[0][...]
    for other in traces[1:]:
        tile = tile + other[...]
    sums = jnp.sum(tile, axis=1, keepdims=True) / total
    ratio = jnp.sqrt(sums[0:1] / D / (sums[1:2] / FFW))
    damp = jnp.sqrt(jnp.full((1, 1), 0.1, jnp.float32))
    unfold(own_a, recv_a, count_a, odd, ratio * damp, total, a_ref)
    unfold(own_g, recv_g, count_g, odd, damp / ratio, total, g_ref)


def finish(traces, own_a, recv_a, own_g, recv_g, count_a, count_g, total):
    args = (*traces, own_a, recv_a, own_g, recv_g)
    return pl.pallas_call(
        functools.partial(finish_body, count_a, count_g, total, len(traces)),
        in_specs=[pl.BlockSpec(memory_space=pltpu.VMEM)] * len(args),
        out_specs=[pl.BlockSpec(memory_space=pltpu.VMEM)] * 2,
        out_shape=[
            jax.ShapeDtypeStruct((count_a, B), jnp.float32),
            jax.ShapeDtypeStruct((count_g, B), jnp.float32),
        ],
        compiler_params=pltpu.CompilerParams(vmem_limit_bytes=32 * 2**20),
    )(*args)


def swap(value, mask):
    dp, tensor = lax.axis_size("dp"), lax.axis_size("tensor")
    dp_mask, tensor_mask = mask
    if tensor_mask == 0:
        return lax.ppermute(value, "dp", [(i, i ^ dp_mask) for i in range(dp)])
    pairs = [
        (i * tensor + j, (i ^ dp_mask) * tensor + (j ^ tensor_mask))
        for i in range(dp)
        for j in range(tensor)
    ]
    return lax.ppermute(value, ("dp", "tensor"), pairs)


def halve(keep, got):
    half = keep.shape[0] // 2
    return keep[:half] + got[:half], keep[half:] + got[half:]


def packed(saved_input, saved_pre, grad_act):
    dp = lax.axis_size("dp")
    total = float(saved_input.shape[0] * dp)
    count_a = saved_input.shape[1] // dp
    count_g = saved_pre.shape[1] // dp
    order_a, order_g = (0, 1, 2), (1, 0, 2)
    half = dp // 2
    blank = jnp.zeros((EDGE, B), jnp.float32)

    send_a, trace = pack((saved_input,), order_a, half, half, count_a, blank, 0)
    got_a = swap(send_a, (1 << order_a[0], 0))
    send_g, trace = pack((saved_pre, grad_act), order_g, half, half, count_g, trace, 1)
    got_g = swap(send_g, (1 << order_g[0], 0))
    keep_a, trace = pack((saved_input,), order_a, 0, half, count_a, trace, 0)
    keep_g, trace = pack((saved_pre, grad_act), order_g, 0, half, count_g, trace, 1)

    keep_a, send_a = halve(keep_a, got_a)
    got_a = swap(send_a, (1 << order_a[1], 0))
    keep_g, send_g = halve(keep_g, got_g)
    got_g = swap(send_g, (1 << order_g[1], 0))
    trace = trace + swap(trace, (1, 0)) + swap(trace, (0, 1)) + swap(trace, (1, 1))

    keep_a, send_a = halve(keep_a, got_a)
    got_a = swap(send_a, (1 << order_a[2], 0))
    keep_g, send_g = halve(keep_g, got_g)
    got_g = swap(send_g, (1 << order_g[2], 0))
    traces = (trace, swap(trace, (2, 0)), swap(trace, (4, 0)), swap(trace, (6, 0)))

    a_factor, g_factor = finish(traces, keep_a, got_a, keep_g, got_g, count_a, count_g, total)
    return a_factor[None], g_factor[None]


def fits(count):
    return count % H == 0 and count // B <= EDGE


def on_device(saved_input, saved_pre, grad_act):
    dp = lax.axis_size("dp")
    count_a = saved_input.shape[1] // dp
    count_g = saved_pre.shape[1] // dp
    if dp == 8 and lax.axis_size("tensor") == 2 and fits(count_a) and fits(count_g):
        return packed(saved_input, saved_pre, grad_act)
    return plain(saved_input, saved_pre, grad_act)


def solution(mesh):
    spec = P(("groups", "dp"), "tensor")
    out = P("tensor", ("groups", "dp"), None)
    return jax.shard_map(
        on_device, mesh=mesh, in_specs=(spec, spec, spec), out_specs=(out, out), check_vma=False
    )
```

```python
import functools

import jax
import jax.numpy as jnp
from jax import lax
from jax.experimental import pallas as pl
from jax.experimental.pallas import tpu as pltpu
from jax.sharding import PartitionSpec as P

D = 5120
FFW = 10240
B = 128
H = B // 2
EDGE = 8


def gelu_slope(value):
    return (
        0.5 * (1.0 + lax.erf(value * 0.7071067811865476))
        + value * jnp.exp(-0.5 * value * value) * 0.3989422804014327
    )


def local_blocks(matrix, block, total):
    tokens, width = matrix.shape
    pieces = matrix.reshape(tokens, width // block, block)
    cov = jnp.einsum("tkb,tkc->kbc", pieces, pieces, preferred_element_type=jnp.float32)
    return cov.reshape(width, block) / total


def owned_unit(owned, block):
    count = owned.shape[0]
    rows = lax.axis_index("dp") * count + jnp.arange(count, dtype=jnp.int32)
    cols = jnp.arange(block, dtype=jnp.int32)
    return (cols[None, :] == (rows % block)[:, None]).astype(jnp.float32)


def plain(saved_input, saved_pre, grad_act):
    total = jnp.float32(saved_input.shape[0] * lax.axis_size("dp"))
    slope = gelu_slope(saved_pre.astype(jnp.float32))
    grad_pre = (grad_act.astype(jnp.float32) * slope).astype(jnp.bfloat16)
    terms_a = local_blocks(saved_input, B, total)
    terms_g = local_blocks(grad_pre, B, total)
    owned_a = lax.psum_scatter(terms_a, "dp", scatter_dimension=0, tiled=True)
    owned_g = lax.psum_scatter(terms_g, "dp", scatter_dimension=0, tiled=True)
    unit_a = owned_unit(owned_a, B)
    unit_g = owned_unit(owned_g, B)
    trace_a, trace_g = lax.psum(
        (jnp.sum(owned_a * unit_a), jnp.sum(owned_g * unit_g)), ("dp", "tensor")
    )
    ratio = jnp.sqrt(trace_a / D / (trace_g / FFW))
    damp = jnp.sqrt(jnp.float32(0.1))
    return (
        (owned_a + ratio * damp * unit_a)[None],
        (owned_g + damp / ratio * unit_g)[None],
    )


def split_rows(count):
    return count // B, (count % B) // H


def piece_rows(piece):
    a_blocks, a_half, g_blocks, _ = piece
    return (len(a_blocks) + a_half + len(g_blocks)) * H + EDGE


def iotas():
    shape = (H, B)
    return lax.broadcasted_iota(jnp.int32, shape, 0), lax.broadcasted_iota(jnp.int32, shape, 1)


def slot_owner(slot, turn):
    flip = lax.axis_index("tensor") ^ turn
    high, middle, low = (slot >> 2) & 1, (slot >> 1) & 1, slot & 1
    mask = (high << flip) | (middle << (1 - flip)) | (low << 2)
    return lax.axis_index("dp") ^ mask


def lanes(start, size):
    return pl.ds(start if isinstance(start, int) else pl.multiple_of(start, B), size)


def pack_body(pieces, first, slots, count_a, count_g, *refs):
    n = len(pieces)
    a_hbm, pre_hbm, grad_hbm, trace_in = refs[:4]
    outs, trace_ref = refs[4 : 4 + n], refs[4 + n]
    buffers, sems = refs[5 + n : 5 + 4 * n], refs[5 + 4 * n]
    full, half = split_rows(count_a)
    row, col = iotas()
    low = col < row
    diag_low, diag_high = col == row, col == row + H
    zero = jnp.zeros((H, B), jnp.float32)

    def copies(i, slot):
        a_blocks, a_half, g_blocks, turn = pieces[i]
        a_buf, pre_buf, grad_buf = buffers[3 * i : 3 * i + 3]
        owner = slot_owner(first + slot, turn)
        found = []
        if a_blocks:
            start = owner * full * B if not half else (owner >> 1) * (2 * full + 1) * B + (owner & 1) * full * B
            found.append(
                pltpu.make_async_copy(
                    a_hbm.at[:, lanes(start, a_buf.shape[2])], a_buf.at[slot], sems.at[i, slot, 0]
                )
            )
        if g_blocks:
            start = owner * count_g + g_blocks[0] * B
            size = len(g_blocks) * B
            for k, (src, dst) in enumerate(((pre_hbm, pre_buf), (grad_hbm, grad_buf))):
                found.append(
                    pltpu.make_async_copy(
                        src.at[:, lanes(start, size)], dst.at[slot], sems.at[i, slot, 1 + k]
                    )
                )
        return found

    def cov(part):
        return lax.dot_general(
            part, part, (((0,), (0,)), ((), ())), preferred_element_type=jnp.float32
        )

    places = [(i, slot) for i in range(n) for slot in range(slots)]
    for place in places:
        for copy in copies(*place):
            copy.start()

    trace_a, trace_g = zero, zero
    for i, slot in places:
        a_blocks, a_half, g_blocks, turn = pieces[i]
        a_buf, pre_buf, grad_buf = buffers[3 * i : 3 * i + 3]
        out = outs[i]
        odd = slot_owner(first + slot, turn) & 1
        edge = piece_rows(pieces[i]) - EDGE
        for copy in copies(i, slot):
            copy.wait()
        at = 0
        corners = 0

        def fold(block):
            nonlocal at, corners
            top, bottom = block[:H], block[H:]
            out[slot, at * H : (at + 1) * H, :] = jnp.where(low, pltpu.roll(bottom, H, 1), top)
            corner = jnp.where(diag_high, bottom, zero)
            out[slot, edge + corners : edge + corners + 1, :] = jnp.sum(
                corner, axis=0, keepdims=True
            )
            at, corners = at + 1, corners + 1
            return corner + jnp.where(diag_low, top, zero)

        for b in a_blocks:
            place = (b + odd * half) * B
            trace_a = trace_a + fold(cov(a_buf[slot, :, lanes(place, B)]))
        if a_half:
            place = (1 - odd) * full * B
            block = cov(a_buf[slot, :, lanes(place, B)])
            part = jnp.where(odd == 1, block[H:], block[:H])
            out[slot, at * H : (at + 1) * H, :] = part
            trace_a = trace_a + jnp.where(col == row + odd * H, part, zero)
            at = at + 1
        for k in range(len(g_blocks)):
            here = slice(k * B, (k + 1) * B)
            value = pre_buf[slot, :, here].astype(jnp.float32)
            grad = grad_buf[slot, :, here].astype(jnp.float32)
            trace_g = trace_g + fold(cov((grad * gelu_slope(value)).astype(jnp.bfloat16)))
        out[slot, edge + corners :, :] = jnp.zeros((EDGE - corners, B), jnp.float32)

    trace_ref[...] = trace_in[...]
    trace_ref[0:1, :] += jnp.sum(trace_a, axis=0, keepdims=True)
    trace_ref[1:2, :] += jnp.sum(trace_g, axis=0, keepdims=True)


def pack(arrays, pieces, first, slots, count_a, count_g, trace):
    full, half = split_rows(count_a)
    tokens = arrays[0].shape[0]
    dtype = arrays[0].dtype
    scratch = []
    for a_blocks, _, g_blocks, _ in pieces:
        scratch.append(pltpu.VMEM((slots, tokens, (full + half) * B if a_blocks else B), dtype))
        for _ in range(2):
            scratch.append(pltpu.VMEM((slots, tokens, max(len(g_blocks), 1) * B), dtype))
    *chunks, trace = pl.pallas_call(
        functools.partial(pack_body, pieces, first, slots, count_a, count_g),
        in_specs=[pl.BlockSpec(memory_space=pltpu.HBM)] * 3
        + [pl.BlockSpec(memory_space=pltpu.VMEM)],
        out_specs=[pl.BlockSpec(memory_space=pltpu.VMEM)] * (len(pieces) + 1),
        out_shape=[
            jax.ShapeDtypeStruct((slots, piece_rows(piece), B), jnp.float32) for piece in pieces
        ]
        + [jax.ShapeDtypeStruct((EDGE, B), jnp.float32)],
        scratch_shapes=scratch + [pltpu.SemaphoreType.DMA((len(pieces), slots, 3))],
        compiler_params=pltpu.CompilerParams(vmem_limit_bytes=32 * 2**20),
        cost_estimate=pl.CostEstimate(flops=1, bytes_accessed=1, transcendentals=0),
    )(*arrays, trace)
    return chunks, trace


def finish_body(pieces, count_a, total, *refs):
    n = len(pieces)
    trace_ref, owns, gots = refs[0], refs[1 : 1 + n], refs[1 + n : 1 + 2 * n]
    a_ref, g_ref = refs[1 + 2 * n :]
    full, half = split_rows(count_a)
    odd = lax.axis_index("dp") & 1
    row, col = iotas()

    sums = trace_ref[...] + gots[-1][0, -2:, :]
    sums = jnp.sum(sums, axis=1, keepdims=True) / total
    ratio = jnp.sqrt(sums[0:1] / D / (sums[1:2] / FFW))
    damp = jnp.sqrt(jnp.full((1, 1), 0.1, jnp.float32))
    shift_a, shift_g = ratio * damp, damp / ratio

    def unfold(own, got, at, corner_row, shift, out, start):
        part = slice(at * H, (at + 1) * H)
        here = slice(corner_row, corner_row + 1)
        folded = (own[0, part, :] + got[0, part, :]) / total
        corner = (own[0, here, :] + got[0, here, :]) / total
        turned = jnp.concatenate([folded, folded], axis=0).T
        top = jnp.where(col < row, turned[:H], folded)
        last = pltpu.roll(jnp.where(col < row, folded, turned[:H]), H, 1)
        bottom = jnp.where(col < H, turned[H:], jnp.where(col == row + H, corner, last))
        out[pl.ds(start, H), :] = top + jnp.where(col == row, shift, 0.0)
        out[pl.ds(start + H, H), :] = bottom + jnp.where(col == row + H, shift, 0.0)

    for piece, own, got in zip(pieces, owns, gots):
        a_blocks, a_half, g_blocks, _ = piece
        at, corner = 0, piece_rows(piece) - EDGE
        for b in a_blocks:
            start = pl.multiple_of(b * B + odd * H, H) if half else b * B
            unfold(own, got, at, corner, shift_a, a_ref, start)
            at, corner = at + 1, corner + 1
        if a_half:
            part = slice(at * H, (at + 1) * H)
            value = (own[0, part, :] + got[0, part, :]) / total
            start = pl.multiple_of((1 - odd) * full * B, H)
            a_ref[pl.ds(start, H), :] = value + jnp.where(col == row + odd * H, shift_a, 0.0)
            at = at + 1
        for b in g_blocks:
            unfold(own, got, at, corner, shift_g, g_ref, b * B)
            at, corner = at + 1, corner + 1


def finish(pieces, trace, owns, gots, count_a, count_g, total):
    args = (trace, *owns, *gots)
    return pl.pallas_call(
        functools.partial(finish_body, pieces, count_a, total),
        in_specs=[pl.BlockSpec(memory_space=pltpu.VMEM)] * len(args),
        out_specs=[pl.BlockSpec(memory_space=pltpu.VMEM)] * 2,
        out_shape=[
            jax.ShapeDtypeStruct((count_a, B), jnp.float32),
            jax.ShapeDtypeStruct((count_g, B), jnp.float32),
        ],
        compiler_params=pltpu.CompilerParams(vmem_limit_bytes=32 * 2**20),
    )(*args)


def swap(value, partner):
    dp, tensor = lax.axis_size("dp"), lax.axis_size("tensor")
    pairs = []
    for i in range(dp):
        for j in range(tensor):
            other = partner(i, j)
            pairs.append((i * tensor + j, other[0] * tensor + other[1]))
    return lax.ppermute(value, ("dp", "tensor"), pairs)


def along(stage, turn):
    if stage == 2:
        return lambda i, j: (i ^ 4, j)
    return lambda i, j: (i ^ (1 << (j ^ turn ^ stage)), j)


def halve(keep, got):
    half = keep.shape[0] // 2
    return keep[:half] + got[:half], keep[half:] + got[half:]


def with_trace(send, trace):
    return lax.dynamic_update_slice(send, trace[None], (0, send.shape[1] - 2, 0))


def packed(saved_input, saved_pre, grad_act):
    dp = lax.axis_size("dp")
    total = float(saved_input.shape[0] * dp)
    count_a = saved_input.shape[1] // dp
    count_g = saved_pre.shape[1] // dp
    arrays = tuple(
        pltpu.with_memory_space_constraint(array, pltpu.HBM)
        for array in (saved_input, saved_pre, grad_act)
    )
    full_a, half_a = split_rows(count_a)
    full_g, _ = split_rows(count_g)
    pieces = (
        (tuple(range(full_a)), half_a, (0,), 0),
        ((), 0, tuple(range(1, full_g)), 1),
    )
    half = dp // 2
    blank = jnp.zeros((EDGE, B), jnp.float32)

    (send_p,), trace = pack(arrays, pieces[:1], half, half, count_a, count_g, blank)
    got_p = swap(send_p, along(0, 0))
    (send_q,), trace = pack(arrays, pieces[1:], half, half, count_a, count_g, trace)
    got_q = swap(send_q, along(0, 1))
    (keep_p, keep_q), trace = pack(arrays, pieces, 0, half, count_a, count_g, trace)
    trace = trace[:2] + swap(trace, lambda i, j: (i, j ^ 1))[:2]

    keep_p, send_p = halve(keep_p, got_p)
    got_p = swap(with_trace(send_p, trace), along(1, 0))
    trace = trace + got_p[0, -2:, :]
    keep_q, send_q = halve(keep_q, got_q)
    got_q = swap(with_trace(send_q, trace), along(1, 1))
    trace = trace + got_q[0, -2:, :]

    keep_p, send_p = halve(keep_p, got_p)
    got_p = swap(send_p, along(2, 0))
    keep_q, send_q = halve(keep_q, got_q)
    got_q = swap(with_trace(send_q, trace), along(2, 1))

    a_factor, g_factor = finish(
        pieces, trace, (keep_p, keep_q), (got_p, got_q), count_a, count_g, total
    )
    return a_factor[None], g_factor[None]


def fits(count_a, count_g):
    return count_a % H == 0 and 0 < count_a // B <= EDGE - 3 and count_g % B == 0 and 1 < count_g // B <= EDGE - 1


def on_device(saved_input, saved_pre, grad_act):
    dp = lax.axis_size("dp")
    count_a = saved_input.shape[1] // dp
    count_g = saved_pre.shape[1] // dp
    if dp == 8 and lax.axis_size("tensor") == 2 and fits(count_a, count_g):
        return packed(saved_input, saved_pre, grad_act)
    return plain(saved_input, saved_pre, grad_act)


def solution(mesh):
    spec = P(("groups", "dp"), "tensor")
    out = P("tensor", ("groups", "dp"), None)
    return jax.shard_map(
        on_device, mesh=mesh, in_specs=(spec, spec, spec), out_specs=(out, out), check_vma=False
    )
```

```python
import functools

import jax
import jax.numpy as jnp
from jax import lax
from jax.experimental import pallas as pl
from jax.experimental.pallas import tpu as pltpu
from jax.sharding import PartitionSpec as P

D = 5120
FFW = 10240
B = 128
H = B // 2
EDGE = 8


def gelu_slope(value):
    return (
        0.5 * (1.0 + lax.erf(value * 0.7071067811865476))
        + value * jnp.exp(-0.5 * value * value) * 0.3989422804014327
    )


def local_blocks(matrix, block, total):
    tokens, width = matrix.shape
    pieces = matrix.reshape(tokens, width // block, block)
    cov = jnp.einsum("tkb,tkc->kbc", pieces, pieces, preferred_element_type=jnp.float32)
    return cov.reshape(width, block) / total


def owned_unit(owned, block):
    count = owned.shape[0]
    rows = lax.axis_index("dp") * count + jnp.arange(count, dtype=jnp.int32)
    cols = jnp.arange(block, dtype=jnp.int32)
    return (cols[None, :] == (rows % block)[:, None]).astype(jnp.float32)


def plain(saved_input, saved_pre, grad_act):
    total = jnp.float32(saved_input.shape[0] * lax.axis_size("dp"))
    slope = gelu_slope(saved_pre.astype(jnp.float32))
    grad_pre = (grad_act.astype(jnp.float32) * slope).astype(jnp.bfloat16)
    terms_a = local_blocks(saved_input, B, total)
    terms_g = local_blocks(grad_pre, B, total)
    owned_a = lax.psum_scatter(terms_a, "dp", scatter_dimension=0, tiled=True)
    owned_g = lax.psum_scatter(terms_g, "dp", scatter_dimension=0, tiled=True)
    unit_a = owned_unit(owned_a, B)
    unit_g = owned_unit(owned_g, B)
    trace_a, trace_g = lax.psum(
        (jnp.sum(owned_a * unit_a), jnp.sum(owned_g * unit_g)), ("dp", "tensor")
    )
    ratio = jnp.sqrt(trace_a / D / (trace_g / FFW))
    damp = jnp.sqrt(jnp.float32(0.1))
    return (
        (owned_a + ratio * damp * unit_a)[None],
        (owned_g + damp / ratio * unit_g)[None],
    )


def split_rows(count):
    return count // B, (count % B) // H


def piece_rows(piece):
    a_blocks, a_half, g_blocks, _ = piece
    edge = (len(a_blocks) + a_half + len(g_blocks)) * H
    return edge + (EDGE if a_blocks or a_half else len(g_blocks) + 2), edge


def iotas():
    shape = (H, B)
    return lax.broadcasted_iota(jnp.int32, shape, 0), lax.broadcasted_iota(jnp.int32, shape, 1)


def slot_owner(slot, orders):
    core = lax.axis_index("tensor")
    mask = 0
    for stage, (one, other) in enumerate(zip(*orders)):
        mask = mask | (((slot >> (2 - stage)) & 1) << (one + core * (other - one)))
    return lax.axis_index("dp") ^ mask


def lanes(start, size):
    return pl.ds(start if isinstance(start, int) else pl.multiple_of(start, B), size)


def pack_body(pieces, first, slots, count_a, count_g, *refs):
    n = len(pieces)
    a_hbm, pre_hbm, grad_hbm, trace_in = refs[:4]
    outs, trace_ref = refs[4 : 4 + n], refs[4 + n]
    buffers, sems = refs[5 + n : 5 + 5 * n], refs[5 + 5 * n]
    full, half = split_rows(count_a)
    row, col = iotas()
    low = col < row
    diag_low, diag_high = col == row, col == row + H
    zero = jnp.zeros((H, B), jnp.float32)

    def copies(i, slot):
        a_blocks, a_half, g_blocks, orders = pieces[i]
        a_buf, half_buf, pre_buf, grad_buf = buffers[4 * i : 4 * i + 4]
        owner = slot_owner(first + slot, orders)
        odd = owner & half
        base = (owner >> half) * (full * (1 + half) + half) * B
        moves = []
        if a_blocks:
            start = base + odd * (full + 1) * B + a_blocks[0] * B
            moves.append((a_hbm, start, a_buf))
        if a_half:
            moves.append((a_hbm, base + full * B, half_buf))
        if g_blocks:
            start = owner * count_g + g_blocks[0] * B
            moves += [(pre_hbm, start, pre_buf), (grad_hbm, start, grad_buf)]
        return [
            pltpu.make_async_copy(
                src.at[:, lanes(start, dst.shape[2])], dst.at[slot], sems.at[i, slot, k]
            )
            for k, (src, start, dst) in enumerate(moves)
        ]

    def cov(part):
        return lax.dot_general(
            part, part, (((0,), (0,)), ((), ())), preferred_element_type=jnp.float32
        )

    places = [(i, slot) for i in range(n) for slot in range(slots)]
    for place in places:
        for copy in copies(*place):
            copy.start()

    trace_a, trace_g = zero, zero
    for i, slot in places:
        a_blocks, a_half, g_blocks, orders = pieces[i]
        a_buf, half_buf, pre_buf, grad_buf = buffers[4 * i : 4 * i + 4]
        out = outs[i]
        odd = slot_owner(first + slot, orders) & half
        rows, edge = piece_rows(pieces[i])
        for copy in copies(i, slot):
            copy.wait()
        at = 0
        corners = 0

        def fold(block):
            nonlocal at, corners
            top, bottom = block[:H], block[H:]
            out[slot, at * H : (at + 1) * H, :] = jnp.where(low, pltpu.roll(bottom, H, 1), top)
            corner = jnp.where(diag_high, bottom, zero)
            out[slot, edge + corners : edge + corners + 1, :] = jnp.sum(
                corner, axis=0, keepdims=True
            )
            at, corners = at + 1, corners + 1
            return corner + jnp.where(diag_low, top, zero)

        for k in range(len(a_blocks)):
            trace_a = trace_a + fold(cov(a_buf[slot, :, k * B : (k + 1) * B]))
        if a_half:
            block = cov(half_buf[slot])
            part = jnp.where(odd == 1, block[H:], block[:H])
            out[slot, at * H : (at + 1) * H, :] = part
            trace_a = trace_a + jnp.where(col == row + odd * H, part, zero)
            at = at + 1
        for k in range(len(g_blocks)):
            here = slice(k * B, (k + 1) * B)
            value = pre_buf[slot, :, here].astype(jnp.float32)
            grad = grad_buf[slot, :, here].astype(jnp.float32)
            trace_g = trace_g + fold(cov((grad * gelu_slope(value)).astype(jnp.bfloat16)))
        out[slot, edge + corners :, :] = jnp.zeros((rows - edge - corners, B), jnp.float32)

    trace_ref[...] = trace_in[...]
    trace_ref[0:1, :] += jnp.sum(trace_a, axis=0, keepdims=True)
    trace_ref[1:2, :] += jnp.sum(trace_g, axis=0, keepdims=True)


def pack(arrays, pieces, first, slots, count_a, count_g, trace):
    tokens, dtype = arrays[0].shape[0], arrays[0].dtype
    scratch = [
        pltpu.VMEM((slots, tokens, max(size, 1) * B), dtype)
        for a_blocks, _, g_blocks, _ in pieces
        for size in (len(a_blocks), 1, len(g_blocks), len(g_blocks))
    ]
    *chunks, trace = pl.pallas_call(
        functools.partial(pack_body, pieces, first, slots, count_a, count_g),
        in_specs=[pl.BlockSpec(memory_space=pltpu.HBM)] * 3
        + [pl.BlockSpec(memory_space=pltpu.VMEM)],
        out_specs=[pl.BlockSpec(memory_space=pltpu.VMEM)] * (len(pieces) + 1),
        out_shape=[
            jax.ShapeDtypeStruct((slots, piece_rows(piece)[0], B), jnp.float32) for piece in pieces
        ]
        + [jax.ShapeDtypeStruct((EDGE, B), jnp.float32)],
        scratch_shapes=scratch + [pltpu.SemaphoreType.DMA((len(pieces), slots, 4))],
        compiler_params=pltpu.CompilerParams(vmem_limit_bytes=32 * 2**20),
        cost_estimate=pl.CostEstimate(flops=1, bytes_accessed=1, transcendentals=0),
    )(*arrays, trace)
    return chunks, trace


def finish_body(pieces, n_traces, count_a, total, *refs):
    n = len(pieces)
    traces, refs = refs[:n_traces], refs[n_traces:]
    owns, gots, (a_ref, g_ref) = refs[:n], refs[n : 2 * n], refs[2 * n :]
    full, half = split_rows(count_a)
    odd = lax.axis_index("dp") & half
    row, col = iotas()

    sums = sum((trace[...] for trace in traces[1:]), traces[0][...])
    sums = jnp.sum(sums, axis=1, keepdims=True) / total
    ratio = jnp.sqrt(sums[0:1] / D / (sums[1:2] / FFW))
    damp = jnp.sqrt(jnp.full((1, 1), 0.1, jnp.float32))
    shift_a, shift_g = ratio * damp, damp / ratio

    def unfold(own, got, at, corner_row, shift, out, start):
        part = slice(at * H, (at + 1) * H)
        here = slice(corner_row, corner_row + 1)
        folded = (own[0, part, :] + got[0, part, :]) / total
        corner = (own[0, here, :] + got[0, here, :]) / total
        turned = jnp.concatenate([folded, folded], axis=0).T
        top = jnp.where(col < row, turned[:H], folded)
        last = pltpu.roll(jnp.where(col < row, folded, turned[:H]), H, 1)
        bottom = jnp.where(col < H, turned[H:], jnp.where(col == row + H, corner, last))
        out[pl.ds(start, H), :] = top + jnp.where(col == row, shift, 0.0)
        out[pl.ds(start + H, H), :] = bottom + jnp.where(col == row + H, shift, 0.0)

    for piece, own, got in zip(pieces, owns, gots):
        a_blocks, a_half, g_blocks, _ = piece
        at, corner = 0, piece_rows(piece)[1]
        for b in a_blocks:
            start = pl.multiple_of(b * B + odd * H, H) if half else b * B
            unfold(own, got, at, corner, shift_a, a_ref, start)
            at, corner = at + 1, corner + 1
        if a_half:
            part = slice(at * H, (at + 1) * H)
            value = (own[0, part, :] + got[0, part, :]) / total
            start = pl.multiple_of((1 - odd) * full * B, H)
            a_ref[pl.ds(start, H), :] = value + jnp.where(col == row + odd * H, shift_a, 0.0)
            at = at + 1
        for b in g_blocks:
            unfold(own, got, at, corner, shift_g, g_ref, b * B)
            at, corner = at + 1, corner + 1


def finish(pieces, traces, owns, gots, count_a, count_g, total):
    args = (*traces, *owns, *gots)
    return pl.pallas_call(
        functools.partial(finish_body, pieces, len(traces), count_a, total),
        in_specs=[pl.BlockSpec(memory_space=pltpu.VMEM)] * len(args),
        out_specs=[pl.BlockSpec(memory_space=pltpu.VMEM)] * 2,
        out_shape=[
            jax.ShapeDtypeStruct((count_a, B), jnp.float32),
            jax.ShapeDtypeStruct((count_g, B), jnp.float32),
        ],
        compiler_params=pltpu.CompilerParams(vmem_limit_bytes=32 * 2**20),
    )(*args)


def swap(value, partner):
    dp, tensor = lax.axis_size("dp"), lax.axis_size("tensor")
    pairs = []
    for i in range(dp):
        for j in range(tensor):
            other = partner(i, j)
            pairs.append((i * tensor + j, other[0] * tensor + other[1]))
    return lax.ppermute(value, ("dp", "tensor"), pairs)


def along(stage, orders):
    return lambda i, j: (i ^ (1 << orders[j][stage]), j)


def halve(keep, got):
    half = keep.shape[0] // 2
    return keep[:half] + got[:half], keep[half:] + got[half:]


def with_trace(send, trace):
    return lax.dynamic_update_slice(send, trace[None], (0, send.shape[1] - 2, 0))


def cut(count_a, count_g):
    full_a, half_a = split_rows(count_a)
    full_g, _ = split_rows(count_g)
    some = full_g // 2
    x, near, far = 0, 1, 2
    return (
        (tuple(range(full_a)), 0, (), ((near, x, far), (far, x, near))),
        ((), half_a, tuple(range(some)), ((x, near, far), (x, far, near))),
        ((), 0, tuple(range(some, full_g)), ((far, x, near), (near, x, far))),
    )


def packed(saved_input, saved_pre, grad_act):
    dp = lax.axis_size("dp")
    total = float(saved_input.shape[0] * dp)
    count_a = saved_input.shape[1] // dp
    count_g = saved_pre.shape[1] // dp
    arrays = tuple(
        pltpu.with_memory_space_constraint(array, pltpu.HBM)
        for array in (saved_input, saved_pre, grad_act)
    )
    half = dp // 2
    pieces = cut(count_a, count_g)
    chunks = range(len(pieces))

    trace = jnp.zeros((EDGE, B), jnp.float32)
    gots = []
    for part in (pieces[:1], pieces[1:]):
        sends, trace = pack(arrays, part, half, half, count_a, count_g, trace)
        gots += [swap(send, along(0, piece[3])) for send, piece in zip(sends, part)]
    keeps, trace = pack(arrays, pieces, 0, half, count_a, count_g, trace)

    trace = trace[:2] + swap(trace, lambda i, j: (i, j ^ 1))[:2]
    last = len(pieces) - 1
    carriers = ((0, 1), (0, 2), (last, 2))
    for stage in (1, 2):
        for k in chunks:
            keeps[k], send = halve(keeps[k], gots[k])
            if (k, stage) in carriers:
                if (k, stage) != carriers[0]:
                    trace = trace + news
                send = with_trace(send, trace)
            gots[k] = swap(send, along(stage, pieces[k][3]))
            if (k, stage) in carriers:
                news = gots[k][0, -2:, :]

    a_factor, g_factor = finish(pieces, (trace, news), keeps, gots, count_a, count_g, total)
    return a_factor[None], g_factor[None]


def fits(count_a, count_g):
    whole_a, whole_g = count_a // B, count_g // B
    return count_a % H == 0 and 0 < whole_a < EDGE - 1 and count_g % B == 0 and 1 < whole_g < EDGE


def on_device(saved_input, saved_pre, grad_act):
    dp = lax.axis_size("dp")
    count_a = saved_input.shape[1] // dp
    count_g = saved_pre.shape[1] // dp
    if dp == 8 and lax.axis_size("tensor") == 2 and fits(count_a, count_g):
        return packed(saved_input, saved_pre, grad_act)
    return plain(saved_input, saved_pre, grad_act)


def solution(mesh):
    spec = P(("groups", "dp"), "tensor")
    out = P("tensor", ("groups", "dp"), None)
    return jax.shard_map(
        on_device, mesh=mesh, in_specs=(spec, spec, spec), out_specs=(out, out), check_vma=False
    )
```

```python
import functools

import jax
import jax.numpy as jnp
from jax import lax
from jax.experimental import pallas as pl
from jax.experimental.pallas import tpu as pltpu
from jax.sharding import PartitionSpec as P

D = 5120
FFW = 10240
B = 128
H = B // 2
EDGE = 8


def gelu_slope(value):
    return (
        0.5 * (1.0 + lax.erf(value * 0.7071067811865476))
        + value * jnp.exp(-0.5 * value * value) * 0.3989422804014327
    )


def local_blocks(matrix, block, total):
    tokens, width = matrix.shape
    pieces = matrix.reshape(tokens, width // block, block)
    cov = jnp.einsum("tkb,tkc->kbc", pieces, pieces, preferred_element_type=jnp.float32)
    return cov.reshape(width, block) / total


def owned_unit(owned, block):
    count = owned.shape[0]
    rows = lax.axis_index("dp") * count + jnp.arange(count, dtype=jnp.int32)
    cols = jnp.arange(block, dtype=jnp.int32)
    return (cols[None, :] == (rows % block)[:, None]).astype(jnp.float32)


def plain(saved_input, saved_pre, grad_act):
    total = jnp.float32(saved_input.shape[0] * lax.axis_size("dp"))
    slope = gelu_slope(saved_pre.astype(jnp.float32))
    grad_pre = (grad_act.astype(jnp.float32) * slope).astype(jnp.bfloat16)
    terms_a = local_blocks(saved_input, B, total)
    terms_g = local_blocks(grad_pre, B, total)
    owned_a = lax.psum_scatter(terms_a, "dp", scatter_dimension=0, tiled=True)
    owned_g = lax.psum_scatter(terms_g, "dp", scatter_dimension=0, tiled=True)
    unit_a = owned_unit(owned_a, B)
    unit_g = owned_unit(owned_g, B)
    trace_a, trace_g = lax.psum(
        (jnp.sum(owned_a * unit_a), jnp.sum(owned_g * unit_g)), ("dp", "tensor")
    )
    ratio = jnp.sqrt(trace_a / D / (trace_g / FFW))
    damp = jnp.sqrt(jnp.float32(0.1))
    return (
        (owned_a + ratio * damp * unit_a)[None],
        (owned_g + damp / ratio * unit_g)[None],
    )


def split_rows(count):
    return count // B, (count % B) // H


def piece_rows(piece):
    a_blocks, a_half, g_blocks, _ = piece
    edge = (len(a_blocks) + a_half + len(g_blocks)) * H
    return edge + EDGE, edge


def iotas():
    shape = (H, B)
    return lax.broadcasted_iota(jnp.int32, shape, 0), lax.broadcasted_iota(jnp.int32, shape, 1)


def slot_owner(slot, orders):
    core = lax.axis_index("tensor")
    mask = 0
    for stage, (one, other) in enumerate(zip(*orders)):
        mask = mask | (((slot >> (2 - stage)) & 1) << (one + core * (other - one)))
    return lax.axis_index("dp") ^ mask


def lanes(start, size):
    return pl.ds(start if isinstance(start, int) else pl.multiple_of(start, B), size)


def pack_body(pieces, first, slots, count_a, count_g, *refs):
    n = len(pieces)
    a_hbm, pre_hbm, grad_hbm, trace_in = refs[:4]
    outs, trace_ref = refs[4 : 4 + n], refs[4 + n]
    buffers, sems = refs[5 + n : 5 + 5 * n], refs[5 + 5 * n]
    full, half = split_rows(count_a)
    row, col = iotas()
    low = col < row
    diag_low, diag_high = col == row, col == row + H
    zero = jnp.zeros((H, B), jnp.float32)

    def copies(i, slot):
        a_blocks, a_half, g_blocks, orders = pieces[i]
        a_buf, half_buf, pre_buf, grad_buf = buffers[4 * i : 4 * i + 4]
        owner = slot_owner(first + slot, orders)
        odd = owner & half
        base = (owner >> half) * (full * (1 + half) + half) * B
        moves = []
        if a_blocks:
            start = base + odd * (full + 1) * B + a_blocks[0] * B
            moves.append((a_hbm, start, a_buf))
        if a_half:
            moves.append((a_hbm, base + full * B, half_buf))
        if g_blocks:
            start = owner * count_g + g_blocks[0] * B
            moves += [(pre_hbm, start, pre_buf), (grad_hbm, start, grad_buf)]
        return [
            pltpu.make_async_copy(
                src.at[:, lanes(start, dst.shape[2])], dst.at[slot], sems.at[i, slot, k]
            )
            for k, (src, start, dst) in enumerate(moves)
        ]

    def cov(part):
        return lax.dot_general(
            part, part, (((0,), (0,)), ((), ())), preferred_element_type=jnp.float32
        )

    places = [(i, slot) for i in range(n) for slot in range(slots)]
    for place in places:
        for copy in copies(*place):
            copy.start()

    trace_a, trace_g = zero, zero
    for i, slot in places:
        a_blocks, a_half, g_blocks, orders = pieces[i]
        a_buf, half_buf, pre_buf, grad_buf = buffers[4 * i : 4 * i + 4]
        out = outs[i]
        odd = slot_owner(first + slot, orders) & half
        rows, edge = piece_rows(pieces[i])
        if slot == 0:
            for other in range(slots):
                for copy in copies(i, other):
                    copy.wait()
        at = 0
        corners = 0

        def fold(block):
            nonlocal at, corners
            top, bottom = block[:H], block[H:]
            out[slot, at * H : (at + 1) * H, :] = jnp.where(low, pltpu.roll(bottom, H, 1), top)
            corner = jnp.where(diag_high, bottom, zero)
            out[slot, edge + corners : edge + corners + 1, :] = jnp.sum(
                corner, axis=0, keepdims=True
            )
            at, corners = at + 1, corners + 1
            return corner + jnp.where(diag_low, top, zero)

        for k in range(len(a_blocks)):
            trace_a = trace_a + fold(cov(a_buf[slot, :, k * B : (k + 1) * B]))
        if a_half:
            block = cov(half_buf[slot])
            part = jnp.where(odd == 1, block[H:], block[:H])
            out[slot, at * H : (at + 1) * H, :] = part
            trace_a = trace_a + jnp.where(col == row + odd * H, part, zero)
            at = at + 1
        for k in range(len(g_blocks)):
            here = slice(k * B, (k + 1) * B)
            value = pre_buf[slot, :, here].astype(jnp.float32)
            grad = grad_buf[slot, :, here].astype(jnp.float32)
            trace_g = trace_g + fold(cov((grad * gelu_slope(value)).astype(jnp.bfloat16)))
        out[slot, edge + corners :, :] = jnp.zeros((rows - edge - corners, B), jnp.float32)

    trace_ref[...] = trace_in[...]
    trace_ref[0:1, :] += jnp.sum(trace_a, axis=0, keepdims=True)
    trace_ref[1:2, :] += jnp.sum(trace_g, axis=0, keepdims=True)


def pack(arrays, pieces, first, slots, count_a, count_g, trace):
    tokens, dtype = arrays[0].shape[0], arrays[0].dtype
    scratch = [
        pltpu.VMEM((slots, tokens, max(size, 1) * B), dtype)
        for a_blocks, _, g_blocks, _ in pieces
        for size in (len(a_blocks), 1, len(g_blocks), len(g_blocks))
    ]
    *chunks, trace = pl.pallas_call(
        functools.partial(pack_body, pieces, first, slots, count_a, count_g),
        in_specs=[pl.BlockSpec(memory_space=pltpu.HBM)] * 3
        + [pl.BlockSpec(memory_space=pltpu.VMEM)],
        out_specs=[pl.BlockSpec(memory_space=pltpu.VMEM)] * (len(pieces) + 1),
        out_shape=[
            jax.ShapeDtypeStruct((slots, piece_rows(piece)[0], B), jnp.float32) for piece in pieces
        ]
        + [jax.ShapeDtypeStruct((EDGE, B), jnp.float32)],
        scratch_shapes=scratch + [pltpu.SemaphoreType.DMA((len(pieces), slots, 4))],
        compiler_params=pltpu.CompilerParams(vmem_limit_bytes=32 * 2**20),
        cost_estimate=pl.CostEstimate(flops=1, bytes_accessed=1, transcendentals=0),
    )(*arrays, trace)
    return chunks, trace


def finish_body(pieces, count_a, total, *refs):
    n = len(pieces)
    trace_ref, owns, gots, (a_ref, g_ref) = refs[0], refs[1 : n + 1], refs[n + 1 : 2 * n + 1], refs[2 * n + 1 :]
    full, half = split_rows(count_a)
    odd = lax.axis_index("dp") & half
    row, col = iotas()

    sums = jnp.sum(trace_ref[...] + gots[-1][0, -2:, :], axis=1, keepdims=True) / total
    ratio = jnp.sqrt(sums[0:1] / D / (sums[1:2] / FFW))
    damp = jnp.sqrt(jnp.full((1, 1), 0.1, jnp.float32))
    shift_a, shift_g = ratio * damp, damp / ratio

    def unfold(own, got, at, corner_row, shift, out, start):
        part = slice(at * H, (at + 1) * H)
        here = slice(corner_row, corner_row + 1)
        folded = (own[0, part, :] + got[0, part, :]) / total
        corner = (own[0, here, :] + got[0, here, :]) / total
        turned = jnp.concatenate([folded, folded], axis=0).T
        top = jnp.where(col < row, turned[:H], folded)
        last = pltpu.roll(jnp.where(col < row, folded, turned[:H]), H, 1)
        bottom = jnp.where(col < H, turned[H:], jnp.where(col == row + H, corner, last))
        out[pl.ds(start, H), :] = top + jnp.where(col == row, shift, 0.0)
        out[pl.ds(start + H, H), :] = bottom + jnp.where(col == row + H, shift, 0.0)

    for piece, own, got in zip(pieces, owns, gots):
        a_blocks, a_half, g_blocks, _ = piece
        at, corner = 0, piece_rows(piece)[1]
        for b in a_blocks:
            start = pl.multiple_of(b * B + odd * H, H) if half else b * B
            unfold(own, got, at, corner, shift_a, a_ref, start)
            at, corner = at + 1, corner + 1
        if a_half:
            part = slice(at * H, (at + 1) * H)
            value = (own[0, part, :] + got[0, part, :]) / total
            start = pl.multiple_of((1 - odd) * full * B, H)
            a_ref[pl.ds(start, H), :] = value + jnp.where(col == row + odd * H, shift_a, 0.0)
            at = at + 1
        for b in g_blocks:
            unfold(own, got, at, corner, shift_g, g_ref, b * B)
            at, corner = at + 1, corner + 1


def finish(pieces, trace, owns, gots, count_a, count_g, total):
    args = (trace, *owns, *gots)
    return pl.pallas_call(
        functools.partial(finish_body, pieces, count_a, total),
        in_specs=[pl.BlockSpec(memory_space=pltpu.VMEM)] * len(args),
        out_specs=[pl.BlockSpec(memory_space=pltpu.VMEM)] * 2,
        out_shape=[
            jax.ShapeDtypeStruct((count_a, B), jnp.float32),
            jax.ShapeDtypeStruct((count_g, B), jnp.float32),
        ],
        compiler_params=pltpu.CompilerParams(vmem_limit_bytes=32 * 2**20),
    )(*args)


def swap(value, partner):
    dp, tensor = lax.axis_size("dp"), lax.axis_size("tensor")
    pairs = []
    for i in range(dp):
        for j in range(tensor):
            other = partner(i, j)
            pairs.append((i * tensor + j, other[0] * tensor + other[1]))
    return lax.ppermute(value, ("dp", "tensor"), pairs)


def along(stage, orders):
    return lambda i, j: (i ^ (1 << orders[j][stage]), j)


def halve(keep, got):
    half = keep.shape[0] // 2
    return keep[:half] + got[:half], keep[half:] + got[half:]


def with_trace(send, trace):
    return lax.dynamic_update_slice(send, trace[None], (0, send.shape[1] - 2, 0))


def cut(count_a, count_g):
    full_a, half_a = split_rows(count_a)
    full_g, _ = split_rows(count_g)
    some = 1 + (full_g - 1) // 2
    x, near, far = 0, 1, 2
    one = ((x, near, far), (near, x, far))
    other = one[::-1]
    return (
        (tuple(range(full_a)), 0, (), one),
        ((), 0, tuple(range(1, some)), one),
        ((), half_a, (0,), other),
        ((), 0, tuple(range(some, full_g)), other),
    )


def packed(saved_input, saved_pre, grad_act):
    dp = lax.axis_size("dp")
    total = float(saved_input.shape[0] * dp)
    count_a = saved_input.shape[1] // dp
    count_g = saved_pre.shape[1] // dp
    arrays = tuple(
        pltpu.with_memory_space_constraint(array, pltpu.HBM)
        for array in (saved_input, saved_pre, grad_act)
    )
    half = dp // 2
    pieces = cut(count_a, count_g)
    chunks = range(len(pieces))

    trace = jnp.zeros((EDGE, B), jnp.float32)
    gots = [None] * len(pieces)
    for part in ((0, 2), (1, 3)):
        sends, trace = pack(
            arrays, tuple(pieces[k] for k in part), half, half, count_a, count_g, trace
        )
        for k, send in zip(part, sends):
            gots[k] = swap(send, along(0, pieces[k][3]))
    keeps, trace = pack(arrays, pieces, 0, half, count_a, count_g, trace)

    trace = trace[:2] + swap(trace, lambda i, j: (i, j ^ 1))[:2]
    last = len(pieces) - 1
    carriers = ((0, 1), (last, 1), (last, 2))
    for stage in (1, 2):
        for k in chunks:
            keeps[k], send = halve(keeps[k], gots[k])
            if (k, stage) in carriers:
                if (k, stage) != carriers[0]:
                    trace = trace + news[0, -2:, :]
                send = with_trace(send, trace)
            gots[k] = swap(send, along(stage, pieces[k][3]))
            if (k, stage) in carriers:
                news = gots[k]

    a_factor, g_factor = finish(pieces, trace, keeps, gots, count_a, count_g, total)
    return a_factor[None], g_factor[None]


def fits(count_a, count_g):
    whole_a, whole_g = count_a // B, count_g // B
    return count_a % H == 0 and 0 < whole_a < EDGE - 1 and count_g % B == 0 and 2 < whole_g < 2 * EDGE - 4


def on_device(saved_input, saved_pre, grad_act):
    dp = lax.axis_size("dp")
    count_a = saved_input.shape[1] // dp
    count_g = saved_pre.shape[1] // dp
    if dp == 8 and lax.axis_size("tensor") == 2 and fits(count_a, count_g):
        return packed(saved_input, saved_pre, grad_act)
    return plain(saved_input, saved_pre, grad_act)


def solution(mesh):
    spec = P(("groups", "dp"), "tensor")
    out = P("tensor", ("groups", "dp"), None)
    return jax.shard_map(
        on_device, mesh=mesh, in_specs=(spec, spec, spec), out_specs=(out, out), check_vma=False
    )
```

```python
import functools
import math

import jax
import jax.numpy as jnp
from jax import lax
from jax.experimental import pallas as pl
from jax.experimental.pallas import tpu as pltpu
from jax.sharding import PartitionSpec as P

D = 5120
FFW = 10240
B = 128
H = B // 2


def gelu_slope(value):
    return (
        0.5 * (1.0 + lax.erf(value * 0.7071067811865476))
        + value * jnp.exp(-0.5 * value * value) * 0.3989422804014327
    )


def local_blocks(matrix, block, total):
    tokens, width = matrix.shape
    pieces = matrix.reshape(tokens, width // block, block)
    cov = jnp.einsum("tkb,tkc->kbc", pieces, pieces, preferred_element_type=jnp.float32)
    return cov.reshape(width, block) / total


def owned_unit(owned, block):
    count = owned.shape[0]
    rows = lax.axis_index("dp") * count + jnp.arange(count, dtype=jnp.int32)
    cols = jnp.arange(block, dtype=jnp.int32)
    return (cols[None, :] == (rows % block)[:, None]).astype(jnp.float32)


def plain(saved_input, saved_pre, grad_act):
    total = jnp.float32(saved_input.shape[0] * lax.axis_size("dp"))
    slope = gelu_slope(saved_pre.astype(jnp.float32))
    grad_pre = (grad_act.astype(jnp.float32) * slope).astype(jnp.bfloat16)
    terms_a = local_blocks(saved_input, B, total)
    terms_g = local_blocks(grad_pre, B, total)
    owned_a = lax.psum_scatter(terms_a, "dp", scatter_dimension=0, tiled=True)
    owned_g = lax.psum_scatter(terms_g, "dp", scatter_dimension=0, tiled=True)
    unit_a = owned_unit(owned_a, B)
    unit_g = owned_unit(owned_g, B)
    trace_a, trace_g = lax.psum(
        (jnp.sum(owned_a * unit_a), jnp.sum(owned_g * unit_g)), ("dp", "tensor")
    )
    ratio = jnp.sqrt(trace_a / D / (trace_g / FFW))
    damp = jnp.sqrt(jnp.float32(0.1))
    return (
        (owned_a + ratio * damp * unit_a)[None],
        (owned_g + damp / ratio * unit_g)[None],
    )


EDGE = 8
SLOTS = 8
X, NEAR, FAR = 0, 1, 2
KINDS = (((X, NEAR, FAR), (NEAR, X, FAR)), ((NEAR, X, FAR), (X, NEAR, FAR)))
NOTES = len(KINDS) * SLOTS


def split_rows(count):
    return count // B, (count % B) // H


def has_edge(pieces, k):
    return all(later[3] != pieces[k][3] for later in pieces[k + 1 :])


def piece_rows(pieces, k):
    a_blocks, a_half, g_blocks, _ = pieces[k]
    rows = (len(a_blocks) + len(g_blocks)) * H + a_half * (H * 3 // 4)
    return rows + (EDGE if has_edge(pieces, k) else 0)


def corner_indices(pieces, k):
    parts = [len(a) + a_half + len(g) if kind == pieces[k][3] else 0 for a, a_half, g, kind in pieces]
    return iter(range(sum(parts[:k]), sum(parts[: k + 1])))


def iotas(rows):
    shape = (rows, B)
    return lax.broadcasted_iota(jnp.int32, shape, 0), lax.broadcasted_iota(jnp.int32, shape, 1)


def slot_owner(slot, orders):
    core = lax.axis_index("tensor")
    mask = 0
    for stage, (one, other) in enumerate(zip(*orders)):
        mask = mask | (((slot >> (2 - stage)) & 1) << (one + core * (other - one)))
    return lax.axis_index("dp") ^ mask


def lanes(start, size):
    return pl.ds(start if isinstance(start, int) else pl.multiple_of(start, B), size)


def pack_body(pieces, items, count_a, count_g, fresh, *refs):
    a_hbm, pre_hbm, grad_hbm = refs[:3]
    notes_in = None if fresh else refs[3]
    refs = refs[3 if fresh else 4 :]
    n = len(items)
    outs, notes = refs[:n], refs[n]
    buffers, sems = refs[n + 1 : 5 * n + 1], refs[5 * n + 1]
    full, half = split_rows(count_a)
    slots = SLOTS // 2

    def copies(i, slot):
        k, first = items[i]
        a_blocks, a_half, g_blocks, kind = pieces[k]
        a_buf, half_buf, pre_buf, grad_buf = buffers[4 * i : 4 * i + 4]
        owner = slot_owner(first + slot, KINDS[kind])
        odd = owner & half
        base = (owner >> half) * (full * (1 + half) + half) * B
        moves = []
        if a_blocks:
            start = base + odd * (full + 1) * B + a_blocks[0] * B
            moves.append((a_hbm, start, a_buf))
        if a_half:
            moves.append((a_hbm, base + full * B, half_buf))
        if g_blocks:
            start = owner * count_g + g_blocks[0] * B
            moves += [(pre_hbm, start, pre_buf), (grad_hbm, start, grad_buf)]
        return [
            pltpu.make_async_copy(
                src.at[:, lanes(start, dst.shape[2])], dst.at[slot], sems.at[i, slot, m]
            )
            for m, (src, start, dst) in enumerate(moves)
        ]

    for i in range(n):
        for slot in range(slots):
            for copy in copies(i, slot):
                copy.start()

    row, col = iotas(H)
    low = col < row
    diag_low, diag_high = col == row, col == row + H
    quarter = H // 2
    row_q, col_q = row[:quarter], col[:quarter]
    note_row, _ = iotas(EDGE)
    zero = jnp.zeros((H, B), jnp.float32)
    traces = [zero, zero]
    tiles = {}

    def cov(part):
        return lax.dot_general(
            part, part, (((0,), (0,)), ((), ())), preferred_element_type=jnp.float32
        )

    def note(slot, index, corner, natural):
        line = jnp.sum(corner, axis=0, keepdims=True)
        if index % 2 != natural:
            line = pltpu.roll(line, H, 1)
        tiles[slot] = tiles[slot] + jnp.where(note_row == index // 2, line, 0.0)

    def fold(block, slot, index, which):
        top, bottom = block[:H], block[H:]
        corner = jnp.where(diag_high, bottom, zero)
        note(slot, index, corner, 0)
        traces[which] = traces[which] + corner + jnp.where(diag_low, top, zero)
        return jnp.where(low, pltpu.roll(bottom, H, 1), top)

    def fold_half(block, odd, slot, index):
        part = jnp.where(odd == 1, pltpu.roll(block[H:], H, 1), block[:H])
        traces[0] = traces[0] + jnp.where(diag_low, part, zero)
        upper, lower = part[:quarter], part[quarter:]
        corner = jnp.where(col_q == row_q + quarter, lower, 0.0)
        note(slot, index, corner, 1)
        square = jnp.where(col_q < row_q, pltpu.roll(lower, B - quarter, 1), upper)
        rest = lower.reshape(2, quarter // 2, B)
        rest = jnp.where(col[: quarter // 2] < H, pltpu.roll(rest[1], H, 1), rest[0])
        return square, rest

    for i, (k, first) in enumerate(items):
        a_blocks, a_half, g_blocks, kind = pieces[k]
        a_buf, half_buf, pre_buf, grad_buf = buffers[4 * i : 4 * i + 4]
        out = outs[i]
        for slot in range(slots):
            for copy in copies(i, slot):
                copy.wait()
        for slot in range(slots):
            here = kind * SLOTS + first + slot
            if here not in tiles:
                tiles[here] = jnp.zeros((EDGE, B), jnp.float32) if fresh else notes_in[here]
            index = corner_indices(pieces, k)
            at = 0
            for b in range(len(a_blocks)):
                block = cov(a_buf[slot, :, b * B : (b + 1) * B])
                out[slot, at : at + H, :] = fold(block, here, next(index), 0)
                at = at + H
            if a_half:
                odd = slot_owner(first + slot, KINDS[kind]) & 1
                square, rest = fold_half(cov(half_buf[slot]), odd, here, next(index))
                out[slot, at : at + quarter, :] = square
                out[slot, at + quarter : at + quarter * 3 // 2, :] = rest
                at = at + quarter * 3 // 2
            for b in range(len(g_blocks)):
                part = slice(b * B, (b + 1) * B)
                value = pre_buf[slot, :, part].astype(jnp.float32)
                grad = grad_buf[slot, :, part].astype(jnp.float32)
                block = cov((grad * gelu_slope(value)).astype(jnp.bfloat16))
                out[slot, at : at + H, :] = fold(block, here, next(index), 1)
                at = at + H
            if has_edge(pieces, k):
                out[slot, at:, :] = tiles[here]

    for slot in range(NOTES):
        if slot in tiles:
            notes[slot] = tiles[slot]
        else:
            notes[slot] = jnp.zeros((EDGE, B), jnp.float32) if fresh else notes_in[slot]
    lines = [jnp.sum(trace, axis=0, keepdims=True) for trace in traces]
    tile = jnp.where(note_row == 0, lines[0], jnp.where(note_row == 1, lines[1], 0.0))
    notes[NOTES] = tile if fresh else notes_in[NOTES] + tile


def pack(arrays, pieces, items, count_a, count_g, notes):
    tokens, dtype = arrays[0].shape[0], arrays[0].dtype
    slots = SLOTS // 2
    scratch = []
    for k, _ in items:
        a_blocks, _, g_blocks, _ = pieces[k]
        for size in (len(a_blocks), 1, len(g_blocks), len(g_blocks)):
            scratch.append(pltpu.VMEM((slots, tokens, max(size, 1) * B), dtype))
    fresh = notes is None
    *chunks, notes = pl.pallas_call(
        functools.partial(pack_body, pieces, items, count_a, count_g, fresh),
        in_specs=[pl.BlockSpec(memory_space=pltpu.HBM)] * 3
        + [pl.BlockSpec(memory_space=pltpu.VMEM)] * (not fresh),
        out_specs=[pl.BlockSpec(memory_space=pltpu.VMEM)] * (len(items) + 1),
        out_shape=[
            jax.ShapeDtypeStruct((slots, piece_rows(pieces, k), B), jnp.float32)
            for k, _ in items
        ]
        + [jax.ShapeDtypeStruct((NOTES + 1, EDGE, B), jnp.float32)],
        scratch_shapes=scratch + [pltpu.SemaphoreType.DMA((len(items), slots, 4))],
        compiler_params=pltpu.CompilerParams(vmem_limit_bytes=32 * 2**20),
        cost_estimate=pl.CostEstimate(flops=1, bytes_accessed=1, transcendentals=0),
    )(*arrays, *([] if fresh else [notes]))
    return chunks, notes


def finish_body(pieces, count_a, total, *refs):
    n = len(pieces)
    trace_ref, owns, gots = refs[0], refs[1 : n + 1], refs[n + 1 : 2 * n + 1]
    a_ref, g_ref = refs[2 * n + 1 :]
    full, half = split_rows(count_a)
    odd = lax.axis_index("dp") & half
    row, col = iotas(H)
    quarter = H // 2
    row_q, col_q = row[:quarter], col[:quarter]

    def mean(value):
        return value * (1.0 / total) if math.frexp(total)[0] == 0.5 else value / total

    sums = mean(jnp.sum(trace_ref[...] + gots[-1][0, -2:, :], axis=1, keepdims=True))
    ratio = jnp.sqrt(sums[0:1] / D / (sums[1:2] / FFW))
    damp = jnp.sqrt(jnp.full((1, 1), 0.1, jnp.float32))
    shift_a, shift_g = ratio * damp, damp / ratio

    edges = {}
    for k in range(n):
        if has_edge(pieces, k):
            edge = mean(owns[k][0, -EDGE:, :] + gots[k][0, -EDGE:, :])
            edges[pieces[k][3]] = (edge, pltpu.roll(edge, H, 1))

    def corner(kind, index, natural):
        line = index // 2
        return edges[kind][0 if index % 2 == natural else 1][line : line + 1]

    def turn(folded):
        return jnp.concatenate([folded] * (B // folded.shape[0]), axis=0).T

    def unfold(folded, kind, index, shift, out, start):
        turned = turn(folded)
        top = jnp.where(col < row, turned[:H], folded)
        last = pltpu.roll(jnp.where(col < row, folded, turned[:H]), H, 1)
        bottom = jnp.where(
            col < H, turned[H:], jnp.where(col == row + H, corner(kind, index, 0), last)
        )
        out[pl.ds(start, H), :] = top + jnp.where(col == row, shift, 0.0)
        out[pl.ds(start + H, H), :] = bottom + jnp.where(col == row + H, shift, 0.0)

    def unfold_half(square, rest, kind, index, shift, out, start):
        turned = turn(square)
        upper = jnp.where(col_q < row_q, turned[:quarter], square)
        last = pltpu.roll(jnp.where(col_q < row_q, square, turned[:quarter]), quarter, 1)
        last = jnp.where(col_q == row_q + quarter, corner(kind, index, 1), last)
        lower = jnp.where(col_q < quarter, turned[quarter:H], last)
        rest = jnp.concatenate([rest, pltpu.roll(rest, H, 1)], axis=0)
        lower = jnp.where(col_q < H, lower, rest)
        part = jnp.concatenate([upper, lower], axis=0) + jnp.where(col == row, shift, 0.0)
        out[pl.ds(start, H), :] = jnp.where(odd == 1, pltpu.roll(part, H, 1), part)

    for k, (own, got) in enumerate(zip(owns, gots)):
        a_blocks, a_half, g_blocks, kind = pieces[k]
        index = corner_indices(pieces, k)
        at = 0

        def take(rows):
            nonlocal at
            at = at + rows
            return mean(own[0, at - rows : at, :] + got[0, at - rows : at, :])

        for b in a_blocks:
            start = pl.multiple_of(b * B + odd * H, H) if half else b * B
            unfold(take(H), kind, next(index), shift_a, a_ref, start)
        if a_half:
            square, rest = take(quarter), take(quarter // 2)
            start = pl.multiple_of((1 - odd) * full * B, H)
            unfold_half(square, rest, kind, next(index), shift_a, a_ref, start)
        for b in g_blocks:
            unfold(take(H), kind, next(index), shift_g, g_ref, b * B)


def finish(pieces, trace, owns, gots, count_a, count_g, total):
    args = (trace, *owns, *gots)
    return pl.pallas_call(
        functools.partial(finish_body, pieces, count_a, total),
        in_specs=[pl.BlockSpec(memory_space=pltpu.VMEM)] * len(args),
        out_specs=[pl.BlockSpec(memory_space=pltpu.VMEM)] * 2,
        out_shape=[
            jax.ShapeDtypeStruct((count_a, B), jnp.float32),
            jax.ShapeDtypeStruct((count_g, B), jnp.float32),
        ],
        compiler_params=pltpu.CompilerParams(vmem_limit_bytes=32 * 2**20),
    )(*args)


def swap(value, partner):
    dp, tensor = lax.axis_size("dp"), lax.axis_size("tensor")
    pairs = []
    for i in range(dp):
        for j in range(tensor):
            other = partner(i, j)
            pairs.append((i * tensor + j, other[0] * tensor + other[1]))
    return lax.ppermute(value, ("dp", "tensor"), pairs)


def along(stage, kind):
    return lambda i, j: (i ^ (1 << KINDS[kind][j][stage]), j)


def halve(keep, got):
    half = keep.shape[0] // 2
    return keep[:half] + got[:half], keep[half:] + got[half:]


def with_trace(send, trace):
    return lax.dynamic_update_slice(send, trace[None], (0, send.shape[1] - 2, 0))


def packed(saved_input, saved_pre, grad_act):
    dp = lax.axis_size("dp")
    total = float(saved_input.shape[0] * dp)
    count_a = saved_input.shape[1] // dp
    count_g = saved_pre.shape[1] // dp
    full_a, half_a = split_rows(count_a)
    full_g, _ = split_rows(count_g)
    some = 1 + (full_g - 1) // 2
    pieces = (
        (tuple(range(full_a)), 0, (), 0),
        ((), 0, tuple(range(1, some)), 0),
        ((), half_a, (0,), 1),
        ((), 0, tuple(range(some, full_g)), 1),
    )
    arrays = tuple(
        pltpu.with_memory_space_constraint(array, pltpu.HBM)
        for array in (saved_input, saved_pre, grad_act)
    )
    chunks = range(len(pieces))
    last = len(pieces) - 1
    keep, send = 0, SLOTS // 2

    keeps, gots, notes = {}, {}, None
    calls = (
        ((0, send), (2, send)),
        ((1, send), (3, send)),
        ((0, keep), (2, keep), (1, keep), (3, keep)),
    )
    for items in calls:
        parts, notes = pack(arrays, pieces, items, count_a, count_g, notes)
        for (k, first), part in zip(items, parts):
            if first == send:
                gots[k] = swap(part, along(0, pieces[k][3]))
            else:
                keeps[k] = part

    trace = notes[NOTES, :2, :]
    trace = trace + swap(trace, lambda i, j: (i, j ^ 1))
    carriers = ((1, 1), (last, 1), (last, 2))
    for stage in (1, 2):
        for k in chunks:
            keeps[k], part = halve(keeps[k], gots[k])
            if (k, stage) in carriers:
                if (k, stage) != carriers[0]:
                    trace = trace + news[0, -2:, :]
                part = with_trace(part, trace)
            gots[k] = swap(part, along(stage, pieces[k][3]))
            if (k, stage) in carriers:
                news = gots[k]

    a_factor, g_factor = finish(
        pieces, trace, [keeps[k] for k in chunks], [gots[k] for k in chunks], count_a, count_g, total
    )
    return a_factor[None], g_factor[None]


def fits(count_a, count_g):
    (full_a, half_a), full_g = split_rows(count_a), count_g // B
    if count_a % H or count_g % B or full_a < 1 or full_g < 3:
        return False
    return full_a + half_a + full_g <= 2 * (EDGE - 2)


def on_device(saved_input, saved_pre, grad_act):
    dp = lax.axis_size("dp")
    count_a = saved_input.shape[1] // dp
    count_g = saved_pre.shape[1] // dp
    if dp == SLOTS and lax.axis_size("tensor") == 2 and fits(count_a, count_g):
        return packed(saved_input, saved_pre, grad_act)
    return plain(saved_input, saved_pre, grad_act)


def solution(mesh):
    spec = P(("groups", "dp"), "tensor")
    out = P("tensor", ("groups", "dp"), None)
    return jax.shard_map(
        on_device, mesh=mesh, in_specs=(spec, spec, spec), out_specs=(out, out), check_vma=False
    )
```

```python
import functools
import math

import jax
import jax.numpy as jnp
from jax import lax
from jax.experimental import pallas as pl
from jax.experimental.pallas import tpu as pltpu
from jax.sharding import PartitionSpec as P

D = 5120
FFW = 10240
B = 128
H = B // 2


def gelu_slope(value):
    return (
        0.5 * (1.0 + lax.erf(value * 0.7071067811865476))
        + value * jnp.exp(-0.5 * value * value) * 0.3989422804014327
    )


def local_blocks(matrix, block, total):
    tokens, width = matrix.shape
    pieces = matrix.reshape(tokens, width // block, block)
    cov = jnp.einsum("tkb,tkc->kbc", pieces, pieces, preferred_element_type=jnp.float32)
    return cov.reshape(width, block) / total


def owned_unit(owned, block):
    count = owned.shape[0]
    rows = lax.axis_index("dp") * count + jnp.arange(count, dtype=jnp.int32)
    cols = jnp.arange(block, dtype=jnp.int32)
    return (cols[None, :] == (rows % block)[:, None]).astype(jnp.float32)


def plain(saved_input, saved_pre, grad_act):
    total = jnp.float32(saved_input.shape[0] * lax.axis_size("dp"))
    slope = gelu_slope(saved_pre.astype(jnp.float32))
    grad_pre = (grad_act.astype(jnp.float32) * slope).astype(jnp.bfloat16)
    terms_a = local_blocks(saved_input, B, total)
    terms_g = local_blocks(grad_pre, B, total)
    owned_a = lax.psum_scatter(terms_a, "dp", scatter_dimension=0, tiled=True)
    owned_g = lax.psum_scatter(terms_g, "dp", scatter_dimension=0, tiled=True)
    unit_a = owned_unit(owned_a, B)
    unit_g = owned_unit(owned_g, B)
    trace_a, trace_g = lax.psum(
        (jnp.sum(owned_a * unit_a), jnp.sum(owned_g * unit_g)), ("dp", "tensor")
    )
    ratio = jnp.sqrt(trace_a / D / (trace_g / FFW))
    damp = jnp.sqrt(jnp.float32(0.1))
    return (
        (owned_a + ratio * damp * unit_a)[None],
        (owned_g + damp / ratio * unit_g)[None],
    )


EDGE = 8
SLOTS = 8
X, NEAR, FAR = 0, 1, 2
KINDS = (((X, NEAR, FAR), (NEAR, X, FAR)), ((NEAR, X, FAR), (X, NEAR, FAR)))
NOTES = len(KINDS) * SLOTS


def split_rows(count):
    return count // B, (count % B) // H


def has_edge(pieces, k):
    return all(later[3] != pieces[k][3] for later in pieces[k + 1 :])


def piece_rows(pieces, k):
    a_blocks, a_half, g_blocks, _ = pieces[k]
    rows = (len(a_blocks) + len(g_blocks)) * H + a_half * (H * 3 // 4)
    return rows + (EDGE if has_edge(pieces, k) else 0)


def corner_indices(pieces, k):
    parts = [len(a) + a_half + len(g) if kind == pieces[k][3] else 0 for a, a_half, g, kind in pieces]
    return iter(range(sum(parts[:k]), sum(parts[: k + 1])))


def iotas(rows):
    shape = (rows, B)
    return lax.broadcasted_iota(jnp.int32, shape, 0), lax.broadcasted_iota(jnp.int32, shape, 1)


def slot_owner(slot, orders):
    core = lax.axis_index("tensor")
    mask = 0
    for stage, (one, other) in enumerate(zip(*orders)):
        mask = mask | (((slot >> (2 - stage)) & 1) << (one + core * (other - one)))
    return lax.axis_index("dp") ^ mask


def lanes(start, size):
    return pl.ds(start if isinstance(start, int) else pl.multiple_of(start, B), size)


def pack_body(pieces, items, count_a, count_g, fresh, *refs):
    a_hbm, pre_hbm, grad_hbm = refs[:3]
    notes_in = None if fresh else refs[3]
    refs = refs[3 if fresh else 4 :]
    n = len(items)
    outs, notes = refs[:n], refs[n]
    buffers, sems = refs[n + 1 : 5 * n + 1], refs[5 * n + 1]
    full, half = split_rows(count_a)
    slots = SLOTS // 2

    def copies(i, slot):
        k, first = items[i]
        a_blocks, a_half, g_blocks, kind = pieces[k]
        a_buf, half_buf, pre_buf, grad_buf = buffers[4 * i : 4 * i + 4]
        owner = slot_owner(first + slot, KINDS[kind])
        odd = owner & half
        base = (owner >> half) * (full * (1 + half) + half) * B
        moves = []
        if a_blocks:
            start = base + odd * (full + 1) * B + a_blocks[0] * B
            moves.append((a_hbm, start, a_buf))
        if a_half:
            moves.append((a_hbm, base + full * B, half_buf))
        if g_blocks:
            start = owner * count_g + g_blocks[0] * B
            moves += [(pre_hbm, start, pre_buf), (grad_hbm, start, grad_buf)]
        return [
            pltpu.make_async_copy(
                src.at[:, lanes(start, dst.shape[2])], dst.at[slot], sems.at[i, slot, m]
            )
            for m, (src, start, dst) in enumerate(moves)
        ]

    for i in range(n):
        for slot in range(slots):
            for copy in copies(i, slot):
                copy.start()

    row, col = iotas(H)
    low = col < row
    diag_low, diag_high = col == row, col == row + H
    quarter = H // 2
    row_q, col_q = row[:quarter], col[:quarter]
    note_row, _ = iotas(EDGE)
    zero = jnp.zeros((H, B), jnp.float32)
    traces = [zero, zero]
    tiles = {}

    def cov(part):
        return lax.dot_general(
            part, part, (((0,), (0,)), ((), ())), preferred_element_type=jnp.float32
        )

    def note(slot, index, corner, natural):
        line = jnp.sum(corner, axis=0, keepdims=True)
        if index % 2 != natural:
            line = pltpu.roll(line, H, 1)
        tiles[slot] = tiles[slot] + jnp.where(note_row == index // 2, line, 0.0)

    def fold(block, slot, index, which):
        top, bottom = block[:H], block[H:]
        corner = jnp.where(diag_high, bottom, zero)
        note(slot, index, corner, 0)
        traces[which] = traces[which] + corner + jnp.where(diag_low, top, zero)
        return jnp.where(low, pltpu.roll(bottom, H, 1), top)

    def fold_half(block, odd, slot, index):
        part = jnp.where(odd == 1, pltpu.roll(block[H:], H, 1), block[:H])
        traces[0] = traces[0] + jnp.where(diag_low, part, zero)
        upper, lower = part[:quarter], part[quarter:]
        corner = jnp.where(col_q == row_q + quarter, lower, 0.0)
        note(slot, index, corner, 1)
        square = jnp.where(col_q < row_q, pltpu.roll(lower, B - quarter, 1), upper)
        rest = lower.reshape(2, quarter // 2, B)
        rest = jnp.where(col[: quarter // 2] < H, pltpu.roll(rest[1], H, 1), rest[0])
        return square, rest

    for i, (k, first) in enumerate(items):
        a_blocks, a_half, g_blocks, kind = pieces[k]
        a_buf, half_buf, pre_buf, grad_buf = buffers[4 * i : 4 * i + 4]
        out = outs[i]
        for slot in range(slots):
            for copy in copies(i, slot):
                copy.wait()
        for slot in range(slots):
            here = kind * SLOTS + first + slot
            if here not in tiles:
                tiles[here] = jnp.zeros((EDGE, B), jnp.float32) if fresh else notes_in[here]
            index = corner_indices(pieces, k)
            at = 0
            for b in range(len(a_blocks)):
                block = cov(a_buf[slot, :, b * B : (b + 1) * B])
                out[slot, at : at + H, :] = fold(block, here, next(index), 0)
                at = at + H
            if a_half:
                odd = slot_owner(first + slot, KINDS[kind]) & 1
                square, rest = fold_half(cov(half_buf[slot]), odd, here, next(index))
                out[slot, at : at + quarter, :] = square
                out[slot, at + quarter : at + quarter * 3 // 2, :] = rest
                at = at + quarter * 3 // 2
            for b in range(len(g_blocks)):
                part = slice(b * B, (b + 1) * B)
                value = pre_buf[slot, :, part].astype(jnp.float32)
                grad = grad_buf[slot, :, part].astype(jnp.float32)
                block = cov((grad * gelu_slope(value)).astype(jnp.bfloat16))
                out[slot, at : at + H, :] = fold(block, here, next(index), 1)
                at = at + H
            if has_edge(pieces, k):
                out[slot, at:, :] = tiles[here]

    for slot in range(NOTES):
        if slot in tiles:
            notes[slot] = tiles[slot]
        else:
            notes[slot] = jnp.zeros((EDGE, B), jnp.float32) if fresh else notes_in[slot]
    lines = [jnp.sum(trace, axis=0, keepdims=True) for trace in traces]
    tile = jnp.where(note_row == 0, lines[0], jnp.where(note_row == 1, lines[1], 0.0))
    notes[NOTES] = tile if fresh else notes_in[NOTES] + tile


def pack(arrays, pieces, items, count_a, count_g, notes):
    tokens, dtype = arrays[0].shape[0], arrays[0].dtype
    slots = SLOTS // 2
    scratch = []
    for k, _ in items:
        a_blocks, _, g_blocks, _ = pieces[k]
        for size in (len(a_blocks), 1, len(g_blocks), len(g_blocks)):
            scratch.append(pltpu.VMEM((slots, tokens, max(size, 1) * B), dtype))
    fresh = notes is None
    *chunks, notes = pl.pallas_call(
        functools.partial(pack_body, pieces, items, count_a, count_g, fresh),
        in_specs=[pl.BlockSpec(memory_space=pltpu.HBM)] * 3
        + [pl.BlockSpec(memory_space=pltpu.VMEM)] * (not fresh),
        out_specs=[pl.BlockSpec(memory_space=pltpu.VMEM)] * (len(items) + 1),
        out_shape=[
            jax.ShapeDtypeStruct((slots, piece_rows(pieces, k), B), jnp.float32)
            for k, _ in items
        ]
        + [jax.ShapeDtypeStruct((NOTES + 1, EDGE, B), jnp.float32)],
        scratch_shapes=scratch + [pltpu.SemaphoreType.DMA((len(items), slots, 4))],
        compiler_params=pltpu.CompilerParams(vmem_limit_bytes=32 * 2**20),
        cost_estimate=pl.CostEstimate(flops=1, bytes_accessed=1, transcendentals=0),
    )(*arrays, *([] if fresh else [notes]))
    return chunks, notes


def halve_body(traced, n, *refs):
    keeps, gots, refs = refs[:n], refs[n : 2 * n], refs[2 * n :]
    traces, outs = refs[:-2 * n], refs[-2 * n :]
    for k in range(n):
        half = keeps[k].shape[0] // 2
        for part in range(2):
            here = slice(part * half, (part + 1) * half)
            outs[2 * k + part][...] = keeps[k][here] + gots[k][here]
    if traced:
        value = sum((trace[...] for trace in traces[1:]), traces[0][...])
        if len(traces) > 1:
            value = value + sum(got[0, -2:, :] for got in gots)
        for out in outs:
            out[0, -2:, :] = value


def halve(keeps, gots, traces=()):
    n = len(keeps)
    args = (*keeps, *gots, *traces)
    shapes = [(keep.shape[0] // 2, *keep.shape[1:]) for keep in keeps for _ in range(2)]
    outs = pl.pallas_call(
        functools.partial(halve_body, bool(traces), n),
        in_specs=[pl.BlockSpec(memory_space=pltpu.VMEM)] * len(args),
        out_specs=[pl.BlockSpec(memory_space=pltpu.VMEM)] * (2 * n),
        out_shape=[jax.ShapeDtypeStruct(shape, jnp.float32) for shape in shapes],
        compiler_params=pltpu.CompilerParams(vmem_limit_bytes=32 * 2**20),
        cost_estimate=pl.CostEstimate(flops=1, bytes_accessed=1, transcendentals=0),
    )(*args)
    return outs[0::2], outs[1::2]


def mean_of(value, total):
    return value * (1.0 / total) if math.frexp(total)[0] == 0.5 else value / total


def turn(folded):
    return jnp.concatenate([folded] * (B // folded.shape[0]), axis=0).T


def unfold(folded, put):
    row, col = iotas(H)
    turned = turn(folded)
    last = pltpu.roll(jnp.where(col < row, folded, turned[:H]), H, 1)
    put(0, jnp.where(col < row, turned[:H], folded))
    put(H, jnp.where(col < H, turned[H:], last))


def unfold_half(square, rest, odd, put):
    quarter = H // 2
    row, col = iotas(quarter)
    turned = turn(square)
    upper = jnp.where(col < row, turned[:quarter], square)
    last = pltpu.roll(jnp.where(col < row, square, turned[:quarter]), quarter, 1)
    lower = jnp.where(col < quarter, turned[quarter:H], last)
    rest = jnp.concatenate([rest, pltpu.roll(rest, H, 1)], axis=0)
    part = jnp.concatenate([upper, jnp.where(col < H, lower, rest)], axis=0)
    put(0, jnp.where(odd == 1, pltpu.roll(part, H, 1), part))


def places(pieces, ks, count_a):
    full, half = split_rows(count_a)
    odd = lax.axis_index("dp") & half
    for k in ks:
        a_blocks, a_half, g_blocks, kind = pieces[k]
        index = corner_indices(pieces, k)
        for b in a_blocks:
            start = pl.multiple_of(b * B + odd * H, H) if half else b * B
            yield k, 0, start, H, next(index)
        if a_half:
            yield k, 0, pl.multiple_of((1 - odd) * full * B, H), H * 3 // 4, next(index)
        for b in g_blocks:
            yield k, 1, b * B, H, next(index)


def unfold_body(pieces, ks, count_a, total, owns, gots, outs):
    odd = lax.axis_index("dp") & 1
    at = dict.fromkeys(ks, 0)

    def take(k, rows):
        i = ks.index(k)
        at[k] = at[k] + rows
        part = slice(at[k] - rows, at[k])
        return mean_of(owns[i][0, part, :] + gots[i][0, part, :], total)

    for k, which, start, rows, _ in places(pieces, ks, count_a):
        def put(offset, value):
            outs[which][pl.ds(start + offset, value.shape[0]), :] = value

        if rows == H:
            unfold(take(k, H), put)
        else:
            unfold_half(take(k, H // 2), take(k, H // 4), odd, put)


def early_body(pieces, ks, count_a, total, *refs):
    n = len(ks)
    unfold_body(pieces, ks, count_a, total, refs[:n], refs[n : 2 * n], refs[2 * n :])


def finish_body(pieces, early, late, count_a, total, *refs):
    n = len(late)
    owns, gots, (early_a, early_g, a_ref, g_ref) = refs[:n], refs[n : 2 * n], refs[2 * n :]
    outs = (a_ref, g_ref)
    full, half = split_rows(count_a)
    odd = lax.axis_index("dp") & half
    row, col = iotas(H)

    unfold_body(pieces, late, count_a, total, owns, gots, outs)

    edges = {}
    for i, k in enumerate(late):
        edge = mean_of(owns[i][0, -EDGE:, :] + gots[i][0, -EDGE:, :], total)
        edges[pieces[k][3]] = (edge, pltpu.roll(edge, H, 1))
    sums = jnp.sum(edge[-2:], axis=1, keepdims=True)
    ratio = jnp.sqrt(sums[0:1] / D / (sums[1:2] / FFW))
    damp = jnp.sqrt(jnp.full((1, 1), 0.1, jnp.float32))
    shifts = (ratio * damp, damp / ratio)

    def corner(kind, index, natural):
        line = index // 2
        return edges[kind][0 if index % 2 == natural else 1][line : line + 1]

    for ks in (early, late):
        ins = (early_a, early_g) if ks is early else outs
        for k, which, start, rows, index in places(pieces, ks, count_a):
            src, out, shift, kind = ins[which], outs[which], shifts[which], pieces[k][3]
            here = pl.ds(start, H)
            if rows == H:
                low = pl.ds(start + H, H)
                out[here, :] = src[here, :] + jnp.where(col == row, shift, 0.0)
                value = corner(kind, index, 0) + shift
                out[low, :] = jnp.where(col == row + H, value, src[low, :])
            else:
                value = src[here, :] + jnp.where(col == row + odd * H, shift, 0.0)
                line = corner(kind, index, 1)
                line = jnp.where(odd == 1, pltpu.roll(line, H, 1), line) + shift
                last = jnp.logical_and(col == row + odd * H, row >= H // 2)
                out[here, :] = jnp.where(last, line, value)


def unfold_early(pieces, ks, owns, gots, count_a, count_g, total):
    args = (*owns, *gots)
    return pl.pallas_call(
        functools.partial(early_body, pieces, ks, count_a, total),
        in_specs=[pl.BlockSpec(memory_space=pltpu.VMEM)] * len(args),
        out_specs=[pl.BlockSpec(memory_space=pltpu.VMEM)] * 2,
        out_shape=[
            jax.ShapeDtypeStruct((count_a, B), jnp.float32),
            jax.ShapeDtypeStruct((count_g, B), jnp.float32),
        ],
        compiler_params=pltpu.CompilerParams(vmem_limit_bytes=32 * 2**20),
        cost_estimate=pl.CostEstimate(flops=4 * 10**9, bytes_accessed=1, transcendentals=0),
    )(*args)


def finish(pieces, early, late, owns, gots, first, count_a, count_g, total):
    args = (*owns, *gots, *first)
    return pl.pallas_call(
        functools.partial(finish_body, pieces, early, late, count_a, total),
        in_specs=[pl.BlockSpec(memory_space=pltpu.VMEM)] * len(args),
        out_specs=[pl.BlockSpec(memory_space=pltpu.VMEM)] * 2,
        out_shape=[
            jax.ShapeDtypeStruct((count_a, B), jnp.float32),
            jax.ShapeDtypeStruct((count_g, B), jnp.float32),
        ],
        compiler_params=pltpu.CompilerParams(vmem_limit_bytes=32 * 2**20),
    )(*args)


def swap(value, partner):
    dp, tensor = lax.axis_size("dp"), lax.axis_size("tensor")
    pairs = []
    for i in range(dp):
        for j in range(tensor):
            other = partner(i, j)
            pairs.append((i * tensor + j, other[0] * tensor + other[1]))
    return lax.ppermute(value, ("dp", "tensor"), pairs)


def along(stage, kind):
    return lambda i, j: (i ^ (1 << KINDS[kind][j][stage]), j)


def packed(saved_input, saved_pre, grad_act):
    dp = lax.axis_size("dp")
    total = float(saved_input.shape[0] * dp)
    count_a = saved_input.shape[1] // dp
    count_g = saved_pre.shape[1] // dp
    full_a, half_a = split_rows(count_a)
    full_g, _ = split_rows(count_g)
    some = 1 + (full_g - 1) // 2
    pieces = (
        (tuple(range(full_a)), 0, (), 0),
        ((), 0, tuple(range(1, some)), 0),
        ((), half_a, (0,), 1),
        ((), 0, tuple(range(some, full_g)), 1),
    )
    arrays = tuple(
        pltpu.with_memory_space_constraint(array, pltpu.HBM)
        for array in (saved_input, saved_pre, grad_act)
    )
    keep, send = 0, SLOTS // 2
    early, late = (0, 2), (1, 3)
    keeps, gots, notes = {}, {}, None
    for first, ks in ((send, early), (send, late), (keep, early + late)):
        items = tuple((k, first) for k in ks)
        parts, notes = pack(arrays, pieces, items, count_a, count_g, notes)
        for k, part in zip(ks, parts):
            if first == send:
                gots[k] = swap(part, along(0, pieces[k][3]))
            else:
                keeps[k] = part

    trace = notes[NOTES, :2, :]
    trace = trace + swap(trace, lambda i, j: (i, j ^ 1))
    across = swap(trace, lambda i, j: (i ^ (1 << X) ^ (1 << NEAR), j))
    traces = {early: ((), ()), late: ((trace,), (trace, across))}
    for stage in (1, 2):
        for ks in (early, late):
            own, parts = halve(
                [keeps[k] for k in ks], [gots[k] for k in ks], traces[ks][stage - 1]
            )
            for k, mine, part in zip(ks, own, parts):
                keeps[k], gots[k] = mine, swap(part, along(stage, pieces[k][3]))

    def both(ks):
        return [keeps[k] for k in ks], [gots[k] for k in ks]

    first = unfold_early(pieces, early, *both(early), count_a, count_g, total)
    a_factor, g_factor = finish(
        pieces, early, late, *both(late), first, count_a, count_g, total
    )
    return a_factor[None], g_factor[None]


def fits(count_a, count_g):
    (full_a, half_a), full_g = split_rows(count_a), count_g // B
    if count_a % H or count_g % B or full_a < 1 or full_g < 3:
        return False
    return full_a + half_a + full_g <= 2 * (EDGE - 2)


def on_device(saved_input, saved_pre, grad_act):
    dp = lax.axis_size("dp")
    count_a = saved_input.shape[1] // dp
    count_g = saved_pre.shape[1] // dp
    if dp == SLOTS and lax.axis_size("tensor") == 2 and fits(count_a, count_g):
        return packed(saved_input, saved_pre, grad_act)
    return plain(saved_input, saved_pre, grad_act)


def solution(mesh):
    spec = P(("groups", "dp"), "tensor")
    out = P("tensor", ("groups", "dp"), None)
    return jax.shard_map(
        on_device, mesh=mesh, in_specs=(spec, spec, spec), out_specs=(out, out), check_vma=False
    )
```

```python
import functools
import math

import jax
import jax.numpy as jnp
from jax import lax
from jax.experimental import pallas as pl
from jax.experimental.pallas import tpu as pltpu
from jax.sharding import PartitionSpec as P

D = 5120
FFW = 10240
B = 128
H = B // 2


def gelu_slope(value):
    return (
        0.5 * (1.0 + lax.erf(value * 0.7071067811865476))
        + value * jnp.exp(-0.5 * value * value) * 0.3989422804014327
    )


def local_blocks(matrix, block, total):
    tokens, width = matrix.shape
    pieces = matrix.reshape(tokens, width // block, block)
    cov = jnp.einsum("tkb,tkc->kbc", pieces, pieces, preferred_element_type=jnp.float32)
    return cov.reshape(width, block) / total


def owned_unit(owned, block):
    count = owned.shape[0]
    rows = lax.axis_index("dp") * count + jnp.arange(count, dtype=jnp.int32)
    cols = jnp.arange(block, dtype=jnp.int32)
    return (cols[None, :] == (rows % block)[:, None]).astype(jnp.float32)


def plain(saved_input, saved_pre, grad_act):
    total = jnp.float32(saved_input.shape[0] * lax.axis_size("dp"))
    slope = gelu_slope(saved_pre.astype(jnp.float32))
    grad_pre = (grad_act.astype(jnp.float32) * slope).astype(jnp.bfloat16)
    terms_a = local_blocks(saved_input, B, total)
    terms_g = local_blocks(grad_pre, B, total)
    owned_a = lax.psum_scatter(terms_a, "dp", scatter_dimension=0, tiled=True)
    owned_g = lax.psum_scatter(terms_g, "dp", scatter_dimension=0, tiled=True)
    unit_a = owned_unit(owned_a, B)
    unit_g = owned_unit(owned_g, B)
    trace_a, trace_g = lax.psum(
        (jnp.sum(owned_a * unit_a), jnp.sum(owned_g * unit_g)), ("dp", "tensor")
    )
    ratio = jnp.sqrt(trace_a / D / (trace_g / FFW))
    damp = jnp.sqrt(jnp.float32(0.1))
    return (
        (owned_a + ratio * damp * unit_a)[None],
        (owned_g + damp / ratio * unit_g)[None],
    )


EDGE = 8
SLOTS = 8
X, NEAR, FAR = 0, 1, 2
KINDS = (((X, NEAR, FAR), (NEAR, X, FAR)), ((NEAR, X, FAR), (X, NEAR, FAR)))
NOTES = len(KINDS) * SLOTS

WEIGHTS = {((0, 2), 2): 2 * 10**9}


def split_rows(count):
    return count // B, (count % B) // H


def has_edge(pieces, k):
    return all(later[3] != pieces[k][3] for later in pieces[k + 1 :])


def piece_rows(pieces, k):
    a_blocks, a_half, g_blocks, _ = pieces[k]
    rows = (len(a_blocks) + len(g_blocks)) * H + a_half * (H * 3 // 4)
    return rows + (EDGE if has_edge(pieces, k) else 0)


def corner_indices(pieces, k):
    parts = [len(a) + a_half + len(g) if kind == pieces[k][3] else 0 for a, a_half, g, kind in pieces]
    return iter(range(sum(parts[:k]), sum(parts[: k + 1])))


def iotas(rows):
    shape = (rows, B)
    return lax.broadcasted_iota(jnp.int32, shape, 0), lax.broadcasted_iota(jnp.int32, shape, 1)


def slot_owner(slot, orders):
    core = lax.axis_index("tensor")
    mask = 0
    for stage, (one, other) in enumerate(zip(*orders)):
        mask = mask | (((slot >> (2 - stage)) & 1) << (one + core * (other - one)))
    return lax.axis_index("dp") ^ mask


def lanes(start, size):
    return pl.ds(start if isinstance(start, int) else pl.multiple_of(start, B), size)


def columns(pieces, item, count_a, count_g):
    k, first = item
    a_blocks, a_half, g_blocks, kind = pieces[k]
    full, half = split_rows(count_a)

    def base(slot):
        owner = slot_owner(first + slot, KINDS[kind])
        return (owner >> half) * (full * (1 + half) + half) * B, owner & half, owner

    found = []
    if a_blocks:

        def whole(slot):
            start, odd, _ = base(slot)
            return start + odd * (full + 1) * B + a_blocks[0] * B

        found.append((0, whole, len(a_blocks) * B))
    if a_half:
        found.append((0, lambda slot: base(slot)[0] + full * B, B))
    if g_blocks:

        def part(slot):
            return base(slot)[2] * count_g + g_blocks[0] * B

        found += [(1, part, len(g_blocks) * B), (2, part, len(g_blocks) * B)]
    return found


def pack_body(pieces, items, ahead, count_a, count_g, fresh, *refs):
    def reads(of):
        return [
            (array, start, size)
            for item in of
            for array, start, size in columns(pieces, item, count_a, count_g)
        ]

    refs = list(refs)

    def pop(count):
        taken = refs[:count]
        del refs[:count]
        return taken

    n, own, after = len(items), reads(items), reads(ahead)
    slots = SLOTS // 2
    hbm = pop(3)
    notes_in, buffers = (None, None) if fresh else (pop(1)[0], pop(len(own)))
    outs, (notes,), nexts = pop(n), pop(1), pop(len(after))
    if fresh:
        buffers = pop(len(own))
    sems = refs

    def copies(moves, into, sem):
        return [
            pltpu.make_async_copy(
                hbm[array].at[:, lanes(start(slot), size)], into[m].at[slot], sem.at[m, slot]
            )
            for m, (array, start, size) in enumerate(moves)
            for slot in range(slots)
        ]

    mine = copies(own, buffers, sems.pop(0)) if fresh else []
    later = copies(after, nexts, sems.pop(0)) if after else []
    for copy in mine + later:
        copy.start()

    full, half = split_rows(count_a)
    row, col = iotas(H)
    low = col < row
    diag_low, diag_high = col == row, col == row + H
    quarter = H // 2
    row_q, col_q = row[:quarter], col[:quarter]
    note_row, _ = iotas(EDGE)
    zero = jnp.zeros((H, B), jnp.float32)
    traces = [zero, zero]
    tiles = {}

    def cov(part):
        return lax.dot_general(
            part, part, (((0,), (0,)), ((), ())), preferred_element_type=jnp.float32
        )

    def note(slot, index, corner, natural):
        line = jnp.sum(corner, axis=0, keepdims=True)
        if index % 2 != natural:
            line = pltpu.roll(line, H, 1)
        tiles[slot] = tiles[slot] + jnp.where(note_row == index // 2, line, 0.0)

    def fold(block, slot, index, which):
        top, bottom = block[:H], block[H:]
        corner = jnp.where(diag_high, bottom, zero)
        note(slot, index, corner, 0)
        traces[which] = traces[which] + corner + jnp.where(diag_low, top, zero)
        return jnp.where(low, pltpu.roll(bottom, H, 1), top)

    def fold_half(block, odd, slot, index):
        part = jnp.where(odd == 1, pltpu.roll(block[H:], H, 1), block[:H])
        traces[0] = traces[0] + jnp.where(diag_low, part, zero)
        upper, lower = part[:quarter], part[quarter:]
        corner = jnp.where(col_q == row_q + quarter, lower, 0.0)
        note(slot, index, corner, 1)
        square = jnp.where(col_q < row_q, pltpu.roll(lower, B - quarter, 1), upper)
        rest = lower.reshape(2, quarter // 2, B)
        rest = jnp.where(col[: quarter // 2] < H, pltpu.roll(rest[1], H, 1), rest[0])
        return square, rest

    for i, (k, first) in enumerate(items):
        a_blocks, a_half, g_blocks, kind = pieces[k]
        out = outs[i]
        count = len(columns(pieces, (k, first), count_a, count_g))
        (*a_bufs, pre_buf, grad_buf) = buffers[:count] if g_blocks else [*buffers[:count], None, None]
        del buffers[:count]
        for copy in mine[: count * slots]:
            copy.wait()
        del mine[: count * slots]
        for slot in range(slots):
            here = kind * SLOTS + first + slot
            if here not in tiles:
                tiles[here] = jnp.zeros((EDGE, B), jnp.float32) if fresh else notes_in[here]
            index = corner_indices(pieces, k)
            at = 0
            for b in range(len(a_blocks)):
                block = cov(a_bufs[0][slot, :, b * B : (b + 1) * B])
                out[slot, at : at + H, :] = fold(block, here, next(index), 0)
                at = at + H
            if a_half:
                odd = slot_owner(first + slot, KINDS[kind]) & 1
                square, rest = fold_half(cov(a_bufs[-1][slot]), odd, here, next(index))
                out[slot, at : at + quarter, :] = square
                out[slot, at + quarter : at + quarter * 3 // 2, :] = rest
                at = at + quarter * 3 // 2
            for b in range(len(g_blocks)):
                part = slice(b * B, (b + 1) * B)
                value = pre_buf[slot, :, part].astype(jnp.float32)
                grad = grad_buf[slot, :, part].astype(jnp.float32)
                block = cov((grad * gelu_slope(value)).astype(jnp.bfloat16))
                out[slot, at : at + H, :] = fold(block, here, next(index), 1)
                at = at + H
            if has_edge(pieces, k):
                out[slot, at:, :] = tiles[here]

    for slot in range(NOTES):
        if slot in tiles:
            notes[slot] = tiles[slot]
        else:
            notes[slot] = jnp.zeros((EDGE, B), jnp.float32) if fresh else notes_in[slot]
    lines = [jnp.sum(trace, axis=0, keepdims=True) for trace in traces]
    tile = jnp.where(note_row == 0, lines[0], jnp.where(note_row == 1, lines[1], 0.0))
    notes[NOTES] = tile if fresh else notes_in[NOTES] + tile
    for copy in later:
        copy.wait()


def pack(arrays, pieces, items, ahead, count_a, count_g, notes, buffers):
    tokens, dtype = arrays[0].shape[0], arrays[0].dtype
    slots = SLOTS // 2

    def shapes(of):
        return [
            (slots, tokens, size)
            for item in of
            for _, _, size in columns(pieces, item, count_a, count_g)
        ]

    fresh = notes is None
    own, after = shapes(items), shapes(ahead)
    scratch = [pltpu.VMEM(shape, dtype) for shape in own] if fresh else []
    for moves in ((own if fresh else []), after):
        if moves:
            scratch.append(pltpu.SemaphoreType.DMA((len(moves), slots)))
    extra = [] if fresh else [notes, *buffers]
    out_shape = [
        jax.ShapeDtypeStruct((slots, piece_rows(pieces, k), B), jnp.float32) for k, _ in items
    ]
    out_shape.append(jax.ShapeDtypeStruct((NOTES + 1, EDGE, B), jnp.float32))
    out_shape += [jax.ShapeDtypeStruct(shape, dtype) for shape in after]
    outs = pl.pallas_call(
        functools.partial(pack_body, pieces, items, ahead, count_a, count_g, fresh),
        in_specs=[pl.BlockSpec(memory_space=pltpu.HBM)] * 3
        + [pl.BlockSpec(memory_space=pltpu.VMEM)] * len(extra),
        out_specs=[pl.BlockSpec(memory_space=pltpu.VMEM)] * len(out_shape),
        out_shape=out_shape,
        scratch_shapes=scratch,
        compiler_params=pltpu.CompilerParams(vmem_limit_bytes=32 * 2**20),
        cost_estimate=pl.CostEstimate(flops=1, bytes_accessed=1, transcendentals=0),
    )(*arrays, *extra)
    n = len(items)
    return outs[:n], outs[n], outs[n + 1 :]


def halve_body(n, summed, gathered, *refs):
    keeps, gots, refs = refs[:n], refs[n : 2 * n], refs[2 * n :]
    split = len(refs) - 2 * n - summed
    traces, outs = refs[:split], refs[split:]
    for k in range(n):
        half = keeps[k].shape[0] // 2
        for part in range(2):
            here = slice(part * half, (part + 1) * half)
            outs[2 * k + part][...] = keeps[k][here] + gots[k][here]
    if summed:
        outs[-1][...] = traces[0][...] + traces[1][...]
    elif traces:
        value = traces[0][...]
        if gathered:
            value = value + sum(got[0, -2:, :] for got in gots)
        for out in outs:
            out[0, -2:, :] = value


def halve(keeps, gots, traces=(), gathered=False, weight=1):
    summed = len(traces) == 2
    n = len(keeps)
    args = (*keeps, *gots, *traces)
    shapes = [(keep.shape[0] // 2, *keep.shape[1:]) for keep in keeps for _ in range(2)]
    shapes += [trace.shape for trace in traces[:summed]]
    outs = pl.pallas_call(
        functools.partial(halve_body, n, summed, gathered),
        in_specs=[pl.BlockSpec(memory_space=pltpu.VMEM)] * len(args),
        out_specs=[pl.BlockSpec(memory_space=pltpu.VMEM)] * len(shapes),
        out_shape=[jax.ShapeDtypeStruct(shape, jnp.float32) for shape in shapes],
        compiler_params=pltpu.CompilerParams(vmem_limit_bytes=32 * 2**20),
        cost_estimate=pl.CostEstimate(flops=weight, bytes_accessed=1, transcendentals=0),
    )(*args)
    return outs[0 : 2 * n : 2], outs[1 : 2 * n : 2], outs[2 * n :]


def mean_of(value, total):
    return value * (1.0 / total) if math.frexp(total)[0] == 0.5 else value / total


def turn(folded):
    return jnp.concatenate([folded] * (B // folded.shape[0]), axis=0).T


def unfold(folded, put):
    row, col = iotas(H)
    turned = turn(folded)
    last = pltpu.roll(jnp.where(col < row, folded, turned[:H]), H, 1)
    put(0, jnp.where(col < row, turned[:H], folded))
    put(H, jnp.where(col < H, turned[H:], last))


def unfold_half(square, rest, odd, put):
    quarter = H // 2
    row, col = iotas(quarter)
    turned = turn(square)
    upper = jnp.where(col < row, turned[:quarter], square)
    last = pltpu.roll(jnp.where(col < row, square, turned[:quarter]), quarter, 1)
    lower = jnp.where(col < quarter, turned[quarter:H], last)
    rest = jnp.concatenate([rest, pltpu.roll(rest, H, 1)], axis=0)
    part = jnp.concatenate([upper, jnp.where(col < H, lower, rest)], axis=0)
    put(0, jnp.where(odd == 1, pltpu.roll(part, H, 1), part))


def places(pieces, ks, count_a):
    full, half = split_rows(count_a)
    odd = lax.axis_index("dp") & half
    for k in ks:
        a_blocks, a_half, g_blocks, kind = pieces[k]
        index = corner_indices(pieces, k)
        for b in a_blocks:
            start = pl.multiple_of(b * B + odd * H, H) if half else b * B
            yield k, 0, start, H, next(index)
        if a_half:
            yield k, 0, pl.multiple_of((1 - odd) * full * B, H), H * 3 // 4, next(index)
        for b in g_blocks:
            yield k, 1, b * B, H, next(index)


def unfold_body(pieces, ks, count_a, total, owns, gots, outs):
    odd = lax.axis_index("dp") & 1
    at = dict.fromkeys(ks, 0)

    def take(k, rows):
        i = ks.index(k)
        at[k] = at[k] + rows
        part = slice(at[k] - rows, at[k])
        return mean_of(owns[i][0, part, :] + gots[i][0, part, :], total)

    for k, which, start, rows, _ in places(pieces, ks, count_a):
        def put(offset, value):
            outs[which][pl.ds(start + offset, value.shape[0]), :] = value

        if rows == H:
            unfold(take(k, H), put)
        else:
            unfold_half(take(k, H // 2), take(k, H // 4), odd, put)


def early_body(pieces, ks, count_a, total, *refs):
    n = len(ks)
    unfold_body(pieces, ks, count_a, total, refs[:n], refs[n : 2 * n], refs[2 * n :])


def finish_body(pieces, early, late, count_a, total, *refs):
    n = len(late)
    owns, gots, (early_a, early_g, a_ref, g_ref) = refs[:n], refs[n : 2 * n], refs[2 * n :]
    outs = (a_ref, g_ref)
    full, half = split_rows(count_a)
    odd = lax.axis_index("dp") & half
    row, col = iotas(H)

    unfold_body(pieces, late, count_a, total, owns, gots, outs)

    edges = {}
    for i, k in enumerate(late):
        edge = mean_of(owns[i][0, -EDGE:, :] + gots[i][0, -EDGE:, :], total)
        edges[pieces[k][3]] = (edge, pltpu.roll(edge, H, 1))
    sums = jnp.sum(edge[-2:], axis=1, keepdims=True)
    ratio = jnp.sqrt(sums[0:1] / D / (sums[1:2] / FFW))
    damp = jnp.sqrt(jnp.full((1, 1), 0.1, jnp.float32))
    shifts = (ratio * damp, damp / ratio)

    def corner(kind, index, natural):
        line = index // 2
        return edges[kind][0 if index % 2 == natural else 1][line : line + 1]

    for ks in (early, late):
        ins = (early_a, early_g) if ks is early else outs
        for k, which, start, rows, index in places(pieces, ks, count_a):
            src, out, shift, kind = ins[which], outs[which], shifts[which], pieces[k][3]
            here = pl.ds(start, H)
            if rows == H:
                low = pl.ds(start + H, H)
                out[here, :] = src[here, :] + jnp.where(col == row, shift, 0.0)
                value = corner(kind, index, 0) + shift
                out[low, :] = jnp.where(col == row + H, value, src[low, :])
            else:
                value = src[here, :] + jnp.where(col == row + odd * H, shift, 0.0)
                line = corner(kind, index, 1)
                line = jnp.where(odd == 1, pltpu.roll(line, H, 1), line) + shift
                last = jnp.logical_and(col == row + odd * H, row >= H // 2)
                out[here, :] = jnp.where(last, line, value)


def unfold_early(pieces, ks, owns, gots, count_a, count_g, total):
    args = (*owns, *gots)
    return pl.pallas_call(
        functools.partial(early_body, pieces, ks, count_a, total),
        in_specs=[pl.BlockSpec(memory_space=pltpu.VMEM)] * len(args),
        out_specs=[pl.BlockSpec(memory_space=pltpu.VMEM)] * 2,
        out_shape=[
            jax.ShapeDtypeStruct((count_a, B), jnp.float32),
            jax.ShapeDtypeStruct((count_g, B), jnp.float32),
        ],
        compiler_params=pltpu.CompilerParams(vmem_limit_bytes=32 * 2**20),
        cost_estimate=pl.CostEstimate(flops=4 * 10**9, bytes_accessed=1, transcendentals=0),
    )(*args)


def finish(pieces, early, late, owns, gots, first, count_a, count_g, total):
    args = (*owns, *gots, *first)
    return pl.pallas_call(
        functools.partial(finish_body, pieces, early, late, count_a, total),
        in_specs=[pl.BlockSpec(memory_space=pltpu.VMEM)] * len(args),
        out_specs=[pl.BlockSpec(memory_space=pltpu.VMEM)] * 2,
        out_shape=[
            jax.ShapeDtypeStruct((count_a, B), jnp.float32),
            jax.ShapeDtypeStruct((count_g, B), jnp.float32),
        ],
        compiler_params=pltpu.CompilerParams(vmem_limit_bytes=32 * 2**20),
    )(*args)


def swap(value, partner):
    dp, tensor = lax.axis_size("dp"), lax.axis_size("tensor")
    pairs = []
    for i in range(dp):
        for j in range(tensor):
            other = partner(i, j)
            pairs.append((i * tensor + j, other[0] * tensor + other[1]))
    return lax.ppermute(value, ("dp", "tensor"), pairs)


def along(stage, kind):
    return lambda i, j: (i ^ (1 << KINDS[kind][j][stage]), j)


def packed(saved_input, saved_pre, grad_act):
    dp = lax.axis_size("dp")
    total = float(saved_input.shape[0] * dp)
    count_a = saved_input.shape[1] // dp
    count_g = saved_pre.shape[1] // dp
    full_a, half_a = split_rows(count_a)
    full_g, _ = split_rows(count_g)
    some = 1 + (full_g - 1) // 2
    pieces = (
        (tuple(range(full_a)), 0, (), 0),
        ((), 0, tuple(range(1, some)), 0),
        ((), half_a, (0,), 1),
        ((), 0, tuple(range(some, full_g)), 1),
    )
    arrays = tuple(
        pltpu.with_memory_space_constraint(array, pltpu.HBM)
        for array in (saved_input, saved_pre, grad_act)
    )
    keep, send = 0, SLOTS // 2
    early, late = (0, 2), (1, 3)
    keeps, gots, notes, buffers = {}, {}, None, None
    calls = [
        tuple((k, first) for k in ks)
        for first, ks in ((send, early), (send, late), (keep, early), (keep, late))
    ]
    for items, ahead in zip(calls, calls[1:] + [()]):
        parts, notes, buffers = pack(
            arrays, pieces, items, ahead, count_a, count_g, notes, buffers
        )
        for (k, first), part in zip(items, parts):
            if first == send:
                gots[k] = swap(part, along(0, pieces[k][3]))
            else:
                keeps[k] = part

    trace = notes[NOTES, :2, :]
    trace = trace + swap(trace, lambda i, j: (i, j ^ 1))
    across = swap(trace, lambda i, j: (i ^ (1 << X) ^ (1 << NEAR), j))
    for stage in (1, 2):
        for ks in (early, late):
            if ks == late:
                traces = (trace,)
            else:
                traces = (trace, across) if stage == 2 else ()
            own, parts, news = halve(
                [keeps[k] for k in ks], [gots[k] for k in ks], traces,
                gathered=stage == 2, weight=WEIGHTS.get((ks, stage), 1)
            )
            trace = news[0] if news else trace
            for k, mine, part in zip(ks, own, parts):
                keeps[k], gots[k] = mine, swap(part, along(stage, pieces[k][3]))

    def both(ks):
        return [keeps[k] for k in ks], [gots[k] for k in ks]

    first = unfold_early(pieces, early, *both(early), count_a, count_g, total)
    a_factor, g_factor = finish(
        pieces, early, late, *both(late), first, count_a, count_g, total
    )
    return a_factor[None], g_factor[None]


def fits(count_a, count_g):
    (full_a, half_a), full_g = split_rows(count_a), count_g // B
    if count_a % H or count_g % B or full_a < 1 or full_g < 3:
        return False
    return full_a + half_a + full_g <= 2 * (EDGE - 2)


def on_device(saved_input, saved_pre, grad_act):
    dp = lax.axis_size("dp")
    count_a = saved_input.shape[1] // dp
    count_g = saved_pre.shape[1] // dp
    if dp == SLOTS and lax.axis_size("tensor") == 2 and fits(count_a, count_g):
        return packed(saved_input, saved_pre, grad_act)
    return plain(saved_input, saved_pre, grad_act)


def solution(mesh):
    spec = P(("groups", "dp"), "tensor")
    out = P("tensor", ("groups", "dp"), None)
    return jax.shard_map(
        on_device, mesh=mesh, in_specs=(spec, spec, spec), out_specs=(out, out), check_vma=False
    )
```

```python
import functools
import math

import jax
import jax.numpy as jnp
from jax import lax
from jax.experimental import pallas as pl
from jax.experimental.pallas import tpu as pltpu
from jax.sharding import PartitionSpec as P

D = 5120
FFW = 10240
B = 128
H = B // 2


def gelu_slope(value):
    return (
        0.5 * (1.0 + lax.erf(value * 0.7071067811865476))
        + value * jnp.exp(-0.5 * value * value) * 0.3989422804014327
    )


def local_blocks(matrix, block, total):
    tokens, width = matrix.shape
    pieces = matrix.reshape(tokens, width // block, block)
    cov = jnp.einsum("tkb,tkc->kbc", pieces, pieces, preferred_element_type=jnp.float32)
    return cov.reshape(width, block) / total


def owned_unit(owned, block):
    count = owned.shape[0]
    rows = lax.axis_index("dp") * count + jnp.arange(count, dtype=jnp.int32)
    cols = jnp.arange(block, dtype=jnp.int32)
    return (cols[None, :] == (rows % block)[:, None]).astype(jnp.float32)


def plain(saved_input, saved_pre, grad_act):
    total = jnp.float32(saved_input.shape[0] * lax.axis_size("dp"))
    slope = gelu_slope(saved_pre.astype(jnp.float32))
    grad_pre = (grad_act.astype(jnp.float32) * slope).astype(jnp.bfloat16)
    terms_a = local_blocks(saved_input, B, total)
    terms_g = local_blocks(grad_pre, B, total)
    owned_a = lax.psum_scatter(terms_a, "dp", scatter_dimension=0, tiled=True)
    owned_g = lax.psum_scatter(terms_g, "dp", scatter_dimension=0, tiled=True)
    unit_a = owned_unit(owned_a, B)
    unit_g = owned_unit(owned_g, B)
    trace_a, trace_g = lax.psum(
        (jnp.sum(owned_a * unit_a), jnp.sum(owned_g * unit_g)), ("dp", "tensor")
    )
    ratio = jnp.sqrt(trace_a / D / (trace_g / FFW))
    damp = jnp.sqrt(jnp.float32(0.1))
    return (
        (owned_a + ratio * damp * unit_a)[None],
        (owned_g + damp / ratio * unit_g)[None],
    )


EDGE = 8
SLOTS = 8
X, NEAR, FAR = 0, 1, 2
KINDS = (((X, NEAR, FAR), (NEAR, X, FAR)), ((NEAR, X, FAR), (X, NEAR, FAR)))
NOTES = len(KINDS) * SLOTS

WEIGHTS = {((0, 2), 2): 2 * 10**9}


def split_rows(count):
    return count // B, (count % B) // H


def has_edge(pieces, k):
    return all(later[3] != pieces[k][3] for later in pieces[k + 1 :])


def piece_rows(pieces, k):
    a_blocks, a_half, g_blocks, _ = pieces[k]
    rows = (len(a_blocks) + len(g_blocks)) * H + a_half * (H * 3 // 4)
    return rows + (EDGE if has_edge(pieces, k) else 0)


def corner_indices(pieces, k):
    parts = [len(a) + a_half + len(g) if kind == pieces[k][3] else 0 for a, a_half, g, kind in pieces]
    return iter(range(sum(parts[:k]), sum(parts[: k + 1])))


def iotas(rows):
    shape = (rows, B)
    return lax.broadcasted_iota(jnp.int32, shape, 0), lax.broadcasted_iota(jnp.int32, shape, 1)


def slot_owner(slot, orders):
    core = lax.axis_index("tensor")
    mask = 0
    for stage, (one, other) in enumerate(zip(*orders)):
        mask = mask | (((slot >> (2 - stage)) & 1) << (one + core * (other - one)))
    return lax.axis_index("dp") ^ mask


def lanes(start, size):
    return pl.ds(start if isinstance(start, int) else pl.multiple_of(start, B), size)


def columns(pieces, item, count_a, count_g):
    k, first = item
    a_blocks, a_half, g_blocks, kind = pieces[k]
    full, half = split_rows(count_a)

    def base(slot):
        owner = slot_owner(first + slot, KINDS[kind])
        return (owner >> half) * (full * (1 + half) + half) * B, owner & half, owner

    found = []
    if a_blocks:

        def whole(slot):
            start, odd, _ = base(slot)
            return start + odd * (full + 1) * B + a_blocks[0] * B

        found.append((0, whole, len(a_blocks) * B))
    if a_half:
        found.append((0, lambda slot: base(slot)[0] + full * B, B))
    if g_blocks:

        def part(slot):
            return base(slot)[2] * count_g + g_blocks[0] * B

        found += [(1, part, len(g_blocks) * B), (2, part, len(g_blocks) * B)]
    return found


def pack_body(pieces, items, ahead, count_a, count_g, fresh, *refs):
    def reads(of):
        return [
            (array, start, size)
            for item in of
            for array, start, size in columns(pieces, item, count_a, count_g)
        ]

    refs = list(refs)

    def pop(count):
        taken = refs[:count]
        del refs[:count]
        return taken

    n, own, after = len(items), reads(items), reads(ahead)
    slots = SLOTS // 2
    hbm = pop(3)
    notes_in, buffers = (None, None) if fresh else (pop(1)[0], pop(len(own)))
    outs, (notes,), nexts = pop(n), pop(1), pop(len(after))
    if fresh:
        buffers = pop(len(own))
    sems = refs

    def copies(moves, into, sem):
        return [
            pltpu.make_async_copy(
                hbm[array].at[:, lanes(start(slot), size)], into[m].at[slot], sem.at[m, slot]
            )
            for m, (array, start, size) in enumerate(moves)
            for slot in range(slots)
        ]

    mine = copies(own, buffers, sems.pop(0)) if fresh else []
    later = copies(after, nexts, sems.pop(0)) if after else []
    for copy in mine + later:
        copy.start()

    full, half = split_rows(count_a)
    row, col = iotas(H)
    low = col < row
    diag_low, diag_high = col == row, col == row + H
    quarter = H // 2
    row_q, col_q = row[:quarter], col[:quarter]
    note_row, _ = iotas(EDGE)
    zero = jnp.zeros((H, B), jnp.float32)
    traces = [zero, zero]
    tiles = {}

    def cov(part):
        return lax.dot_general(
            part, part, (((0,), (0,)), ((), ())), preferred_element_type=jnp.float32
        )

    def note(slot, index, corner, natural):
        line = jnp.sum(corner, axis=0, keepdims=True)
        if index % 2 != natural:
            line = pltpu.roll(line, H, 1)
        tiles[slot] = tiles[slot] + jnp.where(note_row == index // 2, line, 0.0)

    def fold(block, slot, index, which):
        top, bottom = block[:H], block[H:]
        corner = jnp.where(diag_high, bottom, zero)
        note(slot, index, corner, 0)
        traces[which] = traces[which] + corner + jnp.where(diag_low, top, zero)
        return jnp.where(low, pltpu.roll(bottom, H, 1), top)

    def fold_half(block, odd, slot, index):
        part = jnp.where(odd == 1, pltpu.roll(block[H:], H, 1), block[:H])
        traces[0] = traces[0] + jnp.where(diag_low, part, zero)
        upper, lower = part[:quarter], part[quarter:]
        corner = jnp.where(col_q == row_q + quarter, lower, 0.0)
        note(slot, index, corner, 1)
        square = jnp.where(col_q < row_q, pltpu.roll(lower, B - quarter, 1), upper)
        rest = lower.reshape(2, quarter // 2, B)
        rest = jnp.where(col[: quarter // 2] < H, pltpu.roll(rest[1], H, 1), rest[0])
        return square, rest

    for i, (k, first) in enumerate(items):
        a_blocks, a_half, g_blocks, kind = pieces[k]
        out = outs[i]
        count = len(columns(pieces, (k, first), count_a, count_g))
        (*a_bufs, pre_buf, grad_buf) = buffers[:count] if g_blocks else [*buffers[:count], None, None]
        del buffers[:count]
        for copy in mine[: count * slots]:
            copy.wait()
        del mine[: count * slots]
        for slot in range(slots):
            here = kind * SLOTS + first + slot
            if here not in tiles:
                tiles[here] = jnp.zeros((EDGE, B), jnp.float32) if fresh else notes_in[here]
            index = corner_indices(pieces, k)
            at = 0
            for b in range(len(a_blocks)):
                block = cov(a_bufs[0][slot, :, b * B : (b + 1) * B])
                out[slot, at : at + H, :] = fold(block, here, next(index), 0)
                at = at + H
            if a_half:
                odd = slot_owner(first + slot, KINDS[kind]) & 1
                square, rest = fold_half(cov(a_bufs[-1][slot]), odd, here, next(index))
                out[slot, at : at + quarter, :] = square
                out[slot, at + quarter : at + quarter * 3 // 2, :] = rest
                at = at + quarter * 3 // 2
            for b in range(len(g_blocks)):
                part = slice(b * B, (b + 1) * B)
                value = pre_buf[slot, :, part].astype(jnp.float32)
                grad = grad_buf[slot, :, part].astype(jnp.float32)
                block = cov((grad * gelu_slope(value)).astype(jnp.bfloat16))
                out[slot, at : at + H, :] = fold(block, here, next(index), 1)
                at = at + H
            if has_edge(pieces, k):
                out[slot, at:, :] = tiles[here]

    for slot in range(NOTES):
        if slot in tiles:
            notes[slot] = tiles[slot]
        else:
            notes[slot] = jnp.zeros((EDGE, B), jnp.float32) if fresh else notes_in[slot]
    lines = [jnp.sum(trace, axis=0, keepdims=True) for trace in traces]
    tile = jnp.where(note_row == 0, lines[0], jnp.where(note_row == 1, lines[1], 0.0))
    notes[NOTES] = tile if fresh else notes_in[NOTES] + tile
    for copy in later:
        copy.wait()


def pack(arrays, pieces, items, ahead, count_a, count_g, notes, buffers):
    tokens, dtype = arrays[0].shape[0], arrays[0].dtype
    slots = SLOTS // 2

    def shapes(of):
        return [
            (slots, tokens, size)
            for item in of
            for _, _, size in columns(pieces, item, count_a, count_g)
        ]

    fresh = notes is None
    own, after = shapes(items), shapes(ahead)
    scratch = [pltpu.VMEM(shape, dtype) for shape in own] if fresh else []
    for moves in ((own if fresh else []), after):
        if moves:
            scratch.append(pltpu.SemaphoreType.DMA((len(moves), slots)))
    extra = [] if fresh else [notes, *buffers]
    out_shape = [
        jax.ShapeDtypeStruct((slots, piece_rows(pieces, k), B), jnp.float32) for k, _ in items
    ]
    out_shape.append(jax.ShapeDtypeStruct((NOTES + 1, EDGE, B), jnp.float32))
    out_shape += [jax.ShapeDtypeStruct(shape, dtype) for shape in after]
    outs = pl.pallas_call(
        functools.partial(pack_body, pieces, items, ahead, count_a, count_g, fresh),
        in_specs=[pl.BlockSpec(memory_space=pltpu.HBM)] * 3
        + [pl.BlockSpec(memory_space=pltpu.VMEM)] * len(extra),
        out_specs=[pl.BlockSpec(memory_space=pltpu.VMEM)] * len(out_shape),
        out_shape=out_shape,
        scratch_shapes=scratch,
        compiler_params=pltpu.CompilerParams(vmem_limit_bytes=32 * 2**20),
        cost_estimate=pl.CostEstimate(flops=1, bytes_accessed=1, transcendentals=0),
    )(*arrays, *extra)
    n = len(items)
    return outs[:n], outs[n], outs[n + 1 :]


def halve_body(n, summed, gathered, *refs):
    keeps, gots, refs = refs[:n], refs[n : 2 * n], refs[2 * n :]
    split = len(refs) - 2 * n - summed
    traces, outs = refs[:split], refs[split:]
    for k in range(n):
        half = keeps[k].shape[0] // 2
        for part in range(2):
            here = slice(part * half, (part + 1) * half)
            outs[2 * k + part][...] = keeps[k][here] + gots[k][here]
    if summed:
        outs[-1][...] = traces[0][...] + traces[1][...]
    elif traces:
        value = traces[0][...]
        if gathered:
            value = value + sum(got[0, -2:, :] for got in gots)
        for out in outs:
            out[0, -2:, :] = value


def halve(keeps, gots, traces=(), gathered=False, weight=1):
    summed = len(traces) == 2
    n = len(keeps)
    args = (*keeps, *gots, *traces)
    shapes = [(keep.shape[0] // 2, *keep.shape[1:]) for keep in keeps for _ in range(2)]
    shapes += [trace.shape for trace in traces[:summed]]
    outs = pl.pallas_call(
        functools.partial(halve_body, n, summed, gathered),
        in_specs=[pl.BlockSpec(memory_space=pltpu.VMEM)] * len(args),
        out_specs=[pl.BlockSpec(memory_space=pltpu.VMEM)] * len(shapes),
        out_shape=[jax.ShapeDtypeStruct(shape, jnp.float32) for shape in shapes],
        compiler_params=pltpu.CompilerParams(vmem_limit_bytes=32 * 2**20),
        cost_estimate=pl.CostEstimate(flops=weight, bytes_accessed=1, transcendentals=0),
    )(*args)
    return outs[0 : 2 * n : 2], outs[1 : 2 * n : 2], outs[2 * n :]


def mean_of(value, total):
    return value * (1.0 / total) if math.frexp(total)[0] == 0.5 else value / total


def turn(folded):
    return jnp.concatenate([folded] * (B // folded.shape[0]), axis=0).T


def unfold(folded, put):
    row, col = iotas(H)
    turned = turn(folded)
    last = pltpu.roll(jnp.where(col < row, folded, turned[:H]), H, 1)
    put(0, jnp.where(col < row, turned[:H], folded))
    put(H, jnp.where(col < H, turned[H:], last))


def unfold_half(square, rest, odd, put):
    quarter = H // 2
    row, col = iotas(quarter)
    turned = turn(square)
    upper = jnp.where(col < row, turned[:quarter], square)
    last = pltpu.roll(jnp.where(col < row, square, turned[:quarter]), quarter, 1)
    lower = jnp.where(col < quarter, turned[quarter:H], last)
    rest = jnp.concatenate([rest, pltpu.roll(rest, H, 1)], axis=0)
    part = jnp.concatenate([upper, jnp.where(col < H, lower, rest)], axis=0)
    put(0, jnp.where(odd == 1, pltpu.roll(part, H, 1), part))


def places(pieces, ks, count_a):
    full, half = split_rows(count_a)
    odd = lax.axis_index("dp") & half
    for k in ks:
        a_blocks, a_half, g_blocks, kind = pieces[k]
        index = corner_indices(pieces, k)
        for b in a_blocks:
            start = pl.multiple_of(b * B + odd * H, H) if half else b * B
            yield k, 0, start, H, next(index)
        if a_half:
            yield k, 0, pl.multiple_of((1 - odd) * full * B, H), H * 3 // 4, next(index)
        for b in g_blocks:
            yield k, 1, b * B, H, next(index)


def unfold_body(pieces, ks, count_a, total, owns, gots, outs):
    odd = lax.axis_index("dp") & 1
    at = dict.fromkeys(ks, 0)

    def take(k, rows):
        i = ks.index(k)
        at[k] = at[k] + rows
        part = slice(at[k] - rows, at[k])
        return mean_of(owns[i][0, part, :] + gots[i][0, part, :], total)

    for k, which, start, rows, _ in places(pieces, ks, count_a):
        def put(offset, value):
            outs[which][pl.ds(start + offset, value.shape[0]), :] = value

        if rows == H:
            unfold(take(k, H), put)
        else:
            unfold_half(take(k, H // 2), take(k, H // 4), odd, put)


def early_body(pieces, ks, count_a, total, *refs):
    n = len(ks)
    unfold_body(pieces, ks, count_a, total, refs[:n], refs[n : 2 * n], refs[2 * n :])


def finish_body(pieces, early, late, count_a, total, *refs):
    n = len(late)
    owns, gots, (early_a, early_g, a_ref, g_ref) = refs[:n], refs[n : 2 * n], refs[2 * n :]
    outs = (a_ref, g_ref)
    full, half = split_rows(count_a)
    odd = lax.axis_index("dp") & half
    row, col = iotas(H)

    unfold_body(pieces, late, count_a, total, owns, gots, outs)

    edges = {}
    for i, k in enumerate(late):
        edge = mean_of(owns[i][0, -EDGE:, :] + gots[i][0, -EDGE:, :], total)
        edges[pieces[k][3]] = (edge, pltpu.roll(edge, H, 1))
    sums = jnp.sum(edge[-2:], axis=1, keepdims=True)
    ratio = jnp.sqrt(sums[0:1] / D / (sums[1:2] / FFW))
    damp = jnp.sqrt(jnp.full((1, 1), 0.1, jnp.float32))
    shifts = (ratio * damp, damp / ratio)

    def corner(kind, index, natural):
        line = index // 2
        return edges[kind][0 if index % 2 == natural else 1][line : line + 1]

    for ks in (early, late):
        ins = (early_a, early_g) if ks is early else outs
        for k, which, start, rows, index in places(pieces, ks, count_a):
            src, out, shift, kind = ins[which], outs[which], shifts[which], pieces[k][3]
            here = pl.ds(start, H)
            if rows == H:
                low = pl.ds(start + H, H)
                out[here, :] = src[here, :] + jnp.where(col == row, shift, 0.0)
                value = corner(kind, index, 0) + shift
                out[low, :] = jnp.where(col == row + H, value, src[low, :])
            else:
                value = src[here, :] + jnp.where(col == row + odd * H, shift, 0.0)
                line = corner(kind, index, 1)
                line = jnp.where(odd == 1, pltpu.roll(line, H, 1), line) + shift
                last = jnp.logical_and(col == row + odd * H, row >= H // 2)
                out[here, :] = jnp.where(last, line, value)


def unfold_early(pieces, ks, owns, gots, count_a, count_g, total):
    args = (*owns, *gots)
    return pl.pallas_call(
        functools.partial(early_body, pieces, ks, count_a, total),
        in_specs=[pl.BlockSpec(memory_space=pltpu.VMEM)] * len(args),
        out_specs=[pl.BlockSpec(memory_space=pltpu.VMEM)] * 2,
        out_shape=[
            jax.ShapeDtypeStruct((count_a, B), jnp.float32),
            jax.ShapeDtypeStruct((count_g, B), jnp.float32),
        ],
        compiler_params=pltpu.CompilerParams(vmem_limit_bytes=32 * 2**20),
        cost_estimate=pl.CostEstimate(flops=4 * 10**9, bytes_accessed=1, transcendentals=0),
    )(*args)


def finish(pieces, early, late, owns, gots, first, count_a, count_g, total):
    args = (*owns, *gots, *first)
    return pl.pallas_call(
        functools.partial(finish_body, pieces, early, late, count_a, total),
        in_specs=[pl.BlockSpec(memory_space=pltpu.VMEM)] * len(args),
        out_specs=[pl.BlockSpec(memory_space=pltpu.VMEM)] * 2,
        out_shape=[
            jax.ShapeDtypeStruct((count_a, B), jnp.float32),
            jax.ShapeDtypeStruct((count_g, B), jnp.float32),
        ],
        compiler_params=pltpu.CompilerParams(vmem_limit_bytes=32 * 2**20),
    )(*args)


def swap(value, partner):
    dp, tensor = lax.axis_size("dp"), lax.axis_size("tensor")
    pairs = []
    for i in range(dp):
        for j in range(tensor):
            other = partner(i, j)
            pairs.append((i * tensor + j, other[0] * tensor + other[1]))
    return lax.ppermute(value, ("dp", "tensor"), pairs)


def along(stage, kind):
    return lambda i, j: (i ^ (1 << KINDS[kind][j][stage]), j)


def packed(saved_input, saved_pre, grad_act):
    dp = lax.axis_size("dp")
    total = float(saved_input.shape[0] * dp)
    count_a = saved_input.shape[1] // dp
    count_g = saved_pre.shape[1] // dp
    full_a, half_a = split_rows(count_a)
    full_g, _ = split_rows(count_g)
    some = 1 + (full_g - 1) // 2
    pieces = (
        (tuple(range(full_a)), 0, (), 0),
        ((), 0, tuple(range(1, some)), 0),
        ((), half_a, (0,), 1),
        ((), 0, tuple(range(some, full_g)), 1),
    )
    arrays = tuple(
        pltpu.with_memory_space_constraint(array, pltpu.HBM)
        for array in (saved_input, saved_pre, grad_act)
    )
    keep, send = 0, SLOTS // 2
    early, late = (0, 2), (1, 3)
    keeps, gots, notes, buffers = {}, {}, None, None
    calls = [
        tuple((k, first) for k in ks)
        for first, ks in ((send, early), (keep, early), (keep, late), (send, late))
    ]
    for items, ahead in zip(calls, calls[1:] + [()]):
        parts, notes, buffers = pack(
            arrays, pieces, items, ahead, count_a, count_g, notes, buffers
        )
        for (k, first), part in zip(items, parts):
            if first == send:
                gots[k] = swap(part, along(0, pieces[k][3]))
            else:
                keeps[k] = part

    trace = notes[NOTES, :2, :]
    trace = trace + swap(trace, lambda i, j: (i, j ^ 1))
    across = swap(trace, lambda i, j: (i ^ (1 << X) ^ (1 << NEAR), j))
    for stage in (1, 2):
        for ks in (early, late):
            if ks == late:
                traces = (trace,)
            else:
                traces = (trace, across) if stage == 2 else ()
            own, parts, news = halve(
                [keeps[k] for k in ks], [gots[k] for k in ks], traces,
                gathered=stage == 2, weight=WEIGHTS.get((ks, stage), 1)
            )
            trace = news[0] if news else trace
            for k, mine, part in zip(ks, own, parts):
                keeps[k], gots[k] = mine, swap(part, along(stage, pieces[k][3]))

    def both(ks):
        return [keeps[k] for k in ks], [gots[k] for k in ks]

    first = unfold_early(pieces, early, *both(early), count_a, count_g, total)
    a_factor, g_factor = finish(
        pieces, early, late, *both(late), first, count_a, count_g, total
    )
    return a_factor[None], g_factor[None]


def fits(count_a, count_g):
    (full_a, half_a), full_g = split_rows(count_a), count_g // B
    if count_a % H or count_g % B or full_a < 1 or full_g < 3:
        return False
    return full_a + half_a + full_g <= 2 * (EDGE - 2)


def on_device(saved_input, saved_pre, grad_act):
    dp = lax.axis_size("dp")
    count_a = saved_input.shape[1] // dp
    count_g = saved_pre.shape[1] // dp
    if dp == SLOTS and lax.axis_size("tensor") == 2 and fits(count_a, count_g):
        return packed(saved_input, saved_pre, grad_act)
    return plain(saved_input, saved_pre, grad_act)


def solution(mesh):
    spec = P(("groups", "dp"), "tensor")
    out = P("tensor", ("groups", "dp"), None)
    return jax.shard_map(
        on_device, mesh=mesh, in_specs=(spec, spec, spec), out_specs=(out, out), check_vma=False
    )
```

```python
import functools
import math

import jax
import jax.numpy as jnp
from jax import lax
from jax.experimental import pallas as pl
from jax.experimental.pallas import tpu as pltpu
from jax.sharding import PartitionSpec as P

D = 5120
FFW = 10240
B = 128
H = B // 2


def gelu_slope(value):
    return (
        0.5 * (1.0 + lax.erf(value * 0.7071067811865476))
        + value * jnp.exp(-0.5 * value * value) * 0.3989422804014327
    )


def local_blocks(matrix, block, total):
    tokens, width = matrix.shape
    pieces = matrix.reshape(tokens, width // block, block)
    cov = jnp.einsum("tkb,tkc->kbc", pieces, pieces, preferred_element_type=jnp.float32)
    return cov.reshape(width, block) / total


def owned_unit(owned, block):
    count = owned.shape[0]
    rows = lax.axis_index("dp") * count + jnp.arange(count, dtype=jnp.int32)
    cols = jnp.arange(block, dtype=jnp.int32)
    return (cols[None, :] == (rows % block)[:, None]).astype(jnp.float32)


def plain(saved_input, saved_pre, grad_act):
    total = jnp.float32(saved_input.shape[0] * lax.axis_size("dp"))
    slope = gelu_slope(saved_pre.astype(jnp.float32))
    grad_pre = (grad_act.astype(jnp.float32) * slope).astype(jnp.bfloat16)
    terms_a = local_blocks(saved_input, B, total)
    terms_g = local_blocks(grad_pre, B, total)
    owned_a = lax.psum_scatter(terms_a, "dp", scatter_dimension=0, tiled=True)
    owned_g = lax.psum_scatter(terms_g, "dp", scatter_dimension=0, tiled=True)
    unit_a = owned_unit(owned_a, B)
    unit_g = owned_unit(owned_g, B)
    trace_a, trace_g = lax.psum(
        (jnp.sum(owned_a * unit_a), jnp.sum(owned_g * unit_g)), ("dp", "tensor")
    )
    ratio = jnp.sqrt(trace_a / D / (trace_g / FFW))
    damp = jnp.sqrt(jnp.float32(0.1))
    return (
        (owned_a + ratio * damp * unit_a)[None],
        (owned_g + damp / ratio * unit_g)[None],
    )


EDGE = 8
SLOTS = 8
X, NEAR, FAR = 0, 1, 2
KINDS = (((X, NEAR, FAR), (NEAR, X, FAR)), ((NEAR, X, FAR), (X, NEAR, FAR)))
NOTES = len(KINDS) * SLOTS


def split_rows(count):
    return count // B, (count % B) // H


def has_edge(pieces, k):
    return all(later[3] != pieces[k][3] for later in pieces[k + 1 :])


def piece_rows(pieces, k):
    a_blocks, a_half, g_blocks, _ = pieces[k]
    rows = (len(a_blocks) + len(g_blocks)) * H + a_half * (H * 3 // 4)
    return rows + (EDGE if has_edge(pieces, k) else 0)


def corner_indices(pieces, k):
    parts = [len(a) + a_half + len(g) if kind == pieces[k][3] else 0 for a, a_half, g, kind in pieces]
    return iter(range(sum(parts[:k]), sum(parts[: k + 1])))


def iotas(rows):
    shape = (rows, B)
    return lax.broadcasted_iota(jnp.int32, shape, 0), lax.broadcasted_iota(jnp.int32, shape, 1)


def slot_owner(slot, orders):
    core = lax.axis_index("tensor")
    mask = 0
    for stage, (one, other) in enumerate(zip(*orders)):
        mask = mask | (((slot >> (2 - stage)) & 1) << (one + core * (other - one)))
    return lax.axis_index("dp") ^ mask


def lanes(start, size):
    return pl.ds(start if isinstance(start, int) else pl.multiple_of(start, B), size)


def columns(pieces, item, count_a, count_g):
    k, first = item
    a_blocks, a_half, g_blocks, kind = pieces[k]
    full, half = split_rows(count_a)

    def base(slot):
        owner = slot_owner(first + slot, KINDS[kind])
        return (owner >> half) * (full * (1 + half) + half) * B, owner & half, owner

    found = []
    if a_blocks:

        def whole(slot):
            start, odd, _ = base(slot)
            return start + odd * (full + 1) * B + a_blocks[0] * B

        found.append((0, whole, len(a_blocks) * B))
    if a_half:
        found.append((0, lambda slot: base(slot)[0] + full * B, B))
    if g_blocks:

        def part(slot):
            return base(slot)[2] * count_g + g_blocks[0] * B

        found += [(1, part, len(g_blocks) * B), (2, part, len(g_blocks) * B)]
    return found


def pack_body(pieces, items, ahead, count_a, count_g, fresh, *refs):
    def reads(of):
        return [
            (array, start, size)
            for item in of
            for array, start, size in columns(pieces, item, count_a, count_g)
        ]

    refs = list(refs)

    def pop(count):
        taken = refs[:count]
        del refs[:count]
        return taken

    n, own, after = len(items), reads(items), reads(ahead)
    slots = SLOTS // 2
    hbm = pop(3)
    notes_in, buffers = (None, None) if fresh else (pop(1)[0], pop(len(own)))
    outs, (notes,), nexts = pop(n), pop(1), pop(len(after))
    if fresh:
        buffers = pop(len(own))
    sems = refs

    def copies(moves, into, sem):
        return [
            pltpu.make_async_copy(
                hbm[array].at[:, lanes(start(slot), size)], into[m].at[slot], sem.at[m, slot]
            )
            for m, (array, start, size) in enumerate(moves)
            for slot in range(slots)
        ]

    mine = copies(own, buffers, sems.pop(0)) if fresh else []
    later = copies(after, nexts, sems.pop(0)) if after else []
    for copy in mine + later:
        copy.start()

    full, half = split_rows(count_a)
    row, col = iotas(H)
    low = col < row
    diag_low, diag_high = col == row, col == row + H
    quarter = H // 2
    row_q, col_q = row[:quarter], col[:quarter]
    note_row, _ = iotas(EDGE)
    zero = jnp.zeros((H, B), jnp.float32)
    traces = [zero, zero]
    tiles = {}

    def cov(part):
        return lax.dot_general(
            part, part, (((0,), (0,)), ((), ())), preferred_element_type=jnp.float32
        )

    def note(slot, index, corner, natural):
        line = jnp.sum(corner, axis=0, keepdims=True)
        if index % 2 != natural:
            line = pltpu.roll(line, H, 1)
        tiles[slot] = tiles[slot] + jnp.where(note_row == index // 2, line, 0.0)

    def fold(block, slot, index, which):
        top, bottom = block[:H], block[H:]
        corner = jnp.where(diag_high, bottom, zero)
        note(slot, index, corner, 0)
        traces[which] = traces[which] + corner + jnp.where(diag_low, top, zero)
        return jnp.where(low, pltpu.roll(bottom, H, 1), top)

    def fold_half(block, odd, slot, index):
        part = jnp.where(odd == 1, pltpu.roll(block[H:], H, 1), block[:H])
        traces[0] = traces[0] + jnp.where(diag_low, part, zero)
        upper, lower = part[:quarter], part[quarter:]
        corner = jnp.where(col_q == row_q + quarter, lower, 0.0)
        note(slot, index, corner, 1)
        square = jnp.where(col_q < row_q, pltpu.roll(lower, B - quarter, 1), upper)
        rest = lower.reshape(2, quarter // 2, B)
        rest = jnp.where(col[: quarter // 2] < H, pltpu.roll(rest[1], H, 1), rest[0])
        return square, rest

    for i, (k, first) in enumerate(items):
        a_blocks, a_half, g_blocks, kind = pieces[k]
        out = outs[i]
        count = len(columns(pieces, (k, first), count_a, count_g))
        (*a_bufs, pre_buf, grad_buf) = buffers[:count] if g_blocks else [*buffers[:count], None, None]
        del buffers[:count]
        for copy in mine[: count * slots]:
            copy.wait()
        del mine[: count * slots]
        for slot in range(slots):
            here = kind * SLOTS + first + slot
            if here not in tiles:
                tiles[here] = jnp.zeros((EDGE, B), jnp.float32) if fresh else notes_in[here]
            index = corner_indices(pieces, k)
            at = 0
            for b in range(len(a_blocks)):
                block = cov(a_bufs[0][slot, :, b * B : (b + 1) * B])
                out[slot, at : at + H, :] = fold(block, here, next(index), 0)
                at = at + H
            if a_half:
                odd = slot_owner(first + slot, KINDS[kind]) & 1
                square, rest = fold_half(cov(a_bufs[-1][slot]), odd, here, next(index))
                out[slot, at : at + quarter, :] = square
                out[slot, at + quarter : at + quarter * 3 // 2, :] = rest
                at = at + quarter * 3 // 2
            for b in range(len(g_blocks)):
                part = slice(b * B, (b + 1) * B)
                value = pre_buf[slot, :, part].astype(jnp.float32)
                grad = grad_buf[slot, :, part].astype(jnp.float32)
                block = cov((grad * gelu_slope(value)).astype(jnp.bfloat16))
                out[slot, at : at + H, :] = fold(block, here, next(index), 1)
                at = at + H
            if has_edge(pieces, k):
                out[slot, at:, :] = tiles[here]

    for slot in range(NOTES):
        if slot in tiles:
            notes[slot] = tiles[slot]
        else:
            notes[slot] = jnp.zeros((EDGE, B), jnp.float32) if fresh else notes_in[slot]
    lines = [jnp.sum(trace, axis=0, keepdims=True) for trace in traces]
    tile = jnp.where(note_row == 0, lines[0], jnp.where(note_row == 1, lines[1], 0.0))
    notes[NOTES] = tile if fresh else notes_in[NOTES] + tile
    for copy in later:
        copy.wait()


def pack(arrays, pieces, items, ahead, count_a, count_g, notes, buffers):
    tokens, dtype = arrays[0].shape[0], arrays[0].dtype
    slots = SLOTS // 2

    def shapes(of):
        return [
            (slots, tokens, size)
            for item in of
            for _, _, size in columns(pieces, item, count_a, count_g)
        ]

    fresh = notes is None
    own, after = shapes(items), shapes(ahead)
    scratch = [pltpu.VMEM(shape, dtype) for shape in own] if fresh else []
    for moves in ((own if fresh else []), after):
        if moves:
            scratch.append(pltpu.SemaphoreType.DMA((len(moves), slots)))
    extra = [] if fresh else [notes, *buffers]
    out_shape = [
        jax.ShapeDtypeStruct((slots, piece_rows(pieces, k), B), jnp.float32) for k, _ in items
    ]
    out_shape.append(jax.ShapeDtypeStruct((NOTES + 1, EDGE, B), jnp.float32))
    out_shape += [jax.ShapeDtypeStruct(shape, dtype) for shape in after]
    outs = pl.pallas_call(
        functools.partial(pack_body, pieces, items, ahead, count_a, count_g, fresh),
        in_specs=[pl.BlockSpec(memory_space=pltpu.HBM)] * 3
        + [pl.BlockSpec(memory_space=pltpu.VMEM)] * len(extra),
        out_specs=[pl.BlockSpec(memory_space=pltpu.VMEM)] * len(out_shape),
        out_shape=out_shape,
        scratch_shapes=scratch,
        compiler_params=pltpu.CompilerParams(vmem_limit_bytes=32 * 2**20),
        cost_estimate=pl.CostEstimate(flops=1, bytes_accessed=1, transcendentals=0),
    )(*arrays, *extra)
    n = len(items)
    return outs[:n], outs[n], outs[n + 1 :]


def halve_body(trace, came, put, passed, *refs):
    refs = list(refs)
    keep, got = refs[:2]
    kept, sent, *sums = refs[2 + trace + passed :]
    sums = sums[passed:]
    half, rows, _ = kept.shape
    kept[...] = keep[:half] + got[:half, :rows, :]
    sent[:, :rows, :] = keep[half:] + got[half:, :rows, :]
    if trace:
        value = refs[2][...]
        if came:
            value = value + got[0, -2:, :]
        for out in sums:
            out[...] = value
        if put:
            tail = sent.shape[1] - rows
            if tail:
                sent[:, rows:, :] = jnp.zeros((half, tail, B), jnp.float32)
            for out in (sent,) if tail else (kept, sent):
                out[0, -2:, :] = value


def halve(keep, got, trace=None, came=False, put=False, tail=False, emit=False, passes=()):
    args = [keep, got, *([] if trace is None else [trace]), *passes]
    slots, rows, _ = keep.shape
    shapes = [(slots // 2, rows, B), (slots // 2, rows + EDGE * tail, B)]
    shapes += [*(array.shape for array in passes), *([(2, B)] * emit)]
    first = len(args) - len(passes)
    kept, sent, *others = pl.pallas_call(
        functools.partial(halve_body, trace is not None, came, put, len(passes)),
        in_specs=[pl.BlockSpec(memory_space=pltpu.VMEM)] * len(args),
        out_specs=[pl.BlockSpec(memory_space=pltpu.VMEM)] * len(shapes),
        out_shape=[jax.ShapeDtypeStruct(shape, jnp.float32) for shape in shapes],
        input_output_aliases={first + i: 2 + i for i in range(len(passes))},
        compiler_params=pltpu.CompilerParams(vmem_limit_bytes=32 * 2**20),
        cost_estimate=pl.CostEstimate(flops=1, bytes_accessed=1, transcendentals=0),
    )(*args)
    return kept, sent, others


def mean_of(value, total):
    return value * (1.0 / total) if math.frexp(total)[0] == 0.5 else value / total


def turn(folded):
    return jnp.concatenate([folded] * (B // folded.shape[0]), axis=0).T


def unfold(folded, put):
    row, col = iotas(H)
    turned = turn(folded)
    last = pltpu.roll(jnp.where(col < row, folded, turned[:H]), H, 1)
    put(0, jnp.where(col < row, turned[:H], folded))
    put(H, jnp.where(col < H, turned[H:], last))


def unfold_half(square, rest, odd, put):
    quarter = H // 2
    row, col = iotas(quarter)
    turned = turn(square)
    upper = jnp.where(col < row, turned[:quarter], square)
    last = pltpu.roll(jnp.where(col < row, square, turned[:quarter]), quarter, 1)
    lower = jnp.where(col < quarter, turned[quarter:H], last)
    rest = jnp.concatenate([rest, pltpu.roll(rest, H, 1)], axis=0)
    part = jnp.concatenate([upper, jnp.where(col < H, lower, rest)], axis=0)
    put(0, jnp.where(odd == 1, pltpu.roll(part, H, 1), part))


def places(pieces, ks, count_a):
    full, half = split_rows(count_a)
    odd = lax.axis_index("dp") & half
    for k in ks:
        a_blocks, a_half, g_blocks, kind = pieces[k]
        index = corner_indices(pieces, k)
        for b in a_blocks:
            start = pl.multiple_of(b * B + odd * H, H) if half else b * B
            yield k, 0, start, H, next(index)
        if a_half:
            yield k, 0, pl.multiple_of((1 - odd) * full * B, H), H * 3 // 4, next(index)
        for b in g_blocks:
            yield k, 1, b * B, H, next(index)


def unfold_body(pieces, ks, count_a, total, owns, gots, outs):
    odd = lax.axis_index("dp") & 1
    at = dict.fromkeys(ks, 0)

    def take(k, rows):
        i = ks.index(k)
        at[k] = at[k] + rows
        part = slice(at[k] - rows, at[k])
        return mean_of(owns[i][0, part, :] + gots[i][0, part, :], total)

    for k, which, start, rows, _ in places(pieces, ks, count_a):
        def put(offset, value):
            outs[which][pl.ds(start + offset, value.shape[0]), :] = value

        if rows == H:
            unfold(take(k, H), put)
        else:
            unfold_half(take(k, H // 2), take(k, H // 4), odd, put)


def early_body(pieces, ks, count_a, total, *refs):
    n = len(ks)
    unfold_body(pieces, ks, count_a, total, refs[:n], refs[n : 2 * n], refs[2 * n :])


def finish_body(pieces, early, late, count_a, total, *refs):
    n = len(late)
    owns, gots, (early_a, early_g, a_ref, g_ref) = refs[:n], refs[n : 2 * n], refs[2 * n :]
    outs = (a_ref, g_ref)
    full, half = split_rows(count_a)
    odd = lax.axis_index("dp") & half
    row, col = iotas(H)

    unfold_body(pieces, late, count_a, total, owns, gots, outs)

    edges = {}
    for k, own, got in zip(late, owns, gots):
        edge = mean_of(own[0, -EDGE:, :] + got[0, -EDGE:, :], total)
        edges[pieces[k][3]] = (edge, pltpu.roll(edge, H, 1))
    sums = jnp.sum(edge[-2:], axis=1, keepdims=True)
    ratio = jnp.sqrt(sums[0:1] / D / (sums[1:2] / FFW))
    damp = jnp.sqrt(jnp.full((1, 1), 0.1, jnp.float32))
    shifts = (ratio * damp, damp / ratio)

    def corner(kind, index, natural):
        line = index // 2
        return edges[kind][0 if index % 2 == natural else 1][line : line + 1]

    for ks in (early, late):
        ins = (early_a, early_g) if ks is early else outs
        for k, which, start, rows, index in places(pieces, ks, count_a):
            src, out, shift, kind = ins[which], outs[which], shifts[which], pieces[k][3]
            here = pl.ds(start, H)
            if rows == H:
                low = pl.ds(start + H, H)
                out[here, :] = src[here, :] + jnp.where(col == row, shift, 0.0)
                value = corner(kind, index, 0) + shift
                out[low, :] = jnp.where(col == row + H, value, src[low, :])
            else:
                value = src[here, :] + jnp.where(col == row + odd * H, shift, 0.0)
                line = corner(kind, index, 1)
                line = jnp.where(odd == 1, pltpu.roll(line, H, 1), line) + shift
                last = jnp.logical_and(col == row + odd * H, row >= H // 2)
                out[here, :] = jnp.where(last, line, value)


def unfold_early(pieces, ks, owns, gots, count_a, count_g, total):
    args = (*owns, *gots)
    return pl.pallas_call(
        functools.partial(early_body, pieces, ks, count_a, total),
        in_specs=[pl.BlockSpec(memory_space=pltpu.VMEM)] * len(args),
        out_specs=[pl.BlockSpec(memory_space=pltpu.VMEM)] * 2,
        out_shape=[
            jax.ShapeDtypeStruct((count_a, B), jnp.float32),
            jax.ShapeDtypeStruct((count_g, B), jnp.float32),
        ],
        compiler_params=pltpu.CompilerParams(vmem_limit_bytes=32 * 2**20),
        cost_estimate=pl.CostEstimate(flops=4 * 10**9, bytes_accessed=1, transcendentals=0),
    )(*args)


def finish(pieces, early, late, owns, gots, first, count_a, count_g, total):
    args = (*owns, *gots, *first)
    return pl.pallas_call(
        functools.partial(finish_body, pieces, early, late, count_a, total),
        in_specs=[pl.BlockSpec(memory_space=pltpu.VMEM)] * len(args),
        out_specs=[pl.BlockSpec(memory_space=pltpu.VMEM)] * 2,
        out_shape=[
            jax.ShapeDtypeStruct((count_a, B), jnp.float32),
            jax.ShapeDtypeStruct((count_g, B), jnp.float32),
        ],
        compiler_params=pltpu.CompilerParams(vmem_limit_bytes=32 * 2**20),
    )(*args)


def swap(value, partner):
    dp, tensor = lax.axis_size("dp"), lax.axis_size("tensor")
    pairs = []
    for i in range(dp):
        for j in range(tensor):
            other = partner(i, j)
            pairs.append((i * tensor + j, other[0] * tensor + other[1]))
    return lax.ppermute(value, ("dp", "tensor"), pairs)


def along(stage, kind):
    return lambda i, j: (i ^ (1 << KINDS[kind][j][stage]), j)


def packed(saved_input, saved_pre, grad_act):
    dp = lax.axis_size("dp")
    total = float(saved_input.shape[0] * dp)
    count_a = saved_input.shape[1] // dp
    count_g = saved_pre.shape[1] // dp
    full_a, half_a = split_rows(count_a)
    full_g, _ = split_rows(count_g)
    some = 1 + (full_g - 1) // 2
    pieces = (
        (tuple(range(full_a)), 0, (), 0),
        ((), half_a, (0,), 1),
        ((), 0, tuple(range(1, some)), 0),
        ((), 0, tuple(range(some, full_g)), 1),
    )
    arrays = tuple(
        pltpu.with_memory_space_constraint(array, pltpu.HBM)
        for array in (saved_input, saved_pre, grad_act)
    )
    keep, send = 0, SLOTS // 2
    early, late = (0, 1), (2, 3)
    keeps, gots, notes, buffers = {}, {}, None, None
    calls = [
        tuple((k, first) for k in ks)
        for first, ks in ((send, early), (keep, early), (keep, late), (send, late))
    ]

    def pack_next():
        nonlocal notes, buffers
        items, ahead = calls.pop(0), calls[0] if calls else ()
        parts, notes, buffers = pack(
            arrays, pieces, items, ahead, count_a, count_g, notes, buffers
        )
        return dict(zip((k for k, _ in items), parts))

    def exchange(k, part, stage):
        gots[k] = swap(part, along(stage, pieces[k][3]))

    def halve_piece(k, stage, **kinds):
        keeps[k], part, others = halve(keeps[k], gots[k], **kinds)
        exchange(k, part, stage)
        return others

    for k, part in pack_next().items():
        exchange(k, part, 0)
    keeps.update(pack_next())
    keeps.update(pack_next())
    waiting = pack_next()

    trace = notes[NOTES, :2, :]
    trace = trace + swap(trace, lambda i, j: (i, j ^ 1))
    (part,) = halve_piece(0, 1, trace=trace, put=True, tail=True, passes=(waiting[2],))
    exchange(2, part, 0)
    (part,) = halve_piece(1, 1, passes=(waiting[3],))
    exchange(3, part, 0)
    (trace,) = halve_piece(0, 2, trace=trace, came=True, emit=True)
    halve_piece(1, 2)
    (gots[0],) = halve_piece(2, 1, passes=(gots[0],))
    (gots[1],) = halve_piece(3, 1, trace=trace, put=True, passes=(gots[1],))
    halve_piece(2, 2)
    halve_piece(3, 2, trace=trace, came=True, put=True)

    def both(ks):
        return [keeps[k] for k in ks], [gots[k] for k in ks]

    first = unfold_early(pieces, early, *both(early), count_a, count_g, total)
    a_factor, g_factor = finish(
        pieces, early, late, *both(late), first, count_a, count_g, total
    )
    return a_factor[None], g_factor[None]


def fits(count_a, count_g):
    (full_a, half_a), full_g = split_rows(count_a), count_g // B
    if count_a % H or count_g % B or full_a < 1 or full_g < 3:
        return False
    return full_a + half_a + full_g <= 2 * (EDGE - 2)


def on_device(saved_input, saved_pre, grad_act):
    dp = lax.axis_size("dp")
    count_a = saved_input.shape[1] // dp
    count_g = saved_pre.shape[1] // dp
    if dp == SLOTS and lax.axis_size("tensor") == 2 and fits(count_a, count_g):
        return packed(saved_input, saved_pre, grad_act)
    return plain(saved_input, saved_pre, grad_act)


def solution(mesh):
    spec = P(("groups", "dp"), "tensor")
    out = P("tensor", ("groups", "dp"), None)
    return jax.shard_map(
        on_device, mesh=mesh, in_specs=(spec, spec, spec), out_specs=(out, out), check_vma=False
    )
```

```python
import functools
import math

import jax
import jax.numpy as jnp
from jax import lax
from jax.experimental import pallas as pl
from jax.experimental.pallas import tpu as pltpu
from jax.sharding import PartitionSpec as P

D = 5120
FFW = 10240
B = 128
H = B // 2


def gelu_slope(value):
    return (
        0.5 * (1.0 + lax.erf(value * 0.7071067811865476))
        + value * jnp.exp(-0.5 * value * value) * 0.3989422804014327
    )


def local_blocks(matrix, block, total):
    tokens, width = matrix.shape
    pieces = matrix.reshape(tokens, width // block, block)
    cov = jnp.einsum("tkb,tkc->kbc", pieces, pieces, preferred_element_type=jnp.float32)
    return cov.reshape(width, block) / total


def owned_unit(owned, block):
    count = owned.shape[0]
    rows = lax.axis_index("dp") * count + jnp.arange(count, dtype=jnp.int32)
    cols = jnp.arange(block, dtype=jnp.int32)
    return (cols[None, :] == (rows % block)[:, None]).astype(jnp.float32)


def plain(saved_input, saved_pre, grad_act):
    total = jnp.float32(saved_input.shape[0] * lax.axis_size("dp"))
    slope = gelu_slope(saved_pre.astype(jnp.float32))
    grad_pre = (grad_act.astype(jnp.float32) * slope).astype(jnp.bfloat16)
    terms_a = local_blocks(saved_input, B, total)
    terms_g = local_blocks(grad_pre, B, total)
    owned_a = lax.psum_scatter(terms_a, "dp", scatter_dimension=0, tiled=True)
    owned_g = lax.psum_scatter(terms_g, "dp", scatter_dimension=0, tiled=True)
    unit_a = owned_unit(owned_a, B)
    unit_g = owned_unit(owned_g, B)
    trace_a, trace_g = lax.psum(
        (jnp.sum(owned_a * unit_a), jnp.sum(owned_g * unit_g)), ("dp", "tensor")
    )
    ratio = jnp.sqrt(trace_a / D / (trace_g / FFW))
    damp = jnp.sqrt(jnp.float32(0.1))
    return (
        (owned_a + ratio * damp * unit_a)[None],
        (owned_g + damp / ratio * unit_g)[None],
    )


EDGE = 8
SLOTS = 8
X, NEAR, FAR = 0, 1, 2
KINDS = (((X, NEAR, FAR), (NEAR, X, FAR)), ((NEAR, X, FAR), (X, NEAR, FAR)))
NOTES = len(KINDS) * SLOTS

WEIGHTS = {((0, 2), 2): 2 * 10**9}


def split_rows(count):
    return count // B, (count % B) // H


def has_edge(pieces, k):
    return all(later[3] != pieces[k][3] for later in pieces[k + 1 :])


def piece_rows(pieces, k):
    a_blocks, a_half, g_blocks, _ = pieces[k]
    rows = (len(a_blocks) + len(g_blocks)) * H + a_half * (H * 3 // 4)
    return rows + (EDGE if has_edge(pieces, k) else 0)


def corner_indices(pieces, k):
    parts = [len(a) + a_half + len(g) if kind == pieces[k][3] else 0 for a, a_half, g, kind in pieces]
    return iter(range(sum(parts[:k]), sum(parts[: k + 1])))


def iotas(rows):
    shape = (rows, B)
    return lax.broadcasted_iota(jnp.int32, shape, 0), lax.broadcasted_iota(jnp.int32, shape, 1)


def slot_owner(slot, orders):
    core = lax.axis_index("tensor")
    mask = 0
    for stage, (one, other) in enumerate(zip(*orders)):
        mask = mask | (((slot >> (2 - stage)) & 1) << (one + core * (other - one)))
    return lax.axis_index("dp") ^ mask


def lanes(start, size):
    return pl.ds(start if isinstance(start, int) else pl.multiple_of(start, B), size)


LOADS = 4


def pack_body(pieces, items, count_a, count_g, fresh, *refs):
    n = len(items)
    if fresh:
        arrays, outs, (notes, *held), sems = refs[:3], refs[3 : 3 + n], refs[3 + n : -1], refs[-1]
    else:
        notes_in, held, outs, notes = refs[0], refs[1:4], refs[4 : 4 + n], refs[-1]
    full, half = split_rows(count_a)
    slots = SLOTS // 2

    def copies(i):
        rows = arrays[i].shape[0] // LOADS
        parts = [slice(part * rows, (part + 1) * rows) for part in range(LOADS)]
        return [
            pltpu.make_async_copy(arrays[i].at[part], held[i].at[part], sems.at[i, part_no])
            for part_no, part in enumerate(parts)
        ]

    waiting = [0, 1, 2] if fresh else []
    for i in waiting:
        for copy in copies(i):
            copy.start()

    def arrive(upto):
        while waiting and waiting[0] <= upto:
            for copy in copies(waiting.pop(0)):
                copy.wait()

    def read(i, start):
        return held[i][:, pl.ds(pl.multiple_of(start, B), B)]

    row, col = iotas(H)
    low = col < row
    diag_low, diag_high = col == row, col == row + H
    quarter = H // 2
    row_q, col_q = row[:quarter], col[:quarter]
    note_row, _ = iotas(EDGE)
    zero = jnp.zeros((H, B), jnp.float32)
    traces = [zero, zero]
    tiles = {}

    def cov(part):
        return lax.dot_general(
            part, part, (((0,), (0,)), ((), ())), preferred_element_type=jnp.float32
        )

    def note(slot, index, corner, natural):
        line = jnp.sum(corner, axis=0, keepdims=True)
        if index % 2 != natural:
            line = pltpu.roll(line, H, 1)
        tiles[slot] = tiles[slot] + jnp.where(note_row == index // 2, line, 0.0)

    def fold(block, slot, index, which):
        top, bottom = block[:H], block[H:]
        corner = jnp.where(diag_high, bottom, zero)
        note(slot, index, corner, 0)
        traces[which] = traces[which] + corner + jnp.where(diag_low, top, zero)
        return jnp.where(low, pltpu.roll(bottom, H, 1), top)

    def fold_half(block, odd, slot, index):
        part = jnp.where(odd == 1, pltpu.roll(block[H:], H, 1), block[:H])
        traces[0] = traces[0] + jnp.where(diag_low, part, zero)
        upper, lower = part[:quarter], part[quarter:]
        corner = jnp.where(col_q == row_q + quarter, lower, 0.0)
        note(slot, index, corner, 1)
        square = jnp.where(col_q < row_q, pltpu.roll(lower, B - quarter, 1), upper)
        rest = lower.reshape(2, quarter // 2, B)
        rest = jnp.where(col[: quarter // 2] < H, pltpu.roll(rest[1], H, 1), rest[0])
        return square, rest

    def a_parts(out, k, first, slot, index):
        a_blocks, a_half, _, kind = pieces[k]
        owner = slot_owner(first + slot, KINDS[kind])
        here, odd = kind * SLOTS + first + slot, owner & half
        base = (owner >> half) * (full * (1 + half) + half) * B
        at = 0
        for b in a_blocks:
            block = cov(read(0, base + (odd * (full + 1) + b) * B))
            out[slot, at : at + H, :] = fold(block, here, next(index), 0)
            at = at + H
        if a_half:
            block = cov(read(0, base + full * B))
            square, rest = fold_half(block, odd, here, next(index))
            out[slot, at : at + quarter, :] = square
            out[slot, at + quarter : at + quarter * 3 // 2, :] = rest
            at = at + quarter * 3 // 2
        return at

    def g_parts(out, k, first, slot, index, at):
        _, _, g_blocks, kind = pieces[k]
        owner = slot_owner(first + slot, KINDS[kind])
        here = kind * SLOTS + first + slot
        for b in g_blocks:
            start = owner * count_g + b * B
            value = read(1, start).astype(jnp.float32)
            grad = read(2, start).astype(jnp.float32)
            block = cov((grad * gelu_slope(value)).astype(jnp.bfloat16))
            out[slot, at : at + H, :] = fold(block, here, next(index), 1)
            at = at + H
        return at

    arrive(0)
    begun = []
    for out, (k, first) in zip(outs, items):
        for slot in range(slots):
            here = pieces[k][3] * SLOTS + first + slot
            if here not in tiles:
                tiles[here] = jnp.zeros((EDGE, B), jnp.float32) if fresh else notes_in[here]
            index = corner_indices(pieces, k)
            begun.append((out, k, first, slot, index, a_parts(out, k, first, slot, index)))
    arrive(2)
    for out, k, first, slot, index, at in begun:
        at = g_parts(out, k, first, slot, index, at)
        if has_edge(pieces, k):
            out[slot, at:, :] = tiles[pieces[k][3] * SLOTS + first + slot]

    for slot in range(NOTES):
        if slot in tiles:
            notes[slot] = tiles[slot]
        else:
            notes[slot] = jnp.zeros((EDGE, B), jnp.float32) if fresh else notes_in[slot]
    lines = [jnp.sum(trace, axis=0, keepdims=True) for trace in traces]
    tile = jnp.where(note_row == 0, lines[0], jnp.where(note_row == 1, lines[1], 0.0))
    notes[NOTES] = tile if fresh else notes_in[NOTES] + tile


def pack(arrays, pieces, items, count_a, count_g, notes):
    fresh = notes is None
    out_shape = [
        jax.ShapeDtypeStruct((SLOTS // 2, piece_rows(pieces, k), B), jnp.float32)
        for k, _ in items
    ]
    out_shape.append(jax.ShapeDtypeStruct((NOTES + 1, EDGE, B), jnp.float32))
    if fresh:
        out_shape += [jax.ShapeDtypeStruct(array.shape, array.dtype) for array in arrays]
    args = arrays if fresh else (notes, *arrays)
    space = pltpu.HBM if fresh else pltpu.VMEM
    outs = pl.pallas_call(
        functools.partial(pack_body, pieces, items, count_a, count_g, fresh),
        in_specs=[pl.BlockSpec(memory_space=space)] * len(args),
        out_specs=[pl.BlockSpec(memory_space=pltpu.VMEM)] * len(out_shape),
        out_shape=out_shape,
        scratch_shapes=[pltpu.SemaphoreType.DMA((len(arrays), LOADS))] * fresh,
        compiler_params=pltpu.CompilerParams(vmem_limit_bytes=32 * 2**20),
        cost_estimate=pl.CostEstimate(flops=1, bytes_accessed=1, transcendentals=0),
    )(*args)
    n = len(items)
    return outs[:n], outs[n], outs[n + 1 :]


def halve_body(n, terms, came, put, merged, *refs):
    keeps, gots, refs = refs[:n], refs[n : 2 * n], refs[2 * n :]
    terms, kept, refs = refs[:terms], refs[terms : terms + n], refs[terms + n :]
    sent, sums = (refs[:1], refs[1:]) if merged else (refs[:n], refs[n:])
    if merged:
        ends = [sum(ref.shape[1] for ref in kept[: k + 1]) for k in range(n)]
        sent = [
            sent[0].at[:, end - ref.shape[1] : end, :] for end, ref in zip(ends, kept)
        ]
    for k in range(n):
        half = kept[k].shape[0]
        kept[k][...] = keeps[k][:half] + gots[k][:half]
        sent[k][...] = keeps[k][half:] + gots[k][half:]
    if terms:
        value = sum((term[...] for term in terms[1:]), terms[0][...])
        for k in came:
            value = value + gots[k][0, -2:, :]
        for out in sums:
            out[...] = value
        for k in put:
            rows = kept[k].shape[1]
            kept[k][0, rows - 2 :, :] = value
            sent[k][0, rows - 2 :, :] = value


def halve(keeps, gots, terms=(), came=(), put=(), merged=False, weight=1):
    n = len(keeps)
    emit = bool(terms) and not put
    args = [*keeps, *gots, *terms]
    kept = [(keep.shape[0] // 2, *keep.shape[1:]) for keep in keeps]
    sent = [(kept[0][0], sum(shape[1] for shape in kept), B)] if merged else kept
    shapes = [*kept, *sent, *([(2, B)] * emit)]
    outs = pl.pallas_call(
        functools.partial(halve_body, n, len(terms), came, put, merged),
        in_specs=[pl.BlockSpec(memory_space=pltpu.VMEM)] * len(args),
        out_specs=[pl.BlockSpec(memory_space=pltpu.VMEM)] * len(shapes),
        out_shape=[jax.ShapeDtypeStruct(shape, jnp.float32) for shape in shapes],
        compiler_params=pltpu.CompilerParams(vmem_limit_bytes=32 * 2**20),
        cost_estimate=pl.CostEstimate(flops=weight, bytes_accessed=1, transcendentals=0),
    )(*args)
    return outs[:n], outs[n : n + len(sent)], outs[n + len(sent) :]


def mean_of(value, total):
    return value * (1.0 / total) if math.frexp(total)[0] == 0.5 else value / total


def turn(folded):
    return jnp.concatenate([folded] * (B // folded.shape[0]), axis=0).T


def unfold(folded, put):
    row, col = iotas(H)
    turned = turn(folded)
    last = pltpu.roll(jnp.where(col < row, folded, turned[:H]), H, 1)
    put(0, jnp.where(col < row, turned[:H], folded))
    put(H, jnp.where(col < H, turned[H:], last))


def unfold_half(square, rest, odd, put):
    quarter = H // 2
    row, col = iotas(quarter)
    turned = turn(square)
    upper = jnp.where(col < row, turned[:quarter], square)
    last = pltpu.roll(jnp.where(col < row, square, turned[:quarter]), quarter, 1)
    lower = jnp.where(col < quarter, turned[quarter:H], last)
    rest = jnp.concatenate([rest, pltpu.roll(rest, H, 1)], axis=0)
    part = jnp.concatenate([upper, jnp.where(col < H, lower, rest)], axis=0)
    put(0, jnp.where(odd == 1, pltpu.roll(part, H, 1), part))


def places(pieces, ks, count_a):
    full, half = split_rows(count_a)
    odd = lax.axis_index("dp") & half
    for k in ks:
        a_blocks, a_half, g_blocks, kind = pieces[k]
        index = corner_indices(pieces, k)
        for b in a_blocks:
            start = pl.multiple_of(b * B + odd * H, H) if half else b * B
            yield k, 0, start, H, next(index)
        if a_half:
            yield k, 0, pl.multiple_of((1 - odd) * full * B, H), H * 3 // 4, next(index)
        for b in g_blocks:
            yield k, 1, b * B, H, next(index)


def row_begins(pieces, ks):
    rows = [piece_rows(pieces, k) for k in ks]
    return {k: sum(rows[:i]) for i, k in enumerate(ks)}


def unfold_body(pieces, ks, count_a, total, owns, got, outs):
    odd = lax.axis_index("dp") & 1
    at = dict.fromkeys(ks, 0)
    begins = row_begins(pieces, ks)

    def take(k, rows):
        begin = at[k]
        at[k] = begin + rows
        mine = owns[ks.index(k)][0, begin : begin + rows, :]
        begin = begin + begins[k]
        return mean_of(mine + got[0, begin : begin + rows, :], total)

    for k, which, start, rows, _ in places(pieces, ks, count_a):
        def put(offset, value):
            outs[which][pl.ds(start + offset, value.shape[0]), :] = value

        if rows == H:
            unfold(take(k, H), put)
        else:
            unfold_half(take(k, H // 2), take(k, H // 4), odd, put)


def early_body(pieces, ks, count_a, total, *refs):
    n = len(ks)
    unfold_body(pieces, ks, count_a, total, refs[:n], refs[n], refs[n + 1 :])


def finish_body(pieces, early, late, count_a, total, *refs):
    n = len(late)
    owns, got, (early_a, early_g, a_ref, g_ref) = refs[:n], refs[n], refs[n + 1 :]
    outs = (a_ref, g_ref)
    full, half = split_rows(count_a)
    odd = lax.axis_index("dp") & half
    row, col = iotas(H)

    unfold_body(pieces, late, count_a, total, owns, got, outs)

    edges = {}
    for k, own in zip(late, owns):
        end = row_begins(pieces, late)[k] + piece_rows(pieces, k)
        edge = mean_of(own[0, -EDGE:, :] + got[0, end - EDGE : end, :], total)
        edges[pieces[k][3]] = (edge, pltpu.roll(edge, H, 1))
    sums = jnp.sum(edge[-2:], axis=1, keepdims=True)
    ratio = jnp.sqrt(sums[0:1] / D / (sums[1:2] / FFW))
    damp = jnp.sqrt(jnp.full((1, 1), 0.1, jnp.float32))
    shifts = (ratio * damp, damp / ratio)

    def corner(kind, index, natural):
        line = index // 2
        return edges[kind][0 if index % 2 == natural else 1][line : line + 1]

    for ks in (early, late):
        ins = (early_a, early_g) if ks is early else outs
        for k, which, start, rows, index in places(pieces, ks, count_a):
            src, out, shift, kind = ins[which], outs[which], shifts[which], pieces[k][3]
            here = pl.ds(start, H)
            if rows == H:
                low = pl.ds(start + H, H)
                out[here, :] = src[here, :] + jnp.where(col == row, shift, 0.0)
                value = corner(kind, index, 0) + shift
                out[low, :] = jnp.where(col == row + H, value, src[low, :])
            else:
                value = src[here, :] + jnp.where(col == row + odd * H, shift, 0.0)
                line = corner(kind, index, 1)
                line = jnp.where(odd == 1, pltpu.roll(line, H, 1), line) + shift
                last = jnp.logical_and(col == row + odd * H, row >= H // 2)
                out[here, :] = jnp.where(last, line, value)


def unfold_early(pieces, ks, owns, got, count_a, count_g, total):
    args = (*owns, got)
    return pl.pallas_call(
        functools.partial(early_body, pieces, ks, count_a, total),
        in_specs=[pl.BlockSpec(memory_space=pltpu.VMEM)] * len(args),
        out_specs=[pl.BlockSpec(memory_space=pltpu.VMEM)] * 2,
        out_shape=[
            jax.ShapeDtypeStruct((count_a, B), jnp.float32),
            jax.ShapeDtypeStruct((count_g, B), jnp.float32),
        ],
        compiler_params=pltpu.CompilerParams(vmem_limit_bytes=32 * 2**20),
        cost_estimate=pl.CostEstimate(flops=4 * 10**9, bytes_accessed=1, transcendentals=0),
    )(*args)


def finish(pieces, early, late, owns, got, first, count_a, count_g, total):
    args = (*owns, got, *first)
    return pl.pallas_call(
        functools.partial(finish_body, pieces, early, late, count_a, total),
        in_specs=[pl.BlockSpec(memory_space=pltpu.VMEM)] * len(args),
        out_specs=[pl.BlockSpec(memory_space=pltpu.VMEM)] * 2,
        out_shape=[
            jax.ShapeDtypeStruct((count_a, B), jnp.float32),
            jax.ShapeDtypeStruct((count_g, B), jnp.float32),
        ],
        compiler_params=pltpu.CompilerParams(vmem_limit_bytes=32 * 2**20),
    )(*args)


def swap(value, partner):
    dp, tensor = lax.axis_size("dp"), lax.axis_size("tensor")
    pairs = []
    for i in range(dp):
        for j in range(tensor):
            other = partner(i, j)
            pairs.append((i * tensor + j, other[0] * tensor + other[1]))
    return lax.ppermute(value, ("dp", "tensor"), pairs)


def along(stage, kind):
    return lambda i, j: (i ^ (1 << KINDS[kind][j][stage]), j)


def packed(saved_input, saved_pre, grad_act):
    dp = lax.axis_size("dp")
    total = float(saved_input.shape[0] * dp)
    count_a = saved_input.shape[1] // dp
    count_g = saved_pre.shape[1] // dp
    full_a, half_a = split_rows(count_a)
    full_g, _ = split_rows(count_g)
    some = 1 + (full_g - 1) // 2
    pieces = (
        (tuple(range(full_a)), 0, (), 0),
        ((), 0, tuple(range(1, some)), 0),
        ((), half_a, (0,), 1),
        ((), 0, tuple(range(some, full_g)), 1),
    )
    arrays = tuple(
        pltpu.with_memory_space_constraint(array, pltpu.HBM)
        for array in (saved_input, saved_pre, grad_act)
    )
    keep, send = 0, SLOTS // 2
    early, late = (0, 2), (1, 3)
    keeps, gots, notes = {}, {}, None

    def pack_next(first, ks):
        nonlocal notes, arrays
        items = tuple((k, first) for k in ks)
        parts, notes, held = pack(arrays, pieces, items, count_a, count_g, notes)
        arrays = held or arrays
        return dict(zip(ks, parts))

    def exchange(parts, stage):
        for k, part in parts.items():
            gots[k] = swap(part, along(stage, pieces[k][3]))

    def halve_pair(ks, stage, **kinds):
        own, parts, others = halve(
            [keeps[k] for k in ks], [gots[k] for k in ks], merged=stage == 2,
            weight=WEIGHTS.get((ks, stage), 1), **kinds
        )
        keeps.update(zip(ks, own))
        if stage == 2:
            gots[ks] = swap(parts[0], lambda i, j: (i ^ (1 << FAR), j))
        else:
            exchange(dict(zip(ks, parts)), stage)
        return others

    exchange(pack_next(send, early), 0)
    exchange(pack_next(send, late), 0)
    keeps.update(pack_next(keep, early))
    keeps.update(pack_next(keep, late))

    trace = notes[NOTES, :2, :]
    trace = trace + swap(trace, lambda i, j: (i, j ^ 1))
    across = swap(trace, lambda i, j: (i ^ (1 << X) ^ (1 << NEAR), j))
    halve_pair(early, 1)
    halve_pair(late, 1, terms=(trace,), put=(0, 1))
    (trace,) = halve_pair(early, 2, terms=(trace, across))
    halve_pair(late, 2, terms=(trace,), came=(0, 1), put=(0, 1))

    def both(ks):
        return [keeps[k] for k in ks], gots[ks]

    first = unfold_early(pieces, early, *both(early), count_a, count_g, total)
    a_factor, g_factor = finish(
        pieces, early, late, *both(late), first, count_a, count_g, total
    )
    return a_factor[None], g_factor[None]


def fits(count_a, count_g):
    (full_a, half_a), full_g = split_rows(count_a), count_g // B
    if count_a % H or count_g % B or full_a < 1 or full_g < 3:
        return False
    return full_a + half_a + full_g <= 2 * (EDGE - 2)


def on_device(saved_input, saved_pre, grad_act):
    dp = lax.axis_size("dp")
    count_a = saved_input.shape[1] // dp
    count_g = saved_pre.shape[1] // dp
    if dp == SLOTS and lax.axis_size("tensor") == 2 and fits(count_a, count_g):
        return packed(saved_input, saved_pre, grad_act)
    return plain(saved_input, saved_pre, grad_act)


def solution(mesh):
    spec = P(("groups", "dp"), "tensor")
    out = P("tensor", ("groups", "dp"), None)
    return jax.shard_map(
        on_device, mesh=mesh, in_specs=(spec, spec, spec), out_specs=(out, out), check_vma=False
    )
```

```python
import functools
import math

import jax
import jax.numpy as jnp
from jax import lax
from jax.experimental import pallas as pl
from jax.experimental.pallas import tpu as pltpu
from jax.sharding import PartitionSpec as P

D = 5120
FFW = 10240
B = 128
H = B // 2


def gelu_slope(value):
    return (
        0.5 * (1.0 + lax.erf(value * 0.7071067811865476))
        + value * jnp.exp(-0.5 * value * value) * 0.3989422804014327
    )


def local_blocks(matrix, block, total):
    tokens, width = matrix.shape
    pieces = matrix.reshape(tokens, width // block, block)
    cov = jnp.einsum("tkb,tkc->kbc", pieces, pieces, preferred_element_type=jnp.float32)
    return cov.reshape(width, block) / total


def owned_unit(owned, block):
    count = owned.shape[0]
    rows = lax.axis_index("dp") * count + jnp.arange(count, dtype=jnp.int32)
    cols = jnp.arange(block, dtype=jnp.int32)
    return (cols[None, :] == (rows % block)[:, None]).astype(jnp.float32)


def plain(saved_input, saved_pre, grad_act):
    total = jnp.float32(saved_input.shape[0] * lax.axis_size("dp"))
    slope = gelu_slope(saved_pre.astype(jnp.float32))
    grad_pre = (grad_act.astype(jnp.float32) * slope).astype(jnp.bfloat16)
    terms_a = local_blocks(saved_input, B, total)
    terms_g = local_blocks(grad_pre, B, total)
    owned_a = lax.psum_scatter(terms_a, "dp", scatter_dimension=0, tiled=True)
    owned_g = lax.psum_scatter(terms_g, "dp", scatter_dimension=0, tiled=True)
    unit_a = owned_unit(owned_a, B)
    unit_g = owned_unit(owned_g, B)
    trace_a, trace_g = lax.psum(
        (jnp.sum(owned_a * unit_a), jnp.sum(owned_g * unit_g)), ("dp", "tensor")
    )
    ratio = jnp.sqrt(trace_a / D / (trace_g / FFW))
    damp = jnp.sqrt(jnp.float32(0.1))
    return (
        (owned_a + ratio * damp * unit_a)[None],
        (owned_g + damp / ratio * unit_g)[None],
    )


EDGE = 8
SLOTS = 8
X, NEAR, FAR = 0, 1, 2
KINDS = (((X, NEAR, FAR), (NEAR, X, FAR)), ((NEAR, X, FAR), (X, NEAR, FAR)))
NOTES = len(KINDS) * SLOTS

WEIGHTS = {((0, 2), 2): 2 * 10**9}


def split_rows(count):
    return count // B, (count % B) // H


def has_edge(pieces, k):
    return all(later[3] != pieces[k][3] for later in pieces[k + 1 :])


def piece_rows(pieces, k):
    a_blocks, a_half, g_blocks, _ = pieces[k]
    rows = (len(a_blocks) + len(g_blocks)) * H + a_half * (H * 3 // 4)
    return rows + (EDGE if has_edge(pieces, k) else 0)


def corner_indices(pieces, k):
    parts = [len(a) + a_half + len(g) if kind == pieces[k][3] else 0 for a, a_half, g, kind in pieces]
    return iter(range(sum(parts[:k]), sum(parts[: k + 1])))


def iotas(rows):
    shape = (rows, B)
    return lax.broadcasted_iota(jnp.int32, shape, 0), lax.broadcasted_iota(jnp.int32, shape, 1)


def slot_owner(slot, orders):
    core = lax.axis_index("tensor")
    mask = 0
    for stage, (one, other) in enumerate(zip(*orders)):
        mask = mask | (((slot >> (2 - stage)) & 1) << (one + core * (other - one)))
    return lax.axis_index("dp") ^ mask


def lanes(start, size):
    return pl.ds(start if isinstance(start, int) else pl.multiple_of(start, B), size)


LOADS = 4


def pack_body(pieces, items, count_a, count_g, call, *refs):
    n = len(items)
    refs = list(refs)

    def pop(count):
        taken = refs[:count]
        del refs[:count]
        return taken

    notes_in = pop(call > 0)
    arrays = pop(3)
    outs, (notes,) = pop(n), pop(1)
    held = pop(1) if call == 0 else arrays[:1] + pop(2) if call == 1 else arrays
    columns, sems = (pop(2) if call == 0 else None), (pop(1) if call < 2 else None)
    fresh = call == 0
    notes_in = notes_in[0] if notes_in else None
    full, half = split_rows(count_a)
    slots = SLOTS // 2
    split = [(i, k, first, slot) for i, (k, first) in enumerate(items) for slot in range(slots)]

    def whole(i):
        rows = arrays[i].shape[0] // LOADS
        return [
            pltpu.make_async_copy(
                arrays[i].at[part * rows : (part + 1) * rows],
                held[i].at[part * rows : (part + 1) * rows],
                sems[0].at[i, part],
            )
            for part in range(LOADS)
        ]

    def own_columns():
        found = []
        for i, k, first, slot in split:
            g_blocks, kind = pieces[k][2:]
            if g_blocks:
                start = slot_owner(first + slot, KINDS[kind]) * count_g + g_blocks[0] * B
                size = len(g_blocks) * B
                for m in (0, 1):
                    src = arrays[1 + m].at[:, pl.ds(pl.multiple_of(start, B), size)]
                    dst = columns[m].at[i * slots + slot, :, :size]
                    sem = sems[0].at[1 + m, i * slots + slot]
                    found.append(pltpu.make_async_copy(src, dst, sem))
        return found

    early = whole(0) if call == 0 else []
    late = own_columns() if call == 0 else whole(1) + whole(2) if call == 1 else []
    for copy in early + late:
        copy.start()

    def read(i, start):
        return held[i][:, pl.ds(pl.multiple_of(start, B), B)]

    def read_g(i, k, first, slot, b):
        _, _, g_blocks, kind = pieces[k]
        if call == 0:
            part = slice((b - g_blocks[0]) * B, (b - g_blocks[0] + 1) * B)
            return [columns[m][i * slots + slot, :, part] for m in (0, 1)]
        start = slot_owner(first + slot, KINDS[kind]) * count_g + b * B
        return [read(1, start), read(2, start)]

    row, col = iotas(H)
    low = col < row
    diag_low, diag_high = col == row, col == row + H
    quarter = H // 2
    row_q, col_q = row[:quarter], col[:quarter]
    note_row, _ = iotas(EDGE)
    zero = jnp.zeros((H, B), jnp.float32)
    traces = [zero, zero]
    tiles = {}

    def cov(part):
        return lax.dot_general(
            part, part, (((0,), (0,)), ((), ())), preferred_element_type=jnp.float32
        )

    def note(slot, index, corner, natural):
        line = jnp.sum(corner, axis=0, keepdims=True)
        if index % 2 != natural:
            line = pltpu.roll(line, H, 1)
        tiles[slot] = tiles[slot] + jnp.where(note_row == index // 2, line, 0.0)

    def fold(block, slot, index, which):
        top, bottom = block[:H], block[H:]
        corner = jnp.where(diag_high, bottom, zero)
        note(slot, index, corner, 0)
        traces[which] = traces[which] + corner + jnp.where(diag_low, top, zero)
        return jnp.where(low, pltpu.roll(bottom, H, 1), top)

    def fold_half(block, odd, slot, index):
        part = jnp.where(odd == 1, pltpu.roll(block[H:], H, 1), block[:H])
        traces[0] = traces[0] + jnp.where(diag_low, part, zero)
        upper, lower = part[:quarter], part[quarter:]
        corner = jnp.where(col_q == row_q + quarter, lower, 0.0)
        note(slot, index, corner, 1)
        square = jnp.where(col_q < row_q, pltpu.roll(lower, B - quarter, 1), upper)
        rest = lower.reshape(2, quarter // 2, B)
        rest = jnp.where(col[: quarter // 2] < H, pltpu.roll(rest[1], H, 1), rest[0])
        return square, rest

    def a_parts(out, k, first, slot, index):
        a_blocks, a_half, _, kind = pieces[k]
        owner = slot_owner(first + slot, KINDS[kind])
        here, odd = kind * SLOTS + first + slot, owner & half
        base = (owner >> half) * (full * (1 + half) + half) * B
        at = 0
        for b in a_blocks:
            block = cov(read(0, base + (odd * (full + 1) + b) * B))
            out[slot, at : at + H, :] = fold(block, here, next(index), 0)
            at = at + H
        if a_half:
            block = cov(read(0, base + full * B))
            square, rest = fold_half(block, odd, here, next(index))
            out[slot, at : at + quarter, :] = square
            out[slot, at + quarter : at + quarter * 3 // 2, :] = rest
            at = at + quarter * 3 // 2
        return at

    def g_parts(i, k, first, slot, index, at):
        _, _, g_blocks, kind = pieces[k]
        here = kind * SLOTS + first + slot
        for b in g_blocks:
            value, grad = (part.astype(jnp.float32) for part in read_g(i, k, first, slot, b))
            block = cov((grad * gelu_slope(value)).astype(jnp.bfloat16))
            outs[i][slot, at : at + H, :] = fold(block, here, next(index), 1)
            at = at + H
        return at

    for copy in early:
        copy.wait()
    begun = []
    for i, k, first, slot in split:
        here = pieces[k][3] * SLOTS + first + slot
        if here not in tiles:
            tiles[here] = jnp.zeros((EDGE, B), jnp.float32) if fresh else notes_in[here]
        index = corner_indices(pieces, k)
        begun.append((index, a_parts(outs[i], k, first, slot, index)))
    for copy in late:
        copy.wait()
    for (i, k, first, slot), (index, at) in zip(split, begun):
        at = g_parts(i, k, first, slot, index, at)
        if has_edge(pieces, k):
            outs[i][slot, at:, :] = tiles[pieces[k][3] * SLOTS + first + slot]

    for slot in range(NOTES):
        if slot in tiles:
            notes[slot] = tiles[slot]
        else:
            notes[slot] = jnp.zeros((EDGE, B), jnp.float32) if fresh else notes_in[slot]
    lines = [jnp.sum(trace, axis=0, keepdims=True) for trace in traces]
    tile = jnp.where(note_row == 0, lines[0], jnp.where(note_row == 1, lines[1], 0.0))
    notes[NOTES] = tile if fresh else notes_in[NOTES] + tile


def pack(arrays, pieces, items, count_a, count_g, call, notes):
    slots = SLOTS // 2
    out_shape = [
        jax.ShapeDtypeStruct((slots, piece_rows(pieces, k), B), jnp.float32) for k, _ in items
    ]
    out_shape.append(jax.ShapeDtypeStruct((NOTES + 1, EDGE, B), jnp.float32))
    moved = arrays[:1] if call == 0 else arrays[1:] if call == 1 else ()
    out_shape += [jax.ShapeDtypeStruct(array.shape, array.dtype) for array in moved]
    scratch = []
    if call == 0:
        width = max(len(pieces[k][2]) for k, _ in items) * B
        shape = (len(items) * slots, arrays[1].shape[0], max(width, B))
        scratch += [pltpu.VMEM(shape, arrays[1].dtype)] * 2
    if call < 2:
        scratch.append(pltpu.SemaphoreType.DMA((3, max(LOADS, len(items) * slots))))
    spaces = [pltpu.HBM] * 3 if call == 0 else [pltpu.VMEM] + [pltpu.HBM] * 2
    spaces = [pltpu.VMEM] * 3 if call > 1 else spaces
    args = [*([notes] if call else []), *arrays]
    spaces = [pltpu.VMEM] * (call > 0) + spaces
    outs = pl.pallas_call(
        functools.partial(pack_body, pieces, items, count_a, count_g, call),
        in_specs=[pl.BlockSpec(memory_space=space) for space in spaces],
        out_specs=[pl.BlockSpec(memory_space=pltpu.VMEM)] * len(out_shape),
        out_shape=out_shape,
        scratch_shapes=scratch,
        compiler_params=pltpu.CompilerParams(vmem_limit_bytes=32 * 2**20),
        cost_estimate=pl.CostEstimate(flops=1, bytes_accessed=1, transcendentals=0),
    )(*args)
    n = len(items)
    return outs[:n], outs[n], outs[n + 1 :]


def halve_body(n, terms, came, put, merged, *refs):
    keeps, gots, refs = refs[:n], refs[n : 2 * n], refs[2 * n :]
    terms, kept, refs = refs[:terms], refs[terms : terms + n], refs[terms + n :]
    sent, sums = (refs[:1], refs[1:]) if merged else (refs[:n], refs[n:])
    if merged:
        ends = [sum(ref.shape[1] for ref in kept[: k + 1]) for k in range(n)]
        sent = [
            sent[0].at[:, end - ref.shape[1] : end, :] for end, ref in zip(ends, kept)
        ]
    for k in range(n):
        half = kept[k].shape[0]
        kept[k][...] = keeps[k][:half] + gots[k][:half]
        sent[k][...] = keeps[k][half:] + gots[k][half:]
    if terms:
        value = sum((term[...] for term in terms[1:]), terms[0][...])
        for k in came:
            value = value + gots[k][0, -2:, :]
        for out in sums:
            out[...] = value
        for k in put:
            rows = kept[k].shape[1]
            kept[k][0, rows - 2 :, :] = value
            sent[k][0, rows - 2 :, :] = value


def halve(keeps, gots, terms=(), came=(), put=(), merged=False, weight=1):
    n = len(keeps)
    emit = bool(terms) and not put
    args = [*keeps, *gots, *terms]
    kept = [(keep.shape[0] // 2, *keep.shape[1:]) for keep in keeps]
    sent = [(kept[0][0], sum(shape[1] for shape in kept), B)] if merged else kept
    shapes = [*kept, *sent, *([(2, B)] * emit)]
    outs = pl.pallas_call(
        functools.partial(halve_body, n, len(terms), came, put, merged),
        in_specs=[pl.BlockSpec(memory_space=pltpu.VMEM)] * len(args),
        out_specs=[pl.BlockSpec(memory_space=pltpu.VMEM)] * len(shapes),
        out_shape=[jax.ShapeDtypeStruct(shape, jnp.float32) for shape in shapes],
        compiler_params=pltpu.CompilerParams(vmem_limit_bytes=32 * 2**20),
        cost_estimate=pl.CostEstimate(flops=weight, bytes_accessed=1, transcendentals=0),
    )(*args)
    return outs[:n], outs[n : n + len(sent)], outs[n + len(sent) :]


def mean_of(value, total):
    return value * (1.0 / total) if math.frexp(total)[0] == 0.5 else value / total


def turn(folded):
    return jnp.concatenate([folded] * (B // folded.shape[0]), axis=0).T


def unfold(folded):
    row, col = iotas(H)
    turned = turn(folded)
    last = pltpu.roll(jnp.where(col < row, folded, turned[:H]), H, 1)
    return jnp.where(col < row, turned[:H], folded), jnp.where(col < H, turned[H:], last)


def unfold_half(square, rest, odd):
    quarter = H // 2
    row, col = iotas(quarter)
    turned = turn(square)
    upper = jnp.where(col < row, turned[:quarter], square)
    last = pltpu.roll(jnp.where(col < row, square, turned[:quarter]), quarter, 1)
    lower = jnp.where(col < quarter, turned[quarter:H], last)
    rest = jnp.concatenate([rest, pltpu.roll(rest, H, 1)], axis=0)
    part = jnp.concatenate([upper, jnp.where(col < H, lower, rest)], axis=0)
    return (jnp.where(odd == 1, pltpu.roll(part, H, 1), part),)


def places(pieces, ks, count_a):
    full, half = split_rows(count_a)
    odd = lax.axis_index("dp") & half
    for k in ks:
        a_blocks, a_half, g_blocks, kind = pieces[k]
        index = corner_indices(pieces, k)
        for b in a_blocks:
            start = pl.multiple_of(b * B + odd * H, H) if half else b * B
            yield k, 0, start, H, next(index)
        if a_half:
            yield k, 0, pl.multiple_of((1 - odd) * full * B, H), H * 3 // 4, next(index)
        for b in g_blocks:
            yield k, 1, b * B, H, next(index)


def row_begins(pieces, ks):
    rows = [piece_rows(pieces, k) for k in ks]
    return {k: sum(rows[:i]) for i, k in enumerate(ks)}


def unfolded(pieces, ks, count_a, total, owns, got):
    odd = lax.axis_index("dp") & 1
    at = dict.fromkeys(ks, 0)
    begins = row_begins(pieces, ks)

    def take(k, rows):
        begin = at[k]
        at[k] = begin + rows
        mine = owns[ks.index(k)][0, begin : begin + rows, :]
        begin = begin + begins[k]
        return mean_of(mine + got[0, begin : begin + rows, :], total)

    for place in places(pieces, ks, count_a):
        k, _, _, rows, _ = place
        if rows == H:
            yield place, unfold(take(k, H))
        else:
            yield place, unfold_half(take(k, H // 2), take(k, H // 4), odd)


def early_body(pieces, ks, count_a, total, *refs):
    n = len(ks)
    owns, got, outs = refs[:n], refs[n], refs[n + 1 :]
    for (_, which, start, _, _), halves in unfolded(pieces, ks, count_a, total, owns, got):
        for i, value in enumerate(halves):
            outs[which][pl.ds(start + i * H, H), :] = value


def finish_body(pieces, early, late, count_a, total, *refs):
    n = len(late)
    owns, got, firsts, outs = refs[:n], refs[n], refs[n + 1 : n + 3], refs[n + 3 : n + 5]
    made, sem = refs[n + 5 : n + 7], refs[n + 7]
    _, half = split_rows(count_a)
    odd = lax.axis_index("dp") & half
    row, col = iotas(H)

    edges = {}
    for k, own in zip(late, owns):
        end = row_begins(pieces, late)[k] + piece_rows(pieces, k)
        edge = mean_of(own[0, -EDGE:, :] + got[0, end - EDGE : end, :], total)
        edges[pieces[k][3]] = (edge, pltpu.roll(edge, H, 1))
    sums = jnp.sum(edge[-2:], axis=1, keepdims=True)
    ratio = jnp.sqrt(sums[0:1] / D / (sums[1:2] / FFW))
    damp = jnp.sqrt(jnp.full((1, 1), 0.1, jnp.float32))
    shifts = (ratio * damp, damp / ratio)

    def corner(kind, index, natural):
        line = index // 2
        return edges[kind][0 if index % 2 == natural else 1][line : line + 1]

    copies = []

    def give(place, halves):
        k, which, start, rows, index = place
        shift, kind = shifts[which], pieces[k][3]
        if rows == H:
            top, bottom = halves
            top = top + jnp.where(col == row, shift, 0.0)
            bottom = jnp.where(col == row + H, corner(kind, index, 0) + shift, bottom)
            halves = (top, bottom)
        else:
            line = corner(kind, index, 1)
            line = jnp.where(odd == 1, pltpu.roll(line, H, 1), line) + shift
            diagonal = col == row + odd * H
            value = halves[0] + jnp.where(diagonal, shift, 0.0)
            last = jnp.logical_and(diagonal, row >= H // 2)
            halves = (jnp.where(last, line, value),)
        for i, value in enumerate(halves):
            made[which][pl.ds(start + i * H, H), :] = value
        part = pl.ds(start, len(halves) * H)
        copy = pltpu.make_async_copy(
            made[which].at[part], outs[which].at[part], sem.at[len(copies)]
        )
        copy.start()
        copies.append(copy)

    for place in places(pieces, early, count_a):
        _, which, start, rows, _ = place
        count = 2 if rows == H else 1
        give(place, [firsts[which][pl.ds(start + i * H, H), :] for i in range(count)])
    for place, halves in unfolded(pieces, late, count_a, total, owns, got):
        give(place, halves)
    for copy in copies:
        copy.wait()


def unfold_early(pieces, ks, owns, got, count_a, count_g, total):
    args = (*owns, got)
    return pl.pallas_call(
        functools.partial(early_body, pieces, ks, count_a, total),
        in_specs=[pl.BlockSpec(memory_space=pltpu.VMEM)] * len(args),
        out_specs=[pl.BlockSpec(memory_space=pltpu.VMEM)] * 2,
        out_shape=[
            jax.ShapeDtypeStruct((count_a, B), jnp.float32),
            jax.ShapeDtypeStruct((count_g, B), jnp.float32),
        ],
        compiler_params=pltpu.CompilerParams(vmem_limit_bytes=32 * 2**20),
        cost_estimate=pl.CostEstimate(flops=4 * 10**9, bytes_accessed=1, transcendentals=0),
    )(*args)


def finish(pieces, early, late, owns, got, first, count_a, count_g, total):
    args = (*owns, got, *first)
    parts = sum(len(a_blocks) + a_half + len(g_blocks) for a_blocks, a_half, g_blocks, _ in pieces)
    return pl.pallas_call(
        functools.partial(finish_body, pieces, early, late, count_a, total),
        in_specs=[pl.BlockSpec(memory_space=pltpu.VMEM)] * len(args),
        out_specs=[pl.BlockSpec(memory_space=pltpu.HBM)] * 2,
        out_shape=[
            jax.ShapeDtypeStruct((count_a, B), jnp.float32),
            jax.ShapeDtypeStruct((count_g, B), jnp.float32),
        ],
        scratch_shapes=[
            pltpu.VMEM((count_a, B), jnp.float32),
            pltpu.VMEM((count_g, B), jnp.float32),
            pltpu.SemaphoreType.DMA((parts,)),
        ],
        compiler_params=pltpu.CompilerParams(vmem_limit_bytes=32 * 2**20),
    )(*args)


def swap(value, partner):
    dp, tensor = lax.axis_size("dp"), lax.axis_size("tensor")
    pairs = []
    for i in range(dp):
        for j in range(tensor):
            other = partner(i, j)
            pairs.append((i * tensor + j, other[0] * tensor + other[1]))
    return lax.ppermute(value, ("dp", "tensor"), pairs)


def along(stage, kind):
    return lambda i, j: (i ^ (1 << KINDS[kind][j][stage]), j)


def packed(saved_input, saved_pre, grad_act):
    dp = lax.axis_size("dp")
    total = float(saved_input.shape[0] * dp)
    count_a = saved_input.shape[1] // dp
    count_g = saved_pre.shape[1] // dp
    full_a, half_a = split_rows(count_a)
    full_g, _ = split_rows(count_g)
    some = 1 + (full_g - 1) // 2
    pieces = (
        (tuple(range(full_a)), 0, (), 0),
        ((), 0, tuple(range(1, some)), 0),
        ((), half_a, (0,), 1),
        ((), 0, tuple(range(some, full_g)), 1),
    )
    arrays = tuple(
        pltpu.with_memory_space_constraint(array, pltpu.HBM)
        for array in (saved_input, saved_pre, grad_act)
    )
    keep, send = 0, SLOTS // 2
    early, late = (0, 2), (1, 3)
    keeps, gots, notes = {}, {}, None

    def pack_next(call, first, ks):
        nonlocal notes, arrays
        items = tuple((k, first) for k in ks)
        parts, notes, held = pack(arrays, pieces, items, count_a, count_g, call, notes)
        arrays = (*arrays[:call], *held, *arrays[call + len(held) :])
        return dict(zip(ks, parts))

    def exchange(parts, stage):
        for k, part in parts.items():
            gots[k] = swap(part, along(stage, pieces[k][3]))

    def halve_pair(ks, stage, **kinds):
        own, parts, others = halve(
            [keeps[k] for k in ks], [gots[k] for k in ks], merged=stage == 2,
            weight=WEIGHTS.get((ks, stage), 1), **kinds
        )
        keeps.update(zip(ks, own))
        if stage == 2:
            gots[ks] = swap(parts[0], lambda i, j: (i ^ (1 << FAR), j))
        else:
            exchange(dict(zip(ks, parts)), stage)
        return others

    exchange(pack_next(0, send, early), 0)
    exchange(pack_next(1, send, late), 0)
    keeps.update(pack_next(2, keep, early))
    keeps.update(pack_next(3, keep, late))

    trace = notes[NOTES, :2, :]
    trace = trace + swap(trace, lambda i, j: (i, j ^ 1))
    across = swap(trace, lambda i, j: (i ^ (1 << X) ^ (1 << NEAR), j))
    halve_pair(early, 1)
    halve_pair(late, 1, terms=(trace,), put=(0, 1))
    (trace,) = halve_pair(early, 2, terms=(trace, across))
    halve_pair(late, 2, terms=(trace,), came=(0, 1), put=(0, 1))

    def both(ks):
        return [keeps[k] for k in ks], gots[ks]

    first = unfold_early(pieces, early, *both(early), count_a, count_g, total)
    a_factor, g_factor = finish(
        pieces, early, late, *both(late), first, count_a, count_g, total
    )
    return a_factor[None], g_factor[None]


def fits(count_a, count_g):
    (full_a, half_a), full_g = split_rows(count_a), count_g // B
    if count_a % H or count_g % B or full_a < 1 or full_g < 3:
        return False
    return full_a + half_a + full_g <= 2 * (EDGE - 2)


def on_device(saved_input, saved_pre, grad_act):
    dp = lax.axis_size("dp")
    count_a = saved_input.shape[1] // dp
    count_g = saved_pre.shape[1] // dp
    if dp == SLOTS and lax.axis_size("tensor") == 2 and fits(count_a, count_g):
        return packed(saved_input, saved_pre, grad_act)
    return plain(saved_input, saved_pre, grad_act)


def solution(mesh):
    spec = P(("groups", "dp"), "tensor")
    out = P("tensor", ("groups", "dp"), None)
    return jax.shard_map(
        on_device, mesh=mesh, in_specs=(spec, spec, spec), out_specs=(out, out), check_vma=False
    )
```

```python
import functools
import math

import jax
import jax.numpy as jnp
from jax import lax
from jax.experimental import pallas as pl
from jax.experimental.pallas import tpu as pltpu
from jax.sharding import PartitionSpec as P

D = 5120
FFW = 10240
B = 128
H = B // 2


def gelu_slope(value):
    return (
        0.5 * (1.0 + lax.erf(value * 0.7071067811865476))
        + value * jnp.exp(-0.5 * value * value) * 0.3989422804014327
    )


def local_blocks(matrix, block, total):
    tokens, width = matrix.shape
    pieces = matrix.reshape(tokens, width // block, block)
    cov = jnp.einsum("tkb,tkc->kbc", pieces, pieces, preferred_element_type=jnp.float32)
    return cov.reshape(width, block) / total


def owned_unit(owned, block):
    count = owned.shape[0]
    rows = lax.axis_index("dp") * count + jnp.arange(count, dtype=jnp.int32)
    cols = jnp.arange(block, dtype=jnp.int32)
    return (cols[None, :] == (rows % block)[:, None]).astype(jnp.float32)


def plain(saved_input, saved_pre, grad_act):
    total = jnp.float32(saved_input.shape[0] * lax.axis_size("dp"))
    slope = gelu_slope(saved_pre.astype(jnp.float32))
    grad_pre = (grad_act.astype(jnp.float32) * slope).astype(jnp.bfloat16)
    terms_a = local_blocks(saved_input, B, total)
    terms_g = local_blocks(grad_pre, B, total)
    owned_a = lax.psum_scatter(terms_a, "dp", scatter_dimension=0, tiled=True)
    owned_g = lax.psum_scatter(terms_g, "dp", scatter_dimension=0, tiled=True)
    unit_a = owned_unit(owned_a, B)
    unit_g = owned_unit(owned_g, B)
    trace_a, trace_g = lax.psum(
        (jnp.sum(owned_a * unit_a), jnp.sum(owned_g * unit_g)), ("dp", "tensor")
    )
    ratio = jnp.sqrt(trace_a / D / (trace_g / FFW))
    damp = jnp.sqrt(jnp.float32(0.1))
    return (
        (owned_a + ratio * damp * unit_a)[None],
        (owned_g + damp / ratio * unit_g)[None],
    )


EDGE = 8
SLOTS = 8
X, NEAR, FAR = 0, 1, 2
KINDS = (((X, NEAR, FAR), (NEAR, X, FAR)), ((NEAR, X, FAR), (X, NEAR, FAR)))
NOTES = len(KINDS) * SLOTS

WEIGHTS = {((0, 2), 2): 2 * 10**9}


def split_rows(count):
    return count // B, (count % B) // H


def has_edge(pieces, k):
    return all(later[3] != pieces[k][3] for later in pieces[k + 1 :])


def piece_rows(pieces, k):
    a_blocks, a_half, g_blocks, _ = pieces[k]
    rows = (len(a_blocks) + len(g_blocks)) * H + a_half * (H * 3 // 4)
    return rows + (EDGE if has_edge(pieces, k) else 0)


def corner_indices(pieces, k):
    parts = [len(a) + a_half + len(g) if kind == pieces[k][3] else 0 for a, a_half, g, kind in pieces]
    return iter(range(sum(parts[:k]), sum(parts[: k + 1])))


def iotas(rows):
    shape = (rows, B)
    return lax.broadcasted_iota(jnp.int32, shape, 0), lax.broadcasted_iota(jnp.int32, shape, 1)


def slot_owner(slot, orders):
    core = lax.axis_index("tensor")
    mask = 0
    for stage, (one, other) in enumerate(zip(*orders)):
        mask = mask | (((slot >> (2 - stage)) & 1) << (one + core * (other - one)))
    return lax.axis_index("dp") ^ mask


def lanes(start, size):
    return pl.ds(start if isinstance(start, int) else pl.multiple_of(start, B), size)


LOADS = 4


def pack_body(pieces, items, count_a, count_g, call, *refs):
    n = len(items)
    refs = list(refs)

    def pop(count):
        taken = refs[:count]
        del refs[:count]
        return taken

    notes_in = pop(call > 0)
    arrays = pop(3)
    outs, (notes,) = pop(n), pop(1)
    held = pop(1) if call == 0 else arrays[:1] + pop(2) if call == 1 else arrays
    columns, sems = (pop(2) if call == 0 else None), (pop(1) if call < 2 else None)
    fresh = call == 0
    notes_in = notes_in[0] if notes_in else None
    full, half = split_rows(count_a)
    slots = SLOTS // 2
    split = [(i, k, first, slot) for i, (k, first) in enumerate(items) for slot in range(slots)]

    def whole(i):
        rows = arrays[i].shape[0] // LOADS
        return [
            pltpu.make_async_copy(
                arrays[i].at[part * rows : (part + 1) * rows],
                held[i].at[part * rows : (part + 1) * rows],
                sems[0].at[i, part],
            )
            for part in range(LOADS)
        ]

    def own_columns():
        found = []
        for i, k, first, slot in split:
            g_blocks, kind = pieces[k][2:]
            if g_blocks:
                start = slot_owner(first + slot, KINDS[kind]) * count_g + g_blocks[0] * B
                size = len(g_blocks) * B
                for m in (0, 1):
                    src = arrays[1 + m].at[:, pl.ds(pl.multiple_of(start, B), size)]
                    dst = columns[m].at[i * slots + slot, :, :size]
                    sem = sems[0].at[1 + m, i * slots + slot]
                    found.append(pltpu.make_async_copy(src, dst, sem))
        return found

    early = whole(0) if call == 0 else []
    late = own_columns() if call == 0 else whole(1) + whole(2) if call == 1 else []
    for copy in early + late:
        copy.start()

    def read(i, start):
        return held[i][:, pl.ds(pl.multiple_of(start, B), B)]

    def read_g(i, k, first, slot, b):
        _, _, g_blocks, kind = pieces[k]
        if call == 0:
            part = slice((b - g_blocks[0]) * B, (b - g_blocks[0] + 1) * B)
            return [columns[m][i * slots + slot, :, part] for m in (0, 1)]
        start = slot_owner(first + slot, KINDS[kind]) * count_g + b * B
        return [read(1, start), read(2, start)]

    row, col = iotas(H)
    low = col < row
    diag_low, diag_high = col == row, col == row + H
    quarter = H // 2
    row_q, col_q = row[:quarter], col[:quarter]
    note_row, _ = iotas(EDGE)
    zero = jnp.zeros((H, B), jnp.float32)
    traces = [zero, zero]
    tiles = {}

    def cov(part):
        return lax.dot_general(
            part, part, (((0,), (0,)), ((), ())), preferred_element_type=jnp.float32
        )

    def note(slot, index, corner, natural):
        line = jnp.sum(corner, axis=0, keepdims=True)
        if index % 2 != natural:
            line = pltpu.roll(line, H, 1)
        tiles[slot] = tiles[slot] + jnp.where(note_row == index // 2, line, 0.0)

    def fold(block, slot, index, which):
        top, bottom = block[:H], block[H:]
        corner = jnp.where(diag_high, bottom, zero)
        note(slot, index, corner, 0)
        traces[which] = traces[which] + corner + jnp.where(diag_low, top, zero)
        return jnp.where(low, pltpu.roll(bottom, H, 1), top)

    def fold_half(block, odd, slot, index):
        part = jnp.where(odd == 1, pltpu.roll(block[H:], H, 1), block[:H])
        traces[0] = traces[0] + jnp.where(diag_low, part, zero)
        upper, lower = part[:quarter], part[quarter:]
        corner = jnp.where(col_q == row_q + quarter, lower, 0.0)
        note(slot, index, corner, 1)
        square = jnp.where(col_q < row_q, pltpu.roll(lower, B - quarter, 1), upper)
        rest = lower.reshape(2, quarter // 2, B)
        rest = jnp.where(col[: quarter // 2] < H, pltpu.roll(rest[1], H, 1), rest[0])
        return square, rest

    def a_parts(out, k, first, slot, index):
        a_blocks, a_half, _, kind = pieces[k]
        owner = slot_owner(first + slot, KINDS[kind])
        here, odd = kind * SLOTS + first + slot, owner & half
        base = (owner >> half) * (full * (1 + half) + half) * B
        at = 0
        for b in a_blocks:
            block = cov(read(0, base + (odd * (full + 1) + b) * B))
            out[slot, at : at + H, :] = fold(block, here, next(index), 0)
            at = at + H
        if a_half:
            block = cov(read(0, base + full * B))
            square, rest = fold_half(block, odd, here, next(index))
            out[slot, at : at + quarter, :] = square
            out[slot, at + quarter : at + quarter * 3 // 2, :] = rest
            at = at + quarter * 3 // 2
        return at

    def g_parts(i, k, first, slot, index, at):
        _, _, g_blocks, kind = pieces[k]
        here = kind * SLOTS + first + slot
        for b in g_blocks:
            value, grad = (part.astype(jnp.float32) for part in read_g(i, k, first, slot, b))
            block = cov((grad * gelu_slope(value)).astype(jnp.bfloat16))
            outs[i][slot, at : at + H, :] = fold(block, here, next(index), 1)
            at = at + H
        return at

    for copy in early:
        copy.wait()
    begun = []
    for i, k, first, slot in split:
        here = pieces[k][3] * SLOTS + first + slot
        if here not in tiles:
            tiles[here] = jnp.zeros((EDGE, B), jnp.float32) if fresh else notes_in[here]
        index = corner_indices(pieces, k)
        begun.append((index, a_parts(outs[i], k, first, slot, index)))
    for copy in late:
        copy.wait()
    for (i, k, first, slot), (index, at) in zip(split, begun):
        at = g_parts(i, k, first, slot, index, at)
        if has_edge(pieces, k):
            outs[i][slot, at:, :] = tiles[pieces[k][3] * SLOTS + first + slot]

    for slot in range(NOTES):
        if slot in tiles:
            notes[slot] = tiles[slot]
        else:
            notes[slot] = jnp.zeros((EDGE, B), jnp.float32) if fresh else notes_in[slot]
    lines = [jnp.sum(trace, axis=0, keepdims=True) for trace in traces]
    tile = jnp.where(note_row == 0, lines[0], jnp.where(note_row == 1, lines[1], 0.0))
    notes[NOTES] = tile if fresh else notes_in[NOTES] + tile


def pack(arrays, pieces, items, count_a, count_g, call, notes):
    slots = SLOTS // 2
    out_shape = [
        jax.ShapeDtypeStruct((slots, piece_rows(pieces, k), B), jnp.float32) for k, _ in items
    ]
    out_shape.append(jax.ShapeDtypeStruct((NOTES + 1, EDGE, B), jnp.float32))
    moved = arrays[:1] if call == 0 else arrays[1:] if call == 1 else ()
    out_shape += [jax.ShapeDtypeStruct(array.shape, array.dtype) for array in moved]
    scratch = []
    if call == 0:
        width = max(len(pieces[k][2]) for k, _ in items) * B
        shape = (len(items) * slots, arrays[1].shape[0], max(width, B))
        scratch += [pltpu.VMEM(shape, arrays[1].dtype)] * 2
    if call < 2:
        scratch.append(pltpu.SemaphoreType.DMA((3, max(LOADS, len(items) * slots))))
    spaces = [pltpu.HBM] * 3 if call == 0 else [pltpu.VMEM] + [pltpu.HBM] * 2
    spaces = [pltpu.VMEM] * 3 if call > 1 else spaces
    args = [*([notes] if call else []), *arrays]
    spaces = [pltpu.VMEM] * (call > 0) + spaces
    outs = pl.pallas_call(
        functools.partial(pack_body, pieces, items, count_a, count_g, call),
        in_specs=[pl.BlockSpec(memory_space=space) for space in spaces],
        out_specs=[pl.BlockSpec(memory_space=pltpu.VMEM)] * len(out_shape),
        out_shape=out_shape,
        scratch_shapes=scratch,
        compiler_params=pltpu.CompilerParams(vmem_limit_bytes=32 * 2**20),
        cost_estimate=pl.CostEstimate(flops=1, bytes_accessed=1, transcendentals=0),
    )(*args)
    n = len(items)
    return outs[:n], outs[n], outs[n + 1 :]


def halve_body(n, terms, came, put, merged, *refs):
    keeps, gots, refs = refs[:n], refs[n : 2 * n], refs[2 * n :]
    terms, kept, refs = refs[:terms], refs[terms : terms + n], refs[terms + n :]
    sent, sums = (refs[:1], refs[1:]) if merged else (refs[:n], refs[n:])
    if merged:
        ends = [sum(ref.shape[1] for ref in kept[: k + 1]) for k in range(n)]
        sent = [
            sent[0].at[:, end - ref.shape[1] : end, :] for end, ref in zip(ends, kept)
        ]
    for k in range(n):
        half = kept[k].shape[0]
        kept[k][...] = keeps[k][:half] + gots[k][:half]
        sent[k][...] = keeps[k][half:] + gots[k][half:]
    if terms:
        value = sum((term[...] for term in terms[1:]), terms[0][...])
        for k in came:
            value = value + gots[k][0, -2:, :]
        for out in sums:
            out[...] = value
        for k in put:
            rows = kept[k].shape[1]
            kept[k][0, rows - 2 :, :] = value
            sent[k][0, rows - 2 :, :] = value


def halve(keeps, gots, terms=(), came=(), put=(), merged=False, weight=1):
    n = len(keeps)
    emit = bool(terms) and not put
    args = [*keeps, *gots, *terms]
    kept = [(keep.shape[0] // 2, *keep.shape[1:]) for keep in keeps]
    sent = [(kept[0][0], sum(shape[1] for shape in kept), B)] if merged else kept
    shapes = [*kept, *sent, *([(2, B)] * emit)]
    outs = pl.pallas_call(
        functools.partial(halve_body, n, len(terms), came, put, merged),
        in_specs=[pl.BlockSpec(memory_space=pltpu.VMEM)] * len(args),
        out_specs=[pl.BlockSpec(memory_space=pltpu.VMEM)] * len(shapes),
        out_shape=[jax.ShapeDtypeStruct(shape, jnp.float32) for shape in shapes],
        compiler_params=pltpu.CompilerParams(vmem_limit_bytes=32 * 2**20),
        cost_estimate=pl.CostEstimate(flops=weight, bytes_accessed=1, transcendentals=0),
    )(*args)
    return outs[:n], outs[n : n + len(sent)], outs[n + len(sent) :]


def mean_of(value, total):
    return value * (1.0 / total) if math.frexp(total)[0] == 0.5 else value / total


def turn(folded):
    return jnp.concatenate([folded] * (B // folded.shape[0]), axis=0).T


def unfold(folded):
    row, col = iotas(H)
    turned = turn(folded)
    last = pltpu.roll(jnp.where(col < row, folded, turned[:H]), H, 1)
    return jnp.where(col < row, turned[:H], folded), jnp.where(col < H, turned[H:], last)


def unfold_half(square, rest, odd):
    quarter = H // 2
    row, col = iotas(quarter)
    turned = turn(square)
    upper = jnp.where(col < row, turned[:quarter], square)
    last = pltpu.roll(jnp.where(col < row, square, turned[:quarter]), quarter, 1)
    lower = jnp.where(col < quarter, turned[quarter:H], last)
    rest = jnp.concatenate([rest, pltpu.roll(rest, H, 1)], axis=0)
    part = jnp.concatenate([upper, jnp.where(col < H, lower, rest)], axis=0)
    return (jnp.where(odd == 1, pltpu.roll(part, H, 1), part),)


def places(pieces, ks, count_a):
    full, half = split_rows(count_a)
    odd = lax.axis_index("dp") & half
    for k in ks:
        a_blocks, a_half, g_blocks, kind = pieces[k]
        index = corner_indices(pieces, k)
        for b in a_blocks:
            start = pl.multiple_of(b * B + odd * H, H) if half else b * B
            yield k, 0, start, H, next(index)
        if a_half:
            yield k, 0, pl.multiple_of((1 - odd) * full * B, H), H * 3 // 4, next(index)
        for b in g_blocks:
            yield k, 1, b * B, H, next(index)


def row_begins(pieces, ks):
    rows = [piece_rows(pieces, k) for k in ks]
    return {k: sum(rows[:i]) for i, k in enumerate(ks)}


def unfolded(pieces, ks, count_a, total, owns, got):
    odd = lax.axis_index("dp") & 1
    at = dict.fromkeys(ks, 0)
    begins = row_begins(pieces, ks)

    def take(k, rows):
        begin = at[k]
        at[k] = begin + rows
        mine = owns[ks.index(k)][0, begin : begin + rows, :]
        begin = begin + begins[k]
        return mean_of(mine + got[0, begin : begin + rows, :], total)

    for place in places(pieces, ks, count_a):
        k, _, _, rows, _ = place
        if rows == H:
            yield place, unfold(take(k, H))
        else:
            yield place, unfold_half(take(k, H // 2), take(k, H // 4), odd)


def early_body(pieces, ks, count_a, total, *refs):
    n = len(ks)
    owns, got, outs = refs[:n], refs[n], refs[n + 1 :]
    for (_, which, start, _, _), halves in unfolded(pieces, ks, count_a, total, owns, got):
        for i, value in enumerate(halves):
            outs[which][pl.ds(start + i * H, H), :] = value


def finish_body(pieces, early, late, count_a, total, *refs):
    n = len(late)
    owns, got, firsts, outs = refs[:n], refs[n], refs[n + 1 : n + 3], refs[n + 3 : n + 5]
    made, sem = refs[n + 5 : n + 7], refs[n + 7]
    _, half = split_rows(count_a)
    odd = lax.axis_index("dp") & half
    row, col = iotas(H)

    edges = {}
    for k, own in zip(late, owns):
        end = row_begins(pieces, late)[k] + piece_rows(pieces, k)
        edge = mean_of(own[0, -EDGE:, :] + got[0, end - EDGE : end, :], total)
        edges[pieces[k][3]] = (edge, pltpu.roll(edge, H, 1))
    sums = jnp.sum(edge[-2:], axis=1, keepdims=True)
    ratio = jnp.sqrt(sums[0:1] / D / (sums[1:2] / FFW))
    damp = jnp.sqrt(jnp.full((1, 1), 0.1, jnp.float32))
    shifts = (ratio * damp, damp / ratio)

    def corner(kind, index, natural):
        line = index // 2
        return edges[kind][0 if index % 2 == natural else 1][line : line + 1]

    copies = []

    def give(place, halves):
        k, which, start, rows, index = place
        shift, kind = shifts[which], pieces[k][3]
        if rows == H:
            top, bottom = halves
            top = top + jnp.where(col == row, shift, 0.0)
            bottom = jnp.where(col == row + H, corner(kind, index, 0) + shift, bottom)
            halves = (top, bottom)
        else:
            line = corner(kind, index, 1)
            line = jnp.where(odd == 1, pltpu.roll(line, H, 1), line) + shift
            diagonal = col == row + odd * H
            value = halves[0] + jnp.where(diagonal, shift, 0.0)
            last = jnp.logical_and(diagonal, row >= H // 2)
            halves = (jnp.where(last, line, value),)
        for i, value in enumerate(halves):
            made[which][pl.ds(start + i * H, H), :] = value
        part = pl.ds(start, len(halves) * H)
        copy = pltpu.make_async_copy(
            made[which].at[part], outs[which].at[part], sem.at[len(copies)]
        )
        copy.start()
        copies.append(copy)

    for place in places(pieces, early, count_a):
        _, which, start, rows, _ = place
        count = 2 if rows == H else 1
        give(place, [firsts[which][pl.ds(start + i * H, H), :] for i in range(count)])
    for place, halves in unfolded(pieces, late, count_a, total, owns, got):
        give(place, halves)
    for copy in copies:
        copy.wait()


def unfold_early(pieces, ks, owns, got, count_a, count_g, total):
    args = (*owns, got)
    return pl.pallas_call(
        functools.partial(early_body, pieces, ks, count_a, total),
        in_specs=[pl.BlockSpec(memory_space=pltpu.VMEM)] * len(args),
        out_specs=[pl.BlockSpec(memory_space=pltpu.VMEM)] * 2,
        out_shape=[
            jax.ShapeDtypeStruct((count_a, B), jnp.float32),
            jax.ShapeDtypeStruct((count_g, B), jnp.float32),
        ],
        compiler_params=pltpu.CompilerParams(vmem_limit_bytes=32 * 2**20),
        cost_estimate=pl.CostEstimate(flops=4 * 10**9, bytes_accessed=1, transcendentals=0),
    )(*args)


def finish(pieces, early, late, owns, got, first, count_a, count_g, total):
    args = (*owns, got, *first)
    parts = sum(len(a_blocks) + a_half + len(g_blocks) for a_blocks, a_half, g_blocks, _ in pieces)
    return pl.pallas_call(
        functools.partial(finish_body, pieces, early, late, count_a, total),
        in_specs=[pl.BlockSpec(memory_space=pltpu.VMEM)] * len(args),
        out_specs=[pl.BlockSpec(memory_space=pltpu.HBM)] * 2,
        out_shape=[
            jax.ShapeDtypeStruct((count_a, B), jnp.float32),
            jax.ShapeDtypeStruct((count_g, B), jnp.float32),
        ],
        scratch_shapes=[
            pltpu.VMEM((count_a, B), jnp.float32),
            pltpu.VMEM((count_g, B), jnp.float32),
            pltpu.SemaphoreType.DMA((parts,)),
        ],
        compiler_params=pltpu.CompilerParams(vmem_limit_bytes=32 * 2**20),
    )(*args)


def swap(value, partner):
    dp, tensor = lax.axis_size("dp"), lax.axis_size("tensor")
    pairs = []
    for i in range(dp):
        for j in range(tensor):
            other = partner(i, j)
            pairs.append((i * tensor + j, other[0] * tensor + other[1]))
    return lax.ppermute(value, ("dp", "tensor"), pairs)


def along(stage, kind):
    return lambda i, j: (i ^ (1 << KINDS[kind][j][stage]), j)


def packed(saved_input, saved_pre, grad_act):
    dp = lax.axis_size("dp")
    total = float(saved_input.shape[0] * dp)
    count_a = saved_input.shape[1] // dp
    count_g = saved_pre.shape[1] // dp
    full_a, half_a = split_rows(count_a)
    full_g, _ = split_rows(count_g)
    some, more = (full_a + 1) // 2, full_g // 2
    pieces = (
        (tuple(range(some, full_a)), half_a, (), 0),
        ((), 0, tuple(range(more)), 0),
        (tuple(range(some)), 0, (), 1),
        ((), 0, tuple(range(more, full_g)), 1),
    )
    arrays = tuple(
        pltpu.with_memory_space_constraint(array, pltpu.HBM)
        for array in (saved_input, saved_pre, grad_act)
    )
    keep, send = 0, SLOTS // 2
    early, late = (0, 2), (1, 3)
    keeps, gots, notes = {}, {}, None

    def pack_next(call, first, ks):
        nonlocal notes, arrays
        items = tuple((k, first) for k in ks)
        parts, notes, held = pack(arrays, pieces, items, count_a, count_g, call, notes)
        arrays = (*arrays[:call], *held, *arrays[call + len(held) :])
        return dict(zip(ks, parts))

    def exchange(parts, stage):
        for k, part in parts.items():
            gots[k] = swap(part, along(stage, pieces[k][3]))

    def halve_pair(ks, stage, **kinds):
        own, parts, others = halve(
            [keeps[k] for k in ks], [gots[k] for k in ks], merged=stage == 2,
            weight=WEIGHTS.get((ks, stage), 1), **kinds
        )
        keeps.update(zip(ks, own))
        if stage == 2:
            gots[ks] = swap(parts[0], lambda i, j: (i ^ (1 << FAR), j))
        else:
            exchange(dict(zip(ks, parts)), stage)
        return others

    exchange(pack_next(0, send, early), 0)
    exchange(pack_next(1, send, late), 0)
    keeps.update(pack_next(2, keep, early))
    keeps.update(pack_next(3, keep, late))

    trace = notes[NOTES, :2, :]
    trace = trace + swap(trace, lambda i, j: (i, j ^ 1))
    across = swap(trace, lambda i, j: (i ^ (1 << X) ^ (1 << NEAR), j))
    halve_pair(early, 1)
    halve_pair(late, 1, terms=(trace,), put=(0, 1))
    (trace,) = halve_pair(early, 2, terms=(trace, across))
    halve_pair(late, 2, terms=(trace,), came=(0, 1), put=(0, 1))

    def both(ks):
        return [keeps[k] for k in ks], gots[ks]

    first = unfold_early(pieces, early, *both(early), count_a, count_g, total)
    a_factor, g_factor = finish(
        pieces, early, late, *both(late), first, count_a, count_g, total
    )
    return a_factor[None], g_factor[None]


def fits(count_a, count_g):
    (full_a, half_a), full_g = split_rows(count_a), count_g // B
    if count_a % H or count_g % B or full_a + half_a < 2 or full_g < 2:
        return False
    return full_a + half_a + full_g <= 2 * (EDGE - 2)


def on_device(saved_input, saved_pre, grad_act):
    dp = lax.axis_size("dp")
    count_a = saved_input.shape[1] // dp
    count_g = saved_pre.shape[1] // dp
    if dp == SLOTS and lax.axis_size("tensor") == 2 and fits(count_a, count_g):
        return packed(saved_input, saved_pre, grad_act)
    return plain(saved_input, saved_pre, grad_act)


def solution(mesh):
    spec = P(("groups", "dp"), "tensor")
    out = P("tensor", ("groups", "dp"), None)
    return jax.shard_map(
        on_device, mesh=mesh, in_specs=(spec, spec, spec), out_specs=(out, out), check_vma=False
    )
```

```python
import functools
import math

import jax
import jax.numpy as jnp
from jax import lax
from jax.experimental import pallas as pl
from jax.experimental.pallas import tpu as pltpu
from jax.sharding import PartitionSpec as P

D = 5120
FFW = 10240
B = 128
H = B // 2


def gelu_slope(value):
    return (
        0.5 * (1.0 + lax.erf(value * 0.7071067811865476))
        + value * jnp.exp(-0.5 * value * value) * 0.3989422804014327
    )


def local_blocks(matrix, block, total):
    tokens, width = matrix.shape
    pieces = matrix.reshape(tokens, width // block, block)
    cov = jnp.einsum("tkb,tkc->kbc", pieces, pieces, preferred_element_type=jnp.float32)
    return cov.reshape(width, block) / total


def owned_unit(owned, block):
    count = owned.shape[0]
    rows = lax.axis_index("dp") * count + jnp.arange(count, dtype=jnp.int32)
    cols = jnp.arange(block, dtype=jnp.int32)
    return (cols[None, :] == (rows % block)[:, None]).astype(jnp.float32)


def plain(saved_input, saved_pre, grad_act):
    total = jnp.float32(saved_input.shape[0] * lax.axis_size("dp"))
    slope = gelu_slope(saved_pre.astype(jnp.float32))
    grad_pre = (grad_act.astype(jnp.float32) * slope).astype(jnp.bfloat16)
    terms_a = local_blocks(saved_input, B, total)
    terms_g = local_blocks(grad_pre, B, total)
    owned_a = lax.psum_scatter(terms_a, "dp", scatter_dimension=0, tiled=True)
    owned_g = lax.psum_scatter(terms_g, "dp", scatter_dimension=0, tiled=True)
    unit_a = owned_unit(owned_a, B)
    unit_g = owned_unit(owned_g, B)
    trace_a, trace_g = lax.psum(
        (jnp.sum(owned_a * unit_a), jnp.sum(owned_g * unit_g)), ("dp", "tensor")
    )
    ratio = jnp.sqrt(trace_a / D / (trace_g / FFW))
    damp = jnp.sqrt(jnp.float32(0.1))
    return (
        (owned_a + ratio * damp * unit_a)[None],
        (owned_g + damp / ratio * unit_g)[None],
    )


EDGE = 8
SLOTS = 8
X, NEAR, FAR = 0, 1, 2
KINDS = (((X, NEAR, FAR), (NEAR, X, FAR)), ((NEAR, X, FAR), (X, NEAR, FAR)))
NOTES = len(KINDS) * SLOTS

WEIGHTS = {((0, 2), 2): 2 * 10**9}


def split_rows(count):
    return count // B, (count % B) // H


def has_edge(pieces, k):
    return all(later[3] != pieces[k][3] for later in pieces[k + 1 :])


def piece_rows(pieces, k):
    a_blocks, a_half, g_blocks, _ = pieces[k]
    rows = (len(a_blocks) + len(g_blocks)) * H + a_half * (H * 3 // 4)
    return rows + (EDGE if has_edge(pieces, k) else 0)


def corner_indices(pieces, k):
    parts = [len(a) + a_half + len(g) if kind == pieces[k][3] else 0 for a, a_half, g, kind in pieces]
    return iter(range(sum(parts[:k]), sum(parts[: k + 1])))


def iotas(rows):
    shape = (rows, B)
    return lax.broadcasted_iota(jnp.int32, shape, 0), lax.broadcasted_iota(jnp.int32, shape, 1)


def slot_owner(slot, orders):
    core = lax.axis_index("tensor")
    mask = 0
    for stage, (one, other) in enumerate(zip(*orders)):
        mask = mask | (((slot >> (2 - stage)) & 1) << (one + core * (other - one)))
    return lax.axis_index("dp") ^ mask


def lanes(start, size):
    return pl.ds(start if isinstance(start, int) else pl.multiple_of(start, B), size)


LOADS = 4
FIRST = 4 * 10**9


def pack_body(pieces, items, count_a, count_g, fresh, *refs):
    n = len(items)
    if fresh:
        (a_hbm, *outs), (notes, a_held, sems) = refs[: n + 1], refs[n + 1 :]
        rows = a_hbm.shape[0] // LOADS
        parts = [slice(part * rows, (part + 1) * rows) for part in range(LOADS)]
        copies = [
            pltpu.make_async_copy(a_hbm.at[part], a_held.at[part], sems.at[i])
            for i, part in enumerate(parts)
        ]
        for copy in copies:
            copy.start()
        held = (a_held,)
    else:
        copies = []
        notes_in, held, outs, notes = refs[0], refs[1:4], refs[4 : 4 + n], refs[4 + n]
    full, half = split_rows(count_a)
    slots = SLOTS // 2
    split = [(i, k, first, slot) for i, (k, first) in enumerate(items) for slot in range(slots)]

    def read(i, start):
        return held[i][:, pl.ds(pl.multiple_of(start, B), B)]

    row, col = iotas(H)
    low = col < row
    diag_low, diag_high = col == row, col == row + H
    quarter = H // 2
    row_q, col_q = row[:quarter], col[:quarter]
    note_row, _ = iotas(EDGE)
    zero = jnp.zeros((H, B), jnp.float32)
    traces = [zero, zero]
    tiles = {}

    def cov(part):
        return lax.dot_general(
            part, part, (((0,), (0,)), ((), ())), preferred_element_type=jnp.float32
        )

    def note(slot, index, corner, natural):
        line = jnp.sum(corner, axis=0, keepdims=True)
        if index % 2 != natural:
            line = pltpu.roll(line, H, 1)
        tiles[slot] = tiles[slot] + jnp.where(note_row == index // 2, line, 0.0)

    def fold(block, slot, index, which):
        top, bottom = block[:H], block[H:]
        corner = jnp.where(diag_high, bottom, zero)
        note(slot, index, corner, 0)
        traces[which] = traces[which] + corner + jnp.where(diag_low, top, zero)
        return jnp.where(low, pltpu.roll(bottom, H, 1), top)

    def fold_half(block, odd, slot, index):
        part = jnp.where(odd == 1, pltpu.roll(block[H:], H, 1), block[:H])
        traces[0] = traces[0] + jnp.where(diag_low, part, zero)
        upper, lower = part[:quarter], part[quarter:]
        corner = jnp.where(col_q == row_q + quarter, lower, 0.0)
        note(slot, index, corner, 1)
        square = jnp.where(col_q < row_q, pltpu.roll(lower, B - quarter, 1), upper)
        rest = lower.reshape(2, quarter // 2, B)
        rest = jnp.where(col[: quarter // 2] < H, pltpu.roll(rest[1], H, 1), rest[0])
        return square, rest

    def a_parts(out, k, first, slot, index):
        a_blocks, a_half, _, kind = pieces[k]
        owner = slot_owner(first + slot, KINDS[kind])
        here, odd = kind * SLOTS + first + slot, owner & half
        base = (owner >> half) * (full * (1 + half) + half) * B
        at = 0
        for b in a_blocks:
            block = cov(read(0, base + (odd * (full + 1) + b) * B))
            out[slot, at : at + H, :] = fold(block, here, next(index), 0)
            at = at + H
        if a_half:
            block = cov(read(0, base + full * B))
            square, rest = fold_half(block, odd, here, next(index))
            out[slot, at : at + quarter, :] = square
            out[slot, at + quarter : at + quarter * 3 // 2, :] = rest
            at = at + quarter * 3 // 2
        return at

    def g_parts(out, k, first, slot, index, at):
        _, _, g_blocks, kind = pieces[k]
        here = kind * SLOTS + first + slot
        owner = slot_owner(first + slot, KINDS[kind])
        for b in g_blocks:
            start = owner * count_g + b * B
            value, grad = read(1, start).astype(jnp.float32), read(2, start).astype(jnp.float32)
            block = cov((grad * gelu_slope(value)).astype(jnp.bfloat16))
            out[slot, at : at + H, :] = fold(block, here, next(index), 1)
            at = at + H
        return at

    for copy in copies:
        copy.wait()
    for i, k, first, slot in split:
        here = pieces[k][3] * SLOTS + first + slot
        if here not in tiles:
            tiles[here] = jnp.zeros((EDGE, B), jnp.float32) if fresh else notes_in[here]
        index = corner_indices(pieces, k)
        at = a_parts(outs[i], k, first, slot, index)
        at = g_parts(outs[i], k, first, slot, index, at)
        if has_edge(pieces, k):
            outs[i][slot, at:, :] = tiles[here]

    for slot in range(NOTES):
        if slot in tiles:
            notes[slot] = tiles[slot]
        else:
            notes[slot] = jnp.zeros((EDGE, B), jnp.float32) if fresh else notes_in[slot]
    lines = [jnp.sum(trace, axis=0, keepdims=True) for trace in traces]
    tile = jnp.where(note_row == 0, lines[0], jnp.where(note_row == 1, lines[1], 0.0))
    notes[NOTES] = tile if fresh else notes_in[NOTES] + tile


def pack(arrays, pieces, items, count_a, count_g, notes):
    slots = SLOTS // 2
    fresh = notes is None
    out_shape = [
        jax.ShapeDtypeStruct((slots, piece_rows(pieces, k), B), jnp.float32) for k, _ in items
    ]
    out_shape.append(jax.ShapeDtypeStruct((NOTES + 1, EDGE, B), jnp.float32))
    if fresh:
        args = [pltpu.with_memory_space_constraint(arrays[0], pltpu.HBM)]
        out_shape.append(jax.ShapeDtypeStruct(arrays[0].shape, arrays[0].dtype))
    else:
        args = [notes, *arrays]
    space = pltpu.HBM if fresh else pltpu.VMEM
    outs = pl.pallas_call(
        functools.partial(pack_body, pieces, items, count_a, count_g, fresh),
        in_specs=[pl.BlockSpec(memory_space=space)] * len(args),
        out_specs=[pl.BlockSpec(memory_space=pltpu.VMEM)] * len(out_shape),
        out_shape=out_shape,
        scratch_shapes=[pltpu.SemaphoreType.DMA((LOADS,))] * fresh,
        compiler_params=pltpu.CompilerParams(vmem_limit_bytes=32 * 2**20),
        cost_estimate=pl.CostEstimate(
            flops=FIRST if fresh else 1, bytes_accessed=1, transcendentals=0
        ),
    )(*args)
    n = len(items)
    return outs[:n], outs[n], outs[n + 1 :]


def halve_body(n, terms, came, put, merged, *refs):
    keeps, gots, refs = refs[:n], refs[n : 2 * n], refs[2 * n :]
    terms, kept, refs = refs[:terms], refs[terms : terms + n], refs[terms + n :]
    sent, sums = (refs[:1], refs[1:]) if merged else (refs[:n], refs[n:])
    if merged:
        ends = [sum(ref.shape[1] for ref in kept[: k + 1]) for k in range(n)]
        sent = [
            sent[0].at[:, end - ref.shape[1] : end, :] for end, ref in zip(ends, kept)
        ]
    for k in range(n):
        half = kept[k].shape[0]
        kept[k][...] = keeps[k][:half] + gots[k][:half]
        sent[k][...] = keeps[k][half:] + gots[k][half:]
    if terms:
        value = sum((term[...] for term in terms[1:]), terms[0][...])
        for k in came:
            value = value + gots[k][0, -2:, :]
        for out in sums:
            out[...] = value
        for k in put:
            rows = kept[k].shape[1]
            kept[k][0, rows - 2 :, :] = value
            sent[k][0, rows - 2 :, :] = value


def halve(keeps, gots, terms=(), came=(), put=(), merged=False, weight=1):
    n = len(keeps)
    emit = bool(terms) and not put
    args = [*keeps, *gots, *terms]
    kept = [(keep.shape[0] // 2, *keep.shape[1:]) for keep in keeps]
    sent = [(kept[0][0], sum(shape[1] for shape in kept), B)] if merged else kept
    shapes = [*kept, *sent, *([(2, B)] * emit)]
    outs = pl.pallas_call(
        functools.partial(halve_body, n, len(terms), came, put, merged),
        in_specs=[pl.BlockSpec(memory_space=pltpu.VMEM)] * len(args),
        out_specs=[pl.BlockSpec(memory_space=pltpu.VMEM)] * len(shapes),
        out_shape=[jax.ShapeDtypeStruct(shape, jnp.float32) for shape in shapes],
        compiler_params=pltpu.CompilerParams(vmem_limit_bytes=32 * 2**20),
        cost_estimate=pl.CostEstimate(flops=weight, bytes_accessed=1, transcendentals=0),
    )(*args)
    return outs[:n], outs[n : n + len(sent)], outs[n + len(sent) :]


def mean_of(value, total):
    return value * (1.0 / total) if math.frexp(total)[0] == 0.5 else value / total


def turn(folded):
    return jnp.concatenate([folded] * (B // folded.shape[0]), axis=0).T


def unfold(folded):
    row, col = iotas(H)
    turned = turn(folded)
    last = pltpu.roll(jnp.where(col < row, folded, turned[:H]), H, 1)
    return jnp.where(col < row, turned[:H], folded), jnp.where(col < H, turned[H:], last)


def unfold_half(square, rest, odd):
    quarter = H // 2
    row, col = iotas(quarter)
    turned = turn(square)
    upper = jnp.where(col < row, turned[:quarter], square)
    last = pltpu.roll(jnp.where(col < row, square, turned[:quarter]), quarter, 1)
    lower = jnp.where(col < quarter, turned[quarter:H], last)
    rest = jnp.concatenate([rest, pltpu.roll(rest, H, 1)], axis=0)
    part = jnp.concatenate([upper, jnp.where(col < H, lower, rest)], axis=0)
    return (jnp.where(odd == 1, pltpu.roll(part, H, 1), part),)


def places(pieces, ks, count_a):
    full, half = split_rows(count_a)
    odd = lax.axis_index("dp") & half
    for k in ks:
        a_blocks, a_half, g_blocks, kind = pieces[k]
        index = corner_indices(pieces, k)
        for b in a_blocks:
            start = pl.multiple_of(b * B + odd * H, H) if half else b * B
            yield k, 0, start, H, next(index)
        if a_half:
            yield k, 0, pl.multiple_of((1 - odd) * full * B, H), H * 3 // 4, next(index)
        for b in g_blocks:
            yield k, 1, b * B, H, next(index)


def row_begins(pieces, ks):
    rows = [piece_rows(pieces, k) for k in ks]
    return {k: sum(rows[:i]) for i, k in enumerate(ks)}


def unfolded(pieces, ks, count_a, total, owns, got):
    odd = lax.axis_index("dp") & 1
    at = dict.fromkeys(ks, 0)
    begins = row_begins(pieces, ks)

    def take(k, rows):
        begin = at[k]
        at[k] = begin + rows
        mine = owns[ks.index(k)][0, begin : begin + rows, :]
        begin = begin + begins[k]
        return mean_of(mine + got[0, begin : begin + rows, :], total)

    for place in places(pieces, ks, count_a):
        k, _, _, rows, _ = place
        if rows == H:
            yield place, unfold(take(k, H))
        else:
            yield place, unfold_half(take(k, H // 2), take(k, H // 4), odd)


def early_body(pieces, ks, count_a, total, *refs):
    n = len(ks)
    owns, got, outs = refs[:n], refs[n], refs[n + 1 :]
    for (_, which, start, _, _), halves in unfolded(pieces, ks, count_a, total, owns, got):
        for i, value in enumerate(halves):
            outs[which][pl.ds(start + i * H, H), :] = value


def finish_body(pieces, early, late, count_a, total, *refs):
    n = len(late)
    owns, got, firsts, outs = refs[:n], refs[n], refs[n + 1 : n + 3], refs[n + 3 : n + 5]
    made, sem = refs[n + 5 : n + 7], refs[n + 7]
    _, half = split_rows(count_a)
    odd = lax.axis_index("dp") & half
    row, col = iotas(H)

    edges = {}
    for k, own in zip(late, owns):
        end = row_begins(pieces, late)[k] + piece_rows(pieces, k)
        edge = mean_of(own[0, -EDGE:, :] + got[0, end - EDGE : end, :], total)
        edges[pieces[k][3]] = (edge, pltpu.roll(edge, H, 1))
    sums = jnp.sum(edge[-2:], axis=1, keepdims=True)
    ratio = jnp.sqrt(sums[0:1] / D / (sums[1:2] / FFW))
    damp = jnp.sqrt(jnp.full((1, 1), 0.1, jnp.float32))
    shifts = (ratio * damp, damp / ratio)

    def corner(kind, index, natural):
        line = index // 2
        return edges[kind][0 if index % 2 == natural else 1][line : line + 1]

    copies = []

    def give(place, halves):
        k, which, start, rows, index = place
        shift, kind = shifts[which], pieces[k][3]
        if rows == H:
            top, bottom = halves
            top = top + jnp.where(col == row, shift, 0.0)
            bottom = jnp.where(col == row + H, corner(kind, index, 0) + shift, bottom)
            halves = (top, bottom)
        else:
            line = corner(kind, index, 1)
            line = jnp.where(odd == 1, pltpu.roll(line, H, 1), line) + shift
            diagonal = col == row + odd * H
            value = halves[0] + jnp.where(diagonal, shift, 0.0)
            last = jnp.logical_and(diagonal, row >= H // 2)
            halves = (jnp.where(last, line, value),)
        for i, value in enumerate(halves):
            made[which][pl.ds(start + i * H, H), :] = value
        part = pl.ds(start, len(halves) * H)
        copy = pltpu.make_async_copy(
            made[which].at[part], outs[which].at[part], sem.at[len(copies)]
        )
        copy.start()
        copies.append(copy)

    for place in places(pieces, early, count_a):
        _, which, start, rows, _ = place
        count = 2 if rows == H else 1
        give(place, [firsts[which][pl.ds(start + i * H, H), :] for i in range(count)])
    for place, halves in unfolded(pieces, late, count_a, total, owns, got):
        give(place, halves)
    for copy in copies:
        copy.wait()


def unfold_early(pieces, ks, owns, got, count_a, count_g, total):
    args = (*owns, got)
    return pl.pallas_call(
        functools.partial(early_body, pieces, ks, count_a, total),
        in_specs=[pl.BlockSpec(memory_space=pltpu.VMEM)] * len(args),
        out_specs=[pl.BlockSpec(memory_space=pltpu.VMEM)] * 2,
        out_shape=[
            jax.ShapeDtypeStruct((count_a, B), jnp.float32),
            jax.ShapeDtypeStruct((count_g, B), jnp.float32),
        ],
        compiler_params=pltpu.CompilerParams(vmem_limit_bytes=32 * 2**20),
        cost_estimate=pl.CostEstimate(flops=4 * 10**9, bytes_accessed=1, transcendentals=0),
    )(*args)


def finish(pieces, early, late, owns, got, first, count_a, count_g, total):
    args = (*owns, got, *first)
    parts = sum(len(a_blocks) + a_half + len(g_blocks) for a_blocks, a_half, g_blocks, _ in pieces)
    return pl.pallas_call(
        functools.partial(finish_body, pieces, early, late, count_a, total),
        in_specs=[pl.BlockSpec(memory_space=pltpu.VMEM)] * len(args),
        out_specs=[pl.BlockSpec(memory_space=pltpu.HBM)] * 2,
        out_shape=[
            jax.ShapeDtypeStruct((count_a, B), jnp.float32),
            jax.ShapeDtypeStruct((count_g, B), jnp.float32),
        ],
        scratch_shapes=[
            pltpu.VMEM((count_a, B), jnp.float32),
            pltpu.VMEM((count_g, B), jnp.float32),
            pltpu.SemaphoreType.DMA((parts,)),
        ],
        compiler_params=pltpu.CompilerParams(vmem_limit_bytes=32 * 2**20),
    )(*args)


def swap(value, partner):
    dp, tensor = lax.axis_size("dp"), lax.axis_size("tensor")
    pairs = []
    for i in range(dp):
        for j in range(tensor):
            other = partner(i, j)
            pairs.append((i * tensor + j, other[0] * tensor + other[1]))
    return lax.ppermute(value, ("dp", "tensor"), pairs)


def along(stage, kind):
    return lambda i, j: (i ^ (1 << KINDS[kind][j][stage]), j)


def packed(saved_input, saved_pre, grad_act):
    dp = lax.axis_size("dp")
    total = float(saved_input.shape[0] * dp)
    count_a = saved_input.shape[1] // dp
    count_g = saved_pre.shape[1] // dp
    full_a, half_a = split_rows(count_a)
    full_g, _ = split_rows(count_g)
    some, more = (full_a + 1) // 2, full_g // 2
    pieces = (
        (tuple(range(some, full_a)), half_a, (), 0),
        ((), 0, tuple(range(more)), 0),
        (tuple(range(some)), 0, (), 1),
        ((), 0, tuple(range(more, full_g)), 1),
    )
    arrays = (saved_input, saved_pre, grad_act)
    keep, send = 0, SLOTS // 2
    early, late = (0, 2), (1, 3)
    keeps, gots, notes = {}, {}, None

    def pack_next(first, ks):
        nonlocal notes, arrays
        items = tuple((k, first) for k in ks)
        parts, notes, held = pack(arrays, pieces, items, count_a, count_g, notes)
        arrays = (*held, *arrays[len(held) :])
        return dict(zip(ks, parts))

    def exchange(parts, stage):
        for k, part in parts.items():
            gots[k] = swap(part, along(stage, pieces[k][3]))

    def halve_pair(ks, stage, **kinds):
        own, parts, others = halve(
            [keeps[k] for k in ks], [gots[k] for k in ks], merged=stage == 2,
            weight=WEIGHTS.get((ks, stage), 1), **kinds
        )
        keeps.update(zip(ks, own))
        if stage == 2:
            gots[ks] = swap(parts[0], lambda i, j: (i ^ (1 << FAR), j))
        else:
            exchange(dict(zip(ks, parts)), stage)
        return others

    exchange(pack_next(send, early), 0)
    exchange(pack_next(send, late), 0)
    keeps.update(pack_next(keep, early))
    keeps.update(pack_next(keep, late))

    trace = notes[NOTES, :2, :]
    trace = trace + swap(trace, lambda i, j: (i, j ^ 1))
    across = swap(trace, lambda i, j: (i ^ (1 << X) ^ (1 << NEAR), j))
    halve_pair(early, 1)
    halve_pair(late, 1, terms=(trace,), put=(0, 1))
    (trace,) = halve_pair(early, 2, terms=(trace, across))
    halve_pair(late, 2, terms=(trace,), came=(0, 1), put=(0, 1))

    def both(ks):
        return [keeps[k] for k in ks], gots[ks]

    first = unfold_early(pieces, early, *both(early), count_a, count_g, total)
    a_factor, g_factor = finish(
        pieces, early, late, *both(late), first, count_a, count_g, total
    )
    return a_factor[None], g_factor[None]


def fits(count_a, count_g):
    (full_a, half_a), full_g = split_rows(count_a), count_g // B
    if count_a % H or count_g % B or full_a + half_a < 2 or full_g < 2:
        return False
    return full_a + half_a + full_g <= 2 * (EDGE - 2)


def on_device(saved_input, saved_pre, grad_act):
    dp = lax.axis_size("dp")
    count_a = saved_input.shape[1] // dp
    count_g = saved_pre.shape[1] // dp
    if dp == SLOTS and lax.axis_size("tensor") == 2 and fits(count_a, count_g):
        return packed(saved_input, saved_pre, grad_act)
    return plain(saved_input, saved_pre, grad_act)


def solution(mesh):
    spec = P(("groups", "dp"), "tensor")
    out = P("tensor", ("groups", "dp"), None)
    return jax.shard_map(
        on_device, mesh=mesh, in_specs=(spec, spec, spec), out_specs=(out, out), check_vma=False
    )
```

```python
import functools
import math

import jax
import jax.numpy as jnp
from jax import lax
from jax.experimental import pallas as pl
from jax.experimental.pallas import tpu as pltpu
from jax.sharding import PartitionSpec as P

D = 5120
FFW = 10240
B = 128
H = B // 2


def gelu_slope(value):
    return (
        0.5 * (1.0 + lax.erf(value * 0.7071067811865476))
        + value * jnp.exp(-0.5 * value * value) * 0.3989422804014327
    )


def local_blocks(matrix, block, total):
    tokens, width = matrix.shape
    pieces = matrix.reshape(tokens, width // block, block)
    cov = jnp.einsum("tkb,tkc->kbc", pieces, pieces, preferred_element_type=jnp.float32)
    return cov.reshape(width, block) / total


def owned_unit(owned, block):
    count = owned.shape[0]
    rows = lax.axis_index("dp") * count + jnp.arange(count, dtype=jnp.int32)
    cols = jnp.arange(block, dtype=jnp.int32)
    return (cols[None, :] == (rows % block)[:, None]).astype(jnp.float32)


def plain(saved_input, saved_pre, grad_act):
    total = jnp.float32(saved_input.shape[0] * lax.axis_size("dp"))
    slope = gelu_slope(saved_pre.astype(jnp.float32))
    grad_pre = (grad_act.astype(jnp.float32) * slope).astype(jnp.bfloat16)
    terms_a = local_blocks(saved_input, B, total)
    terms_g = local_blocks(grad_pre, B, total)
    owned_a = lax.psum_scatter(terms_a, "dp", scatter_dimension=0, tiled=True)
    owned_g = lax.psum_scatter(terms_g, "dp", scatter_dimension=0, tiled=True)
    unit_a = owned_unit(owned_a, B)
    unit_g = owned_unit(owned_g, B)
    trace_a, trace_g = lax.psum(
        (jnp.sum(owned_a * unit_a), jnp.sum(owned_g * unit_g)), ("dp", "tensor")
    )
    ratio = jnp.sqrt(trace_a / D / (trace_g / FFW))
    damp = jnp.sqrt(jnp.float32(0.1))
    return (
        (owned_a + ratio * damp * unit_a)[None],
        (owned_g + damp / ratio * unit_g)[None],
    )


EDGE = 8
SLOTS = 8
X, NEAR, FAR = 0, 1, 2
KINDS = (((X, NEAR, FAR), (NEAR, X, FAR)), ((NEAR, X, FAR), (X, NEAR, FAR)))
NOTES = len(KINDS) * SLOTS

WEIGHTS = {((0, 2), 2): 2 * 10**9}


def split_rows(count):
    return count // B, (count % B) // H


def has_edge(pieces, k):
    return all(later[3] != pieces[k][3] for later in pieces[k + 1 :])


def piece_rows(pieces, k):
    a_blocks, a_half, g_blocks, _ = pieces[k]
    rows = (len(a_blocks) + len(g_blocks)) * H + a_half * (H * 3 // 4)
    return rows + (EDGE if has_edge(pieces, k) else 0)


def corner_indices(pieces, k):
    parts = [len(a) + a_half + len(g) if kind == pieces[k][3] else 0 for a, a_half, g, kind in pieces]
    return iter(range(sum(parts[:k]), sum(parts[: k + 1])))


def iotas(rows):
    shape = (rows, B)
    return lax.broadcasted_iota(jnp.int32, shape, 0), lax.broadcasted_iota(jnp.int32, shape, 1)


def slot_owner(slot, orders):
    core = lax.axis_index("tensor")
    mask = 0
    for stage, (one, other) in enumerate(zip(*orders)):
        mask = mask | (((slot >> (2 - stage)) & 1) << (one + core * (other - one)))
    return lax.axis_index("dp") ^ mask


def lanes(start, size):
    return pl.ds(start if isinstance(start, int) else pl.multiple_of(start, B), size)


LOADS = 4
FIRST = 4 * 10**9


def pack_body(pieces, items, count_a, count_g, fresh, *refs):
    n = len(items)
    if fresh:
        (a_hbm, *outs), (notes, a_held, sems) = refs[: n + 1], refs[n + 1 :]
        rows = a_hbm.shape[0] // LOADS
        parts = [slice(part * rows, (part + 1) * rows) for part in range(LOADS)]
        copies = [
            pltpu.make_async_copy(a_hbm.at[part], a_held.at[part], sems.at[i])
            for i, part in enumerate(parts)
        ]
        for copy in copies:
            copy.start()
        held = (a_held,)
    else:
        copies = []
        notes_in, held, outs, notes = refs[0], refs[1:4], refs[4 : 4 + n], refs[4 + n]
    full, half = split_rows(count_a)
    slots = SLOTS // 2
    split = [(i, k, first, slot) for i, (k, first) in enumerate(items) for slot in range(slots)]

    def read(i, start):
        return held[i][:, pl.ds(pl.multiple_of(start, B), B)]

    row, col = iotas(H)
    low = col < row
    diag_low, diag_high = col == row, col == row + H
    quarter = H // 2
    row_q, col_q = row[:quarter], col[:quarter]
    note_row, _ = iotas(EDGE)
    zero = jnp.zeros((H, B), jnp.float32)
    traces = [zero, zero]
    tiles = {}

    def cov(part):
        return lax.dot_general(
            part, part, (((0,), (0,)), ((), ())), preferred_element_type=jnp.float32
        )

    def note(slot, index, corner, natural):
        line = jnp.sum(corner, axis=0, keepdims=True)
        if index % 2 != natural:
            line = pltpu.roll(line, H, 1)
        tiles[slot] = tiles[slot] + jnp.where(note_row == index // 2, line, 0.0)

    def fold(block, slot, index, which):
        top, bottom = block[:H], block[H:]
        corner = jnp.where(diag_high, bottom, zero)
        note(slot, index, corner, 0)
        traces[which] = traces[which] + corner + jnp.where(diag_low, top, zero)
        return jnp.where(low, pltpu.roll(bottom, H, 1), top)

    def fold_half(block, odd, slot, index):
        part = jnp.where(odd == 1, pltpu.roll(block[H:], H, 1), block[:H])
        traces[0] = traces[0] + jnp.where(diag_low, part, zero)
        upper, lower = part[:quarter], part[quarter:]
        corner = jnp.where(col_q == row_q + quarter, lower, 0.0)
        note(slot, index, corner, 1)
        square = jnp.where(col_q < row_q, pltpu.roll(lower, B - quarter, 1), upper)
        rest = lower.reshape(2, quarter // 2, B)
        rest = jnp.where(col[: quarter // 2] < H, pltpu.roll(rest[1], H, 1), rest[0])
        return square, rest

    def a_parts(out, k, first, slot, index):
        a_blocks, a_half, _, kind = pieces[k]
        owner = slot_owner(first + slot, KINDS[kind])
        here, odd = kind * SLOTS + first + slot, owner & half
        base = (owner >> half) * (full * (1 + half) + half) * B
        at = 0
        for b in a_blocks:
            block = cov(read(0, base + (odd * (full + 1) + b) * B))
            out[slot, at : at + H, :] = fold(block, here, next(index), 0)
            at = at + H
        if a_half:
            block = cov(read(0, base + full * B))
            square, rest = fold_half(block, odd, here, next(index))
            out[slot, at : at + quarter, :] = square
            out[slot, at + quarter : at + quarter * 3 // 2, :] = rest
            at = at + quarter * 3 // 2
        return at

    def g_parts(out, k, first, slot, index, at):
        _, _, g_blocks, kind = pieces[k]
        here = kind * SLOTS + first + slot
        owner = slot_owner(first + slot, KINDS[kind])
        for b in g_blocks:
            start = owner * count_g + b * B
            value, grad = read(1, start).astype(jnp.float32), read(2, start).astype(jnp.float32)
            block = cov((grad * gelu_slope(value)).astype(jnp.bfloat16))
            out[slot, at : at + H, :] = fold(block, here, next(index), 1)
            at = at + H
        return at

    for copy in copies:
        copy.wait()
    for i, k, first, slot in split:
        here = pieces[k][3] * SLOTS + first + slot
        if here not in tiles:
            tiles[here] = jnp.zeros((EDGE, B), jnp.float32) if fresh else notes_in[here]
        index = corner_indices(pieces, k)
        at = a_parts(outs[i], k, first, slot, index)
        at = g_parts(outs[i], k, first, slot, index, at)
        if has_edge(pieces, k):
            outs[i][slot, at:, :] = tiles[here]

    for slot in range(NOTES):
        if slot in tiles:
            notes[slot] = tiles[slot]
        else:
            notes[slot] = jnp.zeros((EDGE, B), jnp.float32) if fresh else notes_in[slot]
    lines = [jnp.sum(trace, axis=0, keepdims=True) for trace in traces]
    tile = jnp.where(note_row == 0, lines[0], jnp.where(note_row == 1, lines[1], 0.0))
    notes[NOTES] = tile if fresh else notes_in[NOTES] + tile


def pack(arrays, pieces, items, count_a, count_g, notes):
    slots = SLOTS // 2
    fresh = notes is None
    out_shape = [
        jax.ShapeDtypeStruct((slots, piece_rows(pieces, k), B), jnp.float32) for k, _ in items
    ]
    out_shape.append(jax.ShapeDtypeStruct((NOTES + 1, EDGE, B), jnp.float32))
    if fresh:
        args = [pltpu.with_memory_space_constraint(arrays[0], pltpu.HBM)]
        out_shape.append(jax.ShapeDtypeStruct(arrays[0].shape, arrays[0].dtype))
    else:
        args = [notes, *arrays]
    space = pltpu.HBM if fresh else pltpu.VMEM
    outs = pl.pallas_call(
        functools.partial(pack_body, pieces, items, count_a, count_g, fresh),
        in_specs=[pl.BlockSpec(memory_space=space)] * len(args),
        out_specs=[pl.BlockSpec(memory_space=pltpu.VMEM)] * len(out_shape),
        out_shape=out_shape,
        scratch_shapes=[pltpu.SemaphoreType.DMA((LOADS,))] * fresh,
        compiler_params=pltpu.CompilerParams(vmem_limit_bytes=32 * 2**20),
        cost_estimate=pl.CostEstimate(
            flops=FIRST if fresh else 1, bytes_accessed=1, transcendentals=0
        ),
    )(*args)
    n = len(items)
    return outs[:n], outs[n], outs[n + 1 :]


def halve_body(n, terms, came, put, merged, *refs):
    keeps, gots, refs = refs[:n], refs[n : 2 * n], refs[2 * n :]
    terms, kept, refs = refs[:terms], refs[terms : terms + n], refs[terms + n :]
    sent, sums = (refs[:1], refs[1:]) if merged else (refs[:n], refs[n:])
    if merged:
        ends = [sum(ref.shape[1] for ref in kept[: k + 1]) for k in range(n)]
        sent = [
            sent[0].at[:, end - ref.shape[1] : end, :] for end, ref in zip(ends, kept)
        ]
    for k in range(n):
        half = kept[k].shape[0]
        kept[k][...] = keeps[k][:half] + gots[k][:half]
        sent[k][...] = keeps[k][half:] + gots[k][half:]
    if terms:
        value = sum((term[...] for term in terms[1:]), terms[0][...])
        for k in came:
            value = value + gots[k][0, -2:, :]
        for out in sums:
            out[...] = value
        for k in put:
            rows = kept[k].shape[1]
            kept[k][0, rows - 2 :, :] = value
            sent[k][0, rows - 2 :, :] = value


def halve(keeps, gots, terms=(), came=(), put=(), merged=False, weight=1):
    n = len(keeps)
    emit = bool(terms) and not put
    args = [*keeps, *gots, *terms]
    kept = [(keep.shape[0] // 2, *keep.shape[1:]) for keep in keeps]
    sent = [(kept[0][0], sum(shape[1] for shape in kept), B)] if merged else kept
    shapes = [*kept, *sent, *([(2, B)] * emit)]
    outs = pl.pallas_call(
        functools.partial(halve_body, n, len(terms), came, put, merged),
        in_specs=[pl.BlockSpec(memory_space=pltpu.VMEM)] * len(args),
        out_specs=[pl.BlockSpec(memory_space=pltpu.VMEM)] * len(shapes),
        out_shape=[jax.ShapeDtypeStruct(shape, jnp.float32) for shape in shapes],
        compiler_params=pltpu.CompilerParams(vmem_limit_bytes=32 * 2**20),
        cost_estimate=pl.CostEstimate(flops=weight, bytes_accessed=1, transcendentals=0),
    )(*args)
    return outs[:n], outs[n : n + len(sent)], outs[n + len(sent) :]


def mean_of(value, total):
    return value * (1.0 / total) if math.frexp(total)[0] == 0.5 else value / total


def turn(folded):
    return jnp.concatenate([folded] * (B // folded.shape[0]), axis=0).T


def unfold(folded):
    row, col = iotas(H)
    turned = turn(folded)
    last = pltpu.roll(jnp.where(col < row, folded, turned[:H]), H, 1)
    return jnp.where(col < row, turned[:H], folded), jnp.where(col < H, turned[H:], last)


def unfold_half(square, rest, odd):
    quarter = H // 2
    row, col = iotas(quarter)
    turned = turn(square)
    upper = jnp.where(col < row, turned[:quarter], square)
    last = pltpu.roll(jnp.where(col < row, square, turned[:quarter]), quarter, 1)
    lower = jnp.where(col < quarter, turned[quarter:H], last)
    rest = jnp.concatenate([rest, pltpu.roll(rest, H, 1)], axis=0)
    part = jnp.concatenate([upper, jnp.where(col < H, lower, rest)], axis=0)
    return (jnp.where(odd == 1, pltpu.roll(part, H, 1), part),)


def places(pieces, ks, count_a):
    full, half = split_rows(count_a)
    odd = lax.axis_index("dp") & half
    for k in ks:
        a_blocks, a_half, g_blocks, kind = pieces[k]
        index = corner_indices(pieces, k)
        for b in a_blocks:
            start = pl.multiple_of(b * B + odd * H, H) if half else b * B
            yield k, 0, start, H, next(index)
        if a_half:
            yield k, 0, pl.multiple_of((1 - odd) * full * B, H), H * 3 // 4, next(index)
        for b in g_blocks:
            yield k, 1, b * B, H, next(index)


def row_begins(pieces, ks):
    rows = [piece_rows(pieces, k) for k in ks]
    return {k: sum(rows[:i]) for i, k in enumerate(ks)}


def unfolded(pieces, ks, count_a, total, owns, got):
    odd = lax.axis_index("dp") & 1
    at = dict.fromkeys(ks, 0)
    begins = row_begins(pieces, ks)

    def take(k, rows):
        begin = at[k]
        at[k] = begin + rows
        mine = owns[ks.index(k)][0, begin : begin + rows, :]
        begin = begin + begins[k]
        return mean_of(mine + got[0, begin : begin + rows, :], total)

    for place in places(pieces, ks, count_a):
        k, _, _, rows, _ = place
        if rows == H:
            yield place, unfold(take(k, H))
        else:
            yield place, unfold_half(take(k, H // 2), take(k, H // 4), odd)


def early_body(pieces, ks, count_a, total, *refs):
    n = len(ks)
    owns, got, outs = refs[:n], refs[n], refs[n + 1 :]
    for (_, which, start, _, _), halves in unfolded(pieces, ks, count_a, total, owns, got):
        for i, value in enumerate(halves):
            outs[which][pl.ds(start + i * H, H), :] = value


def finish_body(pieces, early, late, count_a, total, *refs):
    n = len(late)
    owns, got, firsts, outs = refs[:n], refs[n], refs[n + 1 : n + 3], refs[n + 3 : n + 5]
    made, sem = refs[n + 5 : n + 7], refs[n + 7]
    _, half = split_rows(count_a)
    odd = lax.axis_index("dp") & half
    row, col = iotas(H)

    edges = {}
    for k, own in zip(late, owns):
        end = row_begins(pieces, late)[k] + piece_rows(pieces, k)
        edge = mean_of(own[0, -EDGE:, :] + got[0, end - EDGE : end, :], total)
        edges[pieces[k][3]] = (edge, pltpu.roll(edge, H, 1))
    sums = jnp.sum(edge[-2:], axis=1, keepdims=True)
    ratio = jnp.sqrt(sums[0:1] / D / (sums[1:2] / FFW))
    damp = jnp.sqrt(jnp.full((1, 1), 0.1, jnp.float32))
    shifts = (ratio * damp, damp / ratio)

    def corner(kind, index, natural):
        line = index // 2
        return edges[kind][0 if index % 2 == natural else 1][line : line + 1]

    copies = []

    def give(place, halves):
        k, which, start, rows, index = place
        shift, kind = shifts[which], pieces[k][3]
        if rows == H:
            top, bottom = halves
            top = top + jnp.where(col == row, shift, 0.0)
            bottom = jnp.where(col == row + H, corner(kind, index, 0) + shift, bottom)
            halves = (top, bottom)
        else:
            line = corner(kind, index, 1)
            line = jnp.where(odd == 1, pltpu.roll(line, H, 1), line) + shift
            diagonal = col == row + odd * H
            value = halves[0] + jnp.where(diagonal, shift, 0.0)
            last = jnp.logical_and(diagonal, row >= H // 2)
            halves = (jnp.where(last, line, value),)
        for i, value in enumerate(halves):
            made[which][pl.ds(start + i * H, H), :] = value
        part = pl.ds(start, len(halves) * H)
        copy = pltpu.make_async_copy(
            made[which].at[part], outs[which].at[part], sem.at[len(copies)]
        )
        copy.start()
        copies.append(copy)

    for place in places(pieces, early, count_a):
        _, which, start, rows, _ = place
        count = 2 if rows == H else 1
        give(place, [firsts[which][pl.ds(start + i * H, H), :] for i in range(count)])
    for place, halves in unfolded(pieces, late, count_a, total, owns, got):
        give(place, halves)
    for copy in copies:
        copy.wait()


def unfold_early(pieces, ks, owns, got, count_a, count_g, total):
    args = (*owns, got)
    return pl.pallas_call(
        functools.partial(early_body, pieces, ks, count_a, total),
        in_specs=[pl.BlockSpec(memory_space=pltpu.VMEM)] * len(args),
        out_specs=[pl.BlockSpec(memory_space=pltpu.VMEM)] * 2,
        out_shape=[
            jax.ShapeDtypeStruct((count_a, B), jnp.float32),
            jax.ShapeDtypeStruct((count_g, B), jnp.float32),
        ],
        compiler_params=pltpu.CompilerParams(vmem_limit_bytes=32 * 2**20),
        cost_estimate=pl.CostEstimate(flops=4 * 10**9, bytes_accessed=1, transcendentals=0),
    )(*args)


def finish(pieces, early, late, owns, got, first, count_a, count_g, total):
    args = (*owns, got, *first)
    parts = sum(len(a_blocks) + a_half + len(g_blocks) for a_blocks, a_half, g_blocks, _ in pieces)
    return pl.pallas_call(
        functools.partial(finish_body, pieces, early, late, count_a, total),
        in_specs=[pl.BlockSpec(memory_space=pltpu.VMEM)] * len(args),
        out_specs=[pl.BlockSpec(memory_space=pltpu.HBM)] * 2,
        out_shape=[
            jax.ShapeDtypeStruct((count_a, B), jnp.float32),
            jax.ShapeDtypeStruct((count_g, B), jnp.float32),
        ],
        scratch_shapes=[
            pltpu.VMEM((count_a, B), jnp.float32),
            pltpu.VMEM((count_g, B), jnp.float32),
            pltpu.SemaphoreType.DMA((parts,)),
        ],
        compiler_params=pltpu.CompilerParams(vmem_limit_bytes=32 * 2**20),
    )(*args)


def swap(value, partner):
    dp, tensor = lax.axis_size("dp"), lax.axis_size("tensor")
    pairs = []
    for i in range(dp):
        for j in range(tensor):
            other = partner(i, j)
            pairs.append((i * tensor + j, other[0] * tensor + other[1]))
    return lax.ppermute(value, ("dp", "tensor"), pairs)


def along(stage, kind):
    return lambda i, j: (i ^ (1 << KINDS[kind][j][stage]), j)


def packed(saved_input, saved_pre, grad_act):
    dp = lax.axis_size("dp")
    total = float(saved_input.shape[0] * dp)
    count_a = saved_input.shape[1] // dp
    count_g = saved_pre.shape[1] // dp
    full_a, half_a = split_rows(count_a)
    full_g, _ = split_rows(count_g)
    some = 1 + (full_g - 1) // 2
    pieces = (
        (tuple(range(full_a)), 0, (), 0),
        ((), 0, tuple(range(1, some)), 0),
        ((), half_a, (0,), 1),
        ((), 0, tuple(range(some, full_g)), 1),
    )
    arrays = (saved_input, saved_pre, grad_act)
    keep, send = 0, SLOTS // 2
    early, late = (0, 2), (1, 3)
    keeps, gots, notes = {}, {}, None

    def pack_next(first, ks):
        nonlocal notes, arrays
        items = tuple((k, first) for k in ks)
        parts, notes, held = pack(arrays, pieces, items, count_a, count_g, notes)
        arrays = (*held, *arrays[len(held) :])
        return dict(zip(ks, parts))

    def exchange(parts, stage):
        for k, part in parts.items():
            gots[k] = swap(part, along(stage, pieces[k][3]))

    def halve_pair(ks, stage, **kinds):
        own, parts, others = halve(
            [keeps[k] for k in ks], [gots[k] for k in ks], merged=stage == 2,
            weight=WEIGHTS.get((ks, stage), 1), **kinds
        )
        keeps.update(zip(ks, own))
        if stage == 2:
            gots[ks] = swap(parts[0], lambda i, j: (i ^ (1 << FAR), j))
        else:
            exchange(dict(zip(ks, parts)), stage)
        return others

    exchange(pack_next(send, early[:1]), 0)
    exchange(pack_next(send, early[1:]), 0)
    exchange(pack_next(send, late), 0)
    keeps.update(pack_next(keep, early))
    keeps.update(pack_next(keep, late))

    trace = notes[NOTES, :2, :]
    trace = trace + swap(trace, lambda i, j: (i, j ^ 1))
    across = swap(trace, lambda i, j: (i ^ (1 << X) ^ (1 << NEAR), j))
    halve_pair(early, 1)
    halve_pair(late, 1, terms=(trace,), put=(0, 1))
    (trace,) = halve_pair(early, 2, terms=(trace, across))
    halve_pair(late, 2, terms=(trace,), came=(0, 1), put=(0, 1))

    def both(ks):
        return [keeps[k] for k in ks], gots[ks]

    first = unfold_early(pieces, early, *both(early), count_a, count_g, total)
    a_factor, g_factor = finish(
        pieces, early, late, *both(late), first, count_a, count_g, total
    )
    return a_factor[None], g_factor[None]


def fits(count_a, count_g):
    (full_a, half_a), full_g = split_rows(count_a), count_g // B
    if count_a % H or count_g % B or full_a < 1 or full_g < 3:
        return False
    return full_a + half_a + full_g <= 2 * (EDGE - 2)


def on_device(saved_input, saved_pre, grad_act):
    dp = lax.axis_size("dp")
    count_a = saved_input.shape[1] // dp
    count_g = saved_pre.shape[1] // dp
    if dp == SLOTS and lax.axis_size("tensor") == 2 and fits(count_a, count_g):
        return packed(saved_input, saved_pre, grad_act)
    return plain(saved_input, saved_pre, grad_act)


def solution(mesh):
    spec = P(("groups", "dp"), "tensor")
    out = P("tensor", ("groups", "dp"), None)
    return jax.shard_map(
        on_device, mesh=mesh, in_specs=(spec, spec, spec), out_specs=(out, out), check_vma=False
    )
```

```python
import functools
import math

import jax
import jax.numpy as jnp
from jax import lax
from jax.experimental import pallas as pl
from jax.experimental.pallas import tpu as pltpu
from jax.sharding import PartitionSpec as P

D = 5120
FFW = 10240
B = 128
H = B // 2


def gelu_slope(value):
    return (
        0.5 * (1.0 + lax.erf(value * 0.7071067811865476))
        + value * jnp.exp(-0.5 * value * value) * 0.3989422804014327
    )


def local_blocks(matrix, block, total):
    tokens, width = matrix.shape
    pieces = matrix.reshape(tokens, width // block, block)
    cov = jnp.einsum("tkb,tkc->kbc", pieces, pieces, preferred_element_type=jnp.float32)
    return cov.reshape(width, block) / total


def owned_unit(owned, block):
    count = owned.shape[0]
    rows = lax.axis_index("dp") * count + jnp.arange(count, dtype=jnp.int32)
    cols = jnp.arange(block, dtype=jnp.int32)
    return (cols[None, :] == (rows % block)[:, None]).astype(jnp.float32)


def plain(saved_input, saved_pre, grad_act):
    total = jnp.float32(saved_input.shape[0] * lax.axis_size("dp"))
    slope = gelu_slope(saved_pre.astype(jnp.float32))
    grad_pre = (grad_act.astype(jnp.float32) * slope).astype(jnp.bfloat16)
    terms_a = local_blocks(saved_input, B, total)
    terms_g = local_blocks(grad_pre, B, total)
    owned_a = lax.psum_scatter(terms_a, "dp", scatter_dimension=0, tiled=True)
    owned_g = lax.psum_scatter(terms_g, "dp", scatter_dimension=0, tiled=True)
    unit_a = owned_unit(owned_a, B)
    unit_g = owned_unit(owned_g, B)
    trace_a, trace_g = lax.psum(
        (jnp.sum(owned_a * unit_a), jnp.sum(owned_g * unit_g)), ("dp", "tensor")
    )
    ratio = jnp.sqrt(trace_a / D / (trace_g / FFW))
    damp = jnp.sqrt(jnp.float32(0.1))
    return (
        (owned_a + ratio * damp * unit_a)[None],
        (owned_g + damp / ratio * unit_g)[None],
    )


EDGE = 8
SLOTS = 8
X, NEAR, FAR = 0, 1, 2
KINDS = (((X, NEAR, FAR), (NEAR, X, FAR)), ((NEAR, X, FAR), (X, NEAR, FAR)))
NOTES = len(KINDS) * SLOTS

WEIGHTS = {((0, 2), 2): 2 * 10**9}


def split_rows(count):
    return count // B, (count % B) // H


def has_edge(pieces, k):
    return all(later[3] != pieces[k][3] for later in pieces[k + 1 :])


def piece_rows(pieces, k):
    a_blocks, a_half, g_blocks, _ = pieces[k]
    rows = (len(a_blocks) + len(g_blocks)) * H + a_half * (H * 3 // 4)
    return rows + (EDGE if has_edge(pieces, k) else 0)


def corner_indices(pieces, k):
    parts = [len(a) + a_half + len(g) if kind == pieces[k][3] else 0 for a, a_half, g, kind in pieces]
    return iter(range(sum(parts[:k]), sum(parts[: k + 1])))


def iotas(rows):
    shape = (rows, B)
    return lax.broadcasted_iota(jnp.int32, shape, 0), lax.broadcasted_iota(jnp.int32, shape, 1)


def slot_owner(slot, orders):
    core = lax.axis_index("tensor")
    mask = 0
    for stage, (one, other) in enumerate(zip(*orders)):
        mask = mask | (((slot >> (2 - stage)) & 1) << (one + core * (other - one)))
    return lax.axis_index("dp") ^ mask


def lanes(start, size):
    return pl.ds(start if isinstance(start, int) else pl.multiple_of(start, B), size)


LOADS = 4
FIRST = 4 * 10**9


def pack_body(pieces, items, count_a, count_g, fresh, *refs):
    n = len(items)
    if fresh:
        (a_hbm, *outs), (notes, a_held, sems) = refs[: n + 1], refs[n + 1 :]
        rows = a_hbm.shape[0] // LOADS
        parts = [slice(part * rows, (part + 1) * rows) for part in range(LOADS)]
        copies = [
            pltpu.make_async_copy(a_hbm.at[part], a_held.at[part], sems.at[i])
            for i, part in enumerate(parts)
        ]
        for copy in copies:
            copy.start()
        held = (a_held,)
    else:
        copies = []
        notes_in, held, outs, notes = refs[0], refs[1:4], refs[4 : 4 + n], refs[4 + n]
    full, half = split_rows(count_a)
    slots = SLOTS // 2
    split = [(i, k, first, slot) for i, (k, first) in enumerate(items) for slot in range(slots)]

    def read(i, start):
        return held[i][:, pl.ds(pl.multiple_of(start, B), B)]

    row, col = iotas(H)
    low = col < row
    diag_low, diag_high = col == row, col == row + H
    quarter = H // 2
    row_q, col_q = row[:quarter], col[:quarter]
    note_row, _ = iotas(EDGE)
    zero = jnp.zeros((H, B), jnp.float32)
    traces = [zero, zero]
    tiles = {}

    def cov(part):
        return lax.dot_general(
            part, part, (((0,), (0,)), ((), ())), preferred_element_type=jnp.float32
        )

    def note(slot, index, corner, natural):
        line = jnp.sum(corner, axis=0, keepdims=True)
        if index % 2 != natural:
            line = pltpu.roll(line, H, 1)
        tiles[slot] = tiles[slot] + jnp.where(note_row == index // 2, line, 0.0)

    def fold(block, slot, index, which):
        top, bottom = block[:H], block[H:]
        corner = jnp.where(diag_high, bottom, zero)
        note(slot, index, corner, 0)
        traces[which] = traces[which] + corner + jnp.where(diag_low, top, zero)
        return jnp.where(low, pltpu.roll(bottom, H, 1), top)

    def fold_half(block, odd, slot, index):
        part = jnp.where(odd == 1, pltpu.roll(block[H:], H, 1), block[:H])
        traces[0] = traces[0] + jnp.where(diag_low, part, zero)
        upper, lower = part[:quarter], part[quarter:]
        corner = jnp.where(col_q == row_q + quarter, lower, 0.0)
        note(slot, index, corner, 1)
        square = jnp.where(col_q < row_q, pltpu.roll(lower, B - quarter, 1), upper)
        rest = lower.reshape(2, quarter // 2, B)
        rest = jnp.where(col[: quarter // 2] < H, pltpu.roll(rest[1], H, 1), rest[0])
        return square, rest

    def a_parts(out, k, first, slot, index):
        a_blocks, a_half, _, kind = pieces[k]
        owner = slot_owner(first + slot, KINDS[kind])
        here, odd = kind * SLOTS + first + slot, owner & half
        base = (owner >> half) * (full * (1 + half) + half) * B
        at = 0
        for b in a_blocks:
            block = cov(read(0, base + (odd * (full + 1) + b) * B))
            out[slot, at : at + H, :] = fold(block, here, next(index), 0)
            at = at + H
        if a_half:
            block = cov(read(0, base + full * B))
            square, rest = fold_half(block, odd, here, next(index))
            out[slot, at : at + quarter, :] = square
            out[slot, at + quarter : at + quarter * 3 // 2, :] = rest
            at = at + quarter * 3 // 2
        return at

    def g_parts(out, k, first, slot, index, at):
        _, _, g_blocks, kind = pieces[k]
        here = kind * SLOTS + first + slot
        owner = slot_owner(first + slot, KINDS[kind])
        for b in g_blocks:
            start = owner * count_g + b * B
            value, grad = read(1, start).astype(jnp.float32), read(2, start).astype(jnp.float32)
            block = cov((grad * gelu_slope(value)).astype(jnp.bfloat16))
            out[slot, at : at + H, :] = fold(block, here, next(index), 1)
            at = at + H
        return at

    for copy in copies:
        copy.wait()
    for i, k, first, slot in split:
        here = pieces[k][3] * SLOTS + first + slot
        if here not in tiles:
            tiles[here] = jnp.zeros((EDGE, B), jnp.float32) if fresh else notes_in[here]
        index = corner_indices(pieces, k)
        at = a_parts(outs[i], k, first, slot, index)
        at = g_parts(outs[i], k, first, slot, index, at)
        if has_edge(pieces, k):
            outs[i][slot, at:, :] = tiles[here]

    for slot in range(NOTES):
        if slot in tiles:
            notes[slot] = tiles[slot]
        else:
            notes[slot] = jnp.zeros((EDGE, B), jnp.float32) if fresh else notes_in[slot]
    lines = [jnp.sum(trace, axis=0, keepdims=True) for trace in traces]
    tile = jnp.where(note_row == 0, lines[0], jnp.where(note_row == 1, lines[1], 0.0))
    notes[NOTES] = tile if fresh else notes_in[NOTES] + tile


def pack(arrays, pieces, items, count_a, count_g, notes):
    slots = SLOTS // 2
    fresh = notes is None
    out_shape = [
        jax.ShapeDtypeStruct((slots, piece_rows(pieces, k), B), jnp.float32) for k, _ in items
    ]
    out_shape.append(jax.ShapeDtypeStruct((NOTES + 1, EDGE, B), jnp.float32))
    if fresh:
        args = [pltpu.with_memory_space_constraint(arrays[0], pltpu.HBM)]
        out_shape.append(jax.ShapeDtypeStruct(arrays[0].shape, arrays[0].dtype))
    else:
        args = [notes, *arrays]
    space = pltpu.HBM if fresh else pltpu.VMEM
    outs = pl.pallas_call(
        functools.partial(pack_body, pieces, items, count_a, count_g, fresh),
        in_specs=[pl.BlockSpec(memory_space=space)] * len(args),
        out_specs=[pl.BlockSpec(memory_space=pltpu.VMEM)] * len(out_shape),
        out_shape=out_shape,
        scratch_shapes=[pltpu.SemaphoreType.DMA((LOADS,))] * fresh,
        compiler_params=pltpu.CompilerParams(vmem_limit_bytes=32 * 2**20),
        cost_estimate=pl.CostEstimate(
            flops=FIRST if fresh else 1, bytes_accessed=1, transcendentals=0
        ),
    )(*args)
    n = len(items)
    return outs[:n], outs[n], outs[n + 1 :]


def halve_body(n, terms, came, put, merged, *refs):
    keeps, gots, refs = refs[:n], refs[n : 2 * n], refs[2 * n :]
    terms, kept, refs = refs[:terms], refs[terms : terms + n], refs[terms + n :]
    sent, sums = (refs[:1], refs[1:]) if merged else (refs[:n], refs[n:])
    if merged:
        ends = [sum(ref.shape[1] for ref in kept[: k + 1]) for k in range(n)]
        sent = [
            sent[0].at[:, end - ref.shape[1] : end, :] for end, ref in zip(ends, kept)
        ]
    for k in range(n):
        half = kept[k].shape[0]
        kept[k][...] = keeps[k][:half] + gots[k][:half]
        sent[k][...] = keeps[k][half:] + gots[k][half:]
    if terms:
        value = sum((term[...] for term in terms[1:]), terms[0][...])
        for k in came:
            value = value + gots[k][0, -2:, :]
        for out in sums:
            out[...] = value
        for k in put:
            rows = kept[k].shape[1]
            kept[k][0, rows - 2 :, :] = value
            sent[k][0, rows - 2 :, :] = value


def halve(keeps, gots, terms=(), came=(), put=(), merged=False, weight=1):
    n = len(keeps)
    emit = bool(terms) and not put
    args = [*keeps, *gots, *terms]
    kept = [(keep.shape[0] // 2, *keep.shape[1:]) for keep in keeps]
    sent = [(kept[0][0], sum(shape[1] for shape in kept), B)] if merged else kept
    shapes = [*kept, *sent, *([(2, B)] * emit)]
    outs = pl.pallas_call(
        functools.partial(halve_body, n, len(terms), came, put, merged),
        in_specs=[pl.BlockSpec(memory_space=pltpu.VMEM)] * len(args),
        out_specs=[pl.BlockSpec(memory_space=pltpu.VMEM)] * len(shapes),
        out_shape=[jax.ShapeDtypeStruct(shape, jnp.float32) for shape in shapes],
        compiler_params=pltpu.CompilerParams(vmem_limit_bytes=32 * 2**20),
        cost_estimate=pl.CostEstimate(flops=weight, bytes_accessed=1, transcendentals=0),
    )(*args)
    return outs[:n], outs[n : n + len(sent)], outs[n + len(sent) :]


def mean_of(value, total):
    return value * (1.0 / total) if math.frexp(total)[0] == 0.5 else value / total


def turn(folded):
    return jnp.concatenate([folded] * (B // folded.shape[0]), axis=0).T


def unfold(folded):
    row, col = iotas(H)
    turned = turn(folded)
    last = pltpu.roll(jnp.where(col < row, folded, turned[:H]), H, 1)
    return jnp.where(col < row, turned[:H], folded), jnp.where(col < H, turned[H:], last)


def unfold_half(square, rest, odd):
    quarter = H // 2
    row, col = iotas(quarter)
    turned = turn(square)
    upper = jnp.where(col < row, turned[:quarter], square)
    last = pltpu.roll(jnp.where(col < row, square, turned[:quarter]), quarter, 1)
    lower = jnp.where(col < quarter, turned[quarter:H], last)
    rest = jnp.concatenate([rest, pltpu.roll(rest, H, 1)], axis=0)
    part = jnp.concatenate([upper, jnp.where(col < H, lower, rest)], axis=0)
    return (jnp.where(odd == 1, pltpu.roll(part, H, 1), part),)


def places(pieces, ks, count_a):
    full, half = split_rows(count_a)
    odd = lax.axis_index("dp") & half
    for k in ks:
        a_blocks, a_half, g_blocks, kind = pieces[k]
        index = corner_indices(pieces, k)
        for b in a_blocks:
            start = pl.multiple_of(b * B + odd * H, H) if half else b * B
            yield k, 0, start, H, next(index)
        if a_half:
            yield k, 0, pl.multiple_of((1 - odd) * full * B, H), H * 3 // 4, next(index)
        for b in g_blocks:
            yield k, 1, b * B, H, next(index)


def row_begins(pieces, ks):
    rows = [piece_rows(pieces, k) for k in ks]
    return {k: sum(rows[:i]) for i, k in enumerate(ks)}


def unfolded(pieces, ks, count_a, total, owns, got):
    odd = lax.axis_index("dp") & 1
    at = dict.fromkeys(ks, 0)
    begins = row_begins(pieces, ks)

    def take(k, rows):
        begin = at[k]
        at[k] = begin + rows
        mine = owns[ks.index(k)][0, begin : begin + rows, :]
        begin = begin + begins[k]
        return mean_of(mine + got[0, begin : begin + rows, :], total)

    for place in places(pieces, ks, count_a):
        k, _, _, rows, _ = place
        if rows == H:
            yield place, unfold(take(k, H))
        else:
            yield place, unfold_half(take(k, H // 2), take(k, H // 4), odd)


def early_body(pieces, ks, count_a, total, *refs):
    n = len(ks)
    owns, got, outs = refs[:n], refs[n], refs[n + 1 :]
    for (_, which, start, _, _), halves in unfolded(pieces, ks, count_a, total, owns, got):
        for i, value in enumerate(halves):
            outs[which][pl.ds(start + i * H, H), :] = value


def finish_body(pieces, early, late, count_a, total, *refs):
    n = len(late)
    owns, got, firsts, outs = refs[:n], refs[n], refs[n + 1 : n + 3], refs[n + 3 : n + 5]
    made, sem = refs[n + 5 : n + 7], refs[n + 7]
    _, half = split_rows(count_a)
    odd = lax.axis_index("dp") & half
    row, col = iotas(H)

    edges = {}
    for k, own in zip(late, owns):
        end = row_begins(pieces, late)[k] + piece_rows(pieces, k)
        edge = mean_of(own[0, -EDGE:, :] + got[0, end - EDGE : end, :], total)
        edges[pieces[k][3]] = (edge, pltpu.roll(edge, H, 1))
    sums = jnp.sum(edge[-2:], axis=1, keepdims=True)
    ratio = jnp.sqrt(sums[0:1] / D / (sums[1:2] / FFW))
    damp = jnp.sqrt(jnp.full((1, 1), 0.1, jnp.float32))
    shifts = (ratio * damp, damp / ratio)

    def corner(kind, index, natural):
        line = index // 2
        return edges[kind][0 if index % 2 == natural else 1][line : line + 1]

    copies = []

    def give(place, halves):
        k, which, start, rows, index = place
        shift, kind = shifts[which], pieces[k][3]
        if rows == H:
            top, bottom = halves
            top = top + jnp.where(col == row, shift, 0.0)
            bottom = jnp.where(col == row + H, corner(kind, index, 0) + shift, bottom)
            halves = (top, bottom)
        else:
            line = corner(kind, index, 1)
            line = jnp.where(odd == 1, pltpu.roll(line, H, 1), line) + shift
            diagonal = col == row + odd * H
            value = halves[0] + jnp.where(diagonal, shift, 0.0)
            last = jnp.logical_and(diagonal, row >= H // 2)
            halves = (jnp.where(last, line, value),)
        for i, value in enumerate(halves):
            made[which][pl.ds(start + i * H, H), :] = value
        part = pl.ds(start, len(halves) * H)
        copy = pltpu.make_async_copy(
            made[which].at[part], outs[which].at[part], sem.at[len(copies)]
        )
        copy.start()
        copies.append(copy)

    for place in places(pieces, early, count_a):
        _, which, start, rows, _ = place
        count = 2 if rows == H else 1
        give(place, [firsts[which][pl.ds(start + i * H, H), :] for i in range(count)])
    for place, halves in unfolded(pieces, late, count_a, total, owns, got):
        give(place, halves)
    for copy in copies:
        copy.wait()


def unfold_early(pieces, ks, owns, got, count_a, count_g, total):
    args = (*owns, got)
    return pl.pallas_call(
        functools.partial(early_body, pieces, ks, count_a, total),
        in_specs=[pl.BlockSpec(memory_space=pltpu.VMEM)] * len(args),
        out_specs=[pl.BlockSpec(memory_space=pltpu.VMEM)] * 2,
        out_shape=[
            jax.ShapeDtypeStruct((count_a, B), jnp.float32),
            jax.ShapeDtypeStruct((count_g, B), jnp.float32),
        ],
        compiler_params=pltpu.CompilerParams(vmem_limit_bytes=32 * 2**20),
        cost_estimate=pl.CostEstimate(flops=4 * 10**9, bytes_accessed=1, transcendentals=0),
    )(*args)


def finish(pieces, early, late, owns, got, first, count_a, count_g, total):
    args = (*owns, got, *first)
    parts = sum(len(a_blocks) + a_half + len(g_blocks) for a_blocks, a_half, g_blocks, _ in pieces)
    return pl.pallas_call(
        functools.partial(finish_body, pieces, early, late, count_a, total),
        in_specs=[pl.BlockSpec(memory_space=pltpu.VMEM)] * len(args),
        out_specs=[pl.BlockSpec(memory_space=pltpu.HBM)] * 2,
        out_shape=[
            jax.ShapeDtypeStruct((count_a, B), jnp.float32),
            jax.ShapeDtypeStruct((count_g, B), jnp.float32),
        ],
        scratch_shapes=[
            pltpu.VMEM((count_a, B), jnp.float32),
            pltpu.VMEM((count_g, B), jnp.float32),
            pltpu.SemaphoreType.DMA((parts,)),
        ],
        compiler_params=pltpu.CompilerParams(vmem_limit_bytes=32 * 2**20),
    )(*args)


def swap(value, partner):
    dp, tensor = lax.axis_size("dp"), lax.axis_size("tensor")
    pairs = []
    for i in range(dp):
        for j in range(tensor):
            other = partner(i, j)
            pairs.append((i * tensor + j, other[0] * tensor + other[1]))
    return lax.ppermute(value, ("dp", "tensor"), pairs)


def along(stage, kind):
    return lambda i, j: (i ^ (1 << KINDS[kind][j][stage]), j)


def packed(saved_input, saved_pre, grad_act):
    dp = lax.axis_size("dp")
    total = float(saved_input.shape[0] * dp)
    count_a = saved_input.shape[1] // dp
    count_g = saved_pre.shape[1] // dp
    full_a, half_a = split_rows(count_a)
    full_g, _ = split_rows(count_g)
    some, more = (full_a + 1) // 2, full_g // 2
    pieces = (
        (tuple(range(some, full_a)), 0, (), 0),
        ((), half_a, tuple(range(more)), 0),
        (tuple(range(some)), 0, (), 1),
        ((), 0, tuple(range(more, full_g)), 1),
    )
    arrays = (saved_input, saved_pre, grad_act)
    keep, send = 0, SLOTS // 2
    early, late = (0, 2), (1, 3)
    keeps, gots, notes = {}, {}, None

    def pack_next(first, ks):
        nonlocal notes, arrays
        items = tuple((k, first) for k in ks)
        parts, notes, held = pack(arrays, pieces, items, count_a, count_g, notes)
        arrays = (*held, *arrays[len(held) :])
        return dict(zip(ks, parts))

    def exchange(parts, stage):
        for k, part in parts.items():
            gots[k] = swap(part, along(stage, pieces[k][3]))

    def halve_pair(ks, stage, **kinds):
        own, parts, others = halve(
            [keeps[k] for k in ks], [gots[k] for k in ks], merged=stage == 2,
            weight=WEIGHTS.get((ks, stage), 1), **kinds
        )
        keeps.update(zip(ks, own))
        if stage == 2:
            gots[ks] = swap(parts[0], lambda i, j: (i ^ (1 << FAR), j))
        else:
            exchange(dict(zip(ks, parts)), stage)
        return others

    exchange(pack_next(send, early), 0)
    exchange(pack_next(send, late), 0)
    keeps.update(pack_next(keep, early))
    keeps.update(pack_next(keep, late))

    trace = notes[NOTES, :2, :]
    trace = trace + swap(trace, lambda i, j: (i, j ^ 1))
    across = swap(trace, lambda i, j: (i ^ (1 << X) ^ (1 << NEAR), j))
    halve_pair(early, 1)
    halve_pair(late, 1, terms=(trace,), put=(0, 1))
    (trace,) = halve_pair(early, 2, terms=(trace, across))
    halve_pair(late, 2, terms=(trace,), came=(0, 1), put=(0, 1))

    def both(ks):
        return [keeps[k] for k in ks], gots[ks]

    first = unfold_early(pieces, early, *both(early), count_a, count_g, total)
    a_factor, g_factor = finish(
        pieces, early, late, *both(late), first, count_a, count_g, total
    )
    return a_factor[None], g_factor[None]


def fits(count_a, count_g):
    (full_a, half_a), full_g = split_rows(count_a), count_g // B
    if count_a % H or count_g % B or full_a < 2 or full_g < 2:
        return False
    return full_a + half_a + full_g <= 2 * (EDGE - 2)


def on_device(saved_input, saved_pre, grad_act):
    dp = lax.axis_size("dp")
    count_a = saved_input.shape[1] // dp
    count_g = saved_pre.shape[1] // dp
    if dp == SLOTS and lax.axis_size("tensor") == 2 and fits(count_a, count_g):
        return packed(saved_input, saved_pre, grad_act)
    return plain(saved_input, saved_pre, grad_act)


def solution(mesh):
    spec = P(("groups", "dp"), "tensor")
    out = P("tensor", ("groups", "dp"), None)
    return jax.shard_map(
        on_device, mesh=mesh, in_specs=(spec, spec, spec), out_specs=(out, out), check_vma=False
    )
```

```python
import functools
import math

import jax
import jax.numpy as jnp
from jax import lax
from jax.experimental import pallas as pl
from jax.experimental.pallas import tpu as pltpu
from jax.sharding import PartitionSpec as P

D = 5120
FFW = 10240
B = 128
H = B // 2


def gelu_slope(value):
    return (
        0.5 * (1.0 + lax.erf(value * 0.7071067811865476))
        + value * jnp.exp(-0.5 * value * value) * 0.3989422804014327
    )


def local_blocks(matrix, block, total):
    tokens, width = matrix.shape
    pieces = matrix.reshape(tokens, width // block, block)
    cov = jnp.einsum("tkb,tkc->kbc", pieces, pieces, preferred_element_type=jnp.float32)
    return cov.reshape(width, block) / total


def owned_unit(owned, block):
    count = owned.shape[0]
    rows = lax.axis_index("dp") * count + jnp.arange(count, dtype=jnp.int32)
    cols = jnp.arange(block, dtype=jnp.int32)
    return (cols[None, :] == (rows % block)[:, None]).astype(jnp.float32)


def plain(saved_input, saved_pre, grad_act):
    total = jnp.float32(saved_input.shape[0] * lax.axis_size("dp"))
    slope = gelu_slope(saved_pre.astype(jnp.float32))
    grad_pre = (grad_act.astype(jnp.float32) * slope).astype(jnp.bfloat16)
    terms_a = local_blocks(saved_input, B, total)
    terms_g = local_blocks(grad_pre, B, total)
    owned_a = lax.psum_scatter(terms_a, "dp", scatter_dimension=0, tiled=True)
    owned_g = lax.psum_scatter(terms_g, "dp", scatter_dimension=0, tiled=True)
    unit_a = owned_unit(owned_a, B)
    unit_g = owned_unit(owned_g, B)
    trace_a, trace_g = lax.psum(
        (jnp.sum(owned_a * unit_a), jnp.sum(owned_g * unit_g)), ("dp", "tensor")
    )
    ratio = jnp.sqrt(trace_a / D / (trace_g / FFW))
    damp = jnp.sqrt(jnp.float32(0.1))
    return (
        (owned_a + ratio * damp * unit_a)[None],
        (owned_g + damp / ratio * unit_g)[None],
    )


EDGE = 8
SLOTS = 8
X, NEAR, FAR = 0, 1, 2
KINDS = (((X, NEAR, FAR), (NEAR, X, FAR)), ((NEAR, X, FAR), (X, NEAR, FAR)))
NOTES = len(KINDS) * SLOTS

WEIGHTS = {((0, 2), 2): 2 * 10**9}


def split_rows(count):
    return count // B, (count % B) // H


def has_edge(pieces, k):
    return all(later[3] != pieces[k][3] for later in pieces[k + 1 :])


def piece_rows(pieces, k):
    a_blocks, a_half, g_blocks, _ = pieces[k]
    rows = (len(a_blocks) + len(g_blocks)) * H + a_half * (H * 3 // 4)
    return rows + (EDGE if has_edge(pieces, k) else 0)


def corner_indices(pieces, k):
    parts = [len(a) + a_half + len(g) if kind == pieces[k][3] else 0 for a, a_half, g, kind in pieces]
    return iter(range(sum(parts[:k]), sum(parts[: k + 1])))


def iotas(rows):
    shape = (rows, B)
    return lax.broadcasted_iota(jnp.int32, shape, 0), lax.broadcasted_iota(jnp.int32, shape, 1)


def slot_owner(slot, orders):
    core = lax.axis_index("tensor")
    mask = 0
    for stage, (one, other) in enumerate(zip(*orders)):
        mask = mask | (((slot >> (2 - stage)) & 1) << (one + core * (other - one)))
    return lax.axis_index("dp") ^ mask


def lanes(start, size):
    return pl.ds(start if isinstance(start, int) else pl.multiple_of(start, B), size)


LOADS = 4
FIRST = 4 * 10**9


def pack_body(pieces, items, count_a, count_g, fresh, *refs):
    n = len(items)
    if fresh:
        (a_hbm, *outs), (notes, a_held, sems) = refs[: n + 1], refs[n + 1 :]
        rows = a_hbm.shape[0] // LOADS
        parts = [slice(part * rows, (part + 1) * rows) for part in range(LOADS)]
        copies = [
            pltpu.make_async_copy(a_hbm.at[part], a_held.at[part], sems.at[i])
            for i, part in enumerate(parts)
        ]
        for copy in copies:
            copy.start()
        held = (a_held,)
    else:
        copies = []
        notes_in, held, outs, notes = refs[0], refs[1:4], refs[4 : 4 + n], refs[4 + n]
    full, half = split_rows(count_a)
    slots = SLOTS // 2
    split = [(i, k, first, slot) for i, (k, first) in enumerate(items) for slot in range(slots)]

    def read(i, start):
        return held[i][:, pl.ds(pl.multiple_of(start, B), B)]

    row, col = iotas(H)
    low = col < row
    diag_low, diag_high = col == row, col == row + H
    quarter = H // 2
    row_q, col_q = row[:quarter], col[:quarter]
    note_row, _ = iotas(EDGE)
    zero = jnp.zeros((H, B), jnp.float32)
    traces = [zero, zero]
    tiles = {}

    def cov(part):
        return lax.dot_general(
            part, part, (((0,), (0,)), ((), ())), preferred_element_type=jnp.float32
        )

    def note(slot, index, corner, natural):
        line = jnp.sum(corner, axis=0, keepdims=True)
        if index % 2 != natural:
            line = pltpu.roll(line, H, 1)
        tiles[slot] = tiles[slot] + jnp.where(note_row == index // 2, line, 0.0)

    def fold(block, slot, index, which):
        top, bottom = block[:H], block[H:]
        corner = jnp.where(diag_high, bottom, zero)
        note(slot, index, corner, 0)
        traces[which] = traces[which] + corner + jnp.where(diag_low, top, zero)
        return jnp.where(low, pltpu.roll(bottom, H, 1), top)

    def fold_half(block, odd, slot, index):
        part = jnp.where(odd == 1, pltpu.roll(block[H:], H, 1), block[:H])
        traces[0] = traces[0] + jnp.where(diag_low, part, zero)
        upper, lower = part[:quarter], part[quarter:]
        corner = jnp.where(col_q == row_q + quarter, lower, 0.0)
        note(slot, index, corner, 1)
        square = jnp.where(col_q < row_q, pltpu.roll(lower, B - quarter, 1), upper)
        rest = lower.reshape(2, quarter // 2, B)
        rest = jnp.where(col[: quarter // 2] < H, pltpu.roll(rest[1], H, 1), rest[0])
        return square, rest

    def a_parts(out, k, first, slot, index):
        a_blocks, a_half, _, kind = pieces[k]
        owner = slot_owner(first + slot, KINDS[kind])
        here, odd = kind * SLOTS + first + slot, owner & half
        base = (owner >> half) * (full * (1 + half) + half) * B
        at = 0
        for b in a_blocks:
            block = cov(read(0, base + (odd * (full + 1) + b) * B))
            out[slot, at : at + H, :] = fold(block, here, next(index), 0)
            at = at + H
        if a_half:
            block = cov(read(0, base + full * B))
            square, rest = fold_half(block, odd, here, next(index))
            out[slot, at : at + quarter, :] = square
            out[slot, at + quarter : at + quarter * 3 // 2, :] = rest
            at = at + quarter * 3 // 2
        return at

    def g_parts(out, k, first, slot, index, at):
        _, _, g_blocks, kind = pieces[k]
        here = kind * SLOTS + first + slot
        owner = slot_owner(first + slot, KINDS[kind])
        for b in g_blocks:
            start = owner * count_g + b * B
            value, grad = read(1, start).astype(jnp.float32), read(2, start).astype(jnp.float32)
            block = cov((grad * gelu_slope(value)).astype(jnp.bfloat16))
            out[slot, at : at + H, :] = fold(block, here, next(index), 1)
            at = at + H
        return at

    for copy in copies:
        copy.wait()
    for i, k, first, slot in split:
        here = pieces[k][3] * SLOTS + first + slot
        if here not in tiles:
            tiles[here] = jnp.zeros((EDGE, B), jnp.float32) if fresh else notes_in[here]
        index = corner_indices(pieces, k)
        at = a_parts(outs[i], k, first, slot, index)
        at = g_parts(outs[i], k, first, slot, index, at)
        if has_edge(pieces, k):
            outs[i][slot, at:, :] = tiles[here]

    for slot in range(NOTES):
        if slot in tiles:
            notes[slot] = tiles[slot]
        else:
            notes[slot] = jnp.zeros((EDGE, B), jnp.float32) if fresh else notes_in[slot]
    lines = [jnp.sum(trace, axis=0, keepdims=True) for trace in traces]
    tile = jnp.where(note_row == 0, lines[0], jnp.where(note_row == 1, lines[1], 0.0))
    notes[NOTES] = tile if fresh else notes_in[NOTES] + tile


def pack(arrays, pieces, items, count_a, count_g, notes):
    slots = SLOTS // 2
    fresh = notes is None
    out_shape = [
        jax.ShapeDtypeStruct((slots, piece_rows(pieces, k), B), jnp.float32) for k, _ in items
    ]
    out_shape.append(jax.ShapeDtypeStruct((NOTES + 1, EDGE, B), jnp.float32))
    if fresh:
        args = [pltpu.with_memory_space_constraint(arrays[0], pltpu.HBM)]
        out_shape.append(jax.ShapeDtypeStruct(arrays[0].shape, arrays[0].dtype))
    else:
        args = [notes, *arrays]
    space = pltpu.HBM if fresh else pltpu.VMEM
    outs = pl.pallas_call(
        functools.partial(pack_body, pieces, items, count_a, count_g, fresh),
        in_specs=[pl.BlockSpec(memory_space=space)] * len(args),
        out_specs=[pl.BlockSpec(memory_space=pltpu.VMEM)] * len(out_shape),
        out_shape=out_shape,
        scratch_shapes=[pltpu.SemaphoreType.DMA((LOADS,))] * fresh,
        compiler_params=pltpu.CompilerParams(vmem_limit_bytes=32 * 2**20),
        cost_estimate=pl.CostEstimate(
            flops=FIRST if fresh else 1, bytes_accessed=1, transcendentals=0
        ),
    )(*args)
    n = len(items)
    return outs[:n], outs[n], outs[n + 1 :]


def halve_body(n, terms, came, put, merged, *refs):
    keeps, gots, refs = refs[:n], refs[n : 2 * n], refs[2 * n :]
    terms, kept, refs = refs[:terms], refs[terms : terms + n], refs[terms + n :]
    sent, sums = (refs[:1], refs[1:]) if merged else (refs[:n], refs[n:])
    if merged:
        ends = [sum(ref.shape[1] for ref in kept[: k + 1]) for k in range(n)]
        sent = [
            sent[0].at[:, end - ref.shape[1] : end, :] for end, ref in zip(ends, kept)
        ]
    for k in range(n):
        half = kept[k].shape[0]
        kept[k][...] = keeps[k][:half] + gots[k][:half]
        sent[k][...] = keeps[k][half:] + gots[k][half:]
    if terms:
        value = sum((term[...] for term in terms[1:]), terms[0][...])
        for k in came:
            value = value + gots[k][0, -2:, :]
        for out in sums:
            out[...] = value
        for k in put:
            rows = kept[k].shape[1]
            kept[k][0, rows - 2 :, :] = value
            sent[k][0, rows - 2 :, :] = value


def halve(keeps, gots, terms=(), came=(), put=(), merged=False, weight=1):
    n = len(keeps)
    emit = bool(terms) and not put
    args = [*keeps, *gots, *terms]
    kept = [(keep.shape[0] // 2, *keep.shape[1:]) for keep in keeps]
    sent = [(kept[0][0], sum(shape[1] for shape in kept), B)] if merged else kept
    shapes = [*kept, *sent, *([(2, B)] * emit)]
    outs = pl.pallas_call(
        functools.partial(halve_body, n, len(terms), came, put, merged),
        in_specs=[pl.BlockSpec(memory_space=pltpu.VMEM)] * len(args),
        out_specs=[pl.BlockSpec(memory_space=pltpu.VMEM)] * len(shapes),
        out_shape=[jax.ShapeDtypeStruct(shape, jnp.float32) for shape in shapes],
        compiler_params=pltpu.CompilerParams(vmem_limit_bytes=32 * 2**20),
        cost_estimate=pl.CostEstimate(flops=weight, bytes_accessed=1, transcendentals=0),
    )(*args)
    return outs[:n], outs[n : n + len(sent)], outs[n + len(sent) :]


def mean_of(value, total):
    return value * (1.0 / total) if math.frexp(total)[0] == 0.5 else value / total


def turn(folded):
    return jnp.concatenate([folded] * (B // folded.shape[0]), axis=0).T


def unfold(folded):
    row, col = iotas(H)
    turned = turn(folded)
    last = pltpu.roll(jnp.where(col < row, folded, turned[:H]), H, 1)
    return jnp.where(col < row, turned[:H], folded), jnp.where(col < H, turned[H:], last)


def unfold_half(square, rest, odd):
    quarter = H // 2
    row, col = iotas(quarter)
    turned = turn(square)
    upper = jnp.where(col < row, turned[:quarter], square)
    last = pltpu.roll(jnp.where(col < row, square, turned[:quarter]), quarter, 1)
    lower = jnp.where(col < quarter, turned[quarter:H], last)
    rest = jnp.concatenate([rest, pltpu.roll(rest, H, 1)], axis=0)
    part = jnp.concatenate([upper, jnp.where(col < H, lower, rest)], axis=0)
    return (jnp.where(odd == 1, pltpu.roll(part, H, 1), part),)


def places(pieces, ks, count_a):
    full, half = split_rows(count_a)
    odd = lax.axis_index("dp") & half
    for k in ks:
        a_blocks, a_half, g_blocks, kind = pieces[k]
        index = corner_indices(pieces, k)
        for b in a_blocks:
            start = pl.multiple_of(b * B + odd * H, H) if half else b * B
            yield k, 0, start, H, next(index)
        if a_half:
            yield k, 0, pl.multiple_of((1 - odd) * full * B, H), H * 3 // 4, next(index)
        for b in g_blocks:
            yield k, 1, b * B, H, next(index)


def row_begins(pieces, ks):
    rows = [piece_rows(pieces, k) for k in ks]
    return {k: sum(rows[:i]) for i, k in enumerate(ks)}


def unfolded(pieces, ks, count_a, total, owns, got):
    odd = lax.axis_index("dp") & 1
    at = dict.fromkeys(ks, 0)
    begins = row_begins(pieces, ks)

    def take(k, rows):
        begin = at[k]
        at[k] = begin + rows
        mine = owns[ks.index(k)][0, begin : begin + rows, :]
        begin = begin + begins[k]
        return mean_of(mine + got[0, begin : begin + rows, :], total)

    for place in places(pieces, ks, count_a):
        k, _, _, rows, _ = place
        if rows == H:
            yield place, unfold(take(k, H))
        else:
            yield place, unfold_half(take(k, H // 2), take(k, H // 4), odd)


def early_body(pieces, ks, count_a, total, *refs):
    n = len(ks)
    owns, got, outs = refs[:n], refs[n], refs[n + 1 :]
    for (_, which, start, _, _), halves in unfolded(pieces, ks, count_a, total, owns, got):
        for i, value in enumerate(halves):
            outs[which][pl.ds(start + i * H, H), :] = value


def finish_body(pieces, early, late, count_a, total, *refs):
    n = len(late)
    owns, got, firsts, outs = refs[:n], refs[n], refs[n + 1 : n + 3], refs[n + 3 : n + 5]
    made, sem = refs[n + 5 : n + 7], refs[n + 7]
    _, half = split_rows(count_a)
    odd = lax.axis_index("dp") & half
    row, col = iotas(H)

    edges = {}
    for k, own in zip(late, owns):
        end = row_begins(pieces, late)[k] + piece_rows(pieces, k)
        edge = mean_of(own[0, -EDGE:, :] + got[0, end - EDGE : end, :], total)
        edges[pieces[k][3]] = (edge, pltpu.roll(edge, H, 1))
    sums = jnp.sum(edge[-2:], axis=1, keepdims=True)
    ratio = jnp.sqrt(sums[0:1] / D / (sums[1:2] / FFW))
    damp = jnp.sqrt(jnp.full((1, 1), 0.1, jnp.float32))
    shifts = (ratio * damp, damp / ratio)

    def corner(kind, index, natural):
        line = index // 2
        return edges[kind][0 if index % 2 == natural else 1][line : line + 1]

    copies = []

    def give(place, halves):
        k, which, start, rows, index = place
        shift, kind = shifts[which], pieces[k][3]
        if rows == H:
            top, bottom = halves
            top = top + jnp.where(col == row, shift, 0.0)
            bottom = jnp.where(col == row + H, corner(kind, index, 0) + shift, bottom)
            halves = (top, bottom)
        else:
            line = corner(kind, index, 1)
            line = jnp.where(odd == 1, pltpu.roll(line, H, 1), line) + shift
            diagonal = col == row + odd * H
            value = halves[0] + jnp.where(diagonal, shift, 0.0)
            last = jnp.logical_and(diagonal, row >= H // 2)
            halves = (jnp.where(last, line, value),)
        for i, value in enumerate(halves):
            made[which][pl.ds(start + i * H, H), :] = value
        part = pl.ds(start, len(halves) * H)
        copy = pltpu.make_async_copy(
            made[which].at[part], outs[which].at[part], sem.at[len(copies)]
        )
        copy.start()
        copies.append(copy)

    for place in places(pieces, early, count_a):
        _, which, start, rows, _ = place
        count = 2 if rows == H else 1
        give(place, [firsts[which][pl.ds(start + i * H, H), :] for i in range(count)])
    for place, halves in unfolded(pieces, late, count_a, total, owns, got):
        give(place, halves)
    for copy in copies:
        copy.wait()


def unfold_early(pieces, ks, owns, got, count_a, count_g, total):
    args = (*owns, got)
    return pl.pallas_call(
        functools.partial(early_body, pieces, ks, count_a, total),
        in_specs=[pl.BlockSpec(memory_space=pltpu.VMEM)] * len(args),
        out_specs=[pl.BlockSpec(memory_space=pltpu.VMEM)] * 2,
        out_shape=[
            jax.ShapeDtypeStruct((count_a, B), jnp.float32),
            jax.ShapeDtypeStruct((count_g, B), jnp.float32),
        ],
        compiler_params=pltpu.CompilerParams(vmem_limit_bytes=32 * 2**20),
        cost_estimate=pl.CostEstimate(flops=4 * 10**9, bytes_accessed=1, transcendentals=0),
    )(*args)


def finish(pieces, early, late, owns, got, first, count_a, count_g, total):
    args = (*owns, got, *first)
    parts = sum(len(a_blocks) + a_half + len(g_blocks) for a_blocks, a_half, g_blocks, _ in pieces)
    return pl.pallas_call(
        functools.partial(finish_body, pieces, early, late, count_a, total),
        in_specs=[pl.BlockSpec(memory_space=pltpu.VMEM)] * len(args),
        out_specs=[pl.BlockSpec(memory_space=pltpu.HBM)] * 2,
        out_shape=[
            jax.ShapeDtypeStruct((count_a, B), jnp.float32),
            jax.ShapeDtypeStruct((count_g, B), jnp.float32),
        ],
        scratch_shapes=[
            pltpu.VMEM((count_a, B), jnp.float32),
            pltpu.VMEM((count_g, B), jnp.float32),
            pltpu.SemaphoreType.DMA((parts,)),
        ],
        compiler_params=pltpu.CompilerParams(vmem_limit_bytes=32 * 2**20),
    )(*args)


def swap(value, partner):
    dp, tensor = lax.axis_size("dp"), lax.axis_size("tensor")
    pairs = []
    for i in range(dp):
        for j in range(tensor):
            other = partner(i, j)
            pairs.append((i * tensor + j, other[0] * tensor + other[1]))
    return lax.ppermute(value, ("dp", "tensor"), pairs)


def along(stage, kind):
    return lambda i, j: (i ^ (1 << KINDS[kind][j][stage]), j)


def packed(saved_input, saved_pre, grad_act):
    dp = lax.axis_size("dp")
    total = float(saved_input.shape[0] * dp)
    count_a = saved_input.shape[1] // dp
    count_g = saved_pre.shape[1] // dp
    full_a, half_a = split_rows(count_a)
    full_g, _ = split_rows(count_g)
    some, more = full_g // 2, full_g - full_g // 4
    pieces = (
        (tuple(range(full_a)), 0, (), 0),
        ((), 0, tuple(range(some, more)), 0),
        ((), half_a, tuple(range(some)), 1),
        ((), 0, tuple(range(more, full_g)), 1),
    )
    arrays = (saved_input, saved_pre, grad_act)
    keep, send = 0, SLOTS // 2
    early, late = (0, 2), (1, 3)
    keeps, gots, notes = {}, {}, None

    def pack_next(first, ks):
        nonlocal notes, arrays
        items = tuple((k, first) for k in ks)
        parts, notes, held = pack(arrays, pieces, items, count_a, count_g, notes)
        arrays = (*held, *arrays[len(held) :])
        return dict(zip(ks, parts))

    def exchange(parts, stage):
        for k, part in parts.items():
            gots[k] = swap(part, along(stage, pieces[k][3]))

    def halve_pair(ks, stage, **kinds):
        own, parts, others = halve(
            [keeps[k] for k in ks], [gots[k] for k in ks], merged=stage == 2,
            weight=WEIGHTS.get((ks, stage), 1), **kinds
        )
        keeps.update(zip(ks, own))
        if stage == 2:
            gots[ks] = swap(parts[0], lambda i, j: (i ^ (1 << FAR), j))
        else:
            exchange(dict(zip(ks, parts)), stage)
        return others

    exchange(pack_next(send, early[:1]), 0)
    exchange(pack_next(send, early[1:]), 0)
    exchange(pack_next(send, late), 0)
    keeps.update(pack_next(keep, early))
    keeps.update(pack_next(keep, late))

    trace = notes[NOTES, :2, :]
    trace = trace + swap(trace, lambda i, j: (i, j ^ 1))
    across = swap(trace, lambda i, j: (i ^ (1 << X) ^ (1 << NEAR), j))
    halve_pair(early, 1)
    halve_pair(late, 1, terms=(trace,), put=(0, 1))
    (trace,) = halve_pair(early, 2, terms=(trace, across))
    halve_pair(late, 2, terms=(trace,), came=(0, 1), put=(0, 1))

    def both(ks):
        return [keeps[k] for k in ks], gots[ks]

    first = unfold_early(pieces, early, *both(early), count_a, count_g, total)
    a_factor, g_factor = finish(
        pieces, early, late, *both(late), first, count_a, count_g, total
    )
    return a_factor[None], g_factor[None]


def fits(count_a, count_g):
    (full_a, half_a), full_g = split_rows(count_a), count_g // B
    if count_a % H or count_g % B or full_a < 1 or full_g < 4:
        return False
    return full_a + half_a + full_g <= 2 * (EDGE - 2)


def on_device(saved_input, saved_pre, grad_act):
    dp = lax.axis_size("dp")
    count_a = saved_input.shape[1] // dp
    count_g = saved_pre.shape[1] // dp
    if dp == SLOTS and lax.axis_size("tensor") == 2 and fits(count_a, count_g):
        return packed(saved_input, saved_pre, grad_act)
    return plain(saved_input, saved_pre, grad_act)


def solution(mesh):
    spec = P(("groups", "dp"), "tensor")
    out = P("tensor", ("groups", "dp"), None)
    return jax.shard_map(
        on_device, mesh=mesh, in_specs=(spec, spec, spec), out_specs=(out, out), check_vma=False
    )
```

```python
import functools
import math

import jax
import jax.numpy as jnp
from jax import lax
from jax.experimental import pallas as pl
from jax.experimental.pallas import tpu as pltpu
from jax.sharding import PartitionSpec as P

D = 5120
FFW = 10240
B = 128
H = B // 2


def gelu_slope(value):
    return (
        0.5 * (1.0 + lax.erf(value * 0.7071067811865476))
        + value * jnp.exp(-0.5 * value * value) * 0.3989422804014327
    )


def local_blocks(matrix, block, total):
    tokens, width = matrix.shape
    pieces = matrix.reshape(tokens, width // block, block)
    cov = jnp.einsum("tkb,tkc->kbc", pieces, pieces, preferred_element_type=jnp.float32)
    return cov.reshape(width, block) / total


def owned_unit(owned, block):
    count = owned.shape[0]
    rows = lax.axis_index("dp") * count + jnp.arange(count, dtype=jnp.int32)
    cols = jnp.arange(block, dtype=jnp.int32)
    return (cols[None, :] == (rows % block)[:, None]).astype(jnp.float32)


def plain(saved_input, saved_pre, grad_act):
    total = jnp.float32(saved_input.shape[0] * lax.axis_size("dp"))
    slope = gelu_slope(saved_pre.astype(jnp.float32))
    grad_pre = (grad_act.astype(jnp.float32) * slope).astype(jnp.bfloat16)
    terms_a = local_blocks(saved_input, B, total)
    terms_g = local_blocks(grad_pre, B, total)
    owned_a = lax.psum_scatter(terms_a, "dp", scatter_dimension=0, tiled=True)
    owned_g = lax.psum_scatter(terms_g, "dp", scatter_dimension=0, tiled=True)
    unit_a = owned_unit(owned_a, B)
    unit_g = owned_unit(owned_g, B)
    trace_a, trace_g = lax.psum(
        (jnp.sum(owned_a * unit_a), jnp.sum(owned_g * unit_g)), ("dp", "tensor")
    )
    ratio = jnp.sqrt(trace_a / D / (trace_g / FFW))
    damp = jnp.sqrt(jnp.float32(0.1))
    return (
        (owned_a + ratio * damp * unit_a)[None],
        (owned_g + damp / ratio * unit_g)[None],
    )


EDGE = 8
SLOTS = 8
X, NEAR, FAR = 0, 1, 2
KINDS = (((X, NEAR, FAR), (X, NEAR, FAR)), ((NEAR, X, FAR), (NEAR, X, FAR)))
NOTES = len(KINDS) * SLOTS

WEIGHTS = {((0, 2), 2): 2 * 10**9}


def split_rows(count):
    return count // B, (count % B) // H


def has_edge(pieces, k):
    return all(later[3] != pieces[k][3] for later in pieces[k + 1 :])


def piece_rows(pieces, k):
    a_blocks, a_half, g_blocks, _ = pieces[k]
    rows = (len(a_blocks) + len(g_blocks)) * H + a_half * (H * 3 // 4)
    return rows + (EDGE if has_edge(pieces, k) else 0)


def corner_indices(pieces, k):
    parts = [len(a) + a_half + len(g) if kind == pieces[k][3] else 0 for a, a_half, g, kind in pieces]
    return iter(range(sum(parts[:k]), sum(parts[: k + 1])))


def iotas(rows):
    shape = (rows, B)
    return lax.broadcasted_iota(jnp.int32, shape, 0), lax.broadcasted_iota(jnp.int32, shape, 1)


def slot_owner(slot, orders):
    core = lax.axis_index("tensor")
    mask = 0
    for stage, (one, other) in enumerate(zip(*orders)):
        mask = mask | (((slot >> (2 - stage)) & 1) << (one + core * (other - one)))
    return lax.axis_index("dp") ^ mask


def lanes(start, size):
    return pl.ds(start if isinstance(start, int) else pl.multiple_of(start, B), size)


LOADS = 4
FIRST = 4 * 10**9


def pack_body(pieces, items, count_a, count_g, fresh, *refs):
    n = len(items)
    if fresh:
        (a_hbm, *outs), (notes, a_held, sems) = refs[: n + 1], refs[n + 1 :]
        rows = a_hbm.shape[0] // LOADS
        parts = [slice(part * rows, (part + 1) * rows) for part in range(LOADS)]
        copies = [
            pltpu.make_async_copy(a_hbm.at[part], a_held.at[part], sems.at[i])
            for i, part in enumerate(parts)
        ]
        for copy in copies:
            copy.start()
        held = (a_held,)
    else:
        copies = []
        notes_in, held, outs, notes = refs[0], refs[1:4], refs[4 : 4 + n], refs[4 + n]
    full, half = split_rows(count_a)
    slots = SLOTS // 2
    split = [(i, k, first, slot) for i, (k, first) in enumerate(items) for slot in range(slots)]

    def read(i, start):
        return held[i][:, pl.ds(pl.multiple_of(start, B), B)]

    row, col = iotas(H)
    low = col < row
    diag_low, diag_high = col == row, col == row + H
    quarter = H // 2
    row_q, col_q = row[:quarter], col[:quarter]
    note_row, _ = iotas(EDGE)
    zero = jnp.zeros((H, B), jnp.float32)
    traces = [zero, zero]
    tiles = {}

    def cov(part):
        return lax.dot_general(
            part, part, (((0,), (0,)), ((), ())), preferred_element_type=jnp.float32
        )

    def note(slot, index, corner, natural):
        line = jnp.sum(corner, axis=0, keepdims=True)
        if index % 2 != natural:
            line = pltpu.roll(line, H, 1)
        tiles[slot] = tiles[slot] + jnp.where(note_row == index // 2, line, 0.0)

    def fold(block, slot, index, which):
        top, bottom = block[:H], block[H:]
        corner = jnp.where(diag_high, bottom, zero)
        note(slot, index, corner, 0)
        traces[which] = traces[which] + corner + jnp.where(diag_low, top, zero)
        return jnp.where(low, pltpu.roll(bottom, H, 1), top)

    def fold_half(block, odd, slot, index):
        part = jnp.where(odd == 1, pltpu.roll(block[H:], H, 1), block[:H])
        traces[0] = traces[0] + jnp.where(diag_low, part, zero)
        upper, lower = part[:quarter], part[quarter:]
        corner = jnp.where(col_q == row_q + quarter, lower, 0.0)
        note(slot, index, corner, 1)
        square = jnp.where(col_q < row_q, pltpu.roll(lower, B - quarter, 1), upper)
        rest = lower.reshape(2, quarter // 2, B)
        rest = jnp.where(col[: quarter // 2] < H, pltpu.roll(rest[1], H, 1), rest[0])
        return square, rest

    def a_parts(out, k, first, slot, index):
        a_blocks, a_half, _, kind = pieces[k]
        owner = slot_owner(first + slot, KINDS[kind])
        here, odd = kind * SLOTS + first + slot, owner & half
        base = (owner >> half) * (full * (1 + half) + half) * B
        at = 0
        for b in a_blocks:
            block = cov(read(0, base + (odd * (full + 1) + b) * B))
            out[slot, at : at + H, :] = fold(block, here, next(index), 0)
            at = at + H
        if a_half:
            block = cov(read(0, base + full * B))
            square, rest = fold_half(block, odd, here, next(index))
            out[slot, at : at + quarter, :] = square
            out[slot, at + quarter : at + quarter * 3 // 2, :] = rest
            at = at + quarter * 3 // 2
        return at

    def g_parts(out, k, first, slot, index, at):
        _, _, g_blocks, kind = pieces[k]
        here = kind * SLOTS + first + slot
        owner = slot_owner(first + slot, KINDS[kind])
        for b in g_blocks:
            start = owner * count_g + b * B
            value, grad = read(1, start).astype(jnp.float32), read(2, start).astype(jnp.float32)
            block = cov((grad * gelu_slope(value)).astype(jnp.bfloat16))
            out[slot, at : at + H, :] = fold(block, here, next(index), 1)
            at = at + H
        return at

    for copy in copies:
        copy.wait()
    for i, k, first, slot in split:
        here = pieces[k][3] * SLOTS + first + slot
        if here not in tiles:
            tiles[here] = jnp.zeros((EDGE, B), jnp.float32) if fresh else notes_in[here]
        index = corner_indices(pieces, k)
        at = a_parts(outs[i], k, first, slot, index)
        at = g_parts(outs[i], k, first, slot, index, at)
        if has_edge(pieces, k):
            outs[i][slot, at:, :] = tiles[here]

    for slot in range(NOTES):
        if slot in tiles:
            notes[slot] = tiles[slot]
        else:
            notes[slot] = jnp.zeros((EDGE, B), jnp.float32) if fresh else notes_in[slot]
    lines = [jnp.sum(trace, axis=0, keepdims=True) for trace in traces]
    tile = jnp.where(note_row == 0, lines[0], jnp.where(note_row == 1, lines[1], 0.0))
    notes[NOTES] = tile if fresh else notes_in[NOTES] + tile


def pack(arrays, pieces, items, count_a, count_g, notes):
    slots = SLOTS // 2
    fresh = notes is None
    out_shape = [
        jax.ShapeDtypeStruct((slots, piece_rows(pieces, k), B), jnp.float32) for k, _ in items
    ]
    out_shape.append(jax.ShapeDtypeStruct((NOTES + 1, EDGE, B), jnp.float32))
    if fresh:
        args = [pltpu.with_memory_space_constraint(arrays[0], pltpu.HBM)]
        out_shape.append(jax.ShapeDtypeStruct(arrays[0].shape, arrays[0].dtype))
    else:
        args = [notes, *arrays]
    space = pltpu.HBM if fresh else pltpu.VMEM
    outs = pl.pallas_call(
        functools.partial(pack_body, pieces, items, count_a, count_g, fresh),
        in_specs=[pl.BlockSpec(memory_space=space)] * len(args),
        out_specs=[pl.BlockSpec(memory_space=pltpu.VMEM)] * len(out_shape),
        out_shape=out_shape,
        scratch_shapes=[pltpu.SemaphoreType.DMA((LOADS,))] * fresh,
        compiler_params=pltpu.CompilerParams(vmem_limit_bytes=32 * 2**20),
        cost_estimate=pl.CostEstimate(
            flops=FIRST if fresh else 1, bytes_accessed=1, transcendentals=0
        ),
    )(*args)
    n = len(items)
    return outs[:n], outs[n], outs[n + 1 :]


def halve_body(n, terms, came, put, merged, *refs):
    keeps, gots, refs = refs[:n], refs[n : 2 * n], refs[2 * n :]
    terms, kept, refs = refs[:terms], refs[terms : terms + n], refs[terms + n :]
    sent, sums = (refs[:1], refs[1:]) if merged else (refs[:n], refs[n:])
    if merged:
        ends = [sum(ref.shape[1] for ref in kept[: k + 1]) for k in range(n)]
        sent = [
            sent[0].at[:, end - ref.shape[1] : end, :] for end, ref in zip(ends, kept)
        ]
    for k in range(n):
        half = kept[k].shape[0]
        kept[k][...] = keeps[k][:half] + gots[k][:half]
        sent[k][...] = keeps[k][half:] + gots[k][half:]
    if terms:
        value = sum((term[...] for term in terms[1:]), terms[0][...])
        for k in came:
            value = value + gots[k][0, -2:, :]
        for out in sums:
            out[...] = value
        for k in put:
            rows = kept[k].shape[1]
            kept[k][0, rows - 2 :, :] = value
            sent[k][0, rows - 2 :, :] = value


def halve(keeps, gots, terms=(), came=(), put=(), merged=False, weight=1):
    n = len(keeps)
    emit = bool(terms) and not put
    args = [*keeps, *gots, *terms]
    kept = [(keep.shape[0] // 2, *keep.shape[1:]) for keep in keeps]
    sent = [(kept[0][0], sum(shape[1] for shape in kept), B)] if merged else kept
    shapes = [*kept, *sent, *([(2, B)] * emit)]
    outs = pl.pallas_call(
        functools.partial(halve_body, n, len(terms), came, put, merged),
        in_specs=[pl.BlockSpec(memory_space=pltpu.VMEM)] * len(args),
        out_specs=[pl.BlockSpec(memory_space=pltpu.VMEM)] * len(shapes),
        out_shape=[jax.ShapeDtypeStruct(shape, jnp.float32) for shape in shapes],
        compiler_params=pltpu.CompilerParams(vmem_limit_bytes=32 * 2**20),
        cost_estimate=pl.CostEstimate(flops=weight, bytes_accessed=1, transcendentals=0),
    )(*args)
    return outs[:n], outs[n : n + len(sent)], outs[n + len(sent) :]


def mean_of(value, total):
    return value * (1.0 / total) if math.frexp(total)[0] == 0.5 else value / total


def turn(folded):
    return jnp.concatenate([folded] * (B // folded.shape[0]), axis=0).T


def unfold(folded):
    row, col = iotas(H)
    turned = turn(folded)
    last = pltpu.roll(jnp.where(col < row, folded, turned[:H]), H, 1)
    return jnp.where(col < row, turned[:H], folded), jnp.where(col < H, turned[H:], last)


def unfold_half(square, rest, odd):
    quarter = H // 2
    row, col = iotas(quarter)
    turned = turn(square)
    upper = jnp.where(col < row, turned[:quarter], square)
    last = pltpu.roll(jnp.where(col < row, square, turned[:quarter]), quarter, 1)
    lower = jnp.where(col < quarter, turned[quarter:H], last)
    rest = jnp.concatenate([rest, pltpu.roll(rest, H, 1)], axis=0)
    part = jnp.concatenate([upper, jnp.where(col < H, lower, rest)], axis=0)
    return (jnp.where(odd == 1, pltpu.roll(part, H, 1), part),)


def places(pieces, ks, count_a):
    full, half = split_rows(count_a)
    odd = lax.axis_index("dp") & half
    for k in ks:
        a_blocks, a_half, g_blocks, kind = pieces[k]
        index = corner_indices(pieces, k)
        for b in a_blocks:
            start = pl.multiple_of(b * B + odd * H, H) if half else b * B
            yield k, 0, start, H, next(index)
        if a_half:
            yield k, 0, pl.multiple_of((1 - odd) * full * B, H), H * 3 // 4, next(index)
        for b in g_blocks:
            yield k, 1, b * B, H, next(index)


def row_begins(pieces, ks):
    rows = [piece_rows(pieces, k) for k in ks]
    return {k: sum(rows[:i]) for i, k in enumerate(ks)}


def unfolded(pieces, ks, count_a, total, owns, got):
    odd = lax.axis_index("dp") & 1
    at = dict.fromkeys(ks, 0)
    begins = row_begins(pieces, ks)

    def take(k, rows):
        begin = at[k]
        at[k] = begin + rows
        mine = owns[ks.index(k)][0, begin : begin + rows, :]
        begin = begin + begins[k]
        return mean_of(mine + got[0, begin : begin + rows, :], total)

    for place in places(pieces, ks, count_a):
        k, _, _, rows, _ = place
        if rows == H:
            yield place, unfold(take(k, H))
        else:
            yield place, unfold_half(take(k, H // 2), take(k, H // 4), odd)


def early_body(pieces, ks, count_a, total, *refs):
    n = len(ks)
    owns, got, outs = refs[:n], refs[n], refs[n + 1 :]
    for (_, which, start, _, _), halves in unfolded(pieces, ks, count_a, total, owns, got):
        for i, value in enumerate(halves):
            outs[which][pl.ds(start + i * H, H), :] = value


def finish_body(pieces, early, late, count_a, total, *refs):
    n = len(late)
    owns, got, firsts, outs = refs[:n], refs[n], refs[n + 1 : n + 3], refs[n + 3 : n + 5]
    made, sem = refs[n + 5 : n + 7], refs[n + 7]
    _, half = split_rows(count_a)
    odd = lax.axis_index("dp") & half
    row, col = iotas(H)

    edges = {}
    for k, own in zip(late, owns):
        end = row_begins(pieces, late)[k] + piece_rows(pieces, k)
        edge = mean_of(own[0, -EDGE:, :] + got[0, end - EDGE : end, :], total)
        edges[pieces[k][3]] = (edge, pltpu.roll(edge, H, 1))
    sums = jnp.sum(edge[-2:], axis=1, keepdims=True)
    ratio = jnp.sqrt(sums[0:1] / D / (sums[1:2] / FFW))
    damp = jnp.sqrt(jnp.full((1, 1), 0.1, jnp.float32))
    shifts = (ratio * damp, damp / ratio)

    def corner(kind, index, natural):
        line = index // 2
        return edges[kind][0 if index % 2 == natural else 1][line : line + 1]

    copies = []

    def give(place, halves):
        k, which, start, rows, index = place
        shift, kind = shifts[which], pieces[k][3]
        if rows == H:
            top, bottom = halves
            top = top + jnp.where(col == row, shift, 0.0)
            bottom = jnp.where(col == row + H, corner(kind, index, 0) + shift, bottom)
            halves = (top, bottom)
        else:
            line = corner(kind, index, 1)
            line = jnp.where(odd == 1, pltpu.roll(line, H, 1), line) + shift
            diagonal = col == row + odd * H
            value = halves[0] + jnp.where(diagonal, shift, 0.0)
            last = jnp.logical_and(diagonal, row >= H // 2)
            halves = (jnp.where(last, line, value),)
        for i, value in enumerate(halves):
            made[which][pl.ds(start + i * H, H), :] = value
        part = pl.ds(start, len(halves) * H)
        copy = pltpu.make_async_copy(
            made[which].at[part], outs[which].at[part], sem.at[len(copies)]
        )
        copy.start()
        copies.append(copy)

    for place in places(pieces, early, count_a):
        _, which, start, rows, _ = place
        count = 2 if rows == H else 1
        give(place, [firsts[which][pl.ds(start + i * H, H), :] for i in range(count)])
    for place, halves in unfolded(pieces, late, count_a, total, owns, got):
        give(place, halves)
    for copy in copies:
        copy.wait()


def unfold_early(pieces, ks, owns, got, count_a, count_g, total):
    args = (*owns, got)
    return pl.pallas_call(
        functools.partial(early_body, pieces, ks, count_a, total),
        in_specs=[pl.BlockSpec(memory_space=pltpu.VMEM)] * len(args),
        out_specs=[pl.BlockSpec(memory_space=pltpu.VMEM)] * 2,
        out_shape=[
            jax.ShapeDtypeStruct((count_a, B), jnp.float32),
            jax.ShapeDtypeStruct((count_g, B), jnp.float32),
        ],
        compiler_params=pltpu.CompilerParams(vmem_limit_bytes=32 * 2**20),
        cost_estimate=pl.CostEstimate(flops=4 * 10**9, bytes_accessed=1, transcendentals=0),
    )(*args)


def finish(pieces, early, late, owns, got, first, count_a, count_g, total):
    args = (*owns, got, *first)
    parts = sum(len(a_blocks) + a_half + len(g_blocks) for a_blocks, a_half, g_blocks, _ in pieces)
    return pl.pallas_call(
        functools.partial(finish_body, pieces, early, late, count_a, total),
        in_specs=[pl.BlockSpec(memory_space=pltpu.VMEM)] * len(args),
        out_specs=[pl.BlockSpec(memory_space=pltpu.HBM)] * 2,
        out_shape=[
            jax.ShapeDtypeStruct((count_a, B), jnp.float32),
            jax.ShapeDtypeStruct((count_g, B), jnp.float32),
        ],
        scratch_shapes=[
            pltpu.VMEM((count_a, B), jnp.float32),
            pltpu.VMEM((count_g, B), jnp.float32),
            pltpu.SemaphoreType.DMA((parts,)),
        ],
        compiler_params=pltpu.CompilerParams(vmem_limit_bytes=32 * 2**20),
    )(*args)


def swap(value, partner):
    dp, tensor = lax.axis_size("dp"), lax.axis_size("tensor")
    pairs = []
    for i in range(dp):
        for j in range(tensor):
            other = partner(i, j)
            pairs.append((i * tensor + j, other[0] * tensor + other[1]))
    return lax.ppermute(value, ("dp", "tensor"), pairs)


def along(stage, kind):
    return lambda i, j: (i ^ (1 << KINDS[kind][j][stage]), j)


def packed(saved_input, saved_pre, grad_act):
    dp = lax.axis_size("dp")
    total = float(saved_input.shape[0] * dp)
    count_a = saved_input.shape[1] // dp
    count_g = saved_pre.shape[1] // dp
    full_a, half_a = split_rows(count_a)
    full_g, _ = split_rows(count_g)
    some = 1 + (full_g - 1) // 2
    pieces = (
        (tuple(range(full_a)), 0, (), 0),
        ((), 0, tuple(range(1, some)), 0),
        ((), half_a, (0,), 1),
        ((), 0, tuple(range(some, full_g)), 1),
    )
    arrays = (saved_input, saved_pre, grad_act)
    keep, send = 0, SLOTS // 2
    early, late = (0, 2), (1, 3)
    keeps, gots, notes = {}, {}, None

    def pack_next(first, ks):
        nonlocal notes, arrays
        items = tuple((k, first) for k in ks)
        parts, notes, held = pack(arrays, pieces, items, count_a, count_g, notes)
        arrays = (*held, *arrays[len(held) :])
        return dict(zip(ks, parts))

    def exchange(parts, stage):
        for k, part in parts.items():
            gots[k] = swap(part, along(stage, pieces[k][3]))

    def halve_pair(ks, stage, **kinds):
        own, parts, others = halve(
            [keeps[k] for k in ks], [gots[k] for k in ks], merged=stage == 2,
            weight=WEIGHTS.get((ks, stage), 1), **kinds
        )
        keeps.update(zip(ks, own))
        if stage == 2:
            gots[ks] = swap(parts[0], lambda i, j: (i ^ (1 << FAR), j))
        else:
            exchange(dict(zip(ks, parts)), stage)
        return others

    exchange(pack_next(send, early[:1]), 0)
    exchange(pack_next(send, early[1:]), 0)
    exchange(pack_next(send, late), 0)
    keeps.update(pack_next(keep, early))
    keeps.update(pack_next(keep, late))

    trace = notes[NOTES, :2, :]
    trace = trace + swap(trace, lambda i, j: (i, j ^ 1))
    across = swap(trace, lambda i, j: (i ^ (1 << X) ^ (1 << NEAR), j))
    halve_pair(early, 1)
    halve_pair(late, 1, terms=(trace,), put=(0, 1))
    (trace,) = halve_pair(early, 2, terms=(trace, across))
    halve_pair(late, 2, terms=(trace,), came=(0, 1), put=(0, 1))

    def both(ks):
        return [keeps[k] for k in ks], gots[ks]

    first = unfold_early(pieces, early, *both(early), count_a, count_g, total)
    a_factor, g_factor = finish(
        pieces, early, late, *both(late), first, count_a, count_g, total
    )
    return a_factor[None], g_factor[None]


def fits(count_a, count_g):
    (full_a, half_a), full_g = split_rows(count_a), count_g // B
    if count_a % H or count_g % B or full_a < 1 or full_g < 3:
        return False
    return full_a + half_a + full_g <= 2 * (EDGE - 2)


def on_device(saved_input, saved_pre, grad_act):
    dp = lax.axis_size("dp")
    count_a = saved_input.shape[1] // dp
    count_g = saved_pre.shape[1] // dp
    if dp == SLOTS and lax.axis_size("tensor") == 2 and fits(count_a, count_g):
        return packed(saved_input, saved_pre, grad_act)
    return plain(saved_input, saved_pre, grad_act)


def solution(mesh):
    spec = P(("groups", "dp"), "tensor")
    out = P("tensor", ("groups", "dp"), None)
    return jax.shard_map(
        on_device, mesh=mesh, in_specs=(spec, spec, spec), out_specs=(out, out), check_vma=False
    )
```

```python
import functools
import math

import jax
import jax.numpy as jnp
from jax import lax
from jax.experimental import pallas as pl
from jax.experimental.pallas import tpu as pltpu
from jax.sharding import PartitionSpec as P

D = 5120
FFW = 10240
B = 128
H = B // 2


def gelu_slope(value):
    return (
        0.5 * (1.0 + lax.erf(value * 0.7071067811865476))
        + value * jnp.exp(-0.5 * value * value) * 0.3989422804014327
    )


def local_blocks(matrix, block, total):
    tokens, width = matrix.shape
    pieces = matrix.reshape(tokens, width // block, block)
    cov = jnp.einsum("tkb,tkc->kbc", pieces, pieces, preferred_element_type=jnp.float32)
    return cov.reshape(width, block) / total


def owned_unit(owned, block):
    count = owned.shape[0]
    rows = lax.axis_index("dp") * count + jnp.arange(count, dtype=jnp.int32)
    cols = jnp.arange(block, dtype=jnp.int32)
    return (cols[None, :] == (rows % block)[:, None]).astype(jnp.float32)


def plain(saved_input, saved_pre, grad_act):
    total = jnp.float32(saved_input.shape[0] * lax.axis_size("dp"))
    slope = gelu_slope(saved_pre.astype(jnp.float32))
    grad_pre = (grad_act.astype(jnp.float32) * slope).astype(jnp.bfloat16)
    terms_a = local_blocks(saved_input, B, total)
    terms_g = local_blocks(grad_pre, B, total)
    owned_a = lax.psum_scatter(terms_a, "dp", scatter_dimension=0, tiled=True)
    owned_g = lax.psum_scatter(terms_g, "dp", scatter_dimension=0, tiled=True)
    unit_a = owned_unit(owned_a, B)
    unit_g = owned_unit(owned_g, B)
    trace_a, trace_g = lax.psum(
        (jnp.sum(owned_a * unit_a), jnp.sum(owned_g * unit_g)), ("dp", "tensor")
    )
    ratio = jnp.sqrt(trace_a / D / (trace_g / FFW))
    damp = jnp.sqrt(jnp.float32(0.1))
    return (
        (owned_a + ratio * damp * unit_a)[None],
        (owned_g + damp / ratio * unit_g)[None],
    )


EDGE = 8
SLOTS = 8
X, NEAR, FAR = 0, 1, 2
KINDS = (((X, NEAR, FAR), (X, NEAR, FAR)), ((NEAR, X, FAR), (NEAR, X, FAR)))
NOTES = len(KINDS) * SLOTS

WEIGHTS = {((0, 2), 2): 2 * 10**9}


def split_rows(count):
    return count // B, (count % B) // H


def has_edge(pieces, k):
    return all(later[3] != pieces[k][3] for later in pieces[k + 1 :])


def piece_rows(pieces, k):
    a_blocks, a_half, g_blocks, _ = pieces[k]
    rows = (len(a_blocks) + len(g_blocks)) * H + a_half * (H * 3 // 4)
    return rows + (EDGE if has_edge(pieces, k) else 0)


def corner_indices(pieces, k):
    parts = [len(a) + a_half + len(g) if kind == pieces[k][3] else 0 for a, a_half, g, kind in pieces]
    return iter(range(sum(parts[:k]), sum(parts[: k + 1])))


def iotas(rows):
    shape = (rows, B)
    return lax.broadcasted_iota(jnp.int32, shape, 0), lax.broadcasted_iota(jnp.int32, shape, 1)


def slot_owner(slot, orders):
    core = lax.axis_index("tensor")
    mask = 0
    for stage, (one, other) in enumerate(zip(*orders)):
        mask = mask | (((slot >> (2 - stage)) & 1) << (one + core * (other - one)))
    return lax.axis_index("dp") ^ mask


def lanes(start, size):
    return pl.ds(start if isinstance(start, int) else pl.multiple_of(start, B), size)


LOADS = 4
FIRST = 4 * 10**9


def pack_body(pieces, items, count_a, count_g, fresh, *refs):
    n = len(items)
    if fresh:
        (a_hbm, *outs), (notes, a_held, sems) = refs[: n + 1], refs[n + 1 :]
        rows = a_hbm.shape[0] // LOADS
        parts = [slice(part * rows, (part + 1) * rows) for part in range(LOADS)]
        copies = [
            pltpu.make_async_copy(a_hbm.at[part], a_held.at[part], sems.at[i])
            for i, part in enumerate(parts)
        ]
        for copy in copies:
            copy.start()
        held = (a_held,)
    else:
        copies = []
        notes_in, held, outs, notes = refs[0], refs[1:4], refs[4 : 4 + n], refs[4 + n]
    full, half = split_rows(count_a)
    slots = SLOTS // 2
    split = [(i, k, first, slot) for i, (k, first) in enumerate(items) for slot in range(slots)]

    def read(i, start):
        return held[i][:, pl.ds(pl.multiple_of(start, B), B)]

    row, col = iotas(H)
    low = col < row
    diag_low, diag_high = col == row, col == row + H
    quarter = H // 2
    row_q, col_q = row[:quarter], col[:quarter]
    note_row, _ = iotas(EDGE)
    zero = jnp.zeros((H, B), jnp.float32)
    traces = [zero, zero]
    tiles = {}

    def cov(part):
        return lax.dot_general(
            part, part, (((0,), (0,)), ((), ())), preferred_element_type=jnp.float32
        )

    def note(slot, index, corner, natural):
        line = jnp.sum(corner, axis=0, keepdims=True)
        if index % 2 != natural:
            line = pltpu.roll(line, H, 1)
        tiles[slot] = tiles[slot] + jnp.where(note_row == index // 2, line, 0.0)

    def fold(block, slot, index, which):
        top, bottom = block[:H], block[H:]
        corner = jnp.where(diag_high, bottom, zero)
        note(slot, index, corner, 0)
        traces[which] = traces[which] + corner + jnp.where(diag_low, top, zero)
        return jnp.where(low, pltpu.roll(bottom, H, 1), top)

    def fold_half(block, odd, slot, index):
        part = jnp.where(odd == 1, pltpu.roll(block[H:], H, 1), block[:H])
        traces[0] = traces[0] + jnp.where(diag_low, part, zero)
        upper, lower = part[:quarter], part[quarter:]
        corner = jnp.where(col_q == row_q + quarter, lower, 0.0)
        note(slot, index, corner, 1)
        square = jnp.where(col_q < row_q, pltpu.roll(lower, B - quarter, 1), upper)
        rest = lower.reshape(2, quarter // 2, B)
        rest = jnp.where(col[: quarter // 2] < H, pltpu.roll(rest[1], H, 1), rest[0])
        return square, rest

    def a_parts(out, k, first, slot, index):
        a_blocks, a_half, _, kind = pieces[k]
        owner = slot_owner(first + slot, KINDS[kind])
        here, odd = kind * SLOTS + first + slot, owner & half
        base = (owner >> half) * (full * (1 + half) + half) * B
        at = 0
        for b in a_blocks:
            block = cov(read(0, base + (odd * (full + 1) + b) * B))
            out[slot, at : at + H, :] = fold(block, here, next(index), 0)
            at = at + H
        if a_half:
            block = cov(read(0, base + full * B))
            square, rest = fold_half(block, odd, here, next(index))
            out[slot, at : at + quarter, :] = square
            out[slot, at + quarter : at + quarter * 3 // 2, :] = rest
            at = at + quarter * 3 // 2
        return at

    def g_parts(out, k, first, slot, index, at):
        _, _, g_blocks, kind = pieces[k]
        here = kind * SLOTS + first + slot
        owner = slot_owner(first + slot, KINDS[kind])
        for b in g_blocks:
            start = owner * count_g + b * B
            value, grad = read(1, start).astype(jnp.float32), read(2, start).astype(jnp.float32)
            block = cov((grad * gelu_slope(value)).astype(jnp.bfloat16))
            out[slot, at : at + H, :] = fold(block, here, next(index), 1)
            at = at + H
        return at

    for copy in copies:
        copy.wait()
    for i, k, first, slot in split:
        here = pieces[k][3] * SLOTS + first + slot
        if here not in tiles:
            tiles[here] = jnp.zeros((EDGE, B), jnp.float32) if fresh else notes_in[here]
        index = corner_indices(pieces, k)
        at = a_parts(outs[i], k, first, slot, index)
        at = g_parts(outs[i], k, first, slot, index, at)
        if has_edge(pieces, k):
            outs[i][slot, at:, :] = tiles[here]

    for slot in range(NOTES):
        if slot in tiles:
            notes[slot] = tiles[slot]
        else:
            notes[slot] = jnp.zeros((EDGE, B), jnp.float32) if fresh else notes_in[slot]
    lines = [jnp.sum(trace, axis=0, keepdims=True) for trace in traces]
    tile = jnp.where(note_row == 0, lines[0], jnp.where(note_row == 1, lines[1], 0.0))
    notes[NOTES] = tile if fresh else notes_in[NOTES] + tile


def pack(arrays, pieces, items, count_a, count_g, notes):
    slots = SLOTS // 2
    fresh = notes is None
    out_shape = [
        jax.ShapeDtypeStruct((slots, piece_rows(pieces, k), B), jnp.float32) for k, _ in items
    ]
    out_shape.append(jax.ShapeDtypeStruct((NOTES + 1, EDGE, B), jnp.float32))
    if fresh:
        args = [pltpu.with_memory_space_constraint(arrays[0], pltpu.HBM)]
        out_shape.append(jax.ShapeDtypeStruct(arrays[0].shape, arrays[0].dtype))
    else:
        args = [notes, *arrays]
    space = pltpu.HBM if fresh else pltpu.VMEM
    outs = pl.pallas_call(
        functools.partial(pack_body, pieces, items, count_a, count_g, fresh),
        in_specs=[pl.BlockSpec(memory_space=space)] * len(args),
        out_specs=[pl.BlockSpec(memory_space=pltpu.VMEM)] * len(out_shape),
        out_shape=out_shape,
        scratch_shapes=[pltpu.SemaphoreType.DMA((LOADS,))] * fresh,
        compiler_params=pltpu.CompilerParams(vmem_limit_bytes=32 * 2**20),
        cost_estimate=pl.CostEstimate(
            flops=FIRST if fresh else 1, bytes_accessed=1, transcendentals=0
        ),
    )(*args)
    n = len(items)
    return outs[:n], outs[n], outs[n + 1 :]


def halve_body(n, terms, came, put, merged, *refs):
    keeps, gots, refs = refs[:n], refs[n : 2 * n], refs[2 * n :]
    terms, kept, refs = refs[:terms], refs[terms : terms + n], refs[terms + n :]
    sent, sums = (refs[:1], refs[1:]) if merged else (refs[:n], refs[n:])
    if merged:
        ends = [sum(ref.shape[1] for ref in kept[: k + 1]) for k in range(n)]
        sent = [
            sent[0].at[:, end - ref.shape[1] : end, :] for end, ref in zip(ends, kept)
        ]
    for k in range(n):
        half = kept[k].shape[0]
        kept[k][...] = keeps[k][:half] + gots[k][:half]
        sent[k][...] = keeps[k][half:] + gots[k][half:]
    if terms:
        value = sum((term[...] for term in terms[1:]), terms[0][...])
        for k in came:
            value = value + gots[k][0, -2:, :]
        for out in sums:
            out[...] = value
        for k in put:
            rows = kept[k].shape[1]
            kept[k][0, rows - 2 :, :] = value
            sent[k][0, rows - 2 :, :] = value


def halve(keeps, gots, terms=(), came=(), put=(), merged=False, weight=1):
    n = len(keeps)
    emit = bool(terms) and not put
    args = [*keeps, *gots, *terms]
    kept = [(keep.shape[0] // 2, *keep.shape[1:]) for keep in keeps]
    sent = [(kept[0][0], sum(shape[1] for shape in kept), B)] if merged else kept
    shapes = [*kept, *sent, *([(2, B)] * emit)]
    outs = pl.pallas_call(
        functools.partial(halve_body, n, len(terms), came, put, merged),
        in_specs=[pl.BlockSpec(memory_space=pltpu.VMEM)] * len(args),
        out_specs=[pl.BlockSpec(memory_space=pltpu.VMEM)] * len(shapes),
        out_shape=[jax.ShapeDtypeStruct(shape, jnp.float32) for shape in shapes],
        compiler_params=pltpu.CompilerParams(vmem_limit_bytes=32 * 2**20),
        cost_estimate=pl.CostEstimate(flops=weight, bytes_accessed=1, transcendentals=0),
    )(*args)
    return outs[:n], outs[n : n + len(sent)], outs[n + len(sent) :]


def mean_of(value, total):
    return value * (1.0 / total) if math.frexp(total)[0] == 0.5 else value / total


def turn(folded):
    return jnp.concatenate([folded] * (B // folded.shape[0]), axis=0).T


def unfold(folded):
    row, col = iotas(H)
    turned = turn(folded)
    last = pltpu.roll(jnp.where(col < row, folded, turned[:H]), H, 1)
    return jnp.where(col < row, turned[:H], folded), jnp.where(col < H, turned[H:], last)


def unfold_half(square, rest, odd):
    quarter = H // 2
    row, col = iotas(quarter)
    turned = turn(square)
    upper = jnp.where(col < row, turned[:quarter], square)
    last = pltpu.roll(jnp.where(col < row, square, turned[:quarter]), quarter, 1)
    lower = jnp.where(col < quarter, turned[quarter:H], last)
    rest = jnp.concatenate([rest, pltpu.roll(rest, H, 1)], axis=0)
    part = jnp.concatenate([upper, jnp.where(col < H, lower, rest)], axis=0)
    return (jnp.where(odd == 1, pltpu.roll(part, H, 1), part),)


def places(pieces, ks, count_a):
    full, half = split_rows(count_a)
    odd = lax.axis_index("dp") & half
    for k in ks:
        a_blocks, a_half, g_blocks, kind = pieces[k]
        index = corner_indices(pieces, k)
        for b in a_blocks:
            start = pl.multiple_of(b * B + odd * H, H) if half else b * B
            yield k, 0, start, H, next(index)
        if a_half:
            yield k, 0, pl.multiple_of((1 - odd) * full * B, H), H * 3 // 4, next(index)
        for b in g_blocks:
            yield k, 1, b * B, H, next(index)


def row_begins(pieces, ks):
    rows = [piece_rows(pieces, k) for k in ks]
    return {k: sum(rows[:i]) for i, k in enumerate(ks)}


def unfolded(pieces, ks, count_a, total, owns, got):
    odd = lax.axis_index("dp") & 1
    at = dict.fromkeys(ks, 0)
    begins = row_begins(pieces, ks)

    def take(k, rows):
        begin = at[k]
        at[k] = begin + rows
        mine = owns[ks.index(k)][0, begin : begin + rows, :]
        begin = begin + begins[k]
        return mean_of(mine + got[0, begin : begin + rows, :], total)

    for place in places(pieces, ks, count_a):
        k, _, _, rows, _ = place
        if rows == H:
            yield place, unfold(take(k, H))
        else:
            yield place, unfold_half(take(k, H // 2), take(k, H // 4), odd)


def early_body(pieces, ks, count_a, total, *refs):
    n = len(ks)
    owns, got, outs = refs[:n], refs[n], refs[n + 1 :]
    for (_, which, start, _, _), halves in unfolded(pieces, ks, count_a, total, owns, got):
        for i, value in enumerate(halves):
            outs[which][pl.ds(start + i * H, H), :] = value


def finish_body(pieces, early, late, count_a, total, *refs):
    n = len(late)
    owns, got, firsts, outs = refs[:n], refs[n], refs[n + 1 : n + 3], refs[n + 3 : n + 5]
    made, sem = refs[n + 5 : n + 7], refs[n + 7]
    _, half = split_rows(count_a)
    odd = lax.axis_index("dp") & half
    row, col = iotas(H)

    edges = {}
    for k, own in zip(late, owns):
        end = row_begins(pieces, late)[k] + piece_rows(pieces, k)
        edge = mean_of(own[0, -EDGE:, :] + got[0, end - EDGE : end, :], total)
        edges[pieces[k][3]] = (edge, pltpu.roll(edge, H, 1))
    sums = jnp.sum(edge[-2:], axis=1, keepdims=True)
    ratio = jnp.sqrt(sums[0:1] / D / (sums[1:2] / FFW))
    damp = jnp.sqrt(jnp.full((1, 1), 0.1, jnp.float32))
    shifts = (ratio * damp, damp / ratio)

    def corner(kind, index, natural):
        line = index // 2
        return edges[kind][0 if index % 2 == natural else 1][line : line + 1]

    copies = []

    def give(place, halves):
        k, which, start, rows, index = place
        shift, kind = shifts[which], pieces[k][3]
        if rows == H:
            top, bottom = halves
            top = top + jnp.where(col == row, shift, 0.0)
            bottom = jnp.where(col == row + H, corner(kind, index, 0) + shift, bottom)
            halves = (top, bottom)
        else:
            line = corner(kind, index, 1)
            line = jnp.where(odd == 1, pltpu.roll(line, H, 1), line) + shift
            diagonal = col == row + odd * H
            value = halves[0] + jnp.where(diagonal, shift, 0.0)
            last = jnp.logical_and(diagonal, row >= H // 2)
            halves = (jnp.where(last, line, value),)
        for i, value in enumerate(halves):
            made[which][pl.ds(start + i * H, H), :] = value
        part = pl.ds(start, len(halves) * H)
        copy = pltpu.make_async_copy(
            made[which].at[part], outs[which].at[part], sem.at[len(copies)]
        )
        copy.start()
        copies.append(copy)

    for place in places(pieces, early, count_a):
        _, which, start, rows, _ = place
        count = 2 if rows == H else 1
        give(place, [firsts[which][pl.ds(start + i * H, H), :] for i in range(count)])
    for place, halves in unfolded(pieces, late, count_a, total, owns, got):
        give(place, halves)
    for copy in copies:
        copy.wait()


def unfold_early(pieces, ks, owns, got, count_a, count_g, total):
    args = (*owns, got)
    return pl.pallas_call(
        functools.partial(early_body, pieces, ks, count_a, total),
        in_specs=[pl.BlockSpec(memory_space=pltpu.VMEM)] * len(args),
        out_specs=[pl.BlockSpec(memory_space=pltpu.VMEM)] * 2,
        out_shape=[
            jax.ShapeDtypeStruct((count_a, B), jnp.float32),
            jax.ShapeDtypeStruct((count_g, B), jnp.float32),
        ],
        compiler_params=pltpu.CompilerParams(vmem_limit_bytes=32 * 2**20),
        cost_estimate=pl.CostEstimate(flops=4 * 10**9, bytes_accessed=1, transcendentals=0),
    )(*args)


def finish(pieces, early, late, owns, got, first, count_a, count_g, total):
    args = (*owns, got, *first)
    parts = sum(len(a_blocks) + a_half + len(g_blocks) for a_blocks, a_half, g_blocks, _ in pieces)
    return pl.pallas_call(
        functools.partial(finish_body, pieces, early, late, count_a, total),
        in_specs=[pl.BlockSpec(memory_space=pltpu.VMEM)] * len(args),
        out_specs=[pl.BlockSpec(memory_space=pltpu.HBM)] * 2,
        out_shape=[
            jax.ShapeDtypeStruct((count_a, B), jnp.float32),
            jax.ShapeDtypeStruct((count_g, B), jnp.float32),
        ],
        scratch_shapes=[
            pltpu.VMEM((count_a, B), jnp.float32),
            pltpu.VMEM((count_g, B), jnp.float32),
            pltpu.SemaphoreType.DMA((parts,)),
        ],
        compiler_params=pltpu.CompilerParams(vmem_limit_bytes=32 * 2**20),
    )(*args)


def swap(value, partner):
    dp, tensor = lax.axis_size("dp"), lax.axis_size("tensor")
    pairs = []
    for i in range(dp):
        for j in range(tensor):
            other = partner(i, j)
            pairs.append((i * tensor + j, other[0] * tensor + other[1]))
    return lax.ppermute(value, ("dp", "tensor"), pairs)


def along(stage, kind):
    return lambda i, j: (i ^ (1 << KINDS[kind][j][stage]), j)


def packed(saved_input, saved_pre, grad_act):
    dp = lax.axis_size("dp")
    total = float(saved_input.shape[0] * dp)
    count_a = saved_input.shape[1] // dp
    count_g = saved_pre.shape[1] // dp
    full_a, half_a = split_rows(count_a)
    full_g, _ = split_rows(count_g)
    some = 1 + (full_g - 1) // 2
    pieces = (
        (tuple(range(full_a)), 0, (), 0),
        ((), 0, tuple(range(1, some)), 0),
        ((), half_a, (0,), 1),
        ((), 0, tuple(range(some, full_g)), 1),
    )
    arrays = (saved_input, saved_pre, grad_act)
    keep, send = 0, SLOTS // 2
    early, late = (0, 2), (1, 3)
    keeps, gots, notes = {}, {}, None

    def pack_next(first, ks):
        nonlocal notes, arrays
        items = tuple((k, first) for k in ks)
        parts, notes, held = pack(arrays, pieces, items, count_a, count_g, notes)
        arrays = (*held, *arrays[len(held) :])
        return dict(zip(ks, parts))

    def exchange(parts, stage):
        for k, part in parts.items():
            gots[k] = swap(part, along(stage, pieces[k][3]))

    def halve_pair(ks, stage, **kinds):
        own, parts, others = halve(
            [keeps[k] for k in ks], [gots[k] for k in ks], merged=stage == 2,
            weight=WEIGHTS.get((ks, stage), 1), **kinds
        )
        keeps.update(zip(ks, own))
        if stage == 2:
            gots[ks] = swap(parts[0], lambda i, j: (i ^ (1 << FAR), j))
        else:
            exchange(dict(zip(ks, parts)), stage)
        return others

    exchange(pack_next(send, early[:1]), 0)
    exchange(pack_next(send, early[1:]), 0)
    exchange(pack_next(send, late), 0)
    keeps.update(pack_next(keep, early))
    keeps.update(pack_next(keep, late))

    trace = notes[NOTES, :2, :]
    trace = trace + swap(trace, lambda i, j: (i, j ^ 1))
    across = swap(trace, lambda i, j: (i ^ (1 << X) ^ (1 << NEAR), j))
    halve_pair(early, 1)
    halve_pair(late, 1, terms=(trace,), put=(0, 1))
    halve_pair(early, 2)
    halve_pair(late, 2, terms=(trace, across), came=(0, 1), put=(0, 1))

    def both(ks):
        return [keeps[k] for k in ks], gots[ks]

    first = unfold_early(pieces, early, *both(early), count_a, count_g, total)
    a_factor, g_factor = finish(
        pieces, early, late, *both(late), first, count_a, count_g, total
    )
    return a_factor[None], g_factor[None]


def fits(count_a, count_g):
    (full_a, half_a), full_g = split_rows(count_a), count_g // B
    if count_a % H or count_g % B or full_a < 1 or full_g < 3:
        return False
    return full_a + half_a + full_g <= 2 * (EDGE - 2)


def on_device(saved_input, saved_pre, grad_act):
    dp = lax.axis_size("dp")
    count_a = saved_input.shape[1] // dp
    count_g = saved_pre.shape[1] // dp
    if dp == SLOTS and lax.axis_size("tensor") == 2 and fits(count_a, count_g):
        return packed(saved_input, saved_pre, grad_act)
    return plain(saved_input, saved_pre, grad_act)


def solution(mesh):
    spec = P(("groups", "dp"), "tensor")
    out = P("tensor", ("groups", "dp"), None)
    return jax.shard_map(
        on_device, mesh=mesh, in_specs=(spec, spec, spec), out_specs=(out, out), check_vma=False
    )
```

```python
import functools
import math

import jax
import jax.numpy as jnp
from jax import lax
from jax.experimental import pallas as pl
from jax.experimental.pallas import tpu as pltpu
from jax.sharding import PartitionSpec as P

D = 5120
FFW = 10240
B = 128
H = B // 2


def gelu_slope(value):
    return (
        0.5 * (1.0 + lax.erf(value * 0.7071067811865476))
        + value * jnp.exp(-0.5 * value * value) * 0.3989422804014327
    )


def local_blocks(matrix, block, total):
    tokens, width = matrix.shape
    pieces = matrix.reshape(tokens, width // block, block)
    cov = jnp.einsum("tkb,tkc->kbc", pieces, pieces, preferred_element_type=jnp.float32)
    return cov.reshape(width, block) / total


def owned_unit(owned, block):
    count = owned.shape[0]
    rows = lax.axis_index("dp") * count + jnp.arange(count, dtype=jnp.int32)
    cols = jnp.arange(block, dtype=jnp.int32)
    return (cols[None, :] == (rows % block)[:, None]).astype(jnp.float32)


def plain(saved_input, saved_pre, grad_act):
    total = jnp.float32(saved_input.shape[0] * lax.axis_size("dp"))
    slope = gelu_slope(saved_pre.astype(jnp.float32))
    grad_pre = (grad_act.astype(jnp.float32) * slope).astype(jnp.bfloat16)
    terms_a = local_blocks(saved_input, B, total)
    terms_g = local_blocks(grad_pre, B, total)
    owned_a = lax.psum_scatter(terms_a, "dp", scatter_dimension=0, tiled=True)
    owned_g = lax.psum_scatter(terms_g, "dp", scatter_dimension=0, tiled=True)
    unit_a = owned_unit(owned_a, B)
    unit_g = owned_unit(owned_g, B)
    trace_a, trace_g = lax.psum(
        (jnp.sum(owned_a * unit_a), jnp.sum(owned_g * unit_g)), ("dp", "tensor")
    )
    ratio = jnp.sqrt(trace_a / D / (trace_g / FFW))
    damp = jnp.sqrt(jnp.float32(0.1))
    return (
        (owned_a + ratio * damp * unit_a)[None],
        (owned_g + damp / ratio * unit_g)[None],
    )


EDGE = 8
SLOTS = 8
X, NEAR, FAR = 0, 1, 2
KINDS = (((NEAR, X, FAR), (NEAR, X, FAR)), ((X, NEAR, FAR), (X, NEAR, FAR)))
NOTES = len(KINDS) * SLOTS

WEIGHTS = {((0, 2), 2): 2 * 10**9}


def split_rows(count):
    return count // B, (count % B) // H


def has_edge(pieces, k):
    return all(later[3] != pieces[k][3] for later in pieces[k + 1 :])


def piece_rows(pieces, k):
    a_blocks, a_half, g_blocks, _ = pieces[k]
    rows = (len(a_blocks) + len(g_blocks)) * H + a_half * (H * 3 // 4)
    return rows + (EDGE if has_edge(pieces, k) else 0)


def corner_indices(pieces, k):
    parts = [len(a) + a_half + len(g) if kind == pieces[k][3] else 0 for a, a_half, g, kind in pieces]
    return iter(range(sum(parts[:k]), sum(parts[: k + 1])))


def iotas(rows):
    shape = (rows, B)
    return lax.broadcasted_iota(jnp.int32, shape, 0), lax.broadcasted_iota(jnp.int32, shape, 1)


def slot_owner(slot, orders):
    core = lax.axis_index("tensor")
    mask = 0
    for stage, (one, other) in enumerate(zip(*orders)):
        mask = mask | (((slot >> (2 - stage)) & 1) << (one + core * (other - one)))
    return lax.axis_index("dp") ^ mask


def lanes(start, size):
    return pl.ds(start if isinstance(start, int) else pl.multiple_of(start, B), size)


LOADS = 4
FIRST = 4 * 10**9


def pack_body(pieces, items, count_a, count_g, fresh, *refs):
    n = len(items)
    if fresh:
        (a_hbm, *outs), (notes, a_held, sems) = refs[: n + 1], refs[n + 1 :]
        rows = a_hbm.shape[0] // LOADS
        parts = [slice(part * rows, (part + 1) * rows) for part in range(LOADS)]
        copies = [
            pltpu.make_async_copy(a_hbm.at[part], a_held.at[part], sems.at[i])
            for i, part in enumerate(parts)
        ]
        for copy in copies:
            copy.start()
        held = (a_held,)
    else:
        copies = []
        notes_in, held, outs, notes = refs[0], refs[1:4], refs[4 : 4 + n], refs[4 + n]
    full, half = split_rows(count_a)
    slots = SLOTS // 2
    split = [(i, k, first, slot) for i, (k, first) in enumerate(items) for slot in range(slots)]

    def read(i, start):
        return held[i][:, pl.ds(pl.multiple_of(start, B), B)]

    row, col = iotas(H)
    low = col < row
    diag_low, diag_high = col == row, col == row + H
    quarter = H // 2
    row_q, col_q = row[:quarter], col[:quarter]
    note_row, _ = iotas(EDGE)
    zero = jnp.zeros((H, B), jnp.float32)
    traces = [zero, zero]
    tiles = {}

    def cov(part):
        return lax.dot_general(
            part, part, (((0,), (0,)), ((), ())), preferred_element_type=jnp.float32
        )

    def note(slot, index, corner, natural):
        line = jnp.sum(corner, axis=0, keepdims=True)
        if index % 2 != natural:
            line = pltpu.roll(line, H, 1)
        tiles[slot] = tiles[slot] + jnp.where(note_row == index // 2, line, 0.0)

    def fold(block, slot, index, which):
        top, bottom = block[:H], block[H:]
        corner = jnp.where(diag_high, bottom, zero)
        note(slot, index, corner, 0)
        traces[which] = traces[which] + corner + jnp.where(diag_low, top, zero)
        return jnp.where(low, pltpu.roll(bottom, H, 1), top)

    def fold_half(block, odd, slot, index):
        part = jnp.where(odd == 1, pltpu.roll(block[H:], H, 1), block[:H])
        traces[0] = traces[0] + jnp.where(diag_low, part, zero)
        upper, lower = part[:quarter], part[quarter:]
        corner = jnp.where(col_q == row_q + quarter, lower, 0.0)
        note(slot, index, corner, 1)
        square = jnp.where(col_q < row_q, pltpu.roll(lower, B - quarter, 1), upper)
        rest = lower.reshape(2, quarter // 2, B)
        rest = jnp.where(col[: quarter // 2] < H, pltpu.roll(rest[1], H, 1), rest[0])
        return square, rest

    def a_parts(out, k, first, slot, index):
        a_blocks, a_half, _, kind = pieces[k]
        owner = slot_owner(first + slot, KINDS[kind])
        here, odd = kind * SLOTS + first + slot, owner & half
        base = (owner >> half) * (full * (1 + half) + half) * B
        at = 0
        for b in a_blocks:
            block = cov(read(0, base + (odd * (full + 1) + b) * B))
            out[slot, at : at + H, :] = fold(block, here, next(index), 0)
            at = at + H
        if a_half:
            block = cov(read(0, base + full * B))
            square, rest = fold_half(block, odd, here, next(index))
            out[slot, at : at + quarter, :] = square
            out[slot, at + quarter : at + quarter * 3 // 2, :] = rest
            at = at + quarter * 3 // 2
        return at

    def g_parts(out, k, first, slot, index, at):
        _, _, g_blocks, kind = pieces[k]
        here = kind * SLOTS + first + slot
        owner = slot_owner(first + slot, KINDS[kind])
        for b in g_blocks:
            start = owner * count_g + b * B
            value, grad = read(1, start).astype(jnp.float32), read(2, start).astype(jnp.float32)
            block = cov((grad * gelu_slope(value)).astype(jnp.bfloat16))
            out[slot, at : at + H, :] = fold(block, here, next(index), 1)
            at = at + H
        return at

    for copy in copies:
        copy.wait()
    for i, k, first, slot in split:
        here = pieces[k][3] * SLOTS + first + slot
        if here not in tiles:
            tiles[here] = jnp.zeros((EDGE, B), jnp.float32) if fresh else notes_in[here]
        index = corner_indices(pieces, k)
        at = a_parts(outs[i], k, first, slot, index)
        at = g_parts(outs[i], k, first, slot, index, at)
        if has_edge(pieces, k):
            outs[i][slot, at:, :] = tiles[here]

    for slot in range(NOTES):
        if slot in tiles:
            notes[slot] = tiles[slot]
        else:
            notes[slot] = jnp.zeros((EDGE, B), jnp.float32) if fresh else notes_in[slot]
    lines = [jnp.sum(trace, axis=0, keepdims=True) for trace in traces]
    tile = jnp.where(note_row == 0, lines[0], jnp.where(note_row == 1, lines[1], 0.0))
    notes[NOTES] = tile if fresh else notes_in[NOTES] + tile


def pack(arrays, pieces, items, count_a, count_g, notes):
    slots = SLOTS // 2
    fresh = notes is None
    out_shape = [
        jax.ShapeDtypeStruct((slots, piece_rows(pieces, k), B), jnp.float32) for k, _ in items
    ]
    out_shape.append(jax.ShapeDtypeStruct((NOTES + 1, EDGE, B), jnp.float32))
    if fresh:
        args = [pltpu.with_memory_space_constraint(arrays[0], pltpu.HBM)]
        out_shape.append(jax.ShapeDtypeStruct(arrays[0].shape, arrays[0].dtype))
    else:
        args = [notes, *arrays]
    space = pltpu.HBM if fresh else pltpu.VMEM
    outs = pl.pallas_call(
        functools.partial(pack_body, pieces, items, count_a, count_g, fresh),
        in_specs=[pl.BlockSpec(memory_space=space)] * len(args),
        out_specs=[pl.BlockSpec(memory_space=pltpu.VMEM)] * len(out_shape),
        out_shape=out_shape,
        scratch_shapes=[pltpu.SemaphoreType.DMA((LOADS,))] * fresh,
        compiler_params=pltpu.CompilerParams(vmem_limit_bytes=32 * 2**20),
        cost_estimate=pl.CostEstimate(
            flops=FIRST if fresh else 1, bytes_accessed=1, transcendentals=0
        ),
    )(*args)
    n = len(items)
    return outs[:n], outs[n], outs[n + 1 :]


def halve_body(n, terms, came, put, merged, *refs):
    keeps, gots, refs = refs[:n], refs[n : 2 * n], refs[2 * n :]
    terms, kept, refs = refs[:terms], refs[terms : terms + n], refs[terms + n :]
    sent, sums = (refs[:1], refs[1:]) if merged else (refs[:n], refs[n:])
    if merged:
        ends = [sum(ref.shape[1] for ref in kept[: k + 1]) for k in range(n)]
        sent = [
            sent[0].at[:, end - ref.shape[1] : end, :] for end, ref in zip(ends, kept)
        ]
    for k in range(n):
        half = kept[k].shape[0]
        kept[k][...] = keeps[k][:half] + gots[k][:half]
        sent[k][...] = keeps[k][half:] + gots[k][half:]
    if terms:
        value = sum((term[...] for term in terms[1:]), terms[0][...])
        for k in came:
            value = value + gots[k][0, -2:, :]
        for out in sums:
            out[...] = value
        for k in put:
            rows = kept[k].shape[1]
            kept[k][0, rows - 2 :, :] = value
            sent[k][0, rows - 2 :, :] = value


def halve(keeps, gots, terms=(), came=(), put=(), merged=False, weight=1):
    n = len(keeps)
    emit = bool(terms) and not put
    args = [*keeps, *gots, *terms]
    kept = [(keep.shape[0] // 2, *keep.shape[1:]) for keep in keeps]
    sent = [(kept[0][0], sum(shape[1] for shape in kept), B)] if merged else kept
    shapes = [*kept, *sent, *([(2, B)] * emit)]
    outs = pl.pallas_call(
        functools.partial(halve_body, n, len(terms), came, put, merged),
        in_specs=[pl.BlockSpec(memory_space=pltpu.VMEM)] * len(args),
        out_specs=[pl.BlockSpec(memory_space=pltpu.VMEM)] * len(shapes),
        out_shape=[jax.ShapeDtypeStruct(shape, jnp.float32) for shape in shapes],
        compiler_params=pltpu.CompilerParams(vmem_limit_bytes=32 * 2**20),
        cost_estimate=pl.CostEstimate(flops=weight, bytes_accessed=1, transcendentals=0),
    )(*args)
    return outs[:n], outs[n : n + len(sent)], outs[n + len(sent) :]


def mean_of(value, total):
    return value * (1.0 / total) if math.frexp(total)[0] == 0.5 else value / total


def turn(folded):
    return jnp.concatenate([folded] * (B // folded.shape[0]), axis=0).T


def unfold(folded):
    row, col = iotas(H)
    turned = turn(folded)
    last = pltpu.roll(jnp.where(col < row, folded, turned[:H]), H, 1)
    return jnp.where(col < row, turned[:H], folded), jnp.where(col < H, turned[H:], last)


def unfold_half(square, rest, odd):
    quarter = H // 2
    row, col = iotas(quarter)
    turned = turn(square)
    upper = jnp.where(col < row, turned[:quarter], square)
    last = pltpu.roll(jnp.where(col < row, square, turned[:quarter]), quarter, 1)
    lower = jnp.where(col < quarter, turned[quarter:H], last)
    rest = jnp.concatenate([rest, pltpu.roll(rest, H, 1)], axis=0)
    part = jnp.concatenate([upper, jnp.where(col < H, lower, rest)], axis=0)
    return (jnp.where(odd == 1, pltpu.roll(part, H, 1), part),)


def places(pieces, ks, count_a):
    full, half = split_rows(count_a)
    odd = lax.axis_index("dp") & half
    for k in ks:
        a_blocks, a_half, g_blocks, kind = pieces[k]
        index = corner_indices(pieces, k)
        for b in a_blocks:
            start = pl.multiple_of(b * B + odd * H, H) if half else b * B
            yield k, 0, start, H, next(index)
        if a_half:
            yield k, 0, pl.multiple_of((1 - odd) * full * B, H), H * 3 // 4, next(index)
        for b in g_blocks:
            yield k, 1, b * B, H, next(index)


def row_begins(pieces, ks):
    rows = [piece_rows(pieces, k) for k in ks]
    return {k: sum(rows[:i]) for i, k in enumerate(ks)}


def unfolded(pieces, ks, count_a, total, owns, got):
    odd = lax.axis_index("dp") & 1
    at = dict.fromkeys(ks, 0)
    begins = row_begins(pieces, ks)

    def take(k, rows):
        begin = at[k]
        at[k] = begin + rows
        mine = owns[ks.index(k)][0, begin : begin + rows, :]
        begin = begin + begins[k]
        return mean_of(mine + got[0, begin : begin + rows, :], total)

    for place in places(pieces, ks, count_a):
        k, _, _, rows, _ = place
        if rows == H:
            yield place, unfold(take(k, H))
        else:
            yield place, unfold_half(take(k, H // 2), take(k, H // 4), odd)


def early_body(pieces, ks, count_a, total, *refs):
    n = len(ks)
    owns, got, outs = refs[:n], refs[n], refs[n + 1 :]
    for (_, which, start, _, _), halves in unfolded(pieces, ks, count_a, total, owns, got):
        for i, value in enumerate(halves):
            outs[which][pl.ds(start + i * H, H), :] = value


def finish_body(pieces, early, late, count_a, total, *refs):
    n = len(late)
    owns, got, firsts, outs = refs[:n], refs[n], refs[n + 1 : n + 3], refs[n + 3 : n + 5]
    made, sem = refs[n + 5 : n + 7], refs[n + 7]
    _, half = split_rows(count_a)
    odd = lax.axis_index("dp") & half
    row, col = iotas(H)

    edges = {}
    for k, own in zip(late, owns):
        end = row_begins(pieces, late)[k] + piece_rows(pieces, k)
        edge = mean_of(own[0, -EDGE:, :] + got[0, end - EDGE : end, :], total)
        edges[pieces[k][3]] = (edge, pltpu.roll(edge, H, 1))
    sums = jnp.sum(edge[-2:], axis=1, keepdims=True)
    ratio = jnp.sqrt(sums[0:1] / D / (sums[1:2] / FFW))
    damp = jnp.sqrt(jnp.full((1, 1), 0.1, jnp.float32))
    shifts = (ratio * damp, damp / ratio)

    def corner(kind, index, natural):
        line = index // 2
        return edges[kind][0 if index % 2 == natural else 1][line : line + 1]

    copies = []

    def give(place, halves):
        k, which, start, rows, index = place
        shift, kind = shifts[which], pieces[k][3]
        if rows == H:
            top, bottom = halves
            top = top + jnp.where(col == row, shift, 0.0)
            bottom = jnp.where(col == row + H, corner(kind, index, 0) + shift, bottom)
            halves = (top, bottom)
        else:
            line = corner(kind, index, 1)
            line = jnp.where(odd == 1, pltpu.roll(line, H, 1), line) + shift
            diagonal = col == row + odd * H
            value = halves[0] + jnp.where(diagonal, shift, 0.0)
            last = jnp.logical_and(diagonal, row >= H // 2)
            halves = (jnp.where(last, line, value),)
        for i, value in enumerate(halves):
            made[which][pl.ds(start + i * H, H), :] = value
        part = pl.ds(start, len(halves) * H)
        copy = pltpu.make_async_copy(
            made[which].at[part], outs[which].at[part], sem.at[len(copies)]
        )
        copy.start()
        copies.append(copy)

    for place in places(pieces, early, count_a):
        _, which, start, rows, _ = place
        count = 2 if rows == H else 1
        give(place, [firsts[which][pl.ds(start + i * H, H), :] for i in range(count)])
    for place, halves in unfolded(pieces, late, count_a, total, owns, got):
        give(place, halves)
    for copy in copies:
        copy.wait()


def unfold_early(pieces, ks, owns, got, count_a, count_g, total):
    args = (*owns, got)
    return pl.pallas_call(
        functools.partial(early_body, pieces, ks, count_a, total),
        in_specs=[pl.BlockSpec(memory_space=pltpu.VMEM)] * len(args),
        out_specs=[pl.BlockSpec(memory_space=pltpu.VMEM)] * 2,
        out_shape=[
            jax.ShapeDtypeStruct((count_a, B), jnp.float32),
            jax.ShapeDtypeStruct((count_g, B), jnp.float32),
        ],
        compiler_params=pltpu.CompilerParams(vmem_limit_bytes=32 * 2**20),
        cost_estimate=pl.CostEstimate(flops=4 * 10**9, bytes_accessed=1, transcendentals=0),
    )(*args)


def finish(pieces, early, late, owns, got, first, count_a, count_g, total):
    args = (*owns, got, *first)
    parts = sum(len(a_blocks) + a_half + len(g_blocks) for a_blocks, a_half, g_blocks, _ in pieces)
    return pl.pallas_call(
        functools.partial(finish_body, pieces, early, late, count_a, total),
        in_specs=[pl.BlockSpec(memory_space=pltpu.VMEM)] * len(args),
        out_specs=[pl.BlockSpec(memory_space=pltpu.HBM)] * 2,
        out_shape=[
            jax.ShapeDtypeStruct((count_a, B), jnp.float32),
            jax.ShapeDtypeStruct((count_g, B), jnp.float32),
        ],
        scratch_shapes=[
            pltpu.VMEM((count_a, B), jnp.float32),
            pltpu.VMEM((count_g, B), jnp.float32),
            pltpu.SemaphoreType.DMA((parts,)),
        ],
        compiler_params=pltpu.CompilerParams(vmem_limit_bytes=32 * 2**20),
    )(*args)


def swap(value, partner):
    dp, tensor = lax.axis_size("dp"), lax.axis_size("tensor")
    pairs = []
    for i in range(dp):
        for j in range(tensor):
            other = partner(i, j)
            pairs.append((i * tensor + j, other[0] * tensor + other[1]))
    return lax.ppermute(value, ("dp", "tensor"), pairs)


def along(stage, kind):
    return lambda i, j: (i ^ (1 << KINDS[kind][j][stage]), j)


def packed(saved_input, saved_pre, grad_act):
    dp = lax.axis_size("dp")
    total = float(saved_input.shape[0] * dp)
    count_a = saved_input.shape[1] // dp
    count_g = saved_pre.shape[1] // dp
    full_a, half_a = split_rows(count_a)
    full_g, _ = split_rows(count_g)
    some = 1 + (full_g - 1) // 2
    pieces = (
        (tuple(range(full_a)), 0, (), 0),
        ((), 0, tuple(range(1, some)), 0),
        ((), half_a, (0,), 1),
        ((), 0, tuple(range(some, full_g)), 1),
    )
    arrays = (saved_input, saved_pre, grad_act)
    keep, send = 0, SLOTS // 2
    early, late = (0, 2), (1, 3)
    keeps, gots, notes = {}, {}, None

    def pack_next(first, ks):
        nonlocal notes, arrays
        items = tuple((k, first) for k in ks)
        parts, notes, held = pack(arrays, pieces, items, count_a, count_g, notes)
        arrays = (*held, *arrays[len(held) :])
        return dict(zip(ks, parts))

    def exchange(parts, stage):
        for k, part in parts.items():
            gots[k] = swap(part, along(stage, pieces[k][3]))

    def halve_pair(ks, stage, **kinds):
        own, parts, others = halve(
            [keeps[k] for k in ks], [gots[k] for k in ks], merged=stage == 2,
            weight=WEIGHTS.get((ks, stage), 1), **kinds
        )
        keeps.update(zip(ks, own))
        if stage == 2:
            gots[ks] = swap(parts[0], lambda i, j: (i ^ (1 << FAR), j))
        else:
            exchange(dict(zip(ks, parts)), stage)
        return others

    exchange(pack_next(send, early[:1]), 0)
    exchange(pack_next(send, early[1:]), 0)
    exchange(pack_next(send, late), 0)
    keeps.update(pack_next(keep, early))
    keeps.update(pack_next(keep, late))

    trace = notes[NOTES, :2, :]
    trace = trace + swap(trace, lambda i, j: (i, j ^ 1))
    across = swap(trace, lambda i, j: (i ^ (1 << X) ^ (1 << NEAR), j))
    halve_pair(early, 1)
    halve_pair(late, 1, terms=(trace,), put=(0, 1))
    (trace,) = halve_pair(early, 2, terms=(trace, across))
    halve_pair(late, 2, terms=(trace,), came=(0, 1), put=(0, 1))

    def both(ks):
        return [keeps[k] for k in ks], gots[ks]

    first = unfold_early(pieces, early, *both(early), count_a, count_g, total)
    a_factor, g_factor = finish(
        pieces, early, late, *both(late), first, count_a, count_g, total
    )
    return a_factor[None], g_factor[None]


def fits(count_a, count_g):
    (full_a, half_a), full_g = split_rows(count_a), count_g // B
    if count_a % H or count_g % B or full_a < 1 or full_g < 3:
        return False
    return full_a + half_a + full_g <= 2 * (EDGE - 2)


def on_device(saved_input, saved_pre, grad_act):
    dp = lax.axis_size("dp")
    count_a = saved_input.shape[1] // dp
    count_g = saved_pre.shape[1] // dp
    if dp == SLOTS and lax.axis_size("tensor") == 2 and fits(count_a, count_g):
        return packed(saved_input, saved_pre, grad_act)
    return plain(saved_input, saved_pre, grad_act)


def solution(mesh):
    spec = P(("groups", "dp"), "tensor")
    out = P("tensor", ("groups", "dp"), None)
    return jax.shard_map(
        on_device, mesh=mesh, in_specs=(spec, spec, spec), out_specs=(out, out), check_vma=False
    )
```

```python
import functools
import math

import jax
import jax.numpy as jnp
from jax import lax
from jax.experimental import pallas as pl
from jax.experimental.pallas import tpu as pltpu
from jax.sharding import PartitionSpec as P

D = 5120
FFW = 10240
B = 128
H = B // 2


def gelu_slope(value):
    return (
        0.5 * (1.0 + lax.erf(value * 0.7071067811865476))
        + value * jnp.exp(-0.5 * value * value) * 0.3989422804014327
    )


def local_blocks(matrix, block, total):
    tokens, width = matrix.shape
    pieces = matrix.reshape(tokens, width // block, block)
    cov = jnp.einsum("tkb,tkc->kbc", pieces, pieces, preferred_element_type=jnp.float32)
    return cov.reshape(width, block) / total


def owned_unit(owned, block):
    count = owned.shape[0]
    rows = lax.axis_index("dp") * count + jnp.arange(count, dtype=jnp.int32)
    cols = jnp.arange(block, dtype=jnp.int32)
    return (cols[None, :] == (rows % block)[:, None]).astype(jnp.float32)


def plain(saved_input, saved_pre, grad_act):
    total = jnp.float32(saved_input.shape[0] * lax.axis_size("dp"))
    slope = gelu_slope(saved_pre.astype(jnp.float32))
    grad_pre = (grad_act.astype(jnp.float32) * slope).astype(jnp.bfloat16)
    terms_a = local_blocks(saved_input, B, total)
    terms_g = local_blocks(grad_pre, B, total)
    owned_a = lax.psum_scatter(terms_a, "dp", scatter_dimension=0, tiled=True)
    owned_g = lax.psum_scatter(terms_g, "dp", scatter_dimension=0, tiled=True)
    unit_a = owned_unit(owned_a, B)
    unit_g = owned_unit(owned_g, B)
    trace_a, trace_g = lax.psum(
        (jnp.sum(owned_a * unit_a), jnp.sum(owned_g * unit_g)), ("dp", "tensor")
    )
    ratio = jnp.sqrt(trace_a / D / (trace_g / FFW))
    damp = jnp.sqrt(jnp.float32(0.1))
    return (
        (owned_a + ratio * damp * unit_a)[None],
        (owned_g + damp / ratio * unit_g)[None],
    )


EDGE = 8
SLOTS = 8
X, NEAR, FAR = 0, 1, 2
KINDS = (((X, NEAR, FAR), (X, NEAR, FAR)), ((NEAR, X, FAR), (NEAR, X, FAR)))
NOTES = len(KINDS) * SLOTS

WEIGHTS = {((0, 2), 2): 2 * 10**9}


def split_rows(count):
    return count // B, (count % B) // H


def has_edge(pieces, k):
    return all(later[3] != pieces[k][3] for later in pieces[k + 1 :])


def piece_rows(pieces, k):
    a_blocks, a_half, g_blocks, _ = pieces[k]
    rows = (len(a_blocks) + len(g_blocks)) * H + a_half * (H * 3 // 4)
    return rows + (EDGE if has_edge(pieces, k) else 0)


def corner_indices(pieces, k):
    parts = [len(a) + a_half + len(g) if kind == pieces[k][3] else 0 for a, a_half, g, kind in pieces]
    return iter(range(sum(parts[:k]), sum(parts[: k + 1])))


def iotas(rows):
    shape = (rows, B)
    return lax.broadcasted_iota(jnp.int32, shape, 0), lax.broadcasted_iota(jnp.int32, shape, 1)


def slot_owner(slot, orders):
    core = lax.axis_index("tensor")
    mask = 0
    for stage, (one, other) in enumerate(zip(*orders)):
        mask = mask | (((slot >> (2 - stage)) & 1) << (one + core * (other - one)))
    return lax.axis_index("dp") ^ mask


def lanes(start, size):
    return pl.ds(start if isinstance(start, int) else pl.multiple_of(start, B), size)


FIRST = 4 * 10**9


def pack_body(pieces, items, count_a, count_g, fresh, *refs):
    n = len(items)
    if fresh:
        held, refs = refs[:1], refs[1:]
    else:
        notes_in, held, refs = refs[0], refs[1:4], refs[4:]
    outs, notes = refs[:n], refs[n]
    full, half = split_rows(count_a)
    slots = SLOTS // 2
    split = [(i, k, first, slot) for i, (k, first) in enumerate(items) for slot in range(slots)]

    def read(i, start):
        return held[i][:, pl.ds(pl.multiple_of(start, B), B)]

    row, col = iotas(H)
    low = col < row
    diag_low, diag_high = col == row, col == row + H
    quarter = H // 2
    row_q, col_q = row[:quarter], col[:quarter]
    note_row, _ = iotas(EDGE)
    zero = jnp.zeros((H, B), jnp.float32)
    traces = [zero, zero]
    tiles = {}

    def cov(part):
        return lax.dot_general(
            part, part, (((0,), (0,)), ((), ())), preferred_element_type=jnp.float32
        )

    def note(slot, index, corner, natural):
        line = jnp.sum(corner, axis=0, keepdims=True)
        if index % 2 != natural:
            line = pltpu.roll(line, H, 1)
        tiles[slot] = tiles[slot] + jnp.where(note_row == index // 2, line, 0.0)

    def fold(block, slot, index, which):
        top, bottom = block[:H], block[H:]
        corner = jnp.where(diag_high, bottom, zero)
        note(slot, index, corner, 0)
        traces[which] = traces[which] + corner + jnp.where(diag_low, top, zero)
        return jnp.where(low, pltpu.roll(bottom, H, 1), top)

    def fold_half(block, odd, slot, index):
        part = jnp.where(odd == 1, pltpu.roll(block[H:], H, 1), block[:H])
        traces[0] = traces[0] + jnp.where(diag_low, part, zero)
        upper, lower = part[:quarter], part[quarter:]
        corner = jnp.where(col_q == row_q + quarter, lower, 0.0)
        note(slot, index, corner, 1)
        square = jnp.where(col_q < row_q, pltpu.roll(lower, B - quarter, 1), upper)
        rest = lower.reshape(2, quarter // 2, B)
        rest = jnp.where(col[: quarter // 2] < H, pltpu.roll(rest[1], H, 1), rest[0])
        return square, rest

    def a_parts(out, k, first, slot, index):
        a_blocks, a_half, _, kind = pieces[k]
        owner = slot_owner(first + slot, KINDS[kind])
        here, odd = kind * SLOTS + first + slot, owner & half
        base = (owner >> half) * (full * (1 + half) + half) * B
        at = 0
        for b in a_blocks:
            block = cov(read(0, base + (odd * (full + 1) + b) * B))
            out[slot, at : at + H, :] = fold(block, here, next(index), 0)
            at = at + H
        if a_half:
            block = cov(read(0, base + full * B))
            square, rest = fold_half(block, odd, here, next(index))
            out[slot, at : at + quarter, :] = square
            out[slot, at + quarter : at + quarter * 3 // 2, :] = rest
            at = at + quarter * 3 // 2
        return at

    def g_parts(out, k, first, slot, index, at):
        _, _, g_blocks, kind = pieces[k]
        here = kind * SLOTS + first + slot
        owner = slot_owner(first + slot, KINDS[kind])
        for b in g_blocks:
            start = owner * count_g + b * B
            value, grad = read(1, start).astype(jnp.float32), read(2, start).astype(jnp.float32)
            block = cov((grad * gelu_slope(value)).astype(jnp.bfloat16))
            out[slot, at : at + H, :] = fold(block, here, next(index), 1)
            at = at + H
        return at

    for i, k, first, slot in split:
        here = pieces[k][3] * SLOTS + first + slot
        if here not in tiles:
            tiles[here] = jnp.zeros((EDGE, B), jnp.float32) if fresh else notes_in[here]
        index = corner_indices(pieces, k)
        at = a_parts(outs[i], k, first, slot, index)
        at = g_parts(outs[i], k, first, slot, index, at)
        if has_edge(pieces, k):
            outs[i][slot, at:, :] = tiles[here]

    for slot in range(NOTES):
        if slot in tiles:
            notes[slot] = tiles[slot]
        else:
            notes[slot] = jnp.zeros((EDGE, B), jnp.float32) if fresh else notes_in[slot]
    lines = [jnp.sum(trace, axis=0, keepdims=True) for trace in traces]
    tile = jnp.where(note_row == 0, lines[0], jnp.where(note_row == 1, lines[1], 0.0))
    notes[NOTES] = tile if fresh else notes_in[NOTES] + tile


def pack(arrays, pieces, items, count_a, count_g, notes):
    slots = SLOTS // 2
    fresh = notes is None
    out_shape = [
        jax.ShapeDtypeStruct((slots, piece_rows(pieces, k), B), jnp.float32) for k, _ in items
    ]
    out_shape.append(jax.ShapeDtypeStruct((NOTES + 1, EDGE, B), jnp.float32))
    args = arrays[:1] if fresh else [notes, *arrays]
    outs = pl.pallas_call(
        functools.partial(pack_body, pieces, items, count_a, count_g, fresh),
        in_specs=[pl.BlockSpec(memory_space=pltpu.VMEM)] * len(args),
        out_specs=[pl.BlockSpec(memory_space=pltpu.VMEM)] * len(out_shape),
        out_shape=out_shape,
        compiler_params=pltpu.CompilerParams(vmem_limit_bytes=32 * 2**20),
        cost_estimate=pl.CostEstimate(
            flops=FIRST if fresh else 1, bytes_accessed=1, transcendentals=0
        ),
    )(*args)
    n = len(items)
    return outs[:n], outs[n]


def halve_body(n, terms, came, put, merged, *refs):
    keeps, gots, refs = refs[:n], refs[n : 2 * n], refs[2 * n :]
    terms, kept, refs = refs[:terms], refs[terms : terms + n], refs[terms + n :]
    sent, sums = (refs[:1], refs[1:]) if merged else (refs[:n], refs[n:])
    if merged:
        ends = [sum(ref.shape[1] for ref in kept[: k + 1]) for k in range(n)]
        sent = [
            sent[0].at[:, end - ref.shape[1] : end, :] for end, ref in zip(ends, kept)
        ]
    for k in range(n):
        half = kept[k].shape[0]
        kept[k][...] = keeps[k][:half] + gots[k][:half]
        sent[k][...] = keeps[k][half:] + gots[k][half:]
    if terms:
        value = sum((term[...] for term in terms[1:]), terms[0][...])
        for k in came:
            value = value + gots[k][0, -2:, :]
        for out in sums:
            out[...] = value
        for k in put:
            rows = kept[k].shape[1]
            kept[k][0, rows - 2 :, :] = value
            sent[k][0, rows - 2 :, :] = value


def halve(keeps, gots, terms=(), came=(), put=(), merged=False, weight=1):
    n = len(keeps)
    emit = bool(terms) and not put
    args = [*keeps, *gots, *terms]
    kept = [(keep.shape[0] // 2, *keep.shape[1:]) for keep in keeps]
    sent = [(kept[0][0], sum(shape[1] for shape in kept), B)] if merged else kept
    shapes = [*kept, *sent, *([(2, B)] * emit)]
    outs = pl.pallas_call(
        functools.partial(halve_body, n, len(terms), came, put, merged),
        in_specs=[pl.BlockSpec(memory_space=pltpu.VMEM)] * len(args),
        out_specs=[pl.BlockSpec(memory_space=pltpu.VMEM)] * len(shapes),
        out_shape=[jax.ShapeDtypeStruct(shape, jnp.float32) for shape in shapes],
        compiler_params=pltpu.CompilerParams(vmem_limit_bytes=32 * 2**20),
        cost_estimate=pl.CostEstimate(flops=weight, bytes_accessed=1, transcendentals=0),
    )(*args)
    return outs[:n], outs[n : n + len(sent)], outs[n + len(sent) :]


def mean_of(value, total):
    return value * (1.0 / total) if math.frexp(total)[0] == 0.5 else value / total


def turn(folded):
    return jnp.concatenate([folded] * (B // folded.shape[0]), axis=0).T


def unfold(folded):
    row, col = iotas(H)
    turned = turn(folded)
    last = pltpu.roll(jnp.where(col < row, folded, turned[:H]), H, 1)
    return jnp.where(col < row, turned[:H], folded), jnp.where(col < H, turned[H:], last)


def unfold_half(square, rest, odd):
    quarter = H // 2
    row, col = iotas(quarter)
    turned = turn(square)
    upper = jnp.where(col < row, turned[:quarter], square)
    last = pltpu.roll(jnp.where(col < row, square, turned[:quarter]), quarter, 1)
    lower = jnp.where(col < quarter, turned[quarter:H], last)
    rest = jnp.concatenate([rest, pltpu.roll(rest, H, 1)], axis=0)
    part = jnp.concatenate([upper, jnp.where(col < H, lower, rest)], axis=0)
    return (jnp.where(odd == 1, pltpu.roll(part, H, 1), part),)


def places(pieces, ks, count_a):
    full, half = split_rows(count_a)
    odd = lax.axis_index("dp") & half
    for k in ks:
        a_blocks, a_half, g_blocks, kind = pieces[k]
        index = corner_indices(pieces, k)
        for b in a_blocks:
            start = pl.multiple_of(b * B + odd * H, H) if half else b * B
            yield k, 0, start, H, next(index)
        if a_half:
            yield k, 0, pl.multiple_of((1 - odd) * full * B, H), H * 3 // 4, next(index)
        for b in g_blocks:
            yield k, 1, b * B, H, next(index)


def row_begins(pieces, ks):
    rows = [piece_rows(pieces, k) for k in ks]
    return {k: sum(rows[:i]) for i, k in enumerate(ks)}


def unfolded(pieces, ks, count_a, total, owns, got):
    odd = lax.axis_index("dp") & 1
    at = dict.fromkeys(ks, 0)
    begins = row_begins(pieces, ks)

    def take(k, rows):
        begin = at[k]
        at[k] = begin + rows
        mine = owns[ks.index(k)][0, begin : begin + rows, :]
        begin = begin + begins[k]
        return mean_of(mine + got[0, begin : begin + rows, :], total)

    for place in places(pieces, ks, count_a):
        k, _, _, rows, _ = place
        if rows == H:
            yield place, unfold(take(k, H))
        else:
            yield place, unfold_half(take(k, H // 2), take(k, H // 4), odd)


def early_body(pieces, ks, count_a, total, *refs):
    n = len(ks)
    owns, got, outs = refs[:n], refs[n], refs[n + 1 :]
    for (_, which, start, _, _), halves in unfolded(pieces, ks, count_a, total, owns, got):
        for i, value in enumerate(halves):
            outs[which][pl.ds(start + i * H, H), :] = value


def finish_body(pieces, early, late, count_a, total, *refs):
    n = len(late)
    owns, got, firsts, outs = refs[:n], refs[n], refs[n + 1 : n + 3], refs[n + 3 : n + 5]
    made, sem = refs[n + 5 : n + 7], refs[n + 7]
    _, half = split_rows(count_a)
    odd = lax.axis_index("dp") & half
    row, col = iotas(H)

    edges = {}
    for k, own in zip(late, owns):
        end = row_begins(pieces, late)[k] + piece_rows(pieces, k)
        edge = mean_of(own[0, -EDGE:, :] + got[0, end - EDGE : end, :], total)
        edges[pieces[k][3]] = (edge, pltpu.roll(edge, H, 1))
    sums = jnp.sum(edge[-2:], axis=1, keepdims=True)
    ratio = jnp.sqrt(sums[0:1] / D / (sums[1:2] / FFW))
    damp = jnp.sqrt(jnp.full((1, 1), 0.1, jnp.float32))
    shifts = (ratio * damp, damp / ratio)

    def corner(kind, index, natural):
        line = index // 2
        return edges[kind][0 if index % 2 == natural else 1][line : line + 1]

    copies = []

    def give(place, halves):
        k, which, start, rows, index = place
        shift, kind = shifts[which], pieces[k][3]
        if rows == H:
            top, bottom = halves
            top = top + jnp.where(col == row, shift, 0.0)
            bottom = jnp.where(col == row + H, corner(kind, index, 0) + shift, bottom)
            halves = (top, bottom)
        else:
            line = corner(kind, index, 1)
            line = jnp.where(odd == 1, pltpu.roll(line, H, 1), line) + shift
            diagonal = col == row + odd * H
            value = halves[0] + jnp.where(diagonal, shift, 0.0)
            last = jnp.logical_and(diagonal, row >= H // 2)
            halves = (jnp.where(last, line, value),)
        for i, value in enumerate(halves):
            made[which][pl.ds(start + i * H, H), :] = value
        part = pl.ds(start, len(halves) * H)
        copy = pltpu.make_async_copy(
            made[which].at[part], outs[which].at[part], sem.at[len(copies)]
        )
        copy.start()
        copies.append(copy)

    for place in places(pieces, early, count_a):
        _, which, start, rows, _ = place
        count = 2 if rows == H else 1
        give(place, [firsts[which][pl.ds(start + i * H, H), :] for i in range(count)])
    for place, halves in unfolded(pieces, late, count_a, total, owns, got):
        give(place, halves)
    for copy in copies:
        copy.wait()


def unfold_early(pieces, ks, owns, got, count_a, count_g, total):
    args = (*owns, got)
    return pl.pallas_call(
        functools.partial(early_body, pieces, ks, count_a, total),
        in_specs=[pl.BlockSpec(memory_space=pltpu.VMEM)] * len(args),
        out_specs=[pl.BlockSpec(memory_space=pltpu.VMEM)] * 2,
        out_shape=[
            jax.ShapeDtypeStruct((count_a, B), jnp.float32),
            jax.ShapeDtypeStruct((count_g, B), jnp.float32),
        ],
        compiler_params=pltpu.CompilerParams(vmem_limit_bytes=32 * 2**20),
        cost_estimate=pl.CostEstimate(flops=4 * 10**9, bytes_accessed=1, transcendentals=0),
    )(*args)


def finish(pieces, early, late, owns, got, first, count_a, count_g, total):
    args = (*owns, got, *first)
    parts = sum(len(a_blocks) + a_half + len(g_blocks) for a_blocks, a_half, g_blocks, _ in pieces)
    return pl.pallas_call(
        functools.partial(finish_body, pieces, early, late, count_a, total),
        in_specs=[pl.BlockSpec(memory_space=pltpu.VMEM)] * len(args),
        out_specs=[pl.BlockSpec(memory_space=pltpu.HBM)] * 2,
        out_shape=[
            jax.ShapeDtypeStruct((count_a, B), jnp.float32),
            jax.ShapeDtypeStruct((count_g, B), jnp.float32),
        ],
        scratch_shapes=[
            pltpu.VMEM((count_a, B), jnp.float32),
            pltpu.VMEM((count_g, B), jnp.float32),
            pltpu.SemaphoreType.DMA((parts,)),
        ],
        compiler_params=pltpu.CompilerParams(vmem_limit_bytes=32 * 2**20),
    )(*args)


def swap(value, partner):
    dp, tensor = lax.axis_size("dp"), lax.axis_size("tensor")
    pairs = []
    for i in range(dp):
        for j in range(tensor):
            other = partner(i, j)
            pairs.append((i * tensor + j, other[0] * tensor + other[1]))
    return lax.ppermute(value, ("dp", "tensor"), pairs)


def along(stage, kind):
    return lambda i, j: (i ^ (1 << KINDS[kind][j][stage]), j)


def packed(saved_input, saved_pre, grad_act):
    dp = lax.axis_size("dp")
    total = float(saved_input.shape[0] * dp)
    count_a = saved_input.shape[1] // dp
    count_g = saved_pre.shape[1] // dp
    full_a, half_a = split_rows(count_a)
    full_g, _ = split_rows(count_g)
    some = 1 + (full_g - 1) // 2
    pieces = (
        (tuple(range(full_a)), 0, (), 0),
        ((), 0, tuple(range(1, some)), 0),
        ((), half_a, (0,), 1),
        ((), 0, tuple(range(some, full_g)), 1),
    )
    arrays = (saved_input, saved_pre, grad_act)
    keep, send = 0, SLOTS // 2
    early, late = (0, 2), (1, 3)
    keeps, gots, notes = {}, {}, None

    def pack_next(first, ks):
        nonlocal notes
        items = tuple((k, first) for k in ks)
        parts, notes = pack(arrays, pieces, items, count_a, count_g, notes)
        return dict(zip(ks, parts))

    def exchange(parts, stage):
        for k, part in parts.items():
            gots[k] = swap(part, along(stage, pieces[k][3]))

    def halve_pair(ks, stage, **kinds):
        own, parts, others = halve(
            [keeps[k] for k in ks], [gots[k] for k in ks], merged=stage == 2,
            weight=WEIGHTS.get((ks, stage), 1), **kinds
        )
        keeps.update(zip(ks, own))
        if stage == 2:
            gots[ks] = swap(parts[0], lambda i, j: (i ^ (1 << FAR), j))
        else:
            exchange(dict(zip(ks, parts)), stage)
        return others

    exchange(pack_next(send, early[:1]), 0)
    exchange(pack_next(send, early[1:]), 0)
    exchange(pack_next(send, late), 0)
    keeps.update(pack_next(keep, early))
    keeps.update(pack_next(keep, late))

    trace = notes[NOTES, :2, :]
    trace = trace + swap(trace, lambda i, j: (i, j ^ 1))
    across = swap(trace, lambda i, j: (i ^ (1 << X) ^ (1 << NEAR), j))
    halve_pair(early, 1)
    halve_pair(late, 1, terms=(trace,), put=(0, 1))
    (trace,) = halve_pair(early, 2, terms=(trace, across))
    halve_pair(late, 2, terms=(trace,), came=(0, 1), put=(0, 1))

    def both(ks):
        return [keeps[k] for k in ks], gots[ks]

    first = unfold_early(pieces, early, *both(early), count_a, count_g, total)
    a_factor, g_factor = finish(
        pieces, early, late, *both(late), first, count_a, count_g, total
    )
    return a_factor[None], g_factor[None]


def fits(count_a, count_g):
    (full_a, half_a), full_g = split_rows(count_a), count_g // B
    if count_a % H or count_g % B or full_a < 1 or full_g < 3:
        return False
    return full_a + half_a + full_g <= 2 * (EDGE - 2)


def on_device(saved_input, saved_pre, grad_act):
    dp = lax.axis_size("dp")
    count_a = saved_input.shape[1] // dp
    count_g = saved_pre.shape[1] // dp
    if dp == SLOTS and lax.axis_size("tensor") == 2 and fits(count_a, count_g):
        return packed(saved_input, saved_pre, grad_act)
    return plain(saved_input, saved_pre, grad_act)


def solution(mesh):
    spec = P(("groups", "dp"), "tensor")
    out = P("tensor", ("groups", "dp"), None)
    return jax.shard_map(
        on_device, mesh=mesh, in_specs=(spec, spec, spec), out_specs=(out, out), check_vma=False
    )
```

```python
import functools
import math

import jax
import jax.numpy as jnp
from jax import lax
from jax.experimental import pallas as pl
from jax.experimental.pallas import tpu as pltpu
from jax.sharding import PartitionSpec as P

D = 5120
FFW = 10240
B = 128
H = B // 2


def gelu_slope(value):
    return (
        0.5 * (1.0 + lax.erf(value * 0.7071067811865476))
        + value * jnp.exp(-0.5 * value * value) * 0.3989422804014327
    )


def local_blocks(matrix, block, total):
    tokens, width = matrix.shape
    pieces = matrix.reshape(tokens, width // block, block)
    cov = jnp.einsum("tkb,tkc->kbc", pieces, pieces, preferred_element_type=jnp.float32)
    return cov.reshape(width, block) / total


def owned_unit(owned, block):
    count = owned.shape[0]
    rows = lax.axis_index("dp") * count + jnp.arange(count, dtype=jnp.int32)
    cols = jnp.arange(block, dtype=jnp.int32)
    return (cols[None, :] == (rows % block)[:, None]).astype(jnp.float32)


def plain(saved_input, saved_pre, grad_act):
    total = jnp.float32(saved_input.shape[0] * lax.axis_size("dp"))
    slope = gelu_slope(saved_pre.astype(jnp.float32))
    grad_pre = (grad_act.astype(jnp.float32) * slope).astype(jnp.bfloat16)
    terms_a = local_blocks(saved_input, B, total)
    terms_g = local_blocks(grad_pre, B, total)
    owned_a = lax.psum_scatter(terms_a, "dp", scatter_dimension=0, tiled=True)
    owned_g = lax.psum_scatter(terms_g, "dp", scatter_dimension=0, tiled=True)
    unit_a = owned_unit(owned_a, B)
    unit_g = owned_unit(owned_g, B)
    trace_a, trace_g = lax.psum(
        (jnp.sum(owned_a * unit_a), jnp.sum(owned_g * unit_g)), ("dp", "tensor")
    )
    ratio = jnp.sqrt(trace_a / D / (trace_g / FFW))
    damp = jnp.sqrt(jnp.float32(0.1))
    return (
        (owned_a + ratio * damp * unit_a)[None],
        (owned_g + damp / ratio * unit_g)[None],
    )


EDGE = 8
SLOTS = 8
X, NEAR, FAR = 0, 1, 2
KINDS = (((X, NEAR, FAR), (X, NEAR, FAR)), ((NEAR, X, FAR), (NEAR, X, FAR)))
NOTES = len(KINDS) * SLOTS

WEIGHTS = {((0, 1), 2): 2 * 10**9}


def split_rows(count):
    return count // B, (count % B) // H


def has_edge(pieces, k):
    return all(later[3] != pieces[k][3] for later in pieces[k + 1 :])


def piece_rows(pieces, k):
    a_blocks, a_half, g_blocks, _ = pieces[k]
    rows = (len(a_blocks) + len(g_blocks)) * H + a_half * (H * 3 // 4)
    return rows + (EDGE if has_edge(pieces, k) else 0)


def corner_indices(pieces, k):
    parts = [len(a) + a_half + len(g) if kind == pieces[k][3] else 0 for a, a_half, g, kind in pieces]
    return iter(range(sum(parts[:k]), sum(parts[: k + 1])))


def iotas(rows):
    shape = (rows, B)
    return lax.broadcasted_iota(jnp.int32, shape, 0), lax.broadcasted_iota(jnp.int32, shape, 1)


def slot_owner(slot, orders):
    core = lax.axis_index("tensor")
    mask = 0
    for stage, (one, other) in enumerate(zip(*orders)):
        mask = mask | (((slot >> (2 - stage)) & 1) << (one + core * (other - one)))
    return lax.axis_index("dp") ^ mask


def lanes(start, size):
    return pl.ds(start if isinstance(start, int) else pl.multiple_of(start, B), size)


LOADS = 4
FIRST = 4 * 10**9


def pack_body(pieces, items, count_a, count_g, fresh, *refs):
    n = len(items)
    if fresh:
        (a_hbm, *outs), (notes, a_held, sems) = refs[: n + 1], refs[n + 1 :]
        rows = a_hbm.shape[0] // LOADS
        parts = [slice(part * rows, (part + 1) * rows) for part in range(LOADS)]
        copies = [
            pltpu.make_async_copy(a_hbm.at[part], a_held.at[part], sems.at[i])
            for i, part in enumerate(parts)
        ]
        for copy in copies:
            copy.start()
        held = (a_held,)
    else:
        copies = []
        notes_in, held, outs, notes = refs[0], refs[1:4], refs[4 : 4 + n], refs[4 + n]
    full, half = split_rows(count_a)
    slots = SLOTS // 2
    split = [(i, k, first, slot) for i, (k, first) in enumerate(items) for slot in range(slots)]

    def read(i, start):
        return held[i][:, pl.ds(pl.multiple_of(start, B), B)]

    row, col = iotas(H)
    low = col < row
    diag_low, diag_high = col == row, col == row + H
    quarter = H // 2
    row_q, col_q = row[:quarter], col[:quarter]
    note_row, _ = iotas(EDGE)
    zero = jnp.zeros((H, B), jnp.float32)
    traces = [zero, zero]
    tiles = {}

    def cov(part):
        return lax.dot_general(
            part, part, (((0,), (0,)), ((), ())), preferred_element_type=jnp.float32
        )

    def note(slot, index, corner, natural):
        line = jnp.sum(corner, axis=0, keepdims=True)
        if index % 2 != natural:
            line = pltpu.roll(line, H, 1)
        tiles[slot] = tiles[slot] + jnp.where(note_row == index // 2, line, 0.0)

    def fold(block, slot, index, which):
        top, bottom = block[:H], block[H:]
        corner = jnp.where(diag_high, bottom, zero)
        note(slot, index, corner, 0)
        traces[which] = traces[which] + corner + jnp.where(diag_low, top, zero)
        return jnp.where(low, pltpu.roll(bottom, H, 1), top)

    def fold_half(block, odd, slot, index):
        part = jnp.where(odd == 1, pltpu.roll(block[H:], H, 1), block[:H])
        traces[0] = traces[0] + jnp.where(diag_low, part, zero)
        upper, lower = part[:quarter], part[quarter:]
        corner = jnp.where(col_q == row_q + quarter, lower, 0.0)
        note(slot, index, corner, 1)
        square = jnp.where(col_q < row_q, pltpu.roll(lower, B - quarter, 1), upper)
        rest = lower.reshape(2, quarter // 2, B)
        rest = jnp.where(col[: quarter // 2] < H, pltpu.roll(rest[1], H, 1), rest[0])
        return square, rest

    def a_parts(out, k, first, slot, index):
        a_blocks, a_half, _, kind = pieces[k]
        owner = slot_owner(first + slot, KINDS[kind])
        here, odd = kind * SLOTS + first + slot, owner & half
        base = (owner >> half) * (full * (1 + half) + half) * B
        at = 0
        for b in a_blocks:
            block = cov(read(0, base + (odd * (full + 1) + b) * B))
            out[slot, at : at + H, :] = fold(block, here, next(index), 0)
            at = at + H
        if a_half:
            block = cov(read(0, base + full * B))
            square, rest = fold_half(block, odd, here, next(index))
            out[slot, at : at + quarter, :] = square
            out[slot, at + quarter : at + quarter * 3 // 2, :] = rest
            at = at + quarter * 3 // 2
        return at

    def g_parts(out, k, first, slot, index, at):
        _, _, g_blocks, kind = pieces[k]
        here = kind * SLOTS + first + slot
        owner = slot_owner(first + slot, KINDS[kind])
        for b in g_blocks:
            start = owner * count_g + b * B
            value, grad = read(1, start).astype(jnp.float32), read(2, start).astype(jnp.float32)
            block = cov((grad * gelu_slope(value)).astype(jnp.bfloat16))
            out[slot, at : at + H, :] = fold(block, here, next(index), 1)
            at = at + H
        return at

    for copy in copies:
        copy.wait()
    for i, k, first, slot in split:
        here = pieces[k][3] * SLOTS + first + slot
        if here not in tiles:
            tiles[here] = jnp.zeros((EDGE, B), jnp.float32) if fresh else notes_in[here]
        index = corner_indices(pieces, k)
        at = a_parts(outs[i], k, first, slot, index)
        at = g_parts(outs[i], k, first, slot, index, at)
        if has_edge(pieces, k):
            outs[i][slot, at:, :] = tiles[here]

    for slot in range(NOTES):
        if slot in tiles:
            notes[slot] = tiles[slot]
        else:
            notes[slot] = jnp.zeros((EDGE, B), jnp.float32) if fresh else notes_in[slot]
    lines = [jnp.sum(trace, axis=0, keepdims=True) for trace in traces]
    tile = jnp.where(note_row == 0, lines[0], jnp.where(note_row == 1, lines[1], 0.0))
    notes[NOTES] = tile if fresh else notes_in[NOTES] + tile


def pack(arrays, pieces, items, count_a, count_g, notes):
    slots = SLOTS // 2
    fresh = notes is None
    out_shape = [
        jax.ShapeDtypeStruct((slots, piece_rows(pieces, k), B), jnp.float32) for k, _ in items
    ]
    out_shape.append(jax.ShapeDtypeStruct((NOTES + 1, EDGE, B), jnp.float32))
    if fresh:
        args = [pltpu.with_memory_space_constraint(arrays[0], pltpu.HBM)]
        out_shape.append(jax.ShapeDtypeStruct(arrays[0].shape, arrays[0].dtype))
    else:
        args = [notes, *arrays]
    space = pltpu.HBM if fresh else pltpu.VMEM
    outs = pl.pallas_call(
        functools.partial(pack_body, pieces, items, count_a, count_g, fresh),
        in_specs=[pl.BlockSpec(memory_space=space)] * len(args),
        out_specs=[pl.BlockSpec(memory_space=pltpu.VMEM)] * len(out_shape),
        out_shape=out_shape,
        scratch_shapes=[pltpu.SemaphoreType.DMA((LOADS,))] * fresh,
        compiler_params=pltpu.CompilerParams(vmem_limit_bytes=32 * 2**20),
        cost_estimate=pl.CostEstimate(
            flops=FIRST if fresh else 1, bytes_accessed=1, transcendentals=0
        ),
    )(*args)
    n = len(items)
    return outs[:n], outs[n], outs[n + 1 :]


def halve_body(n, terms, came, put, merged, passed, *refs):
    keeps, gots, refs = refs[:n], refs[n : 2 * n], refs[2 * n :]
    terms, refs = refs[:terms], refs[terms + passed :]
    kept, refs = refs[:n], refs[n:]
    sent, sums = (refs[:1], refs[1:]) if merged else (refs[:n], refs[n:])
    sums = sums[passed:]
    if merged:
        ends = [sum(ref.shape[1] for ref in kept[: k + 1]) for k in range(n)]
        sent = [
            sent[0].at[:, end - ref.shape[1] : end, :] for end, ref in zip(ends, kept)
        ]
    for k in range(n):
        half = kept[k].shape[0]
        kept[k][...] = keeps[k][:half] + gots[k][:half]
        sent[k][...] = keeps[k][half:] + gots[k][half:]
    if terms:
        value = sum((term[...] for term in terms[1:]), terms[0][...])
        for k in came:
            value = value + gots[k][0, -2:, :]
        for out in sums:
            out[...] = value
        for k in put:
            rows = kept[k].shape[1]
            kept[k][0, rows - 2 :, :] = value
            sent[k][0, rows - 2 :, :] = value


def halve(keeps, gots, terms=(), came=(), put=(), merged=False, passes=(), weight=1):
    n = len(keeps)
    emit = bool(terms) and not put
    args = [*keeps, *gots, *terms, *passes]
    first = len(args) - len(passes)
    kept = [(keep.shape[0] // 2, *keep.shape[1:]) for keep in keeps]
    sent = [(kept[0][0], sum(shape[1] for shape in kept), B)] if merged else kept
    shapes = [*kept, *sent, *(array.shape for array in passes), *([(2, B)] * emit)]
    last = n + len(sent)
    outs = pl.pallas_call(
        functools.partial(halve_body, n, len(terms), came, put, merged, len(passes)),
        in_specs=[pl.BlockSpec(memory_space=pltpu.VMEM)] * len(args),
        out_specs=[pl.BlockSpec(memory_space=pltpu.VMEM)] * len(shapes),
        out_shape=[jax.ShapeDtypeStruct(shape, jnp.float32) for shape in shapes],
        input_output_aliases={first + i: last + i for i in range(len(passes))},
        compiler_params=pltpu.CompilerParams(vmem_limit_bytes=32 * 2**20),
        cost_estimate=pl.CostEstimate(flops=weight, bytes_accessed=1, transcendentals=0),
    )(*args)
    return outs[:n], outs[n : n + len(sent)], outs[n + len(sent) :]


def mean_of(value, total):
    return value * (1.0 / total) if math.frexp(total)[0] == 0.5 else value / total


def turn(folded):
    return jnp.concatenate([folded] * (B // folded.shape[0]), axis=0).T


def unfold(folded):
    row, col = iotas(H)
    turned = turn(folded)
    last = pltpu.roll(jnp.where(col < row, folded, turned[:H]), H, 1)
    return jnp.where(col < row, turned[:H], folded), jnp.where(col < H, turned[H:], last)


def unfold_half(square, rest, odd):
    quarter = H // 2
    row, col = iotas(quarter)
    turned = turn(square)
    upper = jnp.where(col < row, turned[:quarter], square)
    last = pltpu.roll(jnp.where(col < row, square, turned[:quarter]), quarter, 1)
    lower = jnp.where(col < quarter, turned[quarter:H], last)
    rest = jnp.concatenate([rest, pltpu.roll(rest, H, 1)], axis=0)
    part = jnp.concatenate([upper, jnp.where(col < H, lower, rest)], axis=0)
    return (jnp.where(odd == 1, pltpu.roll(part, H, 1), part),)


def places(pieces, ks, count_a):
    full, half = split_rows(count_a)
    odd = lax.axis_index("dp") & half
    for k in ks:
        a_blocks, a_half, g_blocks, kind = pieces[k]
        index = corner_indices(pieces, k)
        for b in a_blocks:
            start = pl.multiple_of(b * B + odd * H, H) if half else b * B
            yield k, 0, start, H, next(index)
        if a_half:
            yield k, 0, pl.multiple_of((1 - odd) * full * B, H), H * 3 // 4, next(index)
        for b in g_blocks:
            yield k, 1, b * B, H, next(index)


def row_begins(pieces, ks):
    rows = [piece_rows(pieces, k) for k in ks]
    return {k: sum(rows[:i]) for i, k in enumerate(ks)}


def unfolded(pieces, ks, count_a, total, owns, got):
    odd = lax.axis_index("dp") & 1
    at = dict.fromkeys(ks, 0)
    begins = row_begins(pieces, ks)

    def take(k, rows):
        begin = at[k]
        at[k] = begin + rows
        mine = owns[ks.index(k)][0, begin : begin + rows, :]
        begin = begin + begins[k]
        return mean_of(mine + got[0, begin : begin + rows, :], total)

    for place in places(pieces, ks, count_a):
        k, _, _, rows, _ = place
        if rows == H:
            yield place, unfold(take(k, H))
        else:
            yield place, unfold_half(take(k, H // 2), take(k, H // 4), odd)


def early_body(pieces, ks, count_a, total, *refs):
    n = len(ks)
    owns, got, outs = refs[:n], refs[n], refs[n + 1 :]
    for (_, which, start, _, _), halves in unfolded(pieces, ks, count_a, total, owns, got):
        for i, value in enumerate(halves):
            outs[which][pl.ds(start + i * H, H), :] = value


def finish_body(pieces, befores, late, count_a, total, *refs):
    n = len(late)
    owns, got, firsts, refs = refs[:n], refs[n], refs[n + 1 : -5], refs[-5:]
    outs, made, sem = refs[:2], refs[2:4], refs[4]
    _, half = split_rows(count_a)
    odd = lax.axis_index("dp") & half
    row, col = iotas(H)

    edges = {}
    for k, own in zip(late, owns):
        end = row_begins(pieces, late)[k] + piece_rows(pieces, k)
        edge = mean_of(own[0, -EDGE:, :] + got[0, end - EDGE : end, :], total)
        edges[pieces[k][3]] = (edge, pltpu.roll(edge, H, 1))
    sums = jnp.sum(edge[-2:], axis=1, keepdims=True)
    ratio = jnp.sqrt(sums[0:1] / D / (sums[1:2] / FFW))
    damp = jnp.sqrt(jnp.full((1, 1), 0.1, jnp.float32))
    shifts = (ratio * damp, damp / ratio)

    def corner(kind, index, natural):
        line = index // 2
        return edges[kind][0 if index % 2 == natural else 1][line : line + 1]

    copies = []

    def give(place, halves):
        k, which, start, rows, index = place
        shift, kind = shifts[which], pieces[k][3]
        if rows == H:
            top, bottom = halves
            top = top + jnp.where(col == row, shift, 0.0)
            bottom = jnp.where(col == row + H, corner(kind, index, 0) + shift, bottom)
            halves = (top, bottom)
        else:
            line = corner(kind, index, 1)
            line = jnp.where(odd == 1, pltpu.roll(line, H, 1), line) + shift
            diagonal = col == row + odd * H
            value = halves[0] + jnp.where(diagonal, shift, 0.0)
            last = jnp.logical_and(diagonal, row >= H // 2)
            halves = (jnp.where(last, line, value),)
        for i, value in enumerate(halves):
            made[which][pl.ds(start + i * H, H), :] = value
        part = pl.ds(start, len(halves) * H)
        copy = pltpu.make_async_copy(
            made[which].at[part], outs[which].at[part], sem.at[len(copies)]
        )
        copy.start()
        copies.append(copy)

    for number, ks in enumerate(befores):
        for place in places(pieces, ks, count_a):
            _, which, start, rows, _ = place
            ref, count = firsts[2 * number + which], 2 if rows == H else 1
            give(place, [ref[pl.ds(start + i * H, H), :] for i in range(count)])
    for place, halves in unfolded(pieces, late, count_a, total, owns, got):
        give(place, halves)
    for copy in copies:
        copy.wait()


def unfold_early(pieces, ks, owns, got, count_a, count_g, total):
    args = (*owns, got)
    return pl.pallas_call(
        functools.partial(early_body, pieces, ks, count_a, total),
        in_specs=[pl.BlockSpec(memory_space=pltpu.VMEM)] * len(args),
        out_specs=[pl.BlockSpec(memory_space=pltpu.VMEM)] * 2,
        out_shape=[
            jax.ShapeDtypeStruct((count_a, B), jnp.float32),
            jax.ShapeDtypeStruct((count_g, B), jnp.float32),
        ],
        compiler_params=pltpu.CompilerParams(vmem_limit_bytes=32 * 2**20),
        cost_estimate=pl.CostEstimate(flops=4 * 10**9, bytes_accessed=1, transcendentals=0),
    )(*args)


def finish(pieces, befores, late, owns, got, first, count_a, count_g, total):
    args = (*owns, got, *first)
    parts = sum(len(a_blocks) + a_half + len(g_blocks) for a_blocks, a_half, g_blocks, _ in pieces)
    return pl.pallas_call(
        functools.partial(finish_body, pieces, befores, late, count_a, total),
        in_specs=[pl.BlockSpec(memory_space=pltpu.VMEM)] * len(args),
        out_specs=[pl.BlockSpec(memory_space=pltpu.HBM)] * 2,
        out_shape=[
            jax.ShapeDtypeStruct((count_a, B), jnp.float32),
            jax.ShapeDtypeStruct((count_g, B), jnp.float32),
        ],
        scratch_shapes=[
            pltpu.VMEM((count_a, B), jnp.float32),
            pltpu.VMEM((count_g, B), jnp.float32),
            pltpu.SemaphoreType.DMA((parts,)),
        ],
        compiler_params=pltpu.CompilerParams(vmem_limit_bytes=32 * 2**20),
    )(*args)


def swap(value, partner):
    dp, tensor = lax.axis_size("dp"), lax.axis_size("tensor")
    pairs = []
    for i in range(dp):
        for j in range(tensor):
            other = partner(i, j)
            pairs.append((i * tensor + j, other[0] * tensor + other[1]))
    return lax.ppermute(value, ("dp", "tensor"), pairs)


def along(stage, kind):
    return lambda i, j: (i ^ (1 << KINDS[kind][j][stage]), j)


def packed(saved_input, saved_pre, grad_act):
    dp = lax.axis_size("dp")
    total = float(saved_input.shape[0] * dp)
    count_a = saved_input.shape[1] // dp
    count_g = saved_pre.shape[1] // dp
    full_a, half_a = split_rows(count_a)
    full_g, _ = split_rows(count_g)
    cuts = [0] + [1 + (full_g - 1) * i // 4 for i in range(5)]
    blocks = [tuple(range(begin, end)) for begin, end in zip(cuts, cuts[1:])]
    pieces = (
        (tuple(range(full_a)), 0, (), 0),
        ((), half_a, blocks[0], 1),
        ((), 0, blocks[1], 0),
        ((), 0, blocks[2], 1),
        ((), 0, blocks[3], 0),
        ((), 0, blocks[4], 1),
    )
    arrays = (saved_input, saved_pre, grad_act)
    keep, send = 0, SLOTS // 2
    early, middle, late = (0, 1), (2, 3), (4, 5)
    keeps, gots, notes = {}, {}, None

    def pack_next(first, ks):
        nonlocal notes, arrays
        items = tuple((k, first) for k in ks)
        parts, notes, held = pack(arrays, pieces, items, count_a, count_g, notes)
        arrays = (*held, *arrays[len(held) :])
        return dict(zip(ks, parts))

    def exchange(parts, stage):
        for k, part in parts.items():
            gots[k] = swap(part, along(stage, pieces[k][3]))

    def halve_pair(ks, stage, **kinds):
        own, parts, others = halve(
            [keeps[k] for k in ks], [gots[k] for k in ks], merged=stage == 2,
            weight=WEIGHTS.get((ks, stage), 1), **kinds
        )
        keeps.update(zip(ks, own))
        if stage == 2:
            gots[ks] = swap(parts[0], lambda i, j: (i ^ (1 << FAR), j))
        else:
            exchange(dict(zip(ks, parts)), stage)
        return others

    exchange(pack_next(send, early[:1]), 0)
    exchange(pack_next(send, early[1:]), 0)
    exchange(pack_next(send, middle), 0)
    waiting = pack_next(send, late)
    keeps.update(pack_next(keep, early))
    keeps.update(pack_next(keep, middle))
    keeps.update(pack_next(keep, late))

    trace = notes[NOTES, :2, :]
    trace = trace + swap(trace, lambda i, j: (i, j ^ 1))
    across = swap(trace, lambda i, j: (i ^ (1 << X) ^ (1 << NEAR), j))
    parts = halve_pair(early, 1, passes=tuple(waiting.values()))
    exchange(dict(zip(waiting, parts)), 0)
    halve_pair(middle, 1)
    halve_pair(late, 1, terms=(trace,), put=(0, 1))
    (trace,) = halve_pair(early, 2, terms=(trace, across))
    halve_pair(middle, 2)
    halve_pair(late, 2, terms=(trace,), came=(0, 1), put=(0, 1))

    def both(ks):
        return [keeps[k] for k in ks], gots[ks]

    befores, first = (early, middle), []
    for ks in befores:
        first += unfold_early(pieces, ks, *both(ks), count_a, count_g, total)
    a_factor, g_factor = finish(
        pieces, befores, late, *both(late), first, count_a, count_g, total
    )
    return a_factor[None], g_factor[None]


def fits(count_a, count_g):
    (full_a, half_a), full_g = split_rows(count_a), count_g // B
    if count_a % H or count_g % B or full_a < 1 or full_g < 5:
        return False
    return full_a + half_a + full_g <= 2 * (EDGE - 2)


def on_device(saved_input, saved_pre, grad_act):
    dp = lax.axis_size("dp")
    count_a = saved_input.shape[1] // dp
    count_g = saved_pre.shape[1] // dp
    if dp == SLOTS and lax.axis_size("tensor") == 2 and fits(count_a, count_g):
        return packed(saved_input, saved_pre, grad_act)
    return plain(saved_input, saved_pre, grad_act)


def solution(mesh):
    spec = P(("groups", "dp"), "tensor")
    out = P("tensor", ("groups", "dp"), None)
    return jax.shard_map(
        on_device, mesh=mesh, in_specs=(spec, spec, spec), out_specs=(out, out), check_vma=False
    )
```

```python
import functools
import math

import jax
import jax.numpy as jnp
from jax import lax
from jax.experimental import pallas as pl
from jax.experimental.pallas import tpu as pltpu
from jax.sharding import PartitionSpec as P

D = 5120
FFW = 10240
B = 128
H = B // 2


def gelu_slope(value):
    return (
        0.5 * (1.0 + lax.erf(value * 0.7071067811865476))
        + value * jnp.exp(-0.5 * value * value) * 0.3989422804014327
    )


def local_blocks(matrix, block, total):
    tokens, width = matrix.shape
    pieces = matrix.reshape(tokens, width // block, block)
    cov = jnp.einsum("tkb,tkc->kbc", pieces, pieces, preferred_element_type=jnp.float32)
    return cov.reshape(width, block) / total


def owned_unit(owned, block):
    count = owned.shape[0]
    rows = lax.axis_index("dp") * count + jnp.arange(count, dtype=jnp.int32)
    cols = jnp.arange(block, dtype=jnp.int32)
    return (cols[None, :] == (rows % block)[:, None]).astype(jnp.float32)


def plain(saved_input, saved_pre, grad_act):
    total = jnp.float32(saved_input.shape[0] * lax.axis_size("dp"))
    slope = gelu_slope(saved_pre.astype(jnp.float32))
    grad_pre = (grad_act.astype(jnp.float32) * slope).astype(jnp.bfloat16)
    terms_a = local_blocks(saved_input, B, total)
    terms_g = local_blocks(grad_pre, B, total)
    owned_a = lax.psum_scatter(terms_a, "dp", scatter_dimension=0, tiled=True)
    owned_g = lax.psum_scatter(terms_g, "dp", scatter_dimension=0, tiled=True)
    unit_a = owned_unit(owned_a, B)
    unit_g = owned_unit(owned_g, B)
    trace_a, trace_g = lax.psum(
        (jnp.sum(owned_a * unit_a), jnp.sum(owned_g * unit_g)), ("dp", "tensor")
    )
    ratio = jnp.sqrt(trace_a / D / (trace_g / FFW))
    damp = jnp.sqrt(jnp.float32(0.1))
    return (
        (owned_a + ratio * damp * unit_a)[None],
        (owned_g + damp / ratio * unit_g)[None],
    )


EDGE = 8
SLOTS = 8
X, NEAR, FAR = 0, 1, 2
KINDS = (((NEAR, X, FAR), (NEAR, X, FAR)), ((X, NEAR, FAR), (X, NEAR, FAR)))
NOTES = len(KINDS) * SLOTS

WEIGHTS = {((0, 1), 2): 2 * 10**9}


def split_rows(count):
    return count // B, (count % B) // H


def has_edge(pieces, k):
    return all(later[3] != pieces[k][3] for later in pieces[k + 1 :])


def piece_rows(pieces, k):
    a_blocks, a_half, g_blocks, _ = pieces[k]
    rows = (len(a_blocks) + len(g_blocks)) * H + a_half * (H * 3 // 4)
    return rows + (EDGE if has_edge(pieces, k) else 0)


def corner_indices(pieces, k):
    parts = [len(a) + a_half + len(g) if kind == pieces[k][3] else 0 for a, a_half, g, kind in pieces]
    return iter(range(sum(parts[:k]), sum(parts[: k + 1])))


def iotas(rows):
    shape = (rows, B)
    return lax.broadcasted_iota(jnp.int32, shape, 0), lax.broadcasted_iota(jnp.int32, shape, 1)


def slot_owner(slot, orders):
    core = lax.axis_index("tensor")
    mask = 0
    for stage, (one, other) in enumerate(zip(*orders)):
        mask = mask | (((slot >> (2 - stage)) & 1) << (one + core * (other - one)))
    return lax.axis_index("dp") ^ mask


def lanes(start, size):
    return pl.ds(start if isinstance(start, int) else pl.multiple_of(start, B), size)


LOADS = 4
FIRST = 4 * 10**9


def pack_body(pieces, items, count_a, count_g, fresh, *refs):
    n = len(items)
    if fresh:
        (a_hbm, *outs), (notes, a_held, sems) = refs[: n + 1], refs[n + 1 :]
        rows = a_hbm.shape[0] // LOADS
        parts = [slice(part * rows, (part + 1) * rows) for part in range(LOADS)]
        copies = [
            pltpu.make_async_copy(a_hbm.at[part], a_held.at[part], sems.at[i])
            for i, part in enumerate(parts)
        ]
        for copy in copies:
            copy.start()
        held = (a_held,)
    else:
        copies = []
        notes_in, held, outs, notes = refs[0], refs[1:4], refs[4 : 4 + n], refs[4 + n]
    full, half = split_rows(count_a)
    slots = SLOTS // 2
    split = [(i, k, first, slot) for i, (k, first) in enumerate(items) for slot in range(slots)]

    def read(i, start):
        return held[i][:, pl.ds(pl.multiple_of(start, B), B)]

    row, col = iotas(H)
    low = col < row
    diag_low, diag_high = col == row, col == row + H
    quarter = H // 2
    row_q, col_q = row[:quarter], col[:quarter]
    note_row, _ = iotas(EDGE)
    zero = jnp.zeros((H, B), jnp.float32)
    traces = [zero, zero]
    tiles = {}

    def cov(part):
        return lax.dot_general(
            part, part, (((0,), (0,)), ((), ())), preferred_element_type=jnp.float32
        )

    def note(slot, index, corner, natural):
        line = jnp.sum(corner, axis=0, keepdims=True)
        if index % 2 != natural:
            line = pltpu.roll(line, H, 1)
        tiles[slot] = tiles[slot] + jnp.where(note_row == index // 2, line, 0.0)

    def fold(block, slot, index, which):
        top, bottom = block[:H], block[H:]
        corner = jnp.where(diag_high, bottom, zero)
        note(slot, index, corner, 0)
        traces[which] = traces[which] + corner + jnp.where(diag_low, top, zero)
        return jnp.where(low, pltpu.roll(bottom, H, 1), top)

    def fold_half(block, odd, slot, index):
        part = jnp.where(odd == 1, pltpu.roll(block[H:], H, 1), block[:H])
        traces[0] = traces[0] + jnp.where(diag_low, part, zero)
        upper, lower = part[:quarter], part[quarter:]
        corner = jnp.where(col_q == row_q + quarter, lower, 0.0)
        note(slot, index, corner, 1)
        square = jnp.where(col_q < row_q, pltpu.roll(lower, B - quarter, 1), upper)
        rest = lower.reshape(2, quarter // 2, B)
        rest = jnp.where(col[: quarter // 2] < H, pltpu.roll(rest[1], H, 1), rest[0])
        return square, rest

    def a_parts(out, k, first, slot, index):
        a_blocks, a_half, _, kind = pieces[k]
        owner = slot_owner(first + slot, KINDS[kind])
        here, odd = kind * SLOTS + first + slot, owner & half
        base = (owner >> half) * (full * (1 + half) + half) * B
        at = 0
        for b in a_blocks:
            block = cov(read(0, base + (odd * (full + 1) + b) * B))
            out[slot, at : at + H, :] = fold(block, here, next(index), 0)
            at = at + H
        if a_half:
            block = cov(read(0, base + full * B))
            square, rest = fold_half(block, odd, here, next(index))
            out[slot, at : at + quarter, :] = square
            out[slot, at + quarter : at + quarter * 3 // 2, :] = rest
            at = at + quarter * 3 // 2
        return at

    def g_parts(out, k, first, slot, index, at):
        _, _, g_blocks, kind = pieces[k]
        here = kind * SLOTS + first + slot
        owner = slot_owner(first + slot, KINDS[kind])
        for b in g_blocks:
            start = owner * count_g + b * B
            value, grad = read(1, start).astype(jnp.float32), read(2, start).astype(jnp.float32)
            block = cov((grad * gelu_slope(value)).astype(jnp.bfloat16))
            out[slot, at : at + H, :] = fold(block, here, next(index), 1)
            at = at + H
        return at

    for copy in copies:
        copy.wait()
    for i, k, first, slot in split:
        here = pieces[k][3] * SLOTS + first + slot
        if here not in tiles:
            tiles[here] = jnp.zeros((EDGE, B), jnp.float32) if fresh else notes_in[here]
        index = corner_indices(pieces, k)
        at = a_parts(outs[i], k, first, slot, index)
        at = g_parts(outs[i], k, first, slot, index, at)
        if has_edge(pieces, k):
            outs[i][slot, at:, :] = tiles[here]

    for slot in range(NOTES):
        if slot in tiles:
            notes[slot] = tiles[slot]
        else:
            notes[slot] = jnp.zeros((EDGE, B), jnp.float32) if fresh else notes_in[slot]
    lines = [jnp.sum(trace, axis=0, keepdims=True) for trace in traces]
    tile = jnp.where(note_row == 0, lines[0], jnp.where(note_row == 1, lines[1], 0.0))
    notes[NOTES] = tile if fresh else notes_in[NOTES] + tile


def pack(arrays, pieces, items, count_a, count_g, notes):
    slots = SLOTS // 2
    fresh = notes is None
    out_shape = [
        jax.ShapeDtypeStruct((slots, piece_rows(pieces, k), B), jnp.float32) for k, _ in items
    ]
    out_shape.append(jax.ShapeDtypeStruct((NOTES + 1, EDGE, B), jnp.float32))
    if fresh:
        args = [pltpu.with_memory_space_constraint(arrays[0], pltpu.HBM)]
        out_shape.append(jax.ShapeDtypeStruct(arrays[0].shape, arrays[0].dtype))
    else:
        args = [notes, *arrays]
    space = pltpu.HBM if fresh else pltpu.VMEM
    outs = pl.pallas_call(
        functools.partial(pack_body, pieces, items, count_a, count_g, fresh),
        in_specs=[pl.BlockSpec(memory_space=space)] * len(args),
        out_specs=[pl.BlockSpec(memory_space=pltpu.VMEM)] * len(out_shape),
        out_shape=out_shape,
        scratch_shapes=[pltpu.SemaphoreType.DMA((LOADS,))] * fresh,
        compiler_params=pltpu.CompilerParams(vmem_limit_bytes=32 * 2**20),
        cost_estimate=pl.CostEstimate(
            flops=FIRST if fresh else 1, bytes_accessed=1, transcendentals=0
        ),
    )(*args)
    n = len(items)
    return outs[:n], outs[n], outs[n + 1 :]


def halve_body(n, terms, came, put, merged, *refs):
    keeps, gots, refs = refs[:n], refs[n : 2 * n], refs[2 * n :]
    terms, kept, refs = refs[:terms], refs[terms : terms + n], refs[terms + n :]
    sent, sums = (refs[:1], refs[1:]) if merged else (refs[:n], refs[n:])
    if merged:
        ends = [sum(ref.shape[1] for ref in kept[: k + 1]) for k in range(n)]
        sent = [
            sent[0].at[:, end - ref.shape[1] : end, :] for end, ref in zip(ends, kept)
        ]
    for k in range(n):
        half = kept[k].shape[0]
        kept[k][...] = keeps[k][:half] + gots[k][:half]
        sent[k][...] = keeps[k][half:] + gots[k][half:]
    if terms:
        value = sum((term[...] for term in terms[1:]), terms[0][...])
        for k in came:
            value = value + gots[k][0, -2:, :]
        for out in sums:
            out[...] = value
        for k in put:
            rows = kept[k].shape[1]
            kept[k][0, rows - 2 :, :] = value
            sent[k][0, rows - 2 :, :] = value


def halve(keeps, gots, terms=(), came=(), put=(), merged=False, weight=1):
    n = len(keeps)
    emit = bool(terms) and not put
    args = [*keeps, *gots, *terms]
    kept = [(keep.shape[0] // 2, *keep.shape[1:]) for keep in keeps]
    sent = [(kept[0][0], sum(shape[1] for shape in kept), B)] if merged else kept
    shapes = [*kept, *sent, *([(2, B)] * emit)]
    outs = pl.pallas_call(
        functools.partial(halve_body, n, len(terms), came, put, merged),
        in_specs=[pl.BlockSpec(memory_space=pltpu.VMEM)] * len(args),
        out_specs=[pl.BlockSpec(memory_space=pltpu.VMEM)] * len(shapes),
        out_shape=[jax.ShapeDtypeStruct(shape, jnp.float32) for shape in shapes],
        compiler_params=pltpu.CompilerParams(vmem_limit_bytes=32 * 2**20),
        cost_estimate=pl.CostEstimate(flops=weight, bytes_accessed=1, transcendentals=0),
    )(*args)
    return outs[:n], outs[n : n + len(sent)], outs[n + len(sent) :]


def mean_of(value, total):
    return value * (1.0 / total) if math.frexp(total)[0] == 0.5 else value / total


def turn(folded):
    return jnp.concatenate([folded] * (B // folded.shape[0]), axis=0).T


def unfold(folded):
    row, col = iotas(H)
    turned = turn(folded)
    last = pltpu.roll(jnp.where(col < row, folded, turned[:H]), H, 1)
    return jnp.where(col < row, turned[:H], folded), jnp.where(col < H, turned[H:], last)


def unfold_half(square, rest, odd):
    quarter = H // 2
    row, col = iotas(quarter)
    turned = turn(square)
    upper = jnp.where(col < row, turned[:quarter], square)
    last = pltpu.roll(jnp.where(col < row, square, turned[:quarter]), quarter, 1)
    lower = jnp.where(col < quarter, turned[quarter:H], last)
    rest = jnp.concatenate([rest, pltpu.roll(rest, H, 1)], axis=0)
    part = jnp.concatenate([upper, jnp.where(col < H, lower, rest)], axis=0)
    return (jnp.where(odd == 1, pltpu.roll(part, H, 1), part),)


def places(pieces, ks, count_a):
    full, half = split_rows(count_a)
    odd = lax.axis_index("dp") & half
    for k in ks:
        a_blocks, a_half, g_blocks, kind = pieces[k]
        index = corner_indices(pieces, k)
        for b in a_blocks:
            start = pl.multiple_of(b * B + odd * H, H) if half else b * B
            yield k, 0, start, H, next(index)
        if a_half:
            yield k, 0, pl.multiple_of((1 - odd) * full * B, H), H * 3 // 4, next(index)
        for b in g_blocks:
            yield k, 1, b * B, H, next(index)


def row_begins(pieces, ks):
    rows = [piece_rows(pieces, k) for k in ks]
    return {k: sum(rows[:i]) for i, k in enumerate(ks)}


def unfolded(pieces, ks, count_a, total, owns, got):
    odd = lax.axis_index("dp") & 1
    at = dict.fromkeys(ks, 0)
    begins = row_begins(pieces, ks)

    def take(k, rows):
        begin = at[k]
        at[k] = begin + rows
        mine = owns[ks.index(k)][0, begin : begin + rows, :]
        begin = begin + begins[k]
        return mean_of(mine + got[0, begin : begin + rows, :], total)

    for place in places(pieces, ks, count_a):
        k, _, _, rows, _ = place
        if rows == H:
            yield place, unfold(take(k, H))
        else:
            yield place, unfold_half(take(k, H // 2), take(k, H // 4), odd)


def early_body(pieces, ks, count_a, total, *refs):
    n = len(ks)
    owns, got, outs = refs[:n], refs[n], refs[n + 1 :]
    for (_, which, start, _, _), halves in unfolded(pieces, ks, count_a, total, owns, got):
        for i, value in enumerate(halves):
            outs[which][pl.ds(start + i * H, H), :] = value


def finish_body(pieces, early, late, count_a, total, *refs):
    n = len(late)
    owns, got, firsts, outs = refs[:n], refs[n], refs[n + 1 : n + 3], refs[n + 3 : n + 5]
    made, sem = refs[n + 5 : n + 7], refs[n + 7]
    _, half = split_rows(count_a)
    odd = lax.axis_index("dp") & half
    row, col = iotas(H)

    edges = {}
    for k, own in zip(late, owns):
        end = row_begins(pieces, late)[k] + piece_rows(pieces, k)
        edge = mean_of(own[0, -EDGE:, :] + got[0, end - EDGE : end, :], total)
        edges[pieces[k][3]] = (edge, pltpu.roll(edge, H, 1))
    sums = jnp.sum(edge[-2:], axis=1, keepdims=True)
    ratio = jnp.sqrt(sums[0:1] / D / (sums[1:2] / FFW))
    damp = jnp.sqrt(jnp.full((1, 1), 0.1, jnp.float32))
    shifts = (ratio * damp, damp / ratio)

    def corner(kind, index, natural):
        line = index // 2
        return edges[kind][0 if index % 2 == natural else 1][line : line + 1]

    copies = []

    def give(place, halves):
        k, which, start, rows, index = place
        shift, kind = shifts[which], pieces[k][3]
        if rows == H:
            top, bottom = halves
            top = top + jnp.where(col == row, shift, 0.0)
            bottom = jnp.where(col == row + H, corner(kind, index, 0) + shift, bottom)
            halves = (top, bottom)
        else:
            line = corner(kind, index, 1)
            line = jnp.where(odd == 1, pltpu.roll(line, H, 1), line) + shift
            diagonal = col == row + odd * H
            value = halves[0] + jnp.where(diagonal, shift, 0.0)
            last = jnp.logical_and(diagonal, row >= H // 2)
            halves = (jnp.where(last, line, value),)
        for i, value in enumerate(halves):
            made[which][pl.ds(start + i * H, H), :] = value
        part = pl.ds(start, len(halves) * H)
        copy = pltpu.make_async_copy(
            made[which].at[part], outs[which].at[part], sem.at[len(copies)]
        )
        copy.start()
        copies.append(copy)

    for place in places(pieces, early, count_a):
        _, which, start, rows, _ = place
        count = 2 if rows == H else 1
        give(place, [firsts[which][pl.ds(start + i * H, H), :] for i in range(count)])
    for place, halves in unfolded(pieces, late, count_a, total, owns, got):
        give(place, halves)
    for copy in copies:
        copy.wait()


def unfold_early(pieces, ks, owns, got, count_a, count_g, total):
    args = (*owns, got)
    return pl.pallas_call(
        functools.partial(early_body, pieces, ks, count_a, total),
        in_specs=[pl.BlockSpec(memory_space=pltpu.VMEM)] * len(args),
        out_specs=[pl.BlockSpec(memory_space=pltpu.VMEM)] * 2,
        out_shape=[
            jax.ShapeDtypeStruct((count_a, B), jnp.float32),
            jax.ShapeDtypeStruct((count_g, B), jnp.float32),
        ],
        compiler_params=pltpu.CompilerParams(vmem_limit_bytes=32 * 2**20),
        cost_estimate=pl.CostEstimate(flops=4 * 10**9, bytes_accessed=1, transcendentals=0),
    )(*args)


def finish(pieces, early, late, owns, got, first, count_a, count_g, total):
    args = (*owns, got, *first)
    parts = sum(len(a_blocks) + a_half + len(g_blocks) for a_blocks, a_half, g_blocks, _ in pieces)
    return pl.pallas_call(
        functools.partial(finish_body, pieces, early, late, count_a, total),
        in_specs=[pl.BlockSpec(memory_space=pltpu.VMEM)] * len(args),
        out_specs=[pl.BlockSpec(memory_space=pltpu.HBM)] * 2,
        out_shape=[
            jax.ShapeDtypeStruct((count_a, B), jnp.float32),
            jax.ShapeDtypeStruct((count_g, B), jnp.float32),
        ],
        scratch_shapes=[
            pltpu.VMEM((count_a, B), jnp.float32),
            pltpu.VMEM((count_g, B), jnp.float32),
            pltpu.SemaphoreType.DMA((parts,)),
        ],
        compiler_params=pltpu.CompilerParams(vmem_limit_bytes=32 * 2**20),
    )(*args)


def swap(value, partner):
    dp, tensor = lax.axis_size("dp"), lax.axis_size("tensor")
    pairs = []
    for i in range(dp):
        for j in range(tensor):
            other = partner(i, j)
            pairs.append((i * tensor + j, other[0] * tensor + other[1]))
    return lax.ppermute(value, ("dp", "tensor"), pairs)


def along(stage, kind):
    return lambda i, j: (i ^ (1 << KINDS[kind][j][stage]), j)


def packed(saved_input, saved_pre, grad_act):
    dp = lax.axis_size("dp")
    total = float(saved_input.shape[0] * dp)
    count_a = saved_input.shape[1] // dp
    count_g = saved_pre.shape[1] // dp
    full_a, half_a = split_rows(count_a)
    full_g, _ = split_rows(count_g)
    some = 1 + (full_g - 1) // 2
    pieces = (
        (tuple(range(full_a)), 0, (), 0),
        ((), half_a, (0,), 1),
        ((), 0, tuple(range(1, some)), 1),
        ((), 0, tuple(range(some, full_g)), 0),
    )
    arrays = (saved_input, saved_pre, grad_act)
    keep, send = 0, SLOTS // 2
    early, late = (0, 1), (2, 3)
    keeps, gots, notes = {}, {}, None

    def pack_next(first, ks):
        nonlocal notes, arrays
        items = tuple((k, first) for k in ks)
        parts, notes, held = pack(arrays, pieces, items, count_a, count_g, notes)
        arrays = (*held, *arrays[len(held) :])
        return dict(zip(ks, parts))

    def exchange(parts, stage):
        for k, part in parts.items():
            gots[k] = swap(part, along(stage, pieces[k][3]))

    def halve_pair(ks, stage, **kinds):
        own, parts, others = halve(
            [keeps[k] for k in ks], [gots[k] for k in ks], merged=stage == 2,
            weight=WEIGHTS.get((ks, stage), 1), **kinds
        )
        keeps.update(zip(ks, own))
        if stage == 2:
            gots[ks] = swap(parts[0], lambda i, j: (i ^ (1 << FAR), j))
        else:
            exchange(dict(zip(ks, parts)), stage)
        return others

    exchange(pack_next(send, early[:1]), 0)
    exchange(pack_next(send, early[1:]), 0)
    exchange(pack_next(send, late), 0)
    keeps.update(pack_next(keep, early))
    keeps.update(pack_next(keep, late))

    trace = notes[NOTES, :2, :]
    trace = trace + swap(trace, lambda i, j: (i, j ^ 1))
    across = swap(trace, lambda i, j: (i ^ (1 << X) ^ (1 << NEAR), j))
    halve_pair(early, 1)
    halve_pair(late, 1, terms=(trace,), put=(0, 1))
    (trace,) = halve_pair(early, 2, terms=(trace, across))
    halve_pair(late, 2, terms=(trace,), came=(0, 1), put=(0, 1))

    def both(ks):
        return [keeps[k] for k in ks], gots[ks]

    first = unfold_early(pieces, early, *both(early), count_a, count_g, total)
    a_factor, g_factor = finish(
        pieces, early, late, *both(late), first, count_a, count_g, total
    )
    return a_factor[None], g_factor[None]


def fits(count_a, count_g):
    (full_a, half_a), full_g = split_rows(count_a), count_g // B
    if count_a % H or count_g % B or full_a < 1 or full_g < 3:
        return False
    return full_a + half_a + full_g <= 2 * (EDGE - 2)


def on_device(saved_input, saved_pre, grad_act):
    dp = lax.axis_size("dp")
    count_a = saved_input.shape[1] // dp
    count_g = saved_pre.shape[1] // dp
    if dp == SLOTS and lax.axis_size("tensor") == 2 and fits(count_a, count_g):
        return packed(saved_input, saved_pre, grad_act)
    return plain(saved_input, saved_pre, grad_act)


def solution(mesh):
    spec = P(("groups", "dp"), "tensor")
    out = P("tensor", ("groups", "dp"), None)
    return jax.shard_map(
        on_device, mesh=mesh, in_specs=(spec, spec, spec), out_specs=(out, out), check_vma=False
    )
```

```python
import functools
import math

import jax
import jax.numpy as jnp
from jax import lax
from jax.experimental import pallas as pl
from jax.experimental.pallas import tpu as pltpu
from jax.sharding import PartitionSpec as P

D = 5120
FFW = 10240
B = 128
H = B // 2


def gelu_slope(value):
    return (
        0.5 * (1.0 + lax.erf(value * 0.7071067811865476))
        + value * jnp.exp(-0.5 * value * value) * 0.3989422804014327
    )


def local_blocks(matrix, block, total):
    tokens, width = matrix.shape
    pieces = matrix.reshape(tokens, width // block, block)
    cov = jnp.einsum("tkb,tkc->kbc", pieces, pieces, preferred_element_type=jnp.float32)
    return cov.reshape(width, block) / total


def owned_unit(owned, block):
    count = owned.shape[0]
    rows = lax.axis_index("dp") * count + jnp.arange(count, dtype=jnp.int32)
    cols = jnp.arange(block, dtype=jnp.int32)
    return (cols[None, :] == (rows % block)[:, None]).astype(jnp.float32)


def plain(saved_input, saved_pre, grad_act):
    total = jnp.float32(saved_input.shape[0] * lax.axis_size("dp"))
    slope = gelu_slope(saved_pre.astype(jnp.float32))
    grad_pre = (grad_act.astype(jnp.float32) * slope).astype(jnp.bfloat16)
    terms_a = local_blocks(saved_input, B, total)
    terms_g = local_blocks(grad_pre, B, total)
    owned_a = lax.psum_scatter(terms_a, "dp", scatter_dimension=0, tiled=True)
    owned_g = lax.psum_scatter(terms_g, "dp", scatter_dimension=0, tiled=True)
    unit_a = owned_unit(owned_a, B)
    unit_g = owned_unit(owned_g, B)
    trace_a, trace_g = lax.psum(
        (jnp.sum(owned_a * unit_a), jnp.sum(owned_g * unit_g)), ("dp", "tensor")
    )
    ratio = jnp.sqrt(trace_a / D / (trace_g / FFW))
    damp = jnp.sqrt(jnp.float32(0.1))
    return (
        (owned_a + ratio * damp * unit_a)[None],
        (owned_g + damp / ratio * unit_g)[None],
    )


EDGE = 8
SLOTS = 8
X, NEAR, FAR = 0, 1, 2
KINDS = (((NEAR, X, FAR), (NEAR, X, FAR)), ((X, NEAR, FAR), (X, NEAR, FAR)))
NOTES = len(KINDS) * SLOTS

WEIGHTS = {((0, 1), 2): 2 * 10**9}


def split_rows(count):
    return count // B, (count % B) // H


def has_edge(pieces, k):
    return all(later[3] != pieces[k][3] for later in pieces[k + 1 :])


def piece_rows(pieces, k):
    a_blocks, a_half, g_blocks, _ = pieces[k]
    rows = (len(a_blocks) + len(g_blocks)) * H + a_half * (H * 3 // 4)
    return rows + (EDGE if has_edge(pieces, k) else 0)


def corner_indices(pieces, k):
    parts = [len(a) + a_half + len(g) if kind == pieces[k][3] else 0 for a, a_half, g, kind in pieces]
    return iter(range(sum(parts[:k]), sum(parts[: k + 1])))


def iotas(rows):
    shape = (rows, B)
    return lax.broadcasted_iota(jnp.int32, shape, 0), lax.broadcasted_iota(jnp.int32, shape, 1)


def slot_owner(slot, orders):
    core = lax.axis_index("tensor")
    mask = 0
    for stage, (one, other) in enumerate(zip(*orders)):
        mask = mask | (((slot >> (2 - stage)) & 1) << (one + core * (other - one)))
    return lax.axis_index("dp") ^ mask


def lanes(start, size):
    return pl.ds(start if isinstance(start, int) else pl.multiple_of(start, B), size)


FIRST = 4 * 10**9


def pack_body(pieces, items, count_a, count_g, fresh, *refs):
    n = len(items)
    if fresh:
        held, refs = refs[:1], refs[1:]
    else:
        notes_in, held, refs = refs[0], refs[1:4], refs[4:]
    outs, notes = refs[:n], refs[n]
    full, half = split_rows(count_a)
    slots = SLOTS // 2
    split = [(i, k, first, slot) for i, (k, first) in enumerate(items) for slot in range(slots)]

    def read(i, start):
        return held[i][:, pl.ds(pl.multiple_of(start, B), B)]

    row, col = iotas(H)
    low = col < row
    diag_low, diag_high = col == row, col == row + H
    quarter = H // 2
    row_q, col_q = row[:quarter], col[:quarter]
    note_row, _ = iotas(EDGE)
    zero = jnp.zeros((H, B), jnp.float32)
    traces = [zero, zero]
    tiles = {}

    def cov(part):
        return lax.dot_general(
            part, part, (((0,), (0,)), ((), ())), preferred_element_type=jnp.float32
        )

    def note(slot, index, corner, natural):
        line = jnp.sum(corner, axis=0, keepdims=True)
        if index % 2 != natural:
            line = pltpu.roll(line, H, 1)
        tiles[slot] = tiles[slot] + jnp.where(note_row == index // 2, line, 0.0)

    def fold(block, slot, index, which):
        top, bottom = block[:H], block[H:]
        corner = jnp.where(diag_high, bottom, zero)
        note(slot, index, corner, 0)
        traces[which] = traces[which] + corner + jnp.where(diag_low, top, zero)
        return jnp.where(low, pltpu.roll(bottom, H, 1), top)

    def fold_half(block, odd, slot, index):
        part = jnp.where(odd == 1, pltpu.roll(block[H:], H, 1), block[:H])
        traces[0] = traces[0] + jnp.where(diag_low, part, zero)
        upper, lower = part[:quarter], part[quarter:]
        corner = jnp.where(col_q == row_q + quarter, lower, 0.0)
        note(slot, index, corner, 1)
        square = jnp.where(col_q < row_q, pltpu.roll(lower, B - quarter, 1), upper)
        rest = lower.reshape(2, quarter // 2, B)
        rest = jnp.where(col[: quarter // 2] < H, pltpu.roll(rest[1], H, 1), rest[0])
        return square, rest

    def a_parts(out, k, first, slot, index):
        a_blocks, a_half, _, kind = pieces[k]
        owner = slot_owner(first + slot, KINDS[kind])
        here, odd = kind * SLOTS + first + slot, owner & half
        base = (owner >> half) * (full * (1 + half) + half) * B
        at = 0
        for b in a_blocks:
            block = cov(read(0, base + (odd * (full + 1) + b) * B))
            out[slot, at : at + H, :] = fold(block, here, next(index), 0)
            at = at + H
        if a_half:
            block = cov(read(0, base + full * B))
            square, rest = fold_half(block, odd, here, next(index))
            out[slot, at : at + quarter, :] = square
            out[slot, at + quarter : at + quarter * 3 // 2, :] = rest
            at = at + quarter * 3 // 2
        return at

    def g_parts(out, k, first, slot, index, at):
        _, _, g_blocks, kind = pieces[k]
        here = kind * SLOTS + first + slot
        owner = slot_owner(first + slot, KINDS[kind])
        for b in g_blocks:
            start = owner * count_g + b * B
            value, grad = read(1, start).astype(jnp.float32), read(2, start).astype(jnp.float32)
            block = cov((grad * gelu_slope(value)).astype(jnp.bfloat16))
            out[slot, at : at + H, :] = fold(block, here, next(index), 1)
            at = at + H
        return at

    for i, k, first, slot in split:
        here = pieces[k][3] * SLOTS + first + slot
        if here not in tiles:
            tiles[here] = jnp.zeros((EDGE, B), jnp.float32) if fresh else notes_in[here]
        index = corner_indices(pieces, k)
        at = a_parts(outs[i], k, first, slot, index)
        at = g_parts(outs[i], k, first, slot, index, at)
        if has_edge(pieces, k):
            outs[i][slot, at:, :] = tiles[here]

    for slot in range(NOTES):
        if slot in tiles:
            notes[slot] = tiles[slot]
        else:
            notes[slot] = jnp.zeros((EDGE, B), jnp.float32) if fresh else notes_in[slot]
    lines = [jnp.sum(trace, axis=0, keepdims=True) for trace in traces]
    tile = jnp.where(note_row == 0, lines[0], jnp.where(note_row == 1, lines[1], 0.0))
    notes[NOTES] = tile if fresh else notes_in[NOTES] + tile


def pack(arrays, pieces, items, count_a, count_g, notes):
    slots = SLOTS // 2
    fresh = notes is None
    out_shape = [
        jax.ShapeDtypeStruct((slots, piece_rows(pieces, k), B), jnp.float32) for k, _ in items
    ]
    out_shape.append(jax.ShapeDtypeStruct((NOTES + 1, EDGE, B), jnp.float32))
    args = arrays[:1] if fresh else [notes, *arrays]
    outs = pl.pallas_call(
        functools.partial(pack_body, pieces, items, count_a, count_g, fresh),
        in_specs=[pl.BlockSpec(memory_space=pltpu.VMEM)] * len(args),
        out_specs=[pl.BlockSpec(memory_space=pltpu.VMEM)] * len(out_shape),
        out_shape=out_shape,
        compiler_params=pltpu.CompilerParams(vmem_limit_bytes=32 * 2**20),
        cost_estimate=pl.CostEstimate(
            flops=FIRST if fresh else 1, bytes_accessed=1, transcendentals=0
        ),
    )(*args)
    n = len(items)
    return outs[:n], outs[n]


def halve_body(n, terms, came, put, merged, *refs):
    keeps, gots, refs = refs[:n], refs[n : 2 * n], refs[2 * n :]
    terms, kept, refs = refs[:terms], refs[terms : terms + n], refs[terms + n :]
    sent, sums = (refs[:1], refs[1:]) if merged else (refs[:n], refs[n:])
    if merged:
        ends = [sum(ref.shape[1] for ref in kept[: k + 1]) for k in range(n)]
        sent = [
            sent[0].at[:, end - ref.shape[1] : end, :] for end, ref in zip(ends, kept)
        ]
    for k in range(n):
        half = kept[k].shape[0]
        kept[k][...] = keeps[k][:half] + gots[k][:half]
        sent[k][...] = keeps[k][half:] + gots[k][half:]
    if terms:
        value = sum((term[...] for term in terms[1:]), terms[0][...])
        for k in came:
            value = value + gots[k][0, -2:, :]
        for out in sums:
            out[...] = value
        for k in put:
            rows = kept[k].shape[1]
            kept[k][0, rows - 2 :, :] = value
            sent[k][0, rows - 2 :, :] = value


def halve(keeps, gots, terms=(), came=(), put=(), merged=False, weight=1):
    n = len(keeps)
    emit = bool(terms) and not put
    args = [*keeps, *gots, *terms]
    kept = [(keep.shape[0] // 2, *keep.shape[1:]) for keep in keeps]
    sent = [(kept[0][0], sum(shape[1] for shape in kept), B)] if merged else kept
    shapes = [*kept, *sent, *([(2, B)] * emit)]
    outs = pl.pallas_call(
        functools.partial(halve_body, n, len(terms), came, put, merged),
        in_specs=[pl.BlockSpec(memory_space=pltpu.VMEM)] * len(args),
        out_specs=[pl.BlockSpec(memory_space=pltpu.VMEM)] * len(shapes),
        out_shape=[jax.ShapeDtypeStruct(shape, jnp.float32) for shape in shapes],
        compiler_params=pltpu.CompilerParams(vmem_limit_bytes=32 * 2**20),
        cost_estimate=pl.CostEstimate(flops=weight, bytes_accessed=1, transcendentals=0),
    )(*args)
    return outs[:n], outs[n : n + len(sent)], outs[n + len(sent) :]


def mean_of(value, total):
    return value * (1.0 / total) if math.frexp(total)[0] == 0.5 else value / total


def turn(folded):
    return jnp.concatenate([folded] * (B // folded.shape[0]), axis=0).T


def unfold(folded):
    row, col = iotas(H)
    turned = turn(folded)
    last = pltpu.roll(jnp.where(col < row, folded, turned[:H]), H, 1)
    return jnp.where(col < row, turned[:H], folded), jnp.where(col < H, turned[H:], last)


def unfold_half(square, rest, odd):
    quarter = H // 2
    row, col = iotas(quarter)
    turned = turn(square)
    upper = jnp.where(col < row, turned[:quarter], square)
    last = pltpu.roll(jnp.where(col < row, square, turned[:quarter]), quarter, 1)
    lower = jnp.where(col < quarter, turned[quarter:H], last)
    rest = jnp.concatenate([rest, pltpu.roll(rest, H, 1)], axis=0)
    part = jnp.concatenate([upper, jnp.where(col < H, lower, rest)], axis=0)
    return (jnp.where(odd == 1, pltpu.roll(part, H, 1), part),)


def places(pieces, ks, count_a):
    full, half = split_rows(count_a)
    odd = lax.axis_index("dp") & half
    for k in ks:
        a_blocks, a_half, g_blocks, kind = pieces[k]
        index = corner_indices(pieces, k)
        for b in a_blocks:
            start = pl.multiple_of(b * B + odd * H, H) if half else b * B
            yield k, 0, start, H, next(index)
        if a_half:
            yield k, 0, pl.multiple_of((1 - odd) * full * B, H), H * 3 // 4, next(index)
        for b in g_blocks:
            yield k, 1, b * B, H, next(index)


def row_begins(pieces, ks):
    rows = [piece_rows(pieces, k) for k in ks]
    return {k: sum(rows[:i]) for i, k in enumerate(ks)}


def unfolded(pieces, ks, count_a, total, owns, got):
    odd = lax.axis_index("dp") & 1
    at = dict.fromkeys(ks, 0)
    begins = row_begins(pieces, ks)

    def take(k, rows):
        begin = at[k]
        at[k] = begin + rows
        mine = owns[ks.index(k)][0, begin : begin + rows, :]
        begin = begin + begins[k]
        return mean_of(mine + got[0, begin : begin + rows, :], total)

    for place in places(pieces, ks, count_a):
        k, _, _, rows, _ = place
        if rows == H:
            yield place, unfold(take(k, H))
        else:
            yield place, unfold_half(take(k, H // 2), take(k, H // 4), odd)


def early_body(pieces, ks, count_a, total, *refs):
    n = len(ks)
    owns, got, outs = refs[:n], refs[n], refs[n + 1 :]
    for (_, which, start, _, _), halves in unfolded(pieces, ks, count_a, total, owns, got):
        for i, value in enumerate(halves):
            outs[which][pl.ds(start + i * H, H), :] = value


def finish_body(pieces, early, late, count_a, total, *refs):
    n = len(late)
    owns, got, firsts, outs = refs[:n], refs[n], refs[n + 1 : n + 3], refs[n + 3 : n + 5]
    made, sem = refs[n + 5 : n + 7], refs[n + 7]
    _, half = split_rows(count_a)
    odd = lax.axis_index("dp") & half
    row, col = iotas(H)

    edges = {}
    for k, own in zip(late, owns):
        end = row_begins(pieces, late)[k] + piece_rows(pieces, k)
        edge = mean_of(own[0, -EDGE:, :] + got[0, end - EDGE : end, :], total)
        edges[pieces[k][3]] = (edge, pltpu.roll(edge, H, 1))
    sums = jnp.sum(edge[-2:], axis=1, keepdims=True)
    ratio = jnp.sqrt(sums[0:1] / D / (sums[1:2] / FFW))
    damp = jnp.sqrt(jnp.full((1, 1), 0.1, jnp.float32))
    shifts = (ratio * damp, damp / ratio)

    def corner(kind, index, natural):
        line = index // 2
        return edges[kind][0 if index % 2 == natural else 1][line : line + 1]

    copies = []

    def give(place, halves):
        k, which, start, rows, index = place
        shift, kind = shifts[which], pieces[k][3]
        if rows == H:
            top, bottom = halves
            top = top + jnp.where(col == row, shift, 0.0)
            bottom = jnp.where(col == row + H, corner(kind, index, 0) + shift, bottom)
            halves = (top, bottom)
        else:
            line = corner(kind, index, 1)
            line = jnp.where(odd == 1, pltpu.roll(line, H, 1), line) + shift
            diagonal = col == row + odd * H
            value = halves[0] + jnp.where(diagonal, shift, 0.0)
            last = jnp.logical_and(diagonal, row >= H // 2)
            halves = (jnp.where(last, line, value),)
        for i, value in enumerate(halves):
            made[which][pl.ds(start + i * H, H), :] = value
        part = pl.ds(start, len(halves) * H)
        copy = pltpu.make_async_copy(
            made[which].at[part], outs[which].at[part], sem.at[len(copies)]
        )
        copy.start()
        copies.append(copy)

    for place in places(pieces, early, count_a):
        _, which, start, rows, _ = place
        count = 2 if rows == H else 1
        give(place, [firsts[which][pl.ds(start + i * H, H), :] for i in range(count)])
    for place, halves in unfolded(pieces, late, count_a, total, owns, got):
        give(place, halves)
    for copy in copies:
        copy.wait()


def unfold_early(pieces, ks, owns, got, count_a, count_g, total):
    args = (*owns, got)
    return pl.pallas_call(
        functools.partial(early_body, pieces, ks, count_a, total),
        in_specs=[pl.BlockSpec(memory_space=pltpu.VMEM)] * len(args),
        out_specs=[pl.BlockSpec(memory_space=pltpu.VMEM)] * 2,
        out_shape=[
            jax.ShapeDtypeStruct((count_a, B), jnp.float32),
            jax.ShapeDtypeStruct((count_g, B), jnp.float32),
        ],
        compiler_params=pltpu.CompilerParams(vmem_limit_bytes=32 * 2**20),
        cost_estimate=pl.CostEstimate(flops=4 * 10**9, bytes_accessed=1, transcendentals=0),
    )(*args)


def finish(pieces, early, late, owns, got, first, count_a, count_g, total):
    args = (*owns, got, *first)
    parts = sum(len(a_blocks) + a_half + len(g_blocks) for a_blocks, a_half, g_blocks, _ in pieces)
    return pl.pallas_call(
        functools.partial(finish_body, pieces, early, late, count_a, total),
        in_specs=[pl.BlockSpec(memory_space=pltpu.VMEM)] * len(args),
        out_specs=[pl.BlockSpec(memory_space=pltpu.HBM)] * 2,
        out_shape=[
            jax.ShapeDtypeStruct((count_a, B), jnp.float32),
            jax.ShapeDtypeStruct((count_g, B), jnp.float32),
        ],
        scratch_shapes=[
            pltpu.VMEM((count_a, B), jnp.float32),
            pltpu.VMEM((count_g, B), jnp.float32),
            pltpu.SemaphoreType.DMA((parts,)),
        ],
        compiler_params=pltpu.CompilerParams(vmem_limit_bytes=32 * 2**20),
    )(*args)


def swap(value, partner):
    dp, tensor = lax.axis_size("dp"), lax.axis_size("tensor")
    pairs = []
    for i in range(dp):
        for j in range(tensor):
            other = partner(i, j)
            pairs.append((i * tensor + j, other[0] * tensor + other[1]))
    return lax.ppermute(value, ("dp", "tensor"), pairs)


def along(stage, kind):
    return lambda i, j: (i ^ (1 << KINDS[kind][j][stage]), j)


def packed(saved_input, saved_pre, grad_act):
    dp = lax.axis_size("dp")
    total = float(saved_input.shape[0] * dp)
    count_a = saved_input.shape[1] // dp
    count_g = saved_pre.shape[1] // dp
    full_a, half_a = split_rows(count_a)
    full_g, _ = split_rows(count_g)
    some = 1 + (full_g - 1) // 2
    pieces = (
        (tuple(range(full_a)), 0, (), 0),
        ((), half_a, (0,), 1),
        ((), 0, tuple(range(1, some)), 1),
        ((), 0, tuple(range(some, full_g)), 0),
    )
    arrays = (saved_input, saved_pre, grad_act)
    keep, send = 0, SLOTS // 2
    early, late = (0, 1), (2, 3)
    keeps, gots, notes = {}, {}, None

    def pack_next(first, ks):
        nonlocal notes
        items = tuple((k, first) for k in ks)
        parts, notes = pack(arrays, pieces, items, count_a, count_g, notes)
        return dict(zip(ks, parts))

    def exchange(parts, stage):
        for k, part in parts.items():
            gots[k] = swap(part, along(stage, pieces[k][3]))

    def halve_pair(ks, stage, **kinds):
        own, parts, others = halve(
            [keeps[k] for k in ks], [gots[k] for k in ks], merged=stage == 2,
            weight=WEIGHTS.get((ks, stage), 1), **kinds
        )
        keeps.update(zip(ks, own))
        if stage == 2:
            gots[ks] = swap(parts[0], lambda i, j: (i ^ (1 << FAR), j))
        else:
            exchange(dict(zip(ks, parts)), stage)
        return others

    exchange(pack_next(send, early[:1]), 0)
    exchange(pack_next(send, early[1:]), 0)
    exchange(pack_next(send, late), 0)
    keeps.update(pack_next(keep, early))
    keeps.update(pack_next(keep, late))

    trace = notes[NOTES, :2, :]
    trace = trace + swap(trace, lambda i, j: (i, j ^ 1))
    across = swap(trace, lambda i, j: (i ^ (1 << X) ^ (1 << NEAR), j))
    halve_pair(early, 1)
    halve_pair(late, 1, terms=(trace,), put=(0, 1))
    (trace,) = halve_pair(early, 2, terms=(trace, across))
    halve_pair(late, 2, terms=(trace,), came=(0, 1), put=(0, 1))

    def both(ks):
        return [keeps[k] for k in ks], gots[ks]

    first = unfold_early(pieces, early, *both(early), count_a, count_g, total)
    a_factor, g_factor = finish(
        pieces, early, late, *both(late), first, count_a, count_g, total
    )
    return a_factor[None], g_factor[None]


def fits(count_a, count_g):
    (full_a, half_a), full_g = split_rows(count_a), count_g // B
    if count_a % H or count_g % B or full_a < 1 or full_g < 3:
        return False
    return full_a + half_a + full_g <= 2 * (EDGE - 2)


def on_device(saved_input, saved_pre, grad_act):
    dp = lax.axis_size("dp")
    count_a = saved_input.shape[1] // dp
    count_g = saved_pre.shape[1] // dp
    if dp == SLOTS and lax.axis_size("tensor") == 2 and fits(count_a, count_g):
        return packed(saved_input, saved_pre, grad_act)
    return plain(saved_input, saved_pre, grad_act)


def solution(mesh):
    spec = P(("groups", "dp"), "tensor")
    out = P("tensor", ("groups", "dp"), None)
    return jax.shard_map(
        on_device, mesh=mesh, in_specs=(spec, spec, spec), out_specs=(out, out), check_vma=False
    )
```
